32 devices in a mesh: dp: 4 (over y, core), fsdp: 8 (over z, x).
Axes of the slice: x: 2, y: 2, z: 4, core: 2. Of those that a mesh axis runs over, the one named last changes fastest.
Arguments:
- features: bfloat16 [1536, 49, 2048], P(('dp', 'fsdp')), may hold values from -15 to 15
- view_order: int32 [32, 48], P(('dp', 'fsdp')), may hold values from 0 to 47, each once within a row
- conv_one: float32 [2048, 512], P('fsdp', 'dp'), may hold values from -0.125 to 0.125
- conv_two: float32 [4608, 512], P('fsdp', 'dp'), may hold values from -0.09375 to 0.09375
- conv_three: float32 [512, 2048], P('fsdp', 'dp'), may hold values from -0.25 to 0.25
- proj_one: float32 [2048, 1024], P('fsdp', 'dp'), may hold values from -0.125 to 0.125
- proj_two: float32 [1024, 128], P('fsdp', 'dp'), may hold values from -0.1875 to 0.1875
- norm_params: float32 [2, 4096], P(None, ('dp', 'fsdp')), may hold values from -2 to 3, as said below
- first_conv_one: float32 [2048, 512], P('fsdp', 'dp'), may hold values from -6.1035156e-05 to 6.1035156e-05
- first_conv_two: float32 [4608, 512], P('fsdp', 'dp'), may hold values from -6.1035156e-05 to 6.1035156e-05
- first_conv_three: float32 [512, 2048], P('fsdp', 'dp'), may hold values from -6.1035156e-05 to 6.1035156e-05
- first_proj_one: float32 [2048, 1024], P('fsdp', 'dp'), may hold values from -6.1035156e-05 to 6.1035156e-05
- first_proj_two: float32 [1024, 128], P('fsdp', 'dp'), may hold values from -6.1035156e-05 to 6.1035156e-05
- first_norm: float32 [2, 4096], P(None, ('dp', 'fsdp')), may hold values from -6.1035156e-05 to 6.1035156e-05
- second_conv_one: float32 [2048, 512], P('fsdp', 'dp'), may hold values from 7.4706436e-13 to 1.195303e-11
- second_conv_two: float32 [4608, 512], P('fsdp', 'dp'), may hold values from 7.4706436e-13 to 1.195303e-11
- second_conv_three: float32 [512, 2048], P('fsdp', 'dp'), may hold values from 7.4706436e-13 to 1.195303e-11
- second_proj_one: float32 [2048, 1024], P('fsdp', 'dp'), may hold values from 7.4706436e-13 to 1.195303e-11
- second_proj_two: float32 [1024, 128], P('fsdp', 'dp'), may hold values from 7.4706436e-13 to 1.195303e-11
- second_norm: float32 [2, 4096], P(None, ('dp', 'fsdp')), may hold values from 7.4706436e-13 to 1.195303e-11
Outputs:
- loss: float32 [], replicated
- input_grad: float32 [1536, 49, 2048], P(('dp', 'fsdp'))
- grad_norm: float32 [], replicated
- new_conv_one: float32 [2048, 512], P('fsdp', 'dp')
- new_conv_two: float32 [4608, 512], P('fsdp', 'dp')
- new_conv_three: float32 [512, 2048], P('fsdp', 'dp')
- new_proj_one: float32 [2048, 1024], P('fsdp', 'dp')
- new_proj_two: float32 [1024, 128], P('fsdp', 'dp')
- new_norm: float32 [2, 4096], P(None, ('dp', 'fsdp'))
- new_first_conv_one: float32 [2048, 512], P('fsdp', 'dp')
- new_first_conv_two: float32 [4608, 512], P('fsdp', 'dp')
- new_first_conv_three: float32 [512, 2048], P('fsdp', 'dp')
- new_first_proj_one: float32 [2048, 1024], P('fsdp', 'dp')
- new_first_proj_two: float32 [1024, 128], P('fsdp', 'dp')
- new_first_norm: float32 [2, 4096], P(None, ('dp', 'fsdp'))
- new_second_conv_one: float32 [2048, 512], P('fsdp', 'dp')
- new_second_conv_two: float32 [4608, 512], P('fsdp', 'dp')
- new_second_conv_three: float32 [512, 2048], P('fsdp', 'dp')
- new_second_proj_one: float32 [2048, 1024], P('fsdp', 'dp')
- new_second_proj_two: float32 [1024, 128], P('fsdp', 'dp')
- new_second_norm: float32 [2, 4096], P(None, ('dp', 'fsdp'))
The draws below stay inside these ranges and needn't reach their ends.
Inputs may be any that keep to these rules, and one draw needn't show every extreme that they name: `view_order`: in row d, entry j = 2 i + k says that slot j of that device's views holds view k of image d * 24 + i. `norm_params`: row 0 is positive.
All inputs are finite; a program needn't handle non-finite values.
Results may differ from the reference program's by a relative error of at most 0.039.
Values may be sent and summed in bfloat16 or wider, within the bound.
A program may use at most 384 MiB of HBM per device.

```python
import math
import jax
import jax.numpy as jnp
from jax import lax

C_IN = 2048
C_MID = 512
P_HID = 1024
P_OUT = 128
SIDE = 7
STEP = 10
VIEWS_DEV = 48
PIX = 49
VIEWS = 1536
IMAGES = 768
NORM_CH = 4096
NPARAM = 6692864
DEVICES = 32


def draw_features(key, part):
    key = jax.random.fold_in(key, 11)
    position = jnp.arange(C_IN, dtype=jnp.float32) / (C_IN - 1)
    channel_ramp = 0.6 + 1.2 * position
    values = jnp.clip(jax.random.normal(key, (VIEWS, PIX, C_IN), jnp.float32), -6.0, 6.0)
    return (values * channel_ramp).astype(jnp.bfloat16)


def draw_norm_params(key, part):
    key = jax.random.fold_in(key, 12)
    gain_key, shift_key = jax.random.split(key)
    position = jnp.arange(NORM_CH, dtype=jnp.int32)
    segment_start = jnp.where(position < C_MID, 0, jnp.where(position < 2 * C_MID, C_MID, jnp.where(position < 2 * C_MID + C_IN, 2 * C_MID, 2 * C_MID + C_IN)))
    segment_width = jnp.where(position < 2 * C_MID, C_MID, jnp.where(position < 2 * C_MID + C_IN, C_IN, P_HID))
    fraction = (position - segment_start).astype(jnp.float32) / (segment_width - 1).astype(jnp.float32)
    gain_row = (0.6 + 1.2 * fraction) * (1.0 + 0.1 * jnp.clip(jax.random.normal(gain_key, (NORM_CH,), jnp.float32), -3.0, 3.0))
    shift_row = 0.3 * jnp.clip(jax.random.normal(shift_key, (NORM_CH,), jnp.float32), -6.0, 6.0)
    return jnp.stack([gain_row, shift_row]).astype(jnp.float32)


def steps_of(stream_key, dims, cuts, smallest, largest):
    def one(dim, parts):
        draws = jax.random.uniform(jax.random.fold_in(jax.random.fold_in(stream_key, 6), dim), (parts,), jnp.float32, smallest / len(cuts), largest / len(cuts))
        return jnp.repeat(jnp.exp(draws), dims[dim] // parts).reshape((-1,) + (1,) * (len(dims) - dim - 1))

    level = one(*cuts[0])
    for cut in cuts[1:]:
        level = level * one(*cut)
    return level


def bell_draw(rng, extent, scale, most, cuts=(), kind=jnp.bfloat16):
    values = jax.random.normal(rng, extent, jnp.float32) * scale
    if len(cuts) > 0:
        values = steps_of(rng, extent, cuts, -0.22, 0.18) * values
    return jnp.clip(values, min=-most, max=most).astype(kind)


def setup_inputs(seed: int = 0) -> dict:
    key_list = jax.random.split(jax.random.key(seed), 21)
    features = draw_features(jax.random.fold_in(key_list[20], 71), 0)
    view_order = jax.vmap(lambda own: jax.random.permutation(own, VIEWS_DEV))(jax.random.split(key_list[1], DEVICES)).reshape((DEVICES, VIEWS_DEV)).astype(jnp.int32)
    conv_one = bell_draw(key_list[2], (C_IN, C_MID), C_IN ** -0.5, 0.125, ((0, 8), (1, 4)), jnp.float32)
    conv_two = bell_draw(key_list[3], (9 * C_MID, C_MID), (9 * C_MID) ** -0.5, 0.09375, ((0, 8), (1, 4)), jnp.float32)
    conv_three = bell_draw(key_list[4], (C_MID, C_IN), C_MID ** -0.5, 0.25, ((0, 8), (1, 4)), jnp.float32)
    proj_one = bell_draw(key_list[5], (C_IN, P_HID), C_IN ** -0.5, 0.125, ((0, 8), (1, 4)), jnp.float32)
    proj_two = bell_draw(key_list[6], (P_HID, P_OUT), P_HID ** -0.5, 0.1875, ((0, 8), (1, 4)), jnp.float32)
    norm_params = draw_norm_params(jax.random.fold_in(key_list[20], 71), 0)
    first_conv_one = bell_draw(key_list[8], (C_IN, C_MID), (0.0111 * NPARAM ** -0.5), 6.103515625e-05, ((0, 8), (1, 4)), jnp.float32)
    first_conv_two = bell_draw(key_list[9], (9 * C_MID, C_MID), (0.0111 * NPARAM ** -0.5), 6.103515625e-05, ((0, 8), (1, 4)), jnp.float32)
    first_conv_three = bell_draw(key_list[10], (C_MID, C_IN), (0.0111 * NPARAM ** -0.5), 6.103515625e-05, ((0, 8), (1, 4)), jnp.float32)
    first_proj_one = bell_draw(key_list[11], (C_IN, P_HID), (0.0111 * NPARAM ** -0.5), 6.103515625e-05, ((0, 8), (1, 4)), jnp.float32)
    first_proj_two = bell_draw(key_list[12], (P_HID, P_OUT), (0.0111 * NPARAM ** -0.5), 6.103515625e-05, ((0, 8), (1, 4)), jnp.float32)
    first_norm = bell_draw(key_list[13], (2, NORM_CH), (0.0111 * NPARAM ** -0.5), 6.103515625e-05, ((1, 32),), jnp.float32)
    second_conv_one = jnp.clip(jnp.exp(math.log(1.195302971185308e-11) - 2.7725887 * jax.random.uniform(key_list[14], (C_IN, C_MID), jnp.float32) ** steps_of(key_list[14], (C_IN, C_MID), ((0, 8), (1, 4)), -0.2, 0.2)), 7.470643569908175e-13, 1.195302971185308e-11)
    second_conv_two = jnp.clip(jnp.exp(math.log(1.195302971185308e-11) - 2.7725887 * jax.random.uniform(key_list[15], (9 * C_MID, C_MID), jnp.float32) ** steps_of(key_list[15], (9 * C_MID, C_MID), ((0, 8), (1, 4)), -0.2, 0.2)), 7.470643569908175e-13, 1.195302971185308e-11)
    second_conv_three = jnp.clip(jnp.exp(math.log(1.195302971185308e-11) - 2.7725887 * jax.random.uniform(key_list[16], (C_MID, C_IN), jnp.float32) ** steps_of(key_list[16], (C_MID, C_IN), ((0, 8), (1, 4)), -0.2, 0.2)), 7.470643569908175e-13, 1.195302971185308e-11)
    second_proj_one = jnp.clip(jnp.exp(math.log(1.195302971185308e-11) - 2.7725887 * jax.random.uniform(key_list[17], (C_IN, P_HID), jnp.float32) ** steps_of(key_list[17], (C_IN, P_HID), ((0, 8), (1, 4)), -0.2, 0.2)), 7.470643569908175e-13, 1.195302971185308e-11)
    second_proj_two = jnp.clip(jnp.exp(math.log(1.195302971185308e-11) - 2.7725887 * jax.random.uniform(key_list[18], (P_HID, P_OUT), jnp.float32) ** steps_of(key_list[18], (P_HID, P_OUT), ((0, 8), (1, 4)), -0.2, 0.2)), 7.470643569908175e-13, 1.195302971185308e-11)
    second_norm = jnp.clip(jnp.exp(math.log(1.195302971185308e-11) - 2.7725887 * jax.random.uniform(key_list[19], (2, NORM_CH), jnp.float32) ** steps_of(key_list[19], (2, NORM_CH), ((1, 32),), -0.2, 0.2)), 7.470643569908175e-13, 1.195302971185308e-11)
    return {"features": features, "view_order": view_order, "conv_one": conv_one, "conv_two": conv_two, "conv_three": conv_three, "proj_one": proj_one, "proj_two": proj_two, "norm_params": norm_params, "first_conv_one": first_conv_one, "first_conv_two": first_conv_two, "first_conv_three": first_conv_three, "first_proj_one": first_proj_one, "first_proj_two": first_proj_two, "first_norm": first_norm, "second_conv_one": second_conv_one, "second_conv_two": second_conv_two, "second_conv_three": second_conv_three, "second_proj_one": second_proj_one, "second_proj_two": second_proj_two, "second_norm": second_norm}


@jax.custom_vjp
def low(v):
    return lax.optimization_barrier(v.astype(jnp.bfloat16)).astype(jnp.float32)

@jax.custom_vjp
def low_back(v):
    return v

def low_keep(v):
    return (low(v), None)

def low_pass(kept, grad):
    return (grad,)

def back_keep(v):
    return (v, None)

def back_low(kept, grad):
    return (low(grad),)
low.defvjp(low_keep, low_pass)
low_back.defvjp(back_keep, back_low)
highest = lax.Precision.HIGHEST
norm_epsilon = 1e-05
ridge_term = 0.01
clip_level = 0.1
beta_first = 0.9
beta_second = 0.999
adam_epsilon = 1e-08
decay_rate = 0.05
norm_rate = 0.5

def gelu_exact(values):
    return jax.nn.gelu(values, approximate=False)

def batch_norm(hidden, gain_part, shift_part):
    mean_value = lax.optimization_barrier(jnp.mean(hidden, axis=0))
    square_mean = lax.optimization_barrier(jnp.mean(hidden * hidden, axis=0))
    scaling = lax.rsqrt(square_mean - mean_value * mean_value + norm_epsilon)
    return (hidden - mean_value) * scaling * gain_part + shift_part

def conv_spatial(activation, weight):
    channels = activation.shape[-1]
    picture = activation.reshape(-1, SIDE, SIDE, channels)
    padded = jnp.pad(picture, ((0, 0), (1, 1), (1, 1), (0, 0)))
    result = jnp.zeros((picture.shape[0] * PIX, weight.shape[1]), jnp.float32)
    for vertical in range(3):
        for lateral in range(3):
            window = padded[:, vertical:vertical + SIDE, lateral:lateral + SIDE, :].reshape(-1, channels)
            offset = (3 * vertical + lateral) * channels
            result = result + jnp.dot(window, weight[offset:offset + channels], precision=highest)
    return result

def whiten_view(embeds):
    mean_embed = lax.optimization_barrier(jnp.mean(embeds, axis=0))
    second_moment = jnp.dot(embeds.T, embeds, precision=highest) / IMAGES
    covariance = second_moment - jnp.outer(mean_embed, mean_embed) + ridge_term * jnp.eye(P_OUT, dtype=jnp.float32)
    factor = jnp.linalg.cholesky(covariance)
    whitened = lax.linalg.triangular_solve(factor, (embeds - mean_embed).T, left_side=True, lower=True)
    return whitened * lax.rsqrt(lax.optimization_barrier(jnp.mean(whitened * whitened, axis=0)) + norm_epsilon)

def adam_update(weight, moment_one, moment_two, gradient, step_rate, weight_decay):
    first_new = beta_first * moment_one + (1.0 - beta_first) * gradient
    second_new = beta_second * moment_two + (1.0 - beta_second) * gradient * gradient
    first_hat = first_new / (1.0 - beta_first ** STEP)
    second_hat = second_new / (1.0 - beta_second ** STEP)
    weight_new = weight - step_rate * (first_hat / (jnp.sqrt(second_hat) + adam_epsilon) + weight_decay * weight)
    return (weight_new, first_new, second_new)

def reference(features, view_order, conv_one, conv_two, conv_three, proj_one, proj_two, norm_params, first_conv_one, first_conv_two, first_conv_three, first_proj_one, first_proj_two, first_norm, second_conv_one, second_conv_two, second_conv_three, second_proj_one, second_proj_two, second_norm):
    selector = (view_order[:, :, None] == jnp.arange(VIEWS_DEV, dtype=jnp.int32)[None, None, :]).astype(jnp.float32)
    start_two = C_MID
    start_three = 2 * C_MID
    start_four = 2 * C_MID + C_IN

    def objective_fn(feature_values, weight_one, weight_two, weight_three, weight_four, weight_five, norm_values):
        norm_low = low(norm_values)
        gain_all = norm_low[0]
        shift_all = norm_low[1]
        pixel_rows = feature_values.reshape(VIEWS * PIX, C_IN)
        hidden_one = low_back(jnp.dot(pixel_rows, low(weight_one), precision=highest))
        act_one = low(gelu_exact(batch_norm(hidden_one, gain_all[:start_two], shift_all[:start_two])))
        hidden_two = low_back(conv_spatial(act_one, low(weight_two)))
        act_two = low(gelu_exact(batch_norm(hidden_two, gain_all[start_two:start_three], shift_all[start_two:start_three])))
        hidden_three = low_back(jnp.dot(act_two, low(weight_three), precision=highest))
        block_out = gelu_exact(batch_norm(hidden_three, gain_all[start_three:start_four], shift_all[start_three:start_four]) + pixel_rows)
        pooled = low(lax.optimization_barrier(jnp.mean(block_out.reshape(VIEWS, PIX, C_IN), axis=1)))
        proj_hidden = low_back(jnp.dot(pooled, low(weight_four), precision=highest))
        proj_act = low(gelu_exact(batch_norm(proj_hidden, gain_all[start_four:], shift_all[start_four:])))
        embedding = low_back(jnp.dot(proj_act, low(weight_five), precision=highest))
        sorted_embed = jnp.einsum('bjm,bjp->bmp', selector, embedding.reshape(DEVICES, VIEWS_DEV, P_OUT), precision=highest)
        sorted_embed = sorted_embed.reshape(IMAGES, 2, P_OUT)
        unit_zero = whiten_view(sorted_embed[:, 0])
        unit_one = whiten_view(sorted_embed[:, 1])
        return jnp.sum(lax.optimization_barrier(jnp.mean((unit_zero - unit_one) ** 2, axis=0)))
    masters = (conv_one, conv_two, conv_three, proj_one, proj_two, norm_params)
    objective, pullback = jax.vjp(objective_fn, features.astype(jnp.float32), conv_one, conv_two, conv_three, proj_one, proj_two, norm_params)
    gradients = pullback(jnp.ones((), jnp.float32))
    input_grad = gradients[0]
    param_grads = gradients[1:]
    squares = jnp.float32(0.0)
    for member in param_grads:
        squares = squares + jnp.sum(member * member)
    grad_norm = jnp.sqrt(squares)
    factor = clip_level / jnp.maximum(grad_norm, clip_level)
    step_rates = (C_IN ** (-0.5), (9 * C_MID) ** (-0.5), C_MID ** (-0.5), C_IN ** (-0.5), P_HID ** (-0.5), norm_rate)
    decays = (decay_rate, decay_rate, decay_rate, decay_rate, decay_rate, 0.0)
    firsts = (first_conv_one, first_conv_two, first_conv_three, first_proj_one, first_proj_two, first_norm)
    seconds = (second_conv_one, second_conv_two, second_conv_three, second_proj_one, second_proj_two, second_norm)
    results = [adam_update(masters[place], firsts[place], seconds[place], param_grads[place] * factor, step_rates[place], decays[place]) for place in range(6)]
    return (objective / IMAGES, input_grad, grad_norm, results[0][0], results[1][0], results[2][0], results[3][0], results[4][0], results[5][0], results[0][1], results[1][1], results[2][1], results[3][1], results[4][1], results[5][1], results[0][2], results[1][2], results[2][2], results[3][2], results[4][2], results[5][2])
```

```python
import jax
import jax.numpy as jnp
from jax import lax
from jax.experimental import pallas as pl
from jax.experimental.pallas import tpu as pltpu
from jax.sharding import PartitionSpec as P

C_IN = 2048
C_MID = 512
P_HID = 1024
P_OUT = 128
SIDE = 7
STEP = 10
PIX = 49


highest = lax.Precision.HIGHEST
norm_epsilon = 1e-05
ridge_term = 0.01
clip_level = 0.1
beta_first = 0.9
beta_second = 0.999
adam_epsilon = 1e-08
decay_rate = 0.05
norm_rate = 0.5


def gelu_exact(values):
    return jax.nn.gelu(values, approximate=False)


def gelu_back(values, upstream):
    return jax.vjp(gelu_exact, values)[1](upstream)[0]


def matmul(left, right):
    return jnp.dot(left, right, preferred_element_type=jnp.float32)


def contract_rows(left, right):
    return lax.dot_general(
        left, right, (((0,), (0,)), ((), ())), preferred_element_type=jnp.float32
    )


def contract_cols(left, right):
    return lax.dot_general(
        left, right, (((1,), (1,)), ((), ())), preferred_element_type=jnp.float32
    )


def gather_weights(weight_one, weight_two, weight_three, weight_four, weight_five, norm_low):
    outer = (
        lax.all_gather(weight_one, "fsdp", axis=0, tiled=True),
        lax.all_gather(weight_two, "fsdp", axis=0, tiled=True),
        lax.all_gather(weight_three, "fsdp", axis=0, tiled=True),
        lax.all_gather(weight_four, "fsdp", axis=0, tiled=True),
        lax.all_gather(weight_five, "fsdp", axis=0, tiled=True),
        lax.all_gather(norm_low, "fsdp", axis=1, tiled=True),
    )
    return (
        lax.all_gather(outer[0], "dp", axis=1, tiled=True),
        lax.all_gather(outer[1], "dp", axis=1, tiled=True),
        lax.all_gather(outer[2], "dp", axis=1, tiled=True),
        lax.all_gather(outer[3], "dp", axis=1, tiled=True),
        lax.all_gather(outer[4], "dp", axis=1, tiled=True),
        lax.all_gather(outer[5], "dp", axis=1, tiled=True),
    )


def gather_again(weight_one, weight_two, weight_three, weight_four, weight_five, norm_low):
    outer = (
        lax.all_gather(weight_one, "fsdp", axis=0, tiled=True),
        lax.all_gather(weight_two, "fsdp", axis=0, tiled=True),
        lax.all_gather(weight_three, "fsdp", axis=0, tiled=True),
        lax.all_gather(weight_four, "fsdp", axis=0, tiled=True),
        lax.all_gather(weight_five, "fsdp", axis=0, tiled=True),
        lax.all_gather(norm_low, "fsdp", axis=1, tiled=True),
    )
    return (
        lax.all_gather(outer[0], "dp", axis=1, tiled=True),
        lax.all_gather(outer[1], "dp", axis=1, tiled=True),
        lax.all_gather(outer[2], "dp", axis=1, tiled=True),
        lax.all_gather(outer[3], "dp", axis=1, tiled=True),
        lax.all_gather(outer[4], "dp", axis=1, tiled=True),
        lax.all_gather(outer[5], "dp", axis=1, tiled=True),
    )


def reduce_inner(grad_one, grad_two, grad_three, grad_four, grad_five):
    return (
        lax.psum_scatter(grad_one, "dp", scatter_dimension=1, tiled=True),
        lax.psum_scatter(grad_two, "dp", scatter_dimension=1, tiled=True),
        lax.psum_scatter(grad_three, "dp", scatter_dimension=1, tiled=True),
        lax.psum_scatter(grad_four, "dp", scatter_dimension=1, tiled=True),
        lax.psum_scatter(grad_five, "dp", scatter_dimension=1, tiled=True),
    )


def reduce_outer(grad_one, grad_two, grad_three, grad_four, grad_five):
    return (
        lax.psum_scatter(grad_one, "fsdp", scatter_dimension=0, tiled=True),
        lax.psum_scatter(grad_two, "fsdp", scatter_dimension=0, tiled=True),
        lax.psum_scatter(grad_three, "fsdp", scatter_dimension=0, tiled=True),
        lax.psum_scatter(grad_four, "fsdp", scatter_dimension=0, tiled=True),
        lax.psum_scatter(grad_five, "fsdp", scatter_dimension=0, tiled=True),
    )


def exchange_kernel(dp_size, fsdp_size, value_ref, total_ref, slots_dp, slots_fsdp, send_dp, recv_dp, send_fsdp, recv_fsdp):
    dp_me = lax.axis_index("dp")
    fsdp_me = lax.axis_index("fsdp")
    barrier = pltpu.get_barrier_semaphore()

    @pl.loop(1, dp_size)
    def _(step):
        pl.semaphore_signal(
            barrier, 1, device_id={"dp": lax.rem(dp_me + step, dp_size)}, device_id_type=pl.DeviceIdType.MESH
        )

    @pl.loop(1, fsdp_size)
    def _(step):
        pl.semaphore_signal(
            barrier, 1, device_id={"fsdp": lax.rem(fsdp_me + step, fsdp_size)}, device_id_type=pl.DeviceIdType.MESH
        )

    pl.semaphore_wait(barrier, dp_size + fsdp_size - 2)

    def share(axis, size, me, slots, send, recv):
        def copy_to(step):
            return pltpu.make_async_remote_copy(
                src_ref=slots.at[me],
                dst_ref=slots.at[me],
                send_sem=send.at[step],
                recv_sem=recv.at[me],
                device_id={axis: lax.rem(me + step, size)},
                device_id_type=pl.DeviceIdType.MESH,
            )

        def copy_from(step):
            source = lax.rem(me + step, size)
            return pltpu.make_async_remote_copy(
                src_ref=slots.at[source],
                dst_ref=slots.at[source],
                send_sem=send.at[step],
                recv_sem=recv.at[source],
                device_id={axis: source},
                device_id_type=pl.DeviceIdType.MESH,
            )

        pl.loop(1, size)(lambda step: copy_to(step).start())
        pl.loop(1, size)(lambda step: copy_from(step).wait_recv())
        pl.loop(1, size)(lambda step: copy_to(step).wait_send())

    slots_dp[dp_me] = value_ref[...]
    share("dp", dp_size, dp_me, slots_dp, send_dp, recv_dp)
    total = slots_dp[0]
    for place in range(1, dp_size):
        total = total + slots_dp[place]
    slots_fsdp[fsdp_me] = total
    share("fsdp", fsdp_size, fsdp_me, slots_fsdp, send_fsdp, recv_fsdp)
    total = slots_fsdp[0]
    for place in range(1, fsdp_size):
        total = total + slots_fsdp[place]
    total_ref[...] = total


def sum_all(values, collective_id):
    dp_size, fsdp_size = lax.axis_size("dp"), lax.axis_size("fsdp")
    flat = jnp.concatenate([value.reshape(-1) for value in values])
    length = flat.shape[0]
    rows = -(-length // 1024) * 8
    block = jnp.pad(flat, (0, rows * 128 - length)).reshape(rows, 128)
    total = pl.pallas_call(
        lambda *refs: exchange_kernel(dp_size, fsdp_size, *refs),
        out_shape=jax.ShapeDtypeStruct((rows, 128), jnp.float32),
        in_specs=[pl.BlockSpec(memory_space=pltpu.VMEM)],
        out_specs=pl.BlockSpec(memory_space=pltpu.VMEM),
        scratch_shapes=[
            pltpu.VMEM((dp_size, rows, 128), jnp.float32),
            pltpu.VMEM((fsdp_size, rows, 128), jnp.float32),
            pltpu.SemaphoreType.DMA((dp_size,)),
            pltpu.SemaphoreType.DMA((dp_size,)),
            pltpu.SemaphoreType.DMA((fsdp_size,)),
            pltpu.SemaphoreType.DMA((fsdp_size,)),
        ],
        compiler_params=pltpu.CompilerParams(
            collective_id=collective_id, has_side_effects=True, vmem_limit_bytes=32 * 2**20
        ),
        name="sum_all",
    )(block).reshape(-1)
    parts = []
    start = 0
    for value in values:
        parts.append(total[start : start + value.size].reshape(value.shape))
        start += value.size
    return parts


def norm_forward(hidden, gain_part, shift_part, count_all, collective_id):
    moment_sums = sum_all(
        (jnp.sum(hidden, axis=0), jnp.sum(hidden * hidden, axis=0)), collective_id
    )
    mean_value = moment_sums[0] / count_all
    scaling = lax.rsqrt(moment_sums[1] / count_all - mean_value * mean_value + norm_epsilon)
    normed = (hidden - mean_value) * scaling
    return (normed * gain_part + shift_part, normed, scaling)


def norm_backward(upstream, normed, scaling, gain_part, count_all, collective_id):
    grad_sums = sum_all(
        (jnp.sum(upstream, axis=0), jnp.sum(upstream * normed, axis=0)), collective_id
    )
    shift_grad = grad_sums[0]
    gain_grad = grad_sums[1]
    hidden_grad = (
        gain_part * scaling * (upstream - shift_grad / count_all - normed * gain_grad / count_all)
    )
    return (hidden_grad, gain_grad, shift_grad)


def spread_columns(activation, view_count):
    picture = activation.reshape(view_count, SIDE, SIDE, C_MID)
    padded = jnp.pad(picture, ((0, 0), (1, 1), (1, 1), (0, 0)))
    pieces = [
        padded[:, vertical : vertical + SIDE, lateral : lateral + SIDE, :]
        for vertical in range(3)
        for lateral in range(3)
    ]
    return jnp.stack(pieces, axis=3).reshape(-1, 9 * C_MID)


def fold_columns(columns_grad, view_count):
    picture = columns_grad.reshape(view_count, SIDE, SIDE, 9, C_MID)
    summed = jnp.zeros((view_count, SIDE, SIDE, C_MID), jnp.float32)
    for vertical in range(3):
        for lateral in range(3):
            placed = jnp.pad(
                picture[:, :, :, 3 * vertical + lateral, :],
                ((0, 0), (vertical, 2 - vertical), (lateral, 2 - lateral), (0, 0)),
            )
            summed = summed + placed[:, 1 : 1 + SIDE, 1 : 1 + SIDE, :]
    return summed.reshape(-1, C_MID)


def local_objective(sorted_embed, mean_embed, covariance):
    unit_views = []
    for view_index in range(2):
        factor = jnp.linalg.cholesky(covariance[view_index])
        whitened = lax.linalg.triangular_solve(
            factor,
            (sorted_embed[:, view_index] - mean_embed[view_index]).T,
            left_side=True,
            lower=True,
        )
        unit_views.append(
            whitened * lax.rsqrt(jnp.mean(whitened * whitened, axis=0) + norm_epsilon)
        )
    return jnp.sum(jnp.mean((unit_views[0] - unit_views[1]) ** 2, axis=0))


def adam_update(weight, moment_one, moment_two, gradient, step_rate, weight_decay):
    first_new = beta_first * moment_one + (1.0 - beta_first) * gradient
    second_new = beta_second * moment_two + (1.0 - beta_second) * gradient * gradient
    first_hat = first_new / (1.0 - beta_first**STEP)
    second_hat = second_new / (1.0 - beta_second**STEP)
    weight_new = weight - step_rate * (
        first_hat / (jnp.sqrt(second_hat) + adam_epsilon) + weight_decay * weight
    )
    return (weight_new, first_new, second_new)


def body(
    features,
    view_order,
    conv_one,
    conv_two,
    conv_three,
    proj_one,
    proj_two,
    norm_params,
    first_conv_one,
    first_conv_two,
    first_conv_three,
    first_proj_one,
    first_proj_two,
    first_norm,
    second_conv_one,
    second_conv_two,
    second_conv_three,
    second_proj_one,
    second_proj_two,
    second_norm,
):
    devices = lax.axis_size("dp") * lax.axis_size("fsdp")
    view_count = features.shape[0]
    row_total = view_count * PIX * devices
    view_total = view_count * devices
    image_total = view_total // 2
    start_two = C_MID
    start_three = 2 * C_MID
    start_four = 2 * C_MID + C_IN
    low_one = conv_one.astype(jnp.bfloat16)
    low_two = conv_two.astype(jnp.bfloat16)
    low_three = conv_three.astype(jnp.bfloat16)
    low_four = proj_one.astype(jnp.bfloat16)
    low_five = proj_two.astype(jnp.bfloat16)
    low_norm = norm_params.astype(jnp.bfloat16)
    gathered = gather_weights(low_one, low_two, low_three, low_four, low_five, low_norm)
    norm_full = gathered[5].astype(jnp.float32)
    gain_all = norm_full[0]
    shift_all = norm_full[1]
    gain_one = gain_all[:start_two]
    gain_two = gain_all[start_two:start_three]
    gain_three = gain_all[start_three:start_four]
    gain_four = gain_all[start_four:]
    pixel_rows = features.reshape(-1, C_IN)
    hidden_one = matmul(pixel_rows, gathered[0])
    out_one, normed_one, scale_one = norm_forward(
        hidden_one, gain_one, shift_all[:start_two], row_total, 1
    )
    act_one = gelu_exact(out_one).astype(jnp.bfloat16)
    columns = spread_columns(act_one, view_count)
    hidden_two = matmul(columns, gathered[1])
    out_two, normed_two, scale_two = norm_forward(
        hidden_two, gain_two, shift_all[start_two:start_three], row_total, 2
    )
    act_two = gelu_exact(out_two).astype(jnp.bfloat16)
    hidden_three = matmul(act_two, gathered[2])
    out_three, normed_three, scale_three = norm_forward(
        hidden_three, gain_three, shift_all[start_three:start_four], row_total, 3
    )
    summed = out_three + pixel_rows.astype(jnp.float32)
    block_out = gelu_exact(summed)
    pooled = jnp.mean(block_out.reshape(view_count, PIX, C_IN), axis=1).astype(jnp.bfloat16)
    proj_hidden = matmul(pooled, gathered[3])
    out_four, normed_four, scale_four = norm_forward(
        proj_hidden, gain_four, shift_all[start_four:], view_total, 4
    )
    proj_act = gelu_exact(out_four).astype(jnp.bfloat16)
    embedding = matmul(proj_act, gathered[4])
    selector = (view_order[0][:, None] == jnp.arange(view_count, dtype=jnp.int32)[None, :]).astype(
        jnp.float32
    )
    sorted_flat = lax.dot_general(selector, embedding, (((0,), (0,)), ((), ())), precision=highest)
    sorted_embed = sorted_flat.reshape(view_count // 2, 2, P_OUT)
    view_sums = jnp.sum(sorted_embed, axis=0)
    view_outer = jnp.einsum("ikp,ikq->kpq", sorted_embed, sorted_embed, precision=highest)
    view_sums, view_outer = sum_all((view_sums, view_outer), 9)
    mean_embed = view_sums / image_total
    covariance = (
        view_outer / image_total
        - mean_embed[:, :, None] * mean_embed[:, None, :]
        + ridge_term * jnp.eye(P_OUT, dtype=jnp.float32)[None]
    )
    local_total, pullback = jax.vjp(local_objective, sorted_embed, mean_embed, covariance)
    direct, mean_grad, cov_grad = pullback(jnp.ones((), jnp.float32))
    mean_grad, cov_grad, objective = sum_all((mean_grad, cov_grad, local_total), 10)
    symmetric = cov_grad + jnp.swapaxes(cov_grad, 1, 2)
    correction = mean_grad - jnp.einsum("kpq,kq->kp", symmetric, mean_embed, precision=highest)
    sorted_grad = (
        direct
        + (
            jnp.einsum("ikp,kpq->ikq", sorted_embed, symmetric, precision=highest)
            + correction[None]
        )
        / image_total
    )
    embed_grad = jnp.dot(
        selector, sorted_grad.reshape(view_count, P_OUT), precision=highest
    ).astype(jnp.bfloat16)
    back_weights = gather_again(low_one, low_two, low_three, low_four, low_five, low_norm)
    grad_five = contract_rows(proj_act, embed_grad)
    act_four_grad = contract_cols(embed_grad, back_weights[4])
    four_grad, gain_four_grad, shift_four_grad = norm_backward(
        gelu_back(out_four, act_four_grad), normed_four, scale_four, gain_four, view_total, 5
    )
    four_low = four_grad.astype(jnp.bfloat16)
    grad_four = contract_rows(pooled, four_low)
    pooled_grad = contract_cols(four_low, back_weights[3])
    block_grad = jnp.broadcast_to((pooled_grad / PIX)[:, None, :], (view_count, PIX, C_IN)).reshape(
        -1, C_IN
    )
    summed_grad = gelu_back(summed, block_grad)
    three_grad, gain_three_grad, shift_three_grad = norm_backward(
        summed_grad, normed_three, scale_three, gain_three, row_total, 6
    )
    three_low = three_grad.astype(jnp.bfloat16)
    grad_three = contract_rows(act_two, three_low)
    act_two_grad = contract_cols(three_low, back_weights[2])
    two_grad, gain_two_grad, shift_two_grad = norm_backward(
        gelu_back(out_two, act_two_grad), normed_two, scale_two, gain_two, row_total, 7
    )
    two_low = two_grad.astype(jnp.bfloat16)
    grad_two = contract_rows(columns, two_low)
    act_one_grad = fold_columns(contract_cols(two_low, back_weights[1]), view_count)
    one_grad, gain_one_grad, shift_one_grad = norm_backward(
        gelu_back(out_one, act_one_grad), normed_one, scale_one, gain_one, row_total, 8
    )
    one_low = one_grad.astype(jnp.bfloat16)
    grad_one = contract_rows(pixel_rows, one_low)
    input_grad = (summed_grad + contract_cols(one_low, back_weights[0])).reshape(
        view_count, PIX, C_IN
    )
    partial_value = reduce_inner(grad_one, grad_two, grad_three, grad_four, grad_five)
    owned = reduce_outer(
        partial_value[0], partial_value[1], partial_value[2], partial_value[3], partial_value[4]
    )
    norm_grad_full = jnp.stack(
        [
            jnp.concatenate([gain_one_grad, gain_two_grad, gain_three_grad, gain_four_grad]),
            jnp.concatenate([shift_one_grad, shift_two_grad, shift_three_grad, shift_four_grad]),
        ]
    )
    shard_width = norm_params.shape[1]
    owner_index = lax.axis_index(("dp", "fsdp"))
    norm_owned = lax.dynamic_slice_in_dim(norm_grad_full, owner_index * shard_width, shard_width, 1)
    param_grads = (owned[0], owned[1], owned[2], owned[3], owned[4], norm_owned)
    local_squares = jnp.float32(0.0)
    for member in param_grads:
        local_squares = local_squares + jnp.sum(member * member)
    (squares,) = sum_all((local_squares,), 11)
    grad_norm = jnp.sqrt(squares)
    factor = clip_level / jnp.maximum(grad_norm, clip_level)
    masters = (conv_one, conv_two, conv_three, proj_one, proj_two, norm_params)
    firsts = (
        first_conv_one,
        first_conv_two,
        first_conv_three,
        first_proj_one,
        first_proj_two,
        first_norm,
    )
    seconds = (
        second_conv_one,
        second_conv_two,
        second_conv_three,
        second_proj_one,
        second_proj_two,
        second_norm,
    )
    step_rates = (
        C_IN ** (-0.5),
        (9 * C_MID) ** (-0.5),
        C_MID ** (-0.5),
        C_IN ** (-0.5),
        P_HID ** (-0.5),
        norm_rate,
    )
    decays = (decay_rate, decay_rate, decay_rate, decay_rate, decay_rate, 0.0)
    results = [
        adam_update(
            masters[place],
            firsts[place],
            seconds[place],
            param_grads[place] * factor,
            step_rates[place],
            decays[place],
        )
        for place in range(6)
    ]
    return (
        objective / image_total,
        input_grad,
        grad_norm,
        results[0][0],
        results[1][0],
        results[2][0],
        results[3][0],
        results[4][0],
        results[5][0],
        results[0][1],
        results[1][1],
        results[2][1],
        results[3][1],
        results[4][1],
        results[5][1],
        results[0][2],
        results[1][2],
        results[2][2],
        results[3][2],
        results[4][2],
        results[5][2],
    )


def solution(mesh):
    placed = (
        P(("dp", "fsdp"), None, None),
        P(("dp", "fsdp"), None),
        P("fsdp", "dp"),
        P("fsdp", "dp"),
        P("fsdp", "dp"),
        P("fsdp", "dp"),
        P("fsdp", "dp"),
        P(None, ("dp", "fsdp")),
        P("fsdp", "dp"),
        P("fsdp", "dp"),
        P("fsdp", "dp"),
        P("fsdp", "dp"),
        P("fsdp", "dp"),
        P(None, ("dp", "fsdp")),
        P("fsdp", "dp"),
        P("fsdp", "dp"),
        P("fsdp", "dp"),
        P("fsdp", "dp"),
        P("fsdp", "dp"),
        P(None, ("dp", "fsdp")),
    )
    return jax.shard_map(
        body,
        mesh=mesh,
        in_specs=placed,
        out_specs=(
            P(),
            P(("dp", "fsdp"), None, None),
            P(),
            P("fsdp", "dp"),
            P("fsdp", "dp"),
            P("fsdp", "dp"),
            P("fsdp", "dp"),
            P("fsdp", "dp"),
            P(None, ("dp", "fsdp")),
            P("fsdp", "dp"),
            P("fsdp", "dp"),
            P("fsdp", "dp"),
            P("fsdp", "dp"),
            P("fsdp", "dp"),
            P(None, ("dp", "fsdp")),
            P("fsdp", "dp"),
            P("fsdp", "dp"),
            P("fsdp", "dp"),
            P("fsdp", "dp"),
            P("fsdp", "dp"),
            P(None, ("dp", "fsdp")),
        ),
        check_vma=False,
    )
```

```python
from typing import Any, NamedTuple

import jax
import jax.numpy as jnp
from jax import lax
from jax.experimental import pallas as pl
from jax.experimental.pallas import tpu as pltpu
from jax.sharding import PartitionSpec as P

C_IN = 2048
C_MID = 512
P_HID = 1024
P_OUT = 128
SIDE = 7
STEP = 10
PIX = 49
LANES = 128
BLOCKS = C_IN // C_MID
CHUNKS = SIDE


highest = lax.Precision.HIGHEST
bf16 = jnp.bfloat16
f32 = jnp.float32
norm_epsilon = 1e-05
ridge_term = 0.01
clip_level = 0.1
beta_first = 0.9
beta_second = 0.999
adam_epsilon = 1e-08
decay_rate = 0.05
norm_rate = 0.5
bell_scale = 0.3989422804014327
root_half = 0.5**0.5
bell_rate = -0.7213475204444817
DP, FSDP = "dp", "fsdp"


def gelu_pair(values):
    below = 0.5 + 0.5 * lax.erf(values * root_half)
    bell = jnp.exp2(values * values * bell_rate)
    return values * below, below + values * bell * bell_scale


def dot(left, right):
    return jnp.dot(left, right, preferred_element_type=f32)


def dot_cols(left, right):
    return lax.dot_general(left, right, (((1,), (1,)), ((), ())), preferred_element_type=f32)


def dot_rows(left, right):
    return lax.dot_general(left, right, (((0,), (0,)), ((), ())), preferred_element_type=f32)


def exact_cols(left, right):
    return lax.dot_general(
        left, right, (((1,), (1,)), ((), ())), precision=highest, preferred_element_type=f32
    )


def exact_rows(left, right):
    return lax.dot_general(
        left, right, (((0,), (0,)), ((), ())), precision=highest, preferred_element_type=f32
    )


def exact_dot(left, right):
    return jnp.dot(left, right, precision=highest, preferred_element_type=f32)


def inverse_factors(matrices):
    row_top = lax.broadcasted_iota(jnp.int32, (8, P_OUT), 0)
    row_all = lax.broadcasted_iota(jnp.int32, (P_OUT, P_OUT), 0)
    col_all = lax.broadcasted_iota(jnp.int32, (P_OUT, P_OUT), 1)

    def one_step(place, left, right):
        scale = lax.rsqrt(left[place : place + 1, place : place + 1])
        left_row = left[place : place + 1, :] * scale
        right_row = right[place : place + 1, :] * scale
        column = left[:, place : place + 1] * scale
        left = left - column * left_row
        right = right - column * right_row
        here = row_top == place
        left = jnp.concatenate([jnp.where(here, 0.0, left[:8]), left[8:]], axis=0)
        right = jnp.concatenate(
            [jnp.where(here, jnp.broadcast_to(right_row, (8, P_OUT)), right[:8]), right[8:]], axis=0
        )
        return left, right

    def panel(_, pairs):
        pairs = list(pairs)
        for place in range(8):
            for which in range(len(pairs)):
                pairs[which] = one_step(place, *pairs[which])
        return tuple(
            (
                pltpu.roll(jnp.concatenate([left[8:], left[:8]], axis=0), P_OUT - 8, 1),
                jnp.concatenate([right[8:], right[:8]], axis=0),
            )
            for left, right in pairs
        )

    start = tuple((matrix, (row_all == col_all).astype(f32)) for matrix in matrices)
    done = lax.fori_loop(0, P_OUT // 8, panel, start)
    return [right for _, right in done]


def pack_pair(first, second):
    row = lax.broadcasted_iota(jnp.int32, (P_OUT, P_OUT), 0)
    col = lax.broadcasted_iota(jnp.int32, (P_OUT, P_OUT), 1)
    packed = jnp.where(row >= col, first, second.T)
    diagonal = jnp.sum(jnp.where(row == col, second, 0.0), axis=0, keepdims=True)
    return packed, diagonal


def unpack_pair(packed, diagonal):
    row = lax.broadcasted_iota(jnp.int32, (P_OUT, P_OUT), 0)
    col = lax.broadcasted_iota(jnp.int32, (P_OUT, P_OUT), 1)
    turned = packed.T
    first = jnp.where(row >= col, packed, turned)
    second = jnp.where(row < col, packed, jnp.where(row == col, diagonal, turned))
    return first, second


class Ins(NamedTuple):
    features: Any
    order: Any
    norm: Any
    shards: Any


class Outs(NamedTuple):
    slope: Any
    one_low: Any
    low_one: Any
    pool_grad: Any
    norm_grad: Any
    scalars: Any
    grads: Any


class SumRoom(NamedTuple):
    dp: Any
    fsdp: Any
    s0: Any
    r0: Any
    s1: Any
    r1: Any


class MatrixRoom(NamedTuple):
    pack: Any
    dp: Any
    fsdp: Any
    all: Any
    s0: Any
    r0: Any
    s1: Any
    r1: Any
    s2: Any
    r2: Any


class Mem(NamedTuple):
    w: Any
    r3: Any
    r4: Any
    r5: Any
    stage: Any
    stage_sem: Any
    column_sem: Any
    h1: Any
    d1: Any
    h2: Any
    d2: Any
    a2: Any
    h3: Any
    pad1: Any
    pad2: Any
    pool: Any
    pool_slope: Any
    pool_bend: Any
    pooled: Any
    proj_act: Any
    proj_slope: Any
    proj_hidden: Any
    coef: Any
    stats: Any
    norm: Any
    norm_tiles: Any
    norm_s0: Any
    norm_r0: Any
    norm_s1: Any
    norm_r1: Any
    bulk_send: Any
    bulk_recv: Any
    mats: Any
    sums: Any
    squares: Any


class Plan:
    def __init__(self, dp_size, fsdp_size, views, inside):
        self.dp = dp_size
        self.fsdp = fsdp_size
        self.devices = dp_size * fsdp_size
        self.views = views
        self.rows = views * PIX
        self.chunk = views * SIDE
        self.inside = inside
        self.z = 4
        self.x = 2
        self.half = (128, 288, 32, 128, 16)
        self.width = (128, 128, 512, 256, 128)
        piece = P_OUT + 8
        self.embed_rows = -(-piece // (8 * dp_size)) * 8


def kernel(plan, *refs):
    ins, outs, mem = Ins(*refs[:3], refs[3:8]), Outs(*refs[8:14], refs[14:19]), refs[19]
    views, chunk, rows = plan.views, plan.chunk, plan.rows
    row_total = float(rows * plan.devices)
    view_total = float(views * plan.devices)
    image_total = float(views * plan.devices // 2)
    dp_me, fsdp_me = lax.axis_index(DP), lax.axis_index(FSDP)
    y_me, c_me = dp_me // 2, dp_me % 2
    z_me, x_me = fsdp_me // 2, fsdp_me % 2
    y_other, c_other, x_other = 1 - y_me, 1 - c_me, 1 - x_me

    barrier = pltpu.get_barrier_semaphore()

    @pl.loop(1, plan.dp)
    def _(step):
        pl.semaphore_signal(
            barrier, 1, device_id={DP: lax.rem(dp_me + step, plan.dp)}, device_id_type=pl.DeviceIdType.MESH
        )

    @pl.loop(1, plan.fsdp)
    def _(step):
        pl.semaphore_signal(
            barrier, 1, device_id={FSDP: lax.rem(fsdp_me + step, plan.fsdp)}, device_id_type=pl.DeviceIdType.MESH
        )

    pl.semaphore_wait(barrier, plan.dp + plan.fsdp - 2)

    def share(axis, size, me, source_of, slots, send, recv):
        def outgoing(step):
            partner = lax.rem(me + step, size)
            return pltpu.make_async_remote_copy(
                src_ref=source_of(partner),
                dst_ref=slots.at[me],
                send_sem=send.at[step],
                recv_sem=recv.at[me],
                device_id={axis: partner},
                device_id_type=pl.DeviceIdType.MESH,
            )

        def incoming(step):
            source = lax.rem(me + step, size)
            return pltpu.make_async_remote_copy(
                src_ref=slots.at[source],
                dst_ref=slots.at[source],
                send_sem=send.at[step],
                recv_sem=recv.at[source],
                device_id={axis: source},
                device_id_type=pl.DeviceIdType.MESH,
            )

        def start():
            pl.loop(1, size)(lambda step: outgoing(step).start())

        def wait():
            pl.loop(1, size)(lambda step: incoming(step).wait_recv())
            pl.loop(1, size)(lambda step: outgoing(step).wait_send())

        return start, wait

    def add_slots(slots, size):
        total = slots[0]
        for place in range(1, size):
            total = total + slots[place]
        return total

    class Sum:
        def __init__(self, which):
            part = mem.sums[which if which < 4 else (3, 2, 0, 1, 4)[which - 4]]
            self.dp_slots, self.fsdp_slots = part.dp, part.fsdp
            self.dp_copy = share(
                DP, plan.dp, dp_me, lambda _: self.dp_slots.at[dp_me], self.dp_slots, part.s0, part.r0
            )
            self.fsdp_copy = share(
                FSDP, plan.fsdp, fsdp_me, lambda _: self.fsdp_slots.at[fsdp_me], self.fsdp_slots, part.s1, part.r1
            )

        def start(self, *values):
            for place, value in enumerate(values):
                self.dp_slots[dp_me, place : place + 1, :] = value
            self.dp_copy[0]()

        def middle(self):
            self.dp_copy[1]()
            self.fsdp_slots[fsdp_me] = add_slots(self.dp_slots, plan.dp)
            self.fsdp_copy[0]()

        def finish(self):
            self.fsdp_copy[1]()
            return add_slots(self.fsdp_slots, plan.fsdp)

        def all(self, *values):
            self.start(*values)
            self.middle()
            return self.finish()

    def sum_matrix(which, matrix, extra):
        part = mem.mats[which]
        size = plan.embed_rows
        pack = part.pack
        flat = jnp.concatenate(
            [matrix] + extra + [jnp.zeros((size * plan.dp - P_OUT - len(extra), P_OUT), f32)], axis=0
        )
        for place in range(plan.dp):
            pack[place] = flat[place * size : (place + 1) * size]
        start, wait = share(DP, plan.dp, dp_me, lambda to: pack.at[to], part.dp, part.s0, part.r0)
        start()
        part.dp[dp_me] = pack[dp_me]
        wait()
        part.fsdp[fsdp_me] = add_slots(part.dp, plan.dp)
        start, wait = share(
            FSDP, plan.fsdp, fsdp_me, lambda _: part.fsdp.at[fsdp_me], part.fsdp, part.s1, part.r1
        )
        start()
        wait()
        part.all[dp_me] = add_slots(part.fsdp, plan.fsdp)
        start, wait = share(
            DP, plan.dp, dp_me, lambda _: part.all.at[dp_me], part.all, part.s2, part.r2
        )
        start()
        wait()
        total = jnp.concatenate([part.all[place] for place in range(plan.dp)], axis=0)
        return total[:P_OUT], [total[P_OUT + place : P_OUT + place + 1] for place in range(len(extra))]

    weights = mem.w
    everything = slice(None)

    def row_span(which, half):
        size = plan.half[which]
        if half is None:
            return 0, 2 * size
        return half * size, size

    def column_span(which, dp_index):
        width = plan.width[which]
        return pl.ds(pl.multiple_of(dp_index * width, width), width)

    def places(which, z_index, x_index, dp_index, half):
        start, size = row_span(which, half)
        if which == 1:
            z_list = range(plan.z) if z_index is None else [z_index]
            x_list = range(plan.x) if x_index is None else [x_index]
            return [
                (
                    pl.ds(pl.multiple_of((z_one * plan.x + x_one) * 576 + start, 16), size),
                    column_span(which, dp_index),
                )
                for z_one in z_list
                for x_one in x_list
            ]
        z_one = everything if z_index is None else z_index
        x_one = everything if x_index is None else x_index
        if which == 2:
            return [(dp_index, z_one, x_one, pl.ds(start, size), everything)]
        if which == 4:
            return [(z_one, x_one, pl.ds(pl.multiple_of(dp_index * 32 + start, 16), size), everything)]
        return [(z_one, x_one, pl.ds(start, size), column_span(which, dp_index))]

    recv_parts = {
        1: lambda index: mem.h3.at[index],
        0: lambda index: mem.r4.at[index],
        2: lambda index: mem.r3.at[index],
        3: lambda index: mem.r4.at[index],
        4: lambda index: mem.r5.at[index],
    }

    counter = [0]

    class Batch:
        def __init__(self, sources, targets, landings, axis, partner):
            base = counter[0]
            counter[0] += len(sources)
            send, recv = mem.bulk_send, mem.bulk_recv
            self.out = [
                pltpu.make_async_remote_copy(
                    src_ref=source,
                    dst_ref=target,
                    send_sem=send.at[base + place],
                    recv_sem=recv.at[base + place],
                    device_id={axis: partner},
                    device_id_type=pl.DeviceIdType.MESH,
                )
                for place, (source, target) in enumerate(zip(sources, targets))
            ]
            self.come = [
                pltpu.make_async_remote_copy(
                    src_ref=landing,
                    dst_ref=landing,
                    send_sem=send.at[base + place],
                    recv_sem=recv.at[base + place],
                    device_id={axis: partner},
                    device_id_type=pl.DeviceIdType.MESH,
                )
                for place, landing in enumerate(landings)
            ]

        def start(self):
            for copy in self.out:
                copy.start()

        def arrive(self):
            for copy in self.come:
                copy.wait_recv()

        def leave(self):
            for copy in self.out:
                copy.wait_send()

    class LineBatch:
        def __init__(self, source_of, target_of, landing_of):
            base = counter[0]
            counter[0] += plan.z
            send, recv = mem.bulk_send, mem.bulk_recv
            self.out, self.come = [], []
            for step in range(1, plan.z):
                z_to = (z_me + step) % plan.z
                self.out.append(
                    pltpu.make_async_remote_copy(
                        src_ref=source_of(z_to),
                        dst_ref=target_of(z_to),
                        send_sem=send.at[base + step],
                        recv_sem=recv.at[base + z_me],
                        device_id={FSDP: z_to * plan.x + x_me},
                        device_id_type=pl.DeviceIdType.MESH,
                    )
                )
                self.come.append(
                    pltpu.make_async_remote_copy(
                        src_ref=landing_of(z_to),
                        dst_ref=landing_of(z_to),
                        send_sem=send.at[base + step],
                        recv_sem=recv.at[base + z_to],
                        device_id={FSDP: z_to * plan.x + x_me},
                        device_id_type=pl.DeviceIdType.MESH,
                    )
                )

        start, arrive, leave = Batch.start, Batch.arrive, Batch.leave

    def pick(ref, indexes):
        return [ref.at[index] for index in indexes]

    def own_dp(y_index, c_index):
        return y_index * 2 + c_index

    x_partner = z_me * plan.x + x_other
    y_partner = own_dp(y_other, c_me)
    c_partner = own_dp(y_me, c_other)
    dp_far = own_dp(y_other, c_other)

    class Gather:
        def __init__(self, which):
            ref = weights[which]
            self.which = which

            def at(*index):
                return pick(ref, places(which, *index))

            own = at(z_me, x_me, dp_me, None)[0]
            self.line = LineBatch(
                lambda _: own, lambda _: own, lambda z_from: at(z_from, x_me, dp_me, None)[0]
            )
            sent, come = at(None, x_me, dp_me, 0), at(None, x_other, dp_me, 0)
            self.x_first = Batch(sent, sent, come, FSDP, x_partner)
            sent, come = at(None, x_me, dp_me, 1), at(None, x_me, y_partner, 1)
            self.y_first = Batch(sent, sent, come, DP, y_partner)
            sent, come = at(None, None, dp_me, 0), at(None, None, y_partner, 0)
            self.y_second = Batch(sent, sent, come, DP, y_partner)
            sent = at(None, x_me, dp_me, 1) + at(None, x_me, y_partner, 1)
            come = at(None, x_other, dp_me, 1) + at(None, x_other, y_partner, 1)
            self.x_second = Batch(sent, sent, come, FSDP, x_partner)
            sent = at(None, None, dp_me, None) + at(None, None, y_partner, None)
            come = at(None, None, c_partner, None) + at(None, None, dp_far, None)
            self.core = Batch(sent, sent, come, DP, c_partner)
            self.stages = ((self.line,), (self.x_first, self.y_first), (self.y_second, self.x_second), (self.core,))

        def put_own(self, value):
            weights[self.which][places(self.which, z_me, x_me, dp_me, None)[0]] = value.astype(bf16)

        def start(self, stage):
            if plan.inside:
                for batch in self.stages[stage]:
                    batch.start()

        def arrive(self, stage):
            if plan.inside:
                for batch in self.stages[stage]:
                    batch.arrive()

        def step(self, stage):
            self.arrive(stage)
            self.start(stage + 1)

        def leave(self):
            if plan.inside:
                for stage in self.stages:
                    for batch in stage:
                        batch.leave()

    class Piece:
        def __init__(self, which, ref, room, z_index):
            def at(*index):
                return pick(ref, places(which, z_index, *index))

            def land(*index):
                return [room(index_one) for index_one in places(which, z_index, *index)]

            self.z = z_index
            self.core = Batch(
                at(None, c_partner, None) + at(None, dp_far, None),
                land(None, c_partner, None) + land(None, dp_far, None),
                land(None, dp_me, None) + land(None, y_partner, None),
                DP,
                c_partner,
            )
            self.y_first = Batch(
                at(None, y_partner, 0), land(None, dp_far, 0), land(None, c_partner, 0), DP, y_partner
            )
            self.x_first = Batch(
                at(x_other, dp_me, 1) + at(x_other, y_partner, 1),
                land(x_other, c_partner, 1) + land(x_other, dp_far, 1),
                land(x_me, c_partner, 1) + land(x_me, dp_far, 1),
                FSDP,
                x_partner,
            )
            self.x_second = Batch(
                at(x_other, dp_me, 0), land(x_other, dp_far, 0), land(x_me, dp_far, 0), FSDP, x_partner
            )
            self.y_second = Batch(
                at(x_me, y_partner, 1), land(x_other, dp_far, 1), land(x_other, c_partner, 1), DP, y_partner
            )

    class Reduce:
        def __init__(self, which, ref, cut):
            self.which, self.ref, self.room = which, ref, recv_parts[which]
            self.pieces = [
                Piece(which, ref, self.room, z_index) for z_index in (range(plan.z) if cut else [None])
            ]
            self.base = counter[0]
            counter[0] += plan.z

        def line_copy(self, z_to):
            return pltpu.make_async_remote_copy(
                src_ref=self.ref.at[places(self.which, z_to, x_me, dp_me, None)[0]],
                dst_ref=self.room(places(self.which, z_me, x_other, dp_far, None)[0]),
                send_sem=mem.bulk_send.at[self.base + z_to],
                recv_sem=mem.bulk_recv.at[self.base + z_me],
                device_id={FSDP: z_to * plan.x + x_me},
                device_id_type=pl.DeviceIdType.MESH,
            )

        def line_room(self, z_from):
            return self.room(places(self.which, z_from, x_other, dp_far, None)[0])

        def add(self, z_index, pairs):
            def one(z_one):
                for here, there in pairs:
                    for x_step in range(plan.x) if here[0] is None else [None]:
                        x_here = x_step if here[0] is None else here[0]
                        x_there = x_step if there[0] is None else there[0]
                        index = places(self.which, z_one, x_here, *here[1:])[0]
                        other = places(self.which, z_one, x_there, *there[1:])[0]
                        total = self.ref[index].astype(f32) + self.room(other)[...].astype(f32)
                        self.ref[index] = total.astype(bf16)

            if z_index is None:
                pl.loop(0, plan.z)(one)
            else:
                one(z_index)

        def core_start(self, place=0):
            if plan.inside:
                self.pieces[place].core.start()

        def core_add(self, place=0):
            if plan.inside:
                piece = self.pieces[place]
                piece.core.arrive()
                self.add(piece.z, [((None, dp_me, None),) * 2, ((None, y_partner, None),) * 2])
                piece.y_first.start()
                piece.x_first.start()

        def first_add(self, place=0):
            if plan.inside:
                piece = self.pieces[place]
                piece.y_first.arrive()
                self.add(piece.z, [((None, dp_me, 0), (None, c_partner, 0))])
                piece.x_second.start()
                piece.x_first.arrive()
                self.add(
                    piece.z, [((x_me, dp_me, 1), (x_me, c_partner, 1)), ((x_me, y_partner, 1), (x_me, dp_far, 1))]
                )
                piece.y_second.start()

        def second_add(self, place=0):
            if plan.inside:
                piece = self.pieces[place]
                piece.x_second.arrive()
                piece.y_second.arrive()
                self.add(
                    piece.z, [((x_me, dp_me, 0), (x_me, dp_far, 0)), ((x_me, dp_me, 1), (x_other, c_partner, 1))]
                )
                if piece.z is None:
                    for step in range(1, plan.z):
                        self.line_copy((z_me + step) % plan.z).start()
                else:

                    @pl.when(z_me != piece.z)
                    def _():
                        self.line_copy(piece.z).start()

        def finish(self):
            if not plan.inside:
                return
            total = self.ref[places(self.which, z_me, x_me, dp_me, None)[0]].astype(f32)
            for step in range(1, plan.z):
                z_from = (z_me + step) % plan.z
                room = self.line_room(z_from)
                pltpu.make_async_remote_copy(
                    src_ref=room,
                    dst_ref=room,
                    send_sem=mem.bulk_send.at[self.base + z_from],
                    recv_sem=mem.bulk_recv.at[self.base + z_from],
                    device_id={FSDP: z_from * plan.x + x_me},
                    device_id_type=pl.DeviceIdType.MESH,
                ).wait_recv()
                total = total + room[...].astype(f32)
            outs.grads[self.which][...] = total
            squares = jnp.sum(total * total, axis=0, keepdims=True)
            folded = squares[:, :LANES]
            for place in range(1, squares.shape[1] // LANES):
                folded = folded + squares[:, place * LANES : (place + 1) * LANES]
            mem.squares[...] += folded
            for step in range(1, plan.z):
                self.line_copy((z_me + step) % plan.z).wait_send()
            for piece in self.pieces:
                for batch in (piece.core, piece.y_first, piece.x_first, piece.x_second, piece.y_second):
                    batch.leave()

    gathers = [Gather(which) for which in range(5)]
    gradients = [weights[0], mem.stage.at[pl.ds(0, 9 * C_MID)], weights[2], weights[3], weights[4]]
    reduces = [Reduce(which, gradients[which], which < 2) for which in range(5)]
    mem.squares[...] = jnp.zeros((1, LANES), f32)

    if plan.inside:
        for which in range(5):
            gathers[which].put_own(ins.shards[which][...])
            gathers[which].start(0)
        tiles = mem.norm_tiles
        tiles[dp_me, fsdp_me] = ins.norm[...].astype(bf16).astype(f32)
        norm_dp = share(
            DP, plan.dp, dp_me, lambda _: tiles.at[dp_me, fsdp_me], tiles.at[:, fsdp_me], mem.norm_s0, mem.norm_r0
        )
        norm_dp[0]()
    else:
        loads = [
            pltpu.make_async_copy(ins.shards[which], weights[which], mem.bulk_send.at[which])
            for which in range(5)
        ]
        for load in loads:
            load.start()

    stage_ref, stage_sem = mem.stage, mem.stage_sem
    slot_rows = BLOCKS * chunk

    def chunk_rows(slot, block):
        return pl.ds(pl.multiple_of(slot * slot_rows + block * chunk, 16), chunk)

    def chunk_copies(array, index, into):
        slot = lax.rem(index, 3)
        copies = []
        for block in range(BLOCKS):
            outer = array.at[pl.ds(pl.multiple_of(index * chunk, 16), chunk), pl.ds(block * C_MID, C_MID)]
            inner = stage_ref.at[chunk_rows(slot, block)]
            source, target = (outer, inner) if into else (inner, outer)
            copies.append(pltpu.make_async_copy(source, target, stage_sem.at[0 if into else 1, slot, block]))
        return copies

    def load(array, index):
        for copy in chunk_copies(array, index, True):
            copy.start()

    def load_wait(array, index):
        for copy in chunk_copies(array, index, True):
            copy.wait()

    def save(array, index):
        for copy in chunk_copies(array, index, False):
            copy.start()

    def save_wait(array, index):
        for copy in chunk_copies(array, index, False):
            copy.wait()

    features, slope_hbm = ins.features, outs.slope
    load(features, 0)
    load(features, 1)

    padded_one, padded_two = mem.pad1, mem.pad2
    for padded in (padded_one, padded_two):
        for edge in (0, SIDE + 1):
            padded[edge] = jnp.zeros((padded.shape[1], C_MID), bf16)
        for edge in (0, SIDE + 1):
            padded[:, pl.ds(edge * views, views), :] = jnp.zeros((SIDE + 2, views, C_MID), bf16)

    if plan.inside:
        norm_dp[1]()
        norm_out = []
        norm_in = []
        for step in range(1, plan.fsdp):
            partner = (fsdp_me + step) % plan.fsdp
            norm_out.append(
                pltpu.make_async_remote_copy(
                    src_ref=tiles.at[:, fsdp_me],
                    dst_ref=tiles.at[:, fsdp_me],
                    send_sem=mem.norm_s1.at[step],
                    recv_sem=mem.norm_r1.at[fsdp_me],
                    device_id={FSDP: partner},
                    device_id_type=pl.DeviceIdType.MESH,
                )
            )
            norm_in.append(
                pltpu.make_async_remote_copy(
                    src_ref=tiles.at[:, partner],
                    dst_ref=tiles.at[:, partner],
                    send_sem=mem.norm_s1.at[step],
                    recv_sem=mem.norm_r1.at[partner],
                    device_id={FSDP: partner},
                    device_id_type=pl.DeviceIdType.MESH,
                )
            )
        for copy in norm_out:
            copy.start()
        gathers[0].step(0)
        gathers[0].step(1)
        gathers[0].step(2)
        gathers[1].step(0)
        gathers[0].arrive(3)
        for copy in norm_in:
            copy.wait_recv()
        for copy in norm_out:
            copy.wait_send()
        norm_all = mem.norm
        for dp_one in range(plan.dp):
            for fsdp_one in range(plan.fsdp):
                start = (dp_one * plan.fsdp + fsdp_one) * LANES
                norm_all[:, start : start + LANES] = tiles[dp_one, fsdp_one]
    else:
        for copy in loads:
            copy.wait()
        norm_all = mem.norm
        norm_all[...] = ins.norm[...]

    starts = (0, C_MID, 2 * C_MID, 2 * C_MID + C_IN, 2 * C_MID + C_IN + P_HID)

    def gain(layer):
        return norm_all[0:1, starts[layer] : starts[layer + 1]]

    def shift(layer):
        return norm_all[1:2, starts[layer] : starts[layer + 1]]

    coef, stats = mem.coef, mem.stats

    def norm_coefs(layer, totals, count):
        width = starts[layer + 1] - starts[layer]
        mean = totals[0:1] / count
        scaling = lax.rsqrt(totals[1:2] / count - mean * mean + norm_epsilon)
        slope = scaling * gain(layer)
        stats[0:1, starts[layer] : starts[layer + 1]] = mean
        stats[1:2, starts[layer] : starts[layer + 1]] = scaling
        coef[0:1, :width] = slope
        coef[1:2, :width] = shift(layer) - mean * slope

    def grad_coefs(layer, totals, count):
        width = starts[layer + 1] - starts[layer]
        mean = stats[0:1, starts[layer] : starts[layer + 1]]
        scaling = stats[1:2, starts[layer] : starts[layer + 1]]
        outs.norm_grad[0:1, starts[layer] : starts[layer + 1]] = totals[1:2]
        outs.norm_grad[1:2, starts[layer] : starts[layer + 1]] = totals[0:1]
        slope = scaling * gain(layer)
        bend = slope * scaling * totals[1:2] / count
        coef[0:1, :width] = slope
        coef[1:2, :width] = slope * totals[0:1] / count - mean * bend
        coef[2:3, :width] = bend

    def xhat_sum(layer, plain, product):
        mean = stats[0:1, starts[layer] : starts[layer + 1]]
        scaling = stats[1:2, starts[layer] : starts[layer + 1]]
        return scaling * (product - mean * plain)

    zero_row = jnp.zeros((1, C_MID), f32)

    def at_chunk(index, place, *moves):
        if plan.inside:

            @pl.when(index == place)
            def _():
                for move in moves:
                    move()

    def column_sums(value):
        return jnp.sum(value, axis=0, keepdims=True)

    def whole(which):
        value = weights[which][...]
        return value.reshape(-1, value.shape[-1])

    def stage_chunk(index):
        slot = lax.rem(index, 3)
        return jnp.concatenate([stage_ref[chunk_rows(slot, block), :] for block in range(BLOCKS)], axis=1)

    def span(index):
        return pl.ds(pl.multiple_of(index * chunk, 16), chunk)

    hidden_one, slope_one = mem.h1, mem.d1
    hidden_two, slope_two = mem.h2, mem.d2
    act_two = mem.a2
    hidden_three = mem.h3

    def first_body(index, sums):
        load_wait(features, index)

        @pl.when(index + 2 < CHUNKS)
        def _():
            load(features, index + 2)

        hidden = dot(stage_chunk(index), whole(0))
        hidden_one[span(index), :] = hidden.astype(bf16)
        at_chunk(index, 4, lambda: gathers[1].step(1))
        return sums[0] + column_sums(hidden), sums[1] + column_sums(hidden * hidden)

    sums = lax.fori_loop(0, CHUNKS, first_body, (zero_row, zero_row))
    sum_one = Sum(0)
    sum_one.start(*sums)
    gathers[2].step(0)
    sum_one.middle()
    load(features, 0)
    load(features, 1)
    norm_coefs(0, sum_one.finish(), row_total)

    def activate(hidden_ref, slope_ref, put):
        @pl.loop(0, PIX)
        def _(pixel):
            place = pl.ds(pl.multiple_of(pixel * views, 16), views)
            for block in range(C_MID // LANES):
                cols = slice(block * LANES, (block + 1) * LANES)
                out = hidden_ref[place, cols].astype(f32) * coef[0:1, cols] + coef[1:2, cols]
                value, slope = gelu_pair(out)
                slope_ref[place, cols] = slope.astype(bf16)
                put(pixel, cols, value.astype(bf16))

    def put_padded(padded):
        def put(pixel, cols, value):
            padded[pixel // SIDE + 1, pl.ds(pl.multiple_of((pixel % SIDE + 1) * views, 16), views), cols] = value

        return put

    activate(hidden_one, slope_one, put_padded(padded_one))
    gathers[1].step(2)
    gathers[3].step(0)
    gathers[1].arrive(3)

    def patch(padded, index, flip):
        pieces = []
        for vertical in range(3):
            for lateral in range(3):
                down, across = (2 - vertical, 2 - lateral) if flip else (vertical, lateral)
                pieces.append(padded[index + down, across * views : across * views + chunk, :])
        return jnp.concatenate(pieces, axis=1)

    def second_body(index, sums):
        hidden = dot(patch(padded_one, index, False), weights[1][...])
        hidden_two[span(index), :] = hidden.astype(bf16)
        at_chunk(index, 0, lambda: gathers[2].step(1))
        at_chunk(index, 2, lambda: gathers[4].step(0), lambda: gathers[2].step(2))
        at_chunk(index, 4, lambda: gathers[3].step(1), lambda: gathers[4].step(1))
        return sums[0] + column_sums(hidden), sums[1] + column_sums(hidden * hidden)

    sums = lax.fori_loop(0, CHUNKS, second_body, (zero_row, zero_row))
    sum_two = Sum(1)
    sum_two.start(*sums)
    sum_two.middle()
    norm_coefs(1, sum_two.finish(), row_total)

    def put_rows(pixel, cols, value):
        act_two[pl.ds(pl.multiple_of(pixel * views, 16), views), cols] = value

    activate(hidden_two, slope_two, put_rows)
    gathers[2].arrive(3)

    def block_rows(block, index):
        return pl.ds(pl.multiple_of(block * rows + index * chunk, 16), chunk)

    def weight_three(block):
        return weights[2][block].reshape(C_MID, C_MID)

    def third_body(index, sums):
        left = act_two[span(index), :]
        result = []
        for block in range(BLOCKS):
            hidden = dot(left, weight_three(block))
            hidden_three[block_rows(block, index), :] = hidden.astype(bf16)
            result.append(
                (sums[block][0] + column_sums(hidden), sums[block][1] + column_sums(hidden * hidden))
            )
        at_chunk(index, 4, lambda: gathers[3].step(2), lambda: gathers[4].step(2))
        return tuple(result)

    sums = lax.fori_loop(0, CHUNKS, third_body, ((zero_row, zero_row),) * BLOCKS)
    sum_three = Sum(2)
    sum_three.start(
        jnp.concatenate([pair[0] for pair in sums], axis=1), jnp.concatenate([pair[1] for pair in sums], axis=1)
    )
    sum_three.middle()
    gathers[4].arrive(3)
    norm_coefs(2, sum_three.finish(), row_total)

    pool, pool_slope, pool_bend = mem.pool, mem.pool_slope, mem.pool_bend
    for ref in (pool, pool_slope, pool_bend):
        ref[...] = jnp.zeros_like(ref)

    def pool_body(index, carry):
        load_wait(features, index)
        slot = lax.rem(index, 3)
        for block in range(BLOCKS):

            @pl.loop(0, C_MID // LANES)
            def _(part):
                inner = pl.ds(pl.multiple_of(part * LANES, LANES), LANES)
                cols = pl.ds(pl.multiple_of(block * C_MID + part * LANES, LANES), LANES)
                slope_row, shift_row = coef[0:1, cols], coef[1:2, cols]
                kept = (pool[:, cols], pool_slope[:, cols], pool_bend[:, cols])
                for pixel in range(SIDE):
                    stage_at = pl.ds(
                        pl.multiple_of(slot * slot_rows + block * chunk + pixel * views, 16), views
                    )
                    hidden_at = pl.ds(
                        pl.multiple_of(block * rows + index * chunk + pixel * views, 16), views
                    )
                    hidden = hidden_three[hidden_at, inner].astype(f32)
                    total = hidden * slope_row + shift_row + stage_ref[stage_at, inner].astype(f32)
                    value, slope = gelu_pair(total)
                    stage_ref[stage_at, inner] = slope.astype(bf16)
                    kept = (kept[0] + value, kept[1] + slope, kept[2] + slope * hidden)
                pool[:, cols], pool_slope[:, cols], pool_bend[:, cols] = kept

        save(slope_hbm, index)

        @pl.when(index >= 1)
        def _():
            save_wait(slope_hbm, index - 1)

        @pl.when(index + 2 < CHUNKS)
        def _():
            load(features, index + 2)

        return carry

    lax.fori_loop(0, CHUNKS, pool_body, 0)
    save_wait(slope_hbm, CHUNKS - 1)
    gathers[3].arrive(3)
    for one in gathers:
        one.leave()

    pooled = (pool[...] * (1.0 / PIX)).astype(bf16)
    mem.pooled[...] = pooled
    proj_hidden = dot(pooled, whole(3))
    sum_four = Sum(3)
    totals = sum_four.all(column_sums(proj_hidden), column_sums(proj_hidden * proj_hidden))
    load(slope_hbm, 0)
    load(slope_hbm, 1)
    norm_coefs(3, totals, view_total)
    value, slope = gelu_pair(proj_hidden * coef[0:1, :P_HID] + coef[1:2, :P_HID])
    proj_act = value.astype(bf16)
    mem.proj_act[...] = proj_act
    mem.proj_slope[...] = slope
    mem.proj_hidden[...] = proj_hidden

    def weight_five(block):
        return weights[4][block // plan.x, block % plan.x]

    parts = P_HID // P_OUT
    embedding = jnp.zeros((views, P_OUT), f32)
    for block in range(parts):
        embedding = embedding + dot_cols(proj_act[:, block * P_OUT : (block + 1) * P_OUT], weight_five(block))

    images = views // 2
    order = jnp.broadcast_to(ins.order[...], (images, views))
    image_row = lax.broadcasted_iota(jnp.int32, (images, views), 0)
    selectors = [(order == 2 * image_row + which).astype(f32) for which in range(2)]
    embeds = [exact_dot(selector, embedding) for selector in selectors]
    moments = [exact_rows(embed, embed) for embed in embeds]
    packed, diagonal = pack_pair(*moments)
    packed, extra = sum_matrix(0, packed, [diagonal] + [column_sums(embed) for embed in embeds])
    moments = unpack_pair(packed, extra[0])
    eye = (
        lax.broadcasted_iota(jnp.int32, (P_OUT, P_OUT), 0) == lax.broadcasted_iota(jnp.int32, (P_OUT, P_OUT), 1)
    ).astype(f32)
    centred, covariances = [], []
    for which in range(2):
        mean = extra[1 + which] / image_total
        centred.append(embeds[which] - mean)
        covariances.append(moments[which] / image_total - exact_rows(mean, mean) + ridge_term * eye)
    inverses = inverse_factors(covariances)
    whitened = [exact_cols(centred[which], inverses[which]) for which in range(2)]
    scalings = [
        lax.rsqrt(jnp.mean(white * white, axis=1, keepdims=True) + norm_epsilon) for white in whitened
    ]
    units = [white * scaling for white, scaling in zip(whitened, scalings)]
    difference = units[0] - units[1]
    objective_row = column_sums(difference * difference) * (1.0 / P_OUT)
    unit_grads = [difference * (2.0 / P_OUT), difference * (-2.0 / P_OUT)]
    white_grads = []
    for which in range(2):
        inner = jnp.mean(whitened[which] * unit_grads[which], axis=1, keepdims=True)
        white_grads.append(
            scalings[which] * unit_grads[which] - whitened[which] * (scalings[which] ** 3 * inner)
        )
    directs = [exact_dot(white_grads[which], inverses[which]) for which in range(2)]
    products = [exact_rows(white_grads[which], whitened[which]) for which in range(2)]
    packed, diagonal = pack_pair(*products)
    packed, extra = sum_matrix(
        1, packed, [diagonal] + [column_sums(grad) for grad in white_grads] + [objective_row]
    )
    products = unpack_pair(packed, extra[0])
    embed_grad = jnp.zeros((views, P_OUT), f32)
    for which in range(2):
        symmetric = exact_rows(inverses[which], exact_dot(products[which], inverses[which]))
        mean_grad = exact_dot(extra[1 + which], inverses[which])
        grad = directs[which] - (exact_dot(centred[which], symmetric) + mean_grad) / image_total
        embed_grad = embed_grad + exact_rows(selectors[which], grad)
    objective_row = extra[3]
    embed_low = embed_grad.astype(bf16)

    proj_act, proj_hidden = mem.proj_act[...], mem.proj_hidden[...]
    act_grad = jnp.concatenate([dot(embed_low, weight_five(block)) for block in range(parts)], axis=1)
    upstream = act_grad * mem.proj_slope[...]
    plain = column_sums(upstream)
    sum_four_back = Sum(4)
    sum_four_back.start(plain, xhat_sum(3, plain, column_sums(upstream * proj_hidden)))
    for block in range(parts):
        weights[4][block // plan.x, block % plan.x] = dot_rows(
            embed_low, proj_act[:, block * P_OUT : (block + 1) * P_OUT]
        ).astype(bf16)
    sum_four_back.middle()
    reduces[4].core_start()
    grad_coefs(3, sum_four_back.finish(), view_total)
    four_low = (
        upstream * coef[0:1, :P_HID] - coef[1:2, :P_HID] - proj_hidden * coef[2:3, :P_HID]
    ).astype(bf16)
    pool_grad = dot_cols(four_low, whole(3)) * (1.0 / PIX)
    plain = column_sums(pool_grad * pool_slope[...])
    sum_three_back = Sum(5)
    sum_three_back.start(plain, xhat_sum(2, plain, column_sums(pool_grad * pool_bend[...])))
    grad_four = dot_rows(mem.pooled[...], four_low).astype(bf16)
    weights[3][...] = grad_four.reshape(weights[3].shape)
    sum_three_back.middle()
    reduces[3].core_start()
    grad_coefs(2, sum_three_back.finish(), row_total)
    pool[...] = pool_grad * coef[0:1, :]
    pool_slope[...] = pool_grad
    pool_copy = pltpu.make_async_copy(pool_slope, outs.pool_grad, mem.column_sem.at[BLOCKS + 2])
    pool_copy.start()

    def third_back(index, sums):
        load_wait(slope_hbm, index)

        @pl.when(index + 2 < CHUNKS)
        def _():
            load(slope_hbm, index + 2)

        slot = lax.rem(index, 3)
        for block in range(BLOCKS):

            @pl.loop(0, C_MID // LANES)
            def _(part):
                inner = pl.ds(pl.multiple_of(part * LANES, LANES), LANES)
                cols = pl.ds(pl.multiple_of(block * C_MID + part * LANES, LANES), LANES)
                spread, shift_row, bend_row = pool[:, cols], coef[1:2, cols], coef[2:3, cols]
                for pixel in range(SIDE):
                    stage_at = pl.ds(
                        pl.multiple_of(slot * slot_rows + block * chunk + pixel * views, 16), views
                    )
                    hidden_at = pl.ds(
                        pl.multiple_of(block * rows + index * chunk + pixel * views, 16), views
                    )
                    hidden = hidden_three[hidden_at, inner].astype(f32)
                    grad = stage_ref[stage_at, inner].astype(f32) * spread - shift_row - hidden * bend_row
                    hidden_three[hidden_at, inner] = grad.astype(bf16)

        at_chunk(index, 0, reduces[4].core_add)
        at_chunk(index, 1, reduces[3].core_add)
        at_chunk(index, 2, reduces[4].first_add)
        at_chunk(index, 4, reduces[4].second_add)
        at_chunk(index, 6, reduces[3].first_add)
        left = jnp.concatenate([hidden_three[block_rows(block, index), :] for block in range(BLOCKS)], axis=1)
        right = jnp.concatenate([weight_three(block) for block in range(BLOCKS)], axis=1)
        upstream = dot_cols(left, right) * slope_two[span(index), :].astype(f32)
        slope_two[span(index), :] = upstream.astype(bf16)
        return (
            sums[0] + column_sums(upstream),
            sums[1] + column_sums(upstream * hidden_two[span(index), :].astype(f32)),
        )

    sums = lax.fori_loop(0, CHUNKS, third_back, (zero_row, zero_row))
    sum_two_back = Sum(6)
    sum_two_back.start(sums[0], xhat_sum(1, *sums))
    for block in range(BLOCKS):
        grad = dot_rows(act_two[...], hidden_three[block * rows : (block + 1) * rows, :])
        weights[2][block] = grad.astype(bf16).reshape(plan.z, plan.x, -1, C_MID)
        if block == 1:
            sum_two_back.middle()
    reduces[2].core_start()
    reduces[3].second_add()
    grad_coefs(1, sum_two_back.finish(), row_total)

    def apply_grad(hidden_ref, grad_ref, put):
        @pl.loop(0, PIX)
        def _(pixel):
            place = pl.ds(pl.multiple_of(pixel * views, 16), views)
            for block in range(C_MID // LANES):
                cols = slice(block * LANES, (block + 1) * LANES)
                grad = (
                    grad_ref[place, cols].astype(f32) * coef[0:1, cols]
                    - coef[1:2, cols]
                    - hidden_ref[place, cols].astype(f32) * coef[2:3, cols]
                )
                put(pixel, cols, grad.astype(bf16))

    apply_grad(hidden_two, slope_two, put_padded(padded_two))
    reduces[4].finish()
    reduces[2].core_add()

    feature_rows = (2 * rows, 3 * rows)

    def columns_copy(block):
        return pltpu.make_async_copy(
            features.at[:, pl.ds(block * C_MID, C_MID)],
            hidden_three.at[pl.ds(feature_rows[block % 2], rows)],
            mem.column_sem.at[block],
        )

    def tap_grad(tap):
        down, across = tap // 3, tap % 3
        left = padded_one[pl.ds(down, SIDE), pl.ds(pl.multiple_of(across * views, 16), chunk), :]
        right = padded_two[1 : SIDE + 1, views : views + chunk, :]
        grad = dot_rows(left.reshape(rows, C_MID), right.reshape(rows, C_MID))
        mem.stage[pl.ds(pl.multiple_of(tap * C_MID, 16), C_MID), :] = grad.astype(bf16)

    pl.loop(0, 3)(tap_grad)
    reduces[1].core_start(0)
    reduces[2].first_add()
    pl.loop(3, 5)(tap_grad)
    reduces[1].core_start(1)
    reduces[1].core_add(0)
    reduces[3].finish()
    pl.loop(5, 7)(tap_grad)
    reduces[1].core_start(2)
    reduces[1].core_add(1)
    reduces[2].second_add()
    reduces[1].first_add(0)
    pl.loop(7, 9)(tap_grad)
    reduces[1].core_start(3)
    reduces[1].core_add(2)
    reduces[1].first_add(1)

    def second_back(index, sums):
        right = jnp.concatenate([weights[1][tap * C_MID : (tap + 1) * C_MID, :] for tap in range(9)], axis=1)
        upstream = dot_cols(patch(padded_two, index, True), right) * slope_one[span(index), :].astype(f32)
        slope_one[span(index), :] = upstream.astype(bf16)
        at_chunk(index, 0, lambda: reduces[1].core_add(3), reduces[2].finish, lambda: reduces[1].second_add(0))
        at_chunk(index, 1, lambda: reduces[1].first_add(2))
        at_chunk(index, 2, lambda: reduces[1].second_add(1))
        at_chunk(index, 3, lambda: reduces[1].first_add(3), lambda: reduces[1].second_add(2))
        at_chunk(index, 5, lambda: reduces[1].second_add(3))
        return (
            sums[0] + column_sums(upstream),
            sums[1] + column_sums(upstream * hidden_one[span(index), :].astype(f32)),
        )

    sums = lax.fori_loop(0, CHUNKS, second_back, (zero_row, zero_row))
    sum_one_back = Sum(7)
    sum_one_back.start(sums[0], xhat_sum(0, *sums))
    columns_copy(0).start()
    columns_copy(1).start()
    weight_copy = pltpu.make_async_copy(weights[0], outs.low_one, mem.column_sem.at[BLOCKS])
    weight_copy.start()
    sum_one_back.middle()
    grad_coefs(0, sum_one_back.finish(), row_total)

    def put_one(pixel, cols, value):
        act_two[pl.ds(pl.multiple_of(pixel * views, 16), views), cols] = value

    apply_grad(hidden_one, slope_one, put_one)
    grad_copy = pltpu.make_async_copy(act_two, outs.one_low, mem.column_sem.at[BLOCKS + 1])
    grad_copy.start()
    weight_copy.wait()

    def block_grad(block):
        columns_copy(block).wait()
        start = feature_rows[block % 2]
        grad = dot_rows(hidden_three[start : start + rows, :], act_two[...])
        weights[0][block] = grad.astype(bf16).reshape(plan.x, -1, C_MID)
        if block + 2 < BLOCKS:
            columns_copy(block + 2).start()

    one = reduces[0]
    block_grad(0)
    one.core_start(0)
    block_grad(1)
    one.core_start(1)
    one.core_add(0)
    block_grad(2)
    one.core_start(2)
    one.core_add(1)
    one.first_add(0)
    reduces[1].finish()
    block_grad(3)
    one.core_start(3)
    one.core_add(2)
    one.first_add(1)
    one.second_add(0)
    one.core_add(3)
    one.first_add(2)
    one.second_add(1)
    one.first_add(3)
    one.second_add(2)
    one.second_add(3)
    one.finish()
    grad_copy.wait()
    pool_copy.wait()
    squares = mem.squares[...]
    norm_grads = outs.norm_grad[...]
    scalars = outs.scalars
    if plan.inside:
        squares = Sum(8).all(squares, squares)[0:1]
    norm_squares = column_sums(norm_grads * norm_grads)
    for place in range(norm_squares.shape[1] // LANES):
        squares = squares + norm_squares[:, place * LANES : (place + 1) * LANES]
    scalars[...] = jnp.zeros_like(scalars)
    scalars[0:1, :] = objective_row
    scalars[1:2, :] = squares
    if not plan.inside:
        stores = [
            pltpu.make_async_copy(gradients[which], outs.grads[which], mem.bulk_send.at[which])
            for which in range(5)
        ]
        for store in stores:
            store.start()
        for store in stores:
            store.wait()


def weight_shapes():
    return (
        (4, 2, 256, C_MID),
        (9 * C_MID, C_MID),
        (BLOCKS, 4, 2, 64, C_MID),
        (4, 2, 256, P_HID),
        (4, 2, P_OUT, P_OUT),
    )


def run_kernel(plan, features, order, shards, norm):
    rows, views = plan.rows, plan.views
    in_vmem = pl.BlockSpec(memory_space=pltpu.VMEM)
    anywhere = pl.BlockSpec(memory_space=pl.ANY)
    shapes = weight_shapes()
    operands = [features, order, norm, *shards]
    in_specs = [anywhere, in_vmem, in_vmem] + [in_vmem if plan.inside else anywhere] * 5
    results = [
        ((rows, C_IN), bf16, anywhere),
        ((rows, C_MID), bf16, anywhere),
        (shapes[0], bf16, anywhere),
        ((views, C_IN), f32, anywhere),
        ((2, norm_width()), f32, in_vmem),
        ((8, LANES), f32, in_vmem),
    ]
    for which, shard in enumerate(shards):
        if plan.inside:
            results.append((shard.shape, f32, in_vmem))
        else:
            results.append((shapes[which], bf16, anywhere))
    dma = pltpu.SemaphoreType.DMA

    def sum_room(width):
        return SumRoom(
            pltpu.VMEM((plan.dp, 2, width), f32),
            pltpu.VMEM((plan.fsdp, 2, width), f32),
            dma((plan.dp,)),
            dma((plan.dp,)),
            dma((plan.fsdp,)),
            dma((plan.fsdp,)),
        )

    def matrix_room():
        size = plan.embed_rows
        return MatrixRoom(
            pltpu.VMEM((plan.dp, size, P_OUT), f32),
            pltpu.VMEM((plan.dp, size, P_OUT), f32),
            pltpu.VMEM((plan.fsdp, size, P_OUT), f32),
            pltpu.VMEM((plan.dp, size, P_OUT), f32),
            dma((plan.dp,)),
            dma((plan.dp,)),
            dma((plan.fsdp,)),
            dma((plan.fsdp,)),
            dma((plan.dp,)),
            dma((plan.dp,)),
        )

    scratch = Mem(
        w=[pltpu.VMEM(shape, bf16) for shape in shapes],
        r3=pltpu.VMEM(shapes[2], bf16),
        r4=pltpu.VMEM(shapes[3], bf16),
        r5=pltpu.VMEM(shapes[4], bf16),
        stage=pltpu.VMEM((max(3 * BLOCKS * plan.chunk, 9 * C_MID), C_MID), bf16),
        stage_sem=dma((2, 3, BLOCKS)),
        column_sem=dma((BLOCKS + 3,)),
        h1=pltpu.VMEM((rows, C_MID), bf16),
        d1=pltpu.VMEM((rows, C_MID), bf16),
        h2=pltpu.VMEM((rows, C_MID), bf16),
        d2=pltpu.VMEM((rows, C_MID), bf16),
        a2=pltpu.VMEM((rows, C_MID), bf16),
        h3=pltpu.VMEM((BLOCKS * rows, C_MID), bf16),
        pad1=pltpu.VMEM((SIDE + 2, (SIDE + 2) * views, C_MID), bf16),
        pad2=pltpu.VMEM((SIDE + 2, (SIDE + 2) * views, C_MID), bf16),
        pool=pltpu.VMEM((views, C_IN), f32),
        pool_slope=pltpu.VMEM((views, C_IN), f32),
        pool_bend=pltpu.VMEM((views, C_IN), f32),
        pooled=pltpu.VMEM((views, C_IN), bf16),
        proj_act=pltpu.VMEM((views, P_HID), bf16),
        proj_slope=pltpu.VMEM((views, P_HID), f32),
        proj_hidden=pltpu.VMEM((views, P_HID), f32),
        coef=pltpu.VMEM((8, C_IN), f32),
        stats=pltpu.VMEM((2, norm_width()), f32),
        norm=pltpu.VMEM((2, norm_width()), f32),
        norm_tiles=pltpu.VMEM((plan.dp, plan.fsdp, 2, LANES), f32),
        norm_s0=dma((plan.dp,)),
        norm_r0=dma((plan.dp,)),
        norm_s1=dma((plan.fsdp,)),
        norm_r1=dma((plan.fsdp,)),
        bulk_send=dma((300,)),
        bulk_recv=dma((300,)),
        mats=[matrix_room(), matrix_room()],
        sums=[
            sum_room(width)
            for width in (C_MID, C_MID, C_IN, P_HID, LANES)
        ],
        squares=pltpu.VMEM((1, LANES), f32),
    )
    values = pl.pallas_call(
        lambda *refs: kernel(plan, *refs),
        out_shape=[jax.ShapeDtypeStruct(shape, kind) for shape, kind, _ in results],
        in_specs=in_specs,
        out_specs=[spec for _, _, spec in results],
        scratch_shapes=[scratch],
        compiler_params=pltpu.CompilerParams(
            collective_id=1, has_side_effects=True, vmem_limit_bytes=63 * 2**20
        ),
        name="train_step",
    )(*operands)
    return Outs(*values[:6], values[6:])


def norm_width():
    return 2 * C_MID + C_IN + P_HID


def adam_update(weight, moment_one, moment_two, gradient, step_rate, weight_decay):
    first_new = beta_first * moment_one + (1.0 - beta_first) * gradient
    second_new = beta_second * moment_two + (1.0 - beta_second) * gradient * gradient
    first_hat = first_new / (1.0 - beta_first**STEP)
    second_hat = second_new / (1.0 - beta_second**STEP)
    weight_new = weight - step_rate * (
        first_hat / (jnp.sqrt(second_hat) + adam_epsilon) + weight_decay * weight
    )
    return (weight_new, first_new, second_new)


def gather_full(weight):
    outer = lax.all_gather(weight.astype(bf16), FSDP, axis=0, tiled=True)
    return lax.all_gather(outer, DP, axis=1, tiled=True)


def scatter_full(gradient):
    inner = lax.psum_scatter(gradient.astype(f32), DP, scatter_dimension=1, tiled=True)
    return lax.psum_scatter(inner, FSDP, scatter_dimension=0, tiled=True)


def body(features, view_order, *state):
    masters, firsts, seconds = state[:6], state[6:12], state[12:18]
    dp_size, fsdp_size = lax.axis_size(DP), lax.axis_size(FSDP)
    views = features.shape[0]
    inside = dp_size == 4 and fsdp_size == 8
    plan = Plan(dp_size, fsdp_size, views, inside)
    image_total = views * plan.devices // 2
    pixels = jnp.swapaxes(features, 0, 1).reshape(-1, C_IN)
    norm_params = masters[5]
    shapes = weight_shapes()
    if inside:
        shards = list(masters[:4]) + [masters[4].T]
        norm = norm_params
    else:
        full = [gather_full(weight) for weight in masters[:5]]
        shards = [
            full[0].reshape(shapes[0]),
            full[1],
            full[2].reshape(C_MID, BLOCKS, C_MID).swapaxes(0, 1).reshape(shapes[2]),
            full[3].reshape(shapes[3]),
            full[4].reshape(4, 2, P_OUT, P_OUT).swapaxes(2, 3),
        ]
        norm = lax.all_gather(norm_params.astype(bf16), (DP, FSDP), axis=1, tiled=True).astype(f32)
    got = run_kernel(plan, pixels, view_order, shards, norm)
    grads = list(got.grads)
    squares = jnp.sum(got.scalars[1])
    if inside:
        owned = grads[:4] + [grads[4].T]
    else:
        whole_grads = [
            grads[0].reshape(C_IN, C_MID),
            grads[1],
            grads[2].reshape(BLOCKS, C_MID, C_MID).swapaxes(0, 1).reshape(C_MID, C_IN),
            grads[3].reshape(C_IN, P_HID),
            grads[4].swapaxes(2, 3).reshape(P_HID, P_OUT),
        ]
        owned = [scatter_full(gradient) for gradient in whole_grads]
        squares = squares + lax.psum(sum(jnp.sum(grad * grad) for grad in owned), (DP, FSDP))
    width = norm_params.shape[1]
    owner = lax.axis_index((DP, FSDP))
    owned.append(lax.dynamic_slice_in_dim(got.norm_grad, owner * width, width, 1))
    grad_norm = jnp.sqrt(squares)
    factor = clip_level / jnp.maximum(grad_norm, clip_level)

    summed_grad = got.slope.reshape(PIX, views, C_IN).astype(f32) * got.pool_grad[None]
    back = lax.dot_general(
        got.one_low, got.low_one.reshape(C_IN, C_MID), (((1,), (1,)), ((), ())), preferred_element_type=f32
    )
    input_grad = jnp.swapaxes(summed_grad + back.reshape(PIX, views, C_IN), 0, 1)

    step_rates = (
        C_IN ** (-0.5),
        (9 * C_MID) ** (-0.5),
        C_MID ** (-0.5),
        C_IN ** (-0.5),
        P_HID ** (-0.5),
        norm_rate,
    )
    decays = (decay_rate, decay_rate, decay_rate, decay_rate, decay_rate, 0.0)
    updates = [
        adam_update(masters[i], firsts[i], seconds[i], owned[i] * factor, step_rates[i], decays[i]) for i in range(6)
    ]
    return (
        jnp.sum(got.scalars[0]) / image_total,
        input_grad,
        grad_norm,
        *[update[0] for update in updates],
        *[update[1] for update in updates],
        *[update[2] for update in updates],
    )


def solution(mesh):
    views = P((DP, FSDP), None, None)
    split = P(FSDP, DP)
    norm = P(None, (DP, FSDP))
    params = (split,) * 5 + (norm,)
    return jax.shard_map(
        body,
        mesh=mesh,
        in_specs=(views, P((DP, FSDP), None)) + params * 3,
        out_specs=(P(), views, P()) + params * 3,
        check_vma=False,
    )
```

```python
from typing import Any, NamedTuple

import jax
import jax.numpy as jnp
from jax import lax
from jax.experimental import pallas as pl
from jax.experimental.pallas import tpu as pltpu
from jax.sharding import PartitionSpec as P

C_IN = 2048
C_MID = 512
P_HID = 1024
P_OUT = 128
SIDE = 7
STEP = 10
PIX = 49
LANES = 128
BLOCKS = C_IN // C_MID
CHUNKS = SIDE
SLOTS = 6


highest = lax.Precision.HIGHEST
bf16 = jnp.bfloat16
f32 = jnp.float32
norm_epsilon = 1e-05
ridge_term = 0.01
clip_level = 0.1
beta_first = 0.9
beta_second = 0.999
adam_epsilon = 1e-08
decay_rate = 0.05
norm_rate = 0.5
bell_scale = 0.3989422804014327
root_half = 0.5**0.5
bell_rate = -0.7213475204444817
DP, FSDP = "dp", "fsdp"


def gelu_pair(values):
    below = 0.5 + 0.5 * lax.erf(values * root_half)
    bell = jnp.exp2(values * values * bell_rate)
    return values * below, below + values * bell * bell_scale


def dot(left, right):
    return jnp.dot(left, right, preferred_element_type=f32)


def dot_cols(left, right):
    return lax.dot_general(left, right, (((1,), (1,)), ((), ())), preferred_element_type=f32)


def dot_rows(left, right):
    return lax.dot_general(left, right, (((0,), (0,)), ((), ())), preferred_element_type=f32)


def exact_cols(left, right):
    return lax.dot_general(
        left, right, (((1,), (1,)), ((), ())), precision=highest, preferred_element_type=f32
    )


def exact_rows(left, right):
    return lax.dot_general(
        left, right, (((0,), (0,)), ((), ())), precision=highest, preferred_element_type=f32
    )


def exact_dot(left, right):
    return jnp.dot(left, right, precision=highest, preferred_element_type=f32)


def inverse_factors(matrices):
    row_top = lax.broadcasted_iota(jnp.int32, (8, P_OUT), 0)
    row_all = lax.broadcasted_iota(jnp.int32, (P_OUT, P_OUT), 0)
    col_all = lax.broadcasted_iota(jnp.int32, (P_OUT, P_OUT), 1)

    def one_step(place, left, right):
        scale = lax.rsqrt(left[place : place + 1, place : place + 1])
        left_row = left[place : place + 1, :] * scale
        right_row = right[place : place + 1, :] * scale
        column = left[:, place : place + 1] * scale
        left = left - column * left_row
        right = right - column * right_row
        here = row_top == place
        left = jnp.concatenate([jnp.where(here, 0.0, left[:8]), left[8:]], axis=0)
        right = jnp.concatenate(
            [jnp.where(here, jnp.broadcast_to(right_row, (8, P_OUT)), right[:8]), right[8:]], axis=0
        )
        return left, right

    def panel(_, pairs):
        pairs = list(pairs)
        for place in range(8):
            for which in range(len(pairs)):
                pairs[which] = one_step(place, *pairs[which])
        return tuple(
            (
                pltpu.roll(jnp.concatenate([left[8:], left[:8]], axis=0), P_OUT - 8, 1),
                jnp.concatenate([right[8:], right[:8]], axis=0),
            )
            for left, right in pairs
        )

    start = tuple((matrix, (row_all == col_all).astype(f32)) for matrix in matrices)
    done = lax.fori_loop(0, P_OUT // 8, panel, start)
    return [right for _, right in done]


def pack_pair(first, second):
    row = lax.broadcasted_iota(jnp.int32, (P_OUT, P_OUT), 0)
    col = lax.broadcasted_iota(jnp.int32, (P_OUT, P_OUT), 1)
    packed = jnp.where(row >= col, first, second.T)
    diagonal = jnp.sum(jnp.where(row == col, second, 0.0), axis=0, keepdims=True)
    return packed, diagonal


def unpack_pair(packed, diagonal):
    row = lax.broadcasted_iota(jnp.int32, (P_OUT, P_OUT), 0)
    col = lax.broadcasted_iota(jnp.int32, (P_OUT, P_OUT), 1)
    turned = packed.T
    first = jnp.where(row >= col, packed, turned)
    second = jnp.where(row < col, packed, jnp.where(row == col, diagonal, turned))
    return first, second


class Ins(NamedTuple):
    features: Any
    order: Any
    norm: Any
    shards: Any


class Outs(NamedTuple):
    slope: Any
    features_grad: Any
    norm_grad: Any
    scalars: Any
    grads: Any


class SumRoom(NamedTuple):
    dp: Any
    fsdp: Any
    s0: Any
    r0: Any
    s1: Any
    r1: Any


class MatrixRoom(NamedTuple):
    pack: Any
    dp: Any
    fsdp: Any
    all: Any
    s0: Any
    r0: Any
    s1: Any
    r1: Any
    s2: Any
    r2: Any


class Mem(NamedTuple):
    w: Any
    g1: Any
    row_sums: Any
    r3: Any
    r4: Any
    r5: Any
    stage: Any
    stage_sem: Any
    column_sem: Any
    h1: Any
    d1: Any
    h2: Any
    d2: Any
    a2: Any
    h3: Any
    pad1: Any
    pad2: Any
    pool: Any
    pool_slope: Any
    pool_bend: Any
    pooled: Any
    proj_act: Any
    proj_slope: Any
    proj_hidden: Any
    coef: Any
    stats: Any
    norm: Any
    norm_tiles: Any
    norm_s0: Any
    norm_r0: Any
    norm_s1: Any
    norm_r1: Any
    bulk_send: Any
    bulk_recv: Any
    mats: Any
    sums: Any
    squares: Any


class Plan:
    def __init__(self, dp_size, fsdp_size, views, inside):
        self.dp = dp_size
        self.fsdp = fsdp_size
        self.devices = dp_size * fsdp_size
        self.views = views
        self.rows = views * PIX
        self.chunk = views * SIDE
        self.inside = inside
        self.z = 4
        self.x = 2
        self.half = (128, 288, 32, 128, 16)
        self.width = (128, 128, 512, 256, 128)
        piece = P_OUT + 8
        self.embed_rows = -(-piece // (8 * dp_size)) * 8


def kernel(plan, *refs):
    ins, outs, mem = Ins(*refs[:3], refs[3:8]), Outs(*refs[8:12], refs[12:17]), refs[17]
    views, chunk, rows = plan.views, plan.chunk, plan.rows
    row_total = float(rows * plan.devices)
    view_total = float(views * plan.devices)
    image_total = float(views * plan.devices // 2)
    dp_me, fsdp_me = lax.axis_index(DP), lax.axis_index(FSDP)
    y_me, c_me = dp_me // 2, dp_me % 2
    z_me, x_me = fsdp_me // 2, fsdp_me % 2
    y_other, c_other, x_other = 1 - y_me, 1 - c_me, 1 - x_me

    barrier = pltpu.get_barrier_semaphore()

    @pl.loop(1, plan.dp)
    def _(step):
        pl.semaphore_signal(
            barrier, 1, device_id={DP: lax.rem(dp_me + step, plan.dp)}, device_id_type=pl.DeviceIdType.MESH
        )

    @pl.loop(1, plan.fsdp)
    def _(step):
        pl.semaphore_signal(
            barrier, 1, device_id={FSDP: lax.rem(fsdp_me + step, plan.fsdp)}, device_id_type=pl.DeviceIdType.MESH
        )

    pl.semaphore_wait(barrier, plan.dp + plan.fsdp - 2)

    def share(axis, size, me, source_of, slots, send, recv):
        def outgoing(step):
            partner = lax.rem(me + step, size)
            return pltpu.make_async_remote_copy(
                src_ref=source_of(partner),
                dst_ref=slots.at[me],
                send_sem=send.at[step],
                recv_sem=recv.at[me],
                device_id={axis: partner},
                device_id_type=pl.DeviceIdType.MESH,
            )

        def incoming(step):
            source = lax.rem(me + step, size)
            return pltpu.make_async_remote_copy(
                src_ref=slots.at[source],
                dst_ref=slots.at[source],
                send_sem=send.at[step],
                recv_sem=recv.at[source],
                device_id={axis: source},
                device_id_type=pl.DeviceIdType.MESH,
            )

        def start():
            pl.loop(1, size)(lambda step: outgoing(step).start())

        def wait():
            pl.loop(1, size)(lambda step: incoming(step).wait_recv())
            pl.loop(1, size)(lambda step: outgoing(step).wait_send())

        return start, wait

    def add_slots(slots, size):
        total = slots[0]
        for place in range(1, size):
            total = total + slots[place]
        return total

    class Sum:
        def __init__(self, which):
            part = mem.sums[(0, 1, 2, 3, 4, 4, 5, 0, 1, 6)[which]]
            self.dp_slots, self.fsdp_slots = part.dp, part.fsdp
            self.dp_copy = share(
                DP, plan.dp, dp_me, lambda _: self.dp_slots.at[dp_me], self.dp_slots, part.s0, part.r0
            )
            self.fsdp_copy = share(
                FSDP, plan.fsdp, fsdp_me, lambda _: self.fsdp_slots.at[fsdp_me], self.fsdp_slots, part.s1, part.r1
            )

        def start(self, *values):
            for place, value in enumerate(values):
                self.dp_slots[dp_me, place : place + 1, :] = value
            self.dp_copy[0]()

        def middle(self):
            self.dp_copy[1]()
            self.fsdp_slots[fsdp_me] = add_slots(self.dp_slots, plan.dp)
            self.fsdp_copy[0]()

        def finish(self):
            self.fsdp_copy[1]()
            return add_slots(self.fsdp_slots, plan.fsdp)

        def all(self, *values):
            self.start(*values)
            self.middle()
            return self.finish()

    def sum_matrix(which, matrix, extra):
        part = mem.mats[which]
        size = plan.embed_rows
        pack = part.pack
        flat = jnp.concatenate(
            [matrix] + extra + [jnp.zeros((size * plan.dp - P_OUT - len(extra), P_OUT), f32)], axis=0
        )
        for place in range(plan.dp):
            pack[place] = flat[place * size : (place + 1) * size]
        start, wait = share(DP, plan.dp, dp_me, lambda to: pack.at[to], part.dp, part.s0, part.r0)
        start()
        part.dp[dp_me] = pack[dp_me]
        wait()
        part.fsdp[fsdp_me] = add_slots(part.dp, plan.dp)
        start, wait = share(
            FSDP, plan.fsdp, fsdp_me, lambda _: part.fsdp.at[fsdp_me], part.fsdp, part.s1, part.r1
        )
        start()
        wait()
        part.all[dp_me] = add_slots(part.fsdp, plan.fsdp)
        start, wait = share(
            DP, plan.dp, dp_me, lambda _: part.all.at[dp_me], part.all, part.s2, part.r2
        )
        start()
        wait()
        total = jnp.concatenate([part.all[place] for place in range(plan.dp)], axis=0)
        return total[:P_OUT], [total[P_OUT + place : P_OUT + place + 1] for place in range(len(extra))]

    weights = mem.w
    everything = slice(None)

    def row_span(which, half):
        size = plan.half[which]
        if half is None:
            return 0, 2 * size
        return half * size, size

    def column_span(which, dp_index):
        width = plan.width[which]
        return pl.ds(pl.multiple_of(dp_index * width, width), width)

    def places(which, z_index, x_index, dp_index, half):
        start, size = row_span(which, half)
        if which == 1:
            z_list = range(plan.z) if z_index is None else [z_index]
            x_list = range(plan.x) if x_index is None else [x_index]
            return [
                (
                    pl.ds(pl.multiple_of((z_one * plan.x + x_one) * 576 + start, 16), size),
                    column_span(which, dp_index),
                )
                for z_one in z_list
                for x_one in x_list
            ]
        z_one = everything if z_index is None else z_index
        x_one = everything if x_index is None else x_index
        if which == 2:
            return [(dp_index, z_one, x_one, pl.ds(start, size), everything)]
        if which == 4:
            return [(z_one, x_one, pl.ds(pl.multiple_of(dp_index * 32 + start, 16), size), everything)]
        return [(z_one, x_one, pl.ds(start, size), column_span(which, dp_index))]

    recv_parts = {
        1: lambda index: mem.h3.at[index],
        0: lambda index: mem.r4.at[index],
        2: lambda index: mem.r3.at[index],
        3: lambda index: mem.r4.at[index],
        4: lambda index: mem.r5.at[index],
    }

    counter = [0]

    class Batch:
        def __init__(self, sources, targets, landings, axis, partner):
            base = counter[0]
            counter[0] += len(sources)
            send, recv = mem.bulk_send, mem.bulk_recv
            self.out = [
                pltpu.make_async_remote_copy(
                    src_ref=source,
                    dst_ref=target,
                    send_sem=send.at[base + place],
                    recv_sem=recv.at[base + place],
                    device_id={axis: partner},
                    device_id_type=pl.DeviceIdType.MESH,
                )
                for place, (source, target) in enumerate(zip(sources, targets))
            ]
            self.come = [
                pltpu.make_async_remote_copy(
                    src_ref=landing,
                    dst_ref=landing,
                    send_sem=send.at[base + place],
                    recv_sem=recv.at[base + place],
                    device_id={axis: partner},
                    device_id_type=pl.DeviceIdType.MESH,
                )
                for place, landing in enumerate(landings)
            ]

        def start(self):
            for copy in self.out:
                copy.start()

        def arrive(self):
            for copy in self.come:
                copy.wait_recv()

        def leave(self):
            for copy in self.out:
                copy.wait_send()

    class LineBatch:
        def __init__(self, source_of, target_of, landing_of):
            base = counter[0]
            counter[0] += plan.z
            send, recv = mem.bulk_send, mem.bulk_recv
            self.out, self.come = [], []
            for step in range(1, plan.z):
                z_to = (z_me + step) % plan.z
                self.out.append(
                    pltpu.make_async_remote_copy(
                        src_ref=source_of(z_to),
                        dst_ref=target_of(z_to),
                        send_sem=send.at[base + step],
                        recv_sem=recv.at[base + z_me],
                        device_id={FSDP: z_to * plan.x + x_me},
                        device_id_type=pl.DeviceIdType.MESH,
                    )
                )
                self.come.append(
                    pltpu.make_async_remote_copy(
                        src_ref=landing_of(z_to),
                        dst_ref=landing_of(z_to),
                        send_sem=send.at[base + step],
                        recv_sem=recv.at[base + z_to],
                        device_id={FSDP: z_to * plan.x + x_me},
                        device_id_type=pl.DeviceIdType.MESH,
                    )
                )

        start, arrive, leave = Batch.start, Batch.arrive, Batch.leave

    def pick(ref, indexes):
        return [ref.at[index] for index in indexes]

    def own_dp(y_index, c_index):
        return y_index * 2 + c_index

    x_partner = z_me * plan.x + x_other
    y_partner = own_dp(y_other, c_me)
    c_partner = own_dp(y_me, c_other)
    dp_far = own_dp(y_other, c_other)

    class Gather:
        def __init__(self, which):
            ref = weights[which]
            self.which = which

            def at(*index):
                return pick(ref, places(which, *index))

            own = at(z_me, x_me, dp_me, None)[0]
            self.line = LineBatch(
                lambda _: own, lambda _: own, lambda z_from: at(z_from, x_me, dp_me, None)[0]
            )
            sent, come = at(None, x_me, dp_me, 0), at(None, x_other, dp_me, 0)
            self.x_first = Batch(sent, sent, come, FSDP, x_partner)
            sent, come = at(None, x_me, dp_me, 1), at(None, x_me, y_partner, 1)
            self.y_first = Batch(sent, sent, come, DP, y_partner)
            sent, come = at(None, None, dp_me, 0), at(None, None, y_partner, 0)
            self.y_second = Batch(sent, sent, come, DP, y_partner)
            sent = at(None, x_me, dp_me, 1) + at(None, x_me, y_partner, 1)
            come = at(None, x_other, dp_me, 1) + at(None, x_other, y_partner, 1)
            self.x_second = Batch(sent, sent, come, FSDP, x_partner)
            sent = at(None, None, dp_me, None) + at(None, None, y_partner, None)
            come = at(None, None, c_partner, None) + at(None, None, dp_far, None)
            self.core = Batch(sent, sent, come, DP, c_partner)
            self.stages = ((self.line,), (self.x_first, self.y_first), (self.y_second, self.x_second), (self.core,))

        def put_own(self, value):
            weights[self.which][places(self.which, z_me, x_me, dp_me, None)[0]] = value.astype(bf16)

        def start(self, stage):
            if plan.inside:
                for batch in self.stages[stage]:
                    batch.start()

        def arrive(self, stage):
            if plan.inside:
                for batch in self.stages[stage]:
                    batch.arrive()

        def step(self, stage):
            self.arrive(stage)
            self.start(stage + 1)

        def leave(self):
            if plan.inside:
                for stage in self.stages:
                    for batch in stage:
                        batch.leave()

    class Piece:
        def __init__(self, which, ref, room, z_index):
            def at(*index):
                return pick(ref, places(which, z_index, *index))

            def land(*index):
                return [room(index_one) for index_one in places(which, z_index, *index)]

            self.z = z_index
            self.core = Batch(
                at(None, c_partner, None) + at(None, dp_far, None),
                land(None, c_partner, None) + land(None, dp_far, None),
                land(None, dp_me, None) + land(None, y_partner, None),
                DP,
                c_partner,
            )
            self.y_first = Batch(
                at(None, y_partner, 0), land(None, dp_far, 0), land(None, c_partner, 0), DP, y_partner
            )
            self.x_first = Batch(
                at(x_other, dp_me, 1) + at(x_other, y_partner, 1),
                land(x_other, c_partner, 1) + land(x_other, dp_far, 1),
                land(x_me, c_partner, 1) + land(x_me, dp_far, 1),
                FSDP,
                x_partner,
            )
            self.x_second = Batch(
                at(x_other, dp_me, 0), land(x_other, dp_far, 0), land(x_me, dp_far, 0), FSDP, x_partner
            )
            self.y_second = Batch(
                at(x_me, y_partner, 1), land(x_other, dp_far, 1), land(x_other, c_partner, 1), DP, y_partner
            )

    class Reduce:
        def __init__(self, which, ref, cut):
            self.which, self.ref, self.room = which, ref, recv_parts[which]
            self.pieces = [
                Piece(which, ref, self.room, z_index) for z_index in (range(plan.z) if cut else [None])
            ]
            self.base = counter[0]
            counter[0] += plan.z

        def line_copy(self, z_to):
            return pltpu.make_async_remote_copy(
                src_ref=self.ref.at[places(self.which, z_to, x_me, dp_me, None)[0]],
                dst_ref=self.room(places(self.which, z_me, x_other, dp_far, None)[0]),
                send_sem=mem.bulk_send.at[self.base + z_to],
                recv_sem=mem.bulk_recv.at[self.base + z_me],
                device_id={FSDP: z_to * plan.x + x_me},
                device_id_type=pl.DeviceIdType.MESH,
            )

        def line_room(self, z_from):
            return self.room(places(self.which, z_from, x_other, dp_far, None)[0])

        def add(self, z_index, pairs):
            def one(z_one):
                for here, there in pairs:
                    for x_step in range(plan.x) if here[0] is None else [None]:
                        x_here = x_step if here[0] is None else here[0]
                        x_there = x_step if there[0] is None else there[0]
                        index = places(self.which, z_one, x_here, *here[1:])[0]
                        other = places(self.which, z_one, x_there, *there[1:])[0]
                        total = self.ref[index].astype(f32) + self.room(other)[...].astype(f32)
                        self.ref[index] = total.astype(bf16)

            if z_index is None:
                pl.loop(0, plan.z)(one)
            else:
                one(z_index)

        def core_start(self, place=0):
            if plan.inside:
                self.pieces[place].core.start()

        def core_add(self, place=0):
            if plan.inside:
                piece = self.pieces[place]
                piece.core.arrive()
                self.add(piece.z, [((None, dp_me, None),) * 2, ((None, y_partner, None),) * 2])
                piece.y_first.start()
                piece.x_first.start()

        def first_add(self, place=0):
            if plan.inside:
                piece = self.pieces[place]
                piece.y_first.arrive()
                self.add(piece.z, [((None, dp_me, 0), (None, c_partner, 0))])
                piece.x_second.start()
                piece.x_first.arrive()
                self.add(
                    piece.z, [((x_me, dp_me, 1), (x_me, c_partner, 1)), ((x_me, y_partner, 1), (x_me, dp_far, 1))]
                )
                piece.y_second.start()

        def second_add(self, place=0):
            if plan.inside:
                piece = self.pieces[place]
                piece.x_second.arrive()
                piece.y_second.arrive()
                self.add(
                    piece.z, [((x_me, dp_me, 0), (x_me, dp_far, 0)), ((x_me, dp_me, 1), (x_other, c_partner, 1))]
                )
                if piece.z is None:
                    for step in range(1, plan.z):
                        self.line_copy((z_me + step) % plan.z).start()
                else:

                    @pl.when(z_me != piece.z)
                    def _():
                        self.line_copy(piece.z).start()

        def finish(self):
            if not plan.inside:
                return
            total = self.ref[places(self.which, z_me, x_me, dp_me, None)[0]].astype(f32)
            for step in range(1, plan.z):
                z_from = (z_me + step) % plan.z
                room = self.line_room(z_from)
                pltpu.make_async_remote_copy(
                    src_ref=room,
                    dst_ref=room,
                    send_sem=mem.bulk_send.at[self.base + z_from],
                    recv_sem=mem.bulk_recv.at[self.base + z_from],
                    device_id={FSDP: z_from * plan.x + x_me},
                    device_id_type=pl.DeviceIdType.MESH,
                ).wait_recv()
                total = total + room[...].astype(f32)
            outs.grads[self.which][...] = total
            squares = jnp.sum(total * total, axis=0, keepdims=True)
            folded = squares[:, :LANES]
            for place in range(1, squares.shape[1] // LANES):
                folded = folded + squares[:, place * LANES : (place + 1) * LANES]
            mem.squares[...] += folded
            for step in range(1, plan.z):
                self.line_copy((z_me + step) % plan.z).wait_send()
            for piece in self.pieces:
                for batch in (piece.core, piece.y_first, piece.x_first, piece.x_second, piece.y_second):
                    batch.leave()

    gathers = [Gather(which) for which in range(5)]
    gradients = [mem.g1, mem.stage.at[pl.ds(0, 9 * C_MID)], weights[2], weights[3], weights[4]]
    reduces = [Reduce(which, gradients[which], which < 2) for which in range(5)]
    mem.squares[...] = jnp.zeros((1, LANES), f32)

    if plan.inside:
        for which in range(5):
            gathers[which].put_own(ins.shards[which][...])
            gathers[which].start(0)
        tiles = mem.norm_tiles
        tiles[dp_me, fsdp_me] = ins.norm[...].astype(bf16).astype(f32)
        norm_dp = share(
            DP, plan.dp, dp_me, lambda _: tiles.at[dp_me, fsdp_me], tiles.at[:, fsdp_me], mem.norm_s0, mem.norm_r0
        )
        norm_dp[0]()
    else:
        loads = [
            pltpu.make_async_copy(ins.shards[which], weights[which], mem.bulk_send.at[which])
            for which in range(5)
        ]
        for load in loads:
            load.start()

    stage_ref, stage_sem = mem.stage, mem.stage_sem
    pieces = BLOCKS * CHUNKS

    def stage_rows(index, pixel=0, count=chunk):
        return pl.ds(pl.multiple_of(lax.rem(index, SLOTS) * chunk + pixel * views, 16), count)

    def hidden_rows(index, pixel=0, count=chunk):
        return pl.ds(pl.multiple_of(index * chunk + pixel * views, 16), count)

    def piece_copy(array, index, into):
        block, place = index // CHUNKS, lax.rem(index, CHUNKS)
        outer = array.at[
            pl.ds(pl.multiple_of(place * chunk, 16), chunk), pl.ds(pl.multiple_of(block * C_MID, LANES), C_MID)
        ]
        inner = stage_ref.at[stage_rows(index)]
        source, target = (outer, inner) if into else (inner, outer)
        return pltpu.make_async_copy(source, target, stage_sem.at[0 if into else 1, lax.rem(index, SLOTS)])

    def first_loads(array):
        for index in range(3):
            piece_copy(array, index, True).start()

    def next_load(array, index):
        @pl.when(index + 3 < pieces)
        def _():
            piece_copy(array, index + 3, True).start()

    def save(array, index):
        piece_copy(array, index, False).start()

        @pl.when(index >= 2)
        def _():
            piece_copy(array, index - 2, False).wait()

    def last_saves(array):
        for index in (pieces - 2, pieces - 1):
            piece_copy(array, index, False).wait()

    def piece_columns(index, part):
        return pl.ds(pl.multiple_of(index // CHUNKS * C_MID + part * LANES, LANES), LANES)

    features, slope_hbm = ins.features, outs.slope
    hidden_three = mem.h3

    def feature_copy(block, target):
        return pltpu.make_async_copy(
            features.at[:, pl.ds(block * C_MID, C_MID)], target, mem.column_sem.at[block]
        )

    feature_loads = [
        feature_copy(block, hidden_three.at[pl.ds(block * rows, rows)]) for block in range(BLOCKS)
    ]
    for copy in feature_loads:
        copy.start()
    first_loads(features)

    padded_one, padded_two = mem.pad1, mem.pad2
    for padded in (padded_one, padded_two):
        for edge in (0, SIDE + 1):
            padded[edge] = jnp.zeros((padded.shape[1], C_MID), bf16)
        for edge in (0, SIDE + 1):
            padded[:, pl.ds(edge * views, views), :] = jnp.zeros((SIDE + 2, views, C_MID), bf16)

    if plan.inside:
        norm_dp[1]()
        norm_out = []
        norm_in = []
        for step in range(1, plan.fsdp):
            partner = (fsdp_me + step) % plan.fsdp
            norm_out.append(
                pltpu.make_async_remote_copy(
                    src_ref=tiles.at[:, fsdp_me],
                    dst_ref=tiles.at[:, fsdp_me],
                    send_sem=mem.norm_s1.at[step],
                    recv_sem=mem.norm_r1.at[fsdp_me],
                    device_id={FSDP: partner},
                    device_id_type=pl.DeviceIdType.MESH,
                )
            )
            norm_in.append(
                pltpu.make_async_remote_copy(
                    src_ref=tiles.at[:, partner],
                    dst_ref=tiles.at[:, partner],
                    send_sem=mem.norm_s1.at[step],
                    recv_sem=mem.norm_r1.at[partner],
                    device_id={FSDP: partner},
                    device_id_type=pl.DeviceIdType.MESH,
                )
            )
        for copy in norm_out:
            copy.start()
        gathers[0].step(0)
        gathers[0].step(1)
        gathers[0].step(2)
        gathers[1].step(0)
        for copy in norm_in:
            copy.wait_recv()
        for copy in norm_out:
            copy.wait_send()
        norm_all = mem.norm
        for dp_one in range(plan.dp):
            for fsdp_one in range(plan.fsdp):
                start = (dp_one * plan.fsdp + fsdp_one) * LANES
                norm_all[:, start : start + LANES] = tiles[dp_one, fsdp_one]
    else:
        for copy in loads:
            copy.wait()
        norm_all = mem.norm
        norm_all[...] = ins.norm[...]

    starts = (0, C_MID, 2 * C_MID, 2 * C_MID + C_IN, 2 * C_MID + C_IN + P_HID)

    def gain(layer):
        return norm_all[0:1, starts[layer] : starts[layer + 1]]

    coef, stats = mem.coef, mem.stats

    def norm_coefs(layer, totals, count, low=0):
        width = totals.shape[1]
        here, there = slice(low, low + width), slice(starts[layer] + low, starts[layer] + low + width)
        mean = totals[0:1] / count
        scaling = lax.rsqrt(totals[1:2] / count - mean * mean + norm_epsilon)
        slope = scaling * norm_all[0:1, there]
        stats[0:1, there] = mean
        stats[1:2, there] = scaling
        coef[0:1, here] = slope
        coef[1:2, here] = norm_all[1:2, there] - mean * slope

    def grad_coefs(layer, totals, count):
        width = starts[layer + 1] - starts[layer]
        mean = stats[0:1, starts[layer] : starts[layer + 1]]
        scaling = stats[1:2, starts[layer] : starts[layer + 1]]
        outs.norm_grad[0:1, starts[layer] : starts[layer + 1]] = totals[1:2]
        outs.norm_grad[1:2, starts[layer] : starts[layer + 1]] = totals[0:1]
        slope = scaling * gain(layer)
        bend = slope * scaling * totals[1:2] / count
        coef[0:1, :width] = slope
        coef[1:2, :width] = slope * totals[0:1] / count - mean * bend
        coef[2:3, :width] = bend

    def xhat_sum(layer, plain, product):
        mean = stats[0:1, starts[layer] : starts[layer + 1]]
        scaling = stats[1:2, starts[layer] : starts[layer + 1]]
        return scaling * (product - mean * plain)

    zero_row = jnp.zeros((1, C_MID), f32)

    def at_place(index, place, *moves):
        if plan.inside:

            @pl.when(index == place)
            def _():
                for move in moves:
                    move()

    def column_sums(value):
        return jnp.sum(value, axis=0, keepdims=True)

    def whole(which):
        value = weights[which][...]
        return value.reshape(-1, value.shape[-1])

    row_sums = mem.row_sums

    def clear_sums():
        row_sums[...] = jnp.zeros_like(row_sums)

    def count_in(cols, value, other):
        row_sums[0:1, cols] += column_sums(value)
        row_sums[1:2, cols] += column_sums(value * other)

    def own_columns(side):
        core = (c_me + side) % 2
        return [
            pl.ds(pl.multiple_of(half * (C_MID // 2) + core * LANES, LANES), LANES) for half in range(2)
        ]

    hidden_one, slope_one = mem.h1, mem.d1
    hidden_two, slope_two = mem.h2, mem.d2
    act_two = mem.a2
    long = rows // 3

    def span(index):
        return pl.ds(pl.multiple_of(index * chunk, 16), chunk)

    def long_rows(block, index):
        return pl.ds(pl.multiple_of(block * rows + index * long, 16), long)

    def put_sides(ref, at, sides, hidden):
        for place, cols in enumerate(sides):
            part = hidden[:, place * LANES : (place + 1) * LANES]
            ref[at, cols] = part.astype(bf16)
            count_in(cols, part, part)

    for copy in feature_loads:
        copy.wait()
    clear_sums()

    @pl.loop(0, 2)
    def _(side):
        sides = own_columns(side)

        @pl.loop(0, 3)
        def _(index):
            left = jnp.concatenate([hidden_three[long_rows(block, index), :] for block in range(BLOCKS)], axis=1)
            right = jnp.concatenate([weights[0][:, :, :, cols].reshape(C_IN, LANES) for cols in sides], axis=1)
            put_sides(hidden_one, long_rows(0, index), sides, dot(left, right))

        at_place(side, 0, lambda: gathers[0].arrive(3), lambda: gathers[1].step(1))

    sum_one = Sum(0)
    sum_one.start(row_sums[0:1, :C_MID], row_sums[1:2, :C_MID])
    gathers[2].step(0)
    sum_one.middle()
    clear_sums()
    norm_coefs(0, sum_one.finish(), row_total)

    def activate(hidden_ref, slope_ref, put):
        @pl.loop(0, PIX)
        def _(pixel):
            place = pl.ds(pl.multiple_of(pixel * views, 16), views)
            for block in range(C_MID // LANES):
                cols = slice(block * LANES, (block + 1) * LANES)
                out = hidden_ref[place, cols].astype(f32) * coef[0:1, cols] + coef[1:2, cols]
                value, slope = gelu_pair(out)
                slope_ref[place, cols] = slope.astype(bf16)
                put(pixel, cols, value.astype(bf16))

    def put_padded(padded):
        def put(pixel, cols, value):
            padded[pixel // SIDE + 1, pl.ds(pl.multiple_of((pixel % SIDE + 1) * views, 16), views), cols] = value

        return put

    activate(hidden_one, slope_one, put_padded(padded_one))
    gathers[1].step(2)
    gathers[3].step(0)

    def patch(padded, first, count, flip):
        found = []
        for vertical in range(3):
            for lateral in range(3):
                down, across = (2 - vertical, 2 - lateral) if flip else (vertical, lateral)
                piece = padded[pl.ds(first + down, count), across * views : across * views + chunk, :]
                found.append(piece.reshape(count * chunk, C_MID))
        return jnp.concatenate(found, axis=1)

    def image_rows(first, count):
        return pl.ds(pl.multiple_of(first * chunk, 16), count * chunk)

    def second_part(sides, first, count):
        right = jnp.concatenate([weights[1][:, cols] for cols in sides], axis=1)
        hidden = dot(patch(padded_one, first, count, False), right)
        put_sides(hidden_two, image_rows(first, count), sides, hidden)

    @pl.loop(0, 2)
    def _(side):
        sides = own_columns(side)

        @pl.loop(0, 3)
        def _(index):
            second_part(sides, 2 * index, 2)
            at_place(2 * side + index, 1, lambda: gathers[2].step(1))
            at_place(side * 3 + index, 3, lambda: gathers[2].step(2), lambda: gathers[4].step(0))
            at_place(side * 3 + index, 5, lambda: gathers[3].step(1), lambda: gathers[4].step(1))

        second_part(sides, 6, 1)
        at_place(side, 0, lambda: gathers[1].arrive(3))

    sum_two = Sum(1)
    sum_two.start(row_sums[0:1, :C_MID], row_sums[1:2, :C_MID])
    sum_two.middle()
    clear_sums()
    norm_coefs(1, sum_two.finish(), row_total)

    def put_rows(pixel, cols, value):
        act_two[pl.ds(pl.multiple_of(pixel * views, 16), views), cols] = value

    activate(hidden_two, slope_two, put_rows)
    gathers[2].arrive(3)

    def weight_three(block):
        return weights[2][block].reshape(C_MID, C_MID)

    sums_low, sums_high = Sum(2), Sum(3)
    half_width = C_IN // 2

    @pl.loop(0, BLOCKS)
    def _(block):
        cols = pl.ds(pl.multiple_of(block * C_MID, LANES), C_MID)

        @pl.loop(0, 3)
        def _(index):
            hidden = dot(act_two[long_rows(0, index), :], weight_three(block))
            hidden_three[long_rows(block, index), :] = hidden.astype(bf16)
            count_in(cols, hidden, hidden)

        @pl.when(block == 1)
        def _():
            sums_low.start(row_sums[0:1, :half_width], row_sums[1:2, :half_width])

        @pl.when(block == 2)
        def _():
            sums_low.middle()

    sums_high.start(row_sums[0:1, half_width:], row_sums[1:2, half_width:])
    norm_coefs(2, sums_low.finish(), row_total)

    pool, pool_slope, pool_bend = mem.pool, mem.pool_slope, mem.pool_bend
    for ref in (pool, pool_slope, pool_bend):
        ref[...] = jnp.zeros_like(ref)

    @pl.loop(0, pieces)
    def _(index):
        piece_copy(features, index, True).wait()

        @pl.loop(0, C_MID // LANES)
        def _(part):
            inner = pl.ds(pl.multiple_of(part * LANES, LANES), LANES)
            cols = piece_columns(index, part)
            slope_row, shift_row = coef[0:1, cols], coef[1:2, cols]
            kept = (pool[:, cols], pool_slope[:, cols], pool_bend[:, cols])
            for pixel in range(SIDE):
                stage_at, hidden_at = stage_rows(index, pixel, views), hidden_rows(index, pixel, views)
                hidden = hidden_three[hidden_at, inner].astype(f32)
                total = hidden * slope_row + shift_row + stage_ref[stage_at, inner].astype(f32)
                value, slope = gelu_pair(total)
                stage_ref[stage_at, inner] = slope.astype(bf16)
                kept = (kept[0] + value, kept[1] + slope, kept[2] + slope * hidden)
            pool[:, cols], pool_slope[:, cols], pool_bend[:, cols] = kept

        save(slope_hbm, index)
        next_load(features, index)

        @pl.when(index == 2)
        def _():
            sums_high.middle()

        at_place(index, 8, lambda: gathers[3].step(2), lambda: gathers[4].step(2))

        @pl.when(index == pieces // 2 - 1)
        def _():
            norm_coefs(2, sums_high.finish(), row_total, half_width)

    last_saves(slope_hbm)
    gathers[3].arrive(3)
    gathers[4].arrive(3)
    for one in gathers:
        one.leave()

    pooled = (pool[...] * (1.0 / PIX)).astype(bf16)
    mem.pooled[...] = pooled
    proj_hidden = dot(pooled, whole(3))
    sum_four = Sum(4)
    totals = sum_four.all(column_sums(proj_hidden), column_sums(proj_hidden * proj_hidden))
    first_loads(slope_hbm)
    norm_coefs(3, totals, view_total)
    value, slope = gelu_pair(proj_hidden * coef[0:1, :P_HID] + coef[1:2, :P_HID])
    proj_act = value.astype(bf16)
    mem.proj_act[...] = proj_act
    mem.proj_slope[...] = slope
    mem.proj_hidden[...] = proj_hidden

    def weight_five(block):
        return weights[4][block // plan.x, block % plan.x]

    parts = P_HID // P_OUT
    embedding = jnp.zeros((views, P_OUT), f32)
    for block in range(parts):
        embedding = embedding + dot_cols(proj_act[:, block * P_OUT : (block + 1) * P_OUT], weight_five(block))

    images = views // 2
    order = jnp.broadcast_to(ins.order[...], (images, views))
    image_row = lax.broadcasted_iota(jnp.int32, (images, views), 0)
    selectors = [(order == 2 * image_row + which).astype(f32) for which in range(2)]
    embeds = [exact_dot(selector, embedding) for selector in selectors]
    moments = [exact_rows(embed, embed) for embed in embeds]
    packed, diagonal = pack_pair(*moments)
    packed, extra = sum_matrix(0, packed, [diagonal] + [column_sums(embed) for embed in embeds])
    moments = unpack_pair(packed, extra[0])
    eye = (
        lax.broadcasted_iota(jnp.int32, (P_OUT, P_OUT), 0) == lax.broadcasted_iota(jnp.int32, (P_OUT, P_OUT), 1)
    ).astype(f32)
    centred, covariances = [], []
    for which in range(2):
        mean = extra[1 + which] / image_total
        centred.append(embeds[which] - mean)
        covariances.append(moments[which] / image_total - exact_rows(mean, mean) + ridge_term * eye)
    inverses = inverse_factors(covariances)
    whitened = [exact_cols(centred[which], inverses[which]) for which in range(2)]
    scalings = [
        lax.rsqrt(jnp.mean(white * white, axis=1, keepdims=True) + norm_epsilon) for white in whitened
    ]
    units = [white * scaling for white, scaling in zip(whitened, scalings)]
    difference = units[0] - units[1]
    objective_row = column_sums(difference * difference) * (1.0 / P_OUT)
    unit_grads = [difference * (2.0 / P_OUT), difference * (-2.0 / P_OUT)]
    white_grads = []
    for which in range(2):
        inner = jnp.mean(whitened[which] * unit_grads[which], axis=1, keepdims=True)
        white_grads.append(
            scalings[which] * unit_grads[which] - whitened[which] * (scalings[which] ** 3 * inner)
        )
    directs = [exact_dot(white_grads[which], inverses[which]) for which in range(2)]
    products = [exact_rows(white_grads[which], whitened[which]) for which in range(2)]
    packed, diagonal = pack_pair(*products)
    packed, extra = sum_matrix(
        1, packed, [diagonal] + [column_sums(grad) for grad in white_grads] + [objective_row]
    )
    products = unpack_pair(packed, extra[0])
    embed_grad = jnp.zeros((views, P_OUT), f32)
    for which in range(2):
        symmetric = exact_rows(inverses[which], exact_dot(products[which], inverses[which]))
        mean_grad = exact_dot(extra[1 + which], inverses[which])
        grad = directs[which] - (exact_dot(centred[which], symmetric) + mean_grad) / image_total
        embed_grad = embed_grad + exact_rows(selectors[which], grad)
    objective_row = extra[3]
    embed_low = embed_grad.astype(bf16)

    proj_act, proj_hidden = mem.proj_act[...], mem.proj_hidden[...]
    act_grad = jnp.concatenate([dot(embed_low, weight_five(block)) for block in range(parts)], axis=1)
    upstream = act_grad * mem.proj_slope[...]
    plain = column_sums(upstream)
    sum_four_back = Sum(5)
    sum_four_back.start(plain, xhat_sum(3, plain, column_sums(upstream * proj_hidden)))
    for block in range(parts):
        weights[4][block // plan.x, block % plan.x] = dot_rows(
            embed_low, proj_act[:, block * P_OUT : (block + 1) * P_OUT]
        ).astype(bf16)
    sum_four_back.middle()
    reduces[4].core_start()
    grad_coefs(3, sum_four_back.finish(), view_total)
    four_low = (
        upstream * coef[0:1, :P_HID] - coef[1:2, :P_HID] - proj_hidden * coef[2:3, :P_HID]
    ).astype(bf16)
    pool_grad = dot_cols(four_low, whole(3)) * (1.0 / PIX)
    plain = column_sums(pool_grad * pool_slope[...])
    sum_three_back = Sum(6)
    sum_three_back.start(plain, xhat_sum(2, plain, column_sums(pool_grad * pool_bend[...])))
    grad_four = dot_rows(mem.pooled[...], four_low).astype(bf16)
    weights[3][...] = grad_four.reshape(weights[3].shape)
    sum_three_back.middle()
    reduces[3].core_start()
    grad_coefs(2, sum_three_back.finish(), row_total)
    pool[...] = pool_grad * coef[0:1, :]
    pool_slope[...] = pool_grad

    clear_sums()

    @pl.loop(0, pieces)
    def _(index):
        piece_copy(slope_hbm, index, True).wait()
        next_load(slope_hbm, index)

        @pl.loop(0, C_MID // LANES)
        def _(part):
            inner = pl.ds(pl.multiple_of(part * LANES, LANES), LANES)
            cols = piece_columns(index, part)
            spread, shift_row, bend_row = pool[:, cols], coef[1:2, cols], coef[2:3, cols]
            for pixel in range(SIDE):
                hidden_at = hidden_rows(index, pixel, views)
                hidden = hidden_three[hidden_at, inner].astype(f32)
                slope = stage_ref[stage_rows(index, pixel, views), inner].astype(f32)
                hidden_three[hidden_at, inner] = (slope * spread - shift_row - hidden * bend_row).astype(bf16)

        at_place(index, 10, reduces[4].core_add)

    @pl.loop(0, 3)
    def _(index):
        at = long_rows(0, index)
        left = jnp.concatenate([hidden_three[long_rows(block, index), :] for block in range(BLOCKS)], axis=1)
        right = jnp.concatenate([weight_three(block) for block in range(BLOCKS)], axis=1)
        upstream = dot_cols(left, right) * slope_two[at, :].astype(f32)
        slope_two[at, :] = upstream.astype(bf16)
        count_in(slice(0, C_MID), upstream, hidden_two[at, :].astype(f32))
        at_place(index, 0, reduces[3].core_add)
        at_place(index, 1, reduces[4].first_add)
        at_place(index, 2, reduces[4].second_add)

    sums = row_sums[0:1, :C_MID], row_sums[1:2, :C_MID]
    sum_two_back = Sum(7)
    sum_two_back.start(sums[0], xhat_sum(1, *sums))

    @pl.loop(0, BLOCKS)
    def _(block):
        three = hidden_three[pl.ds(pl.multiple_of(block * rows, 16), rows), :]
        grad = dot_rows(act_two[...], three)
        weights[2][block] = grad.astype(bf16).reshape(plan.z, plan.x, -1, C_MID)

        @pl.when(block == 1)
        def _():
            sum_two_back.middle()

        at_place(block, 3, reduces[3].first_add)

    reduces[2].core_start()
    clear_sums()
    grad_coefs(1, sum_two_back.finish(), row_total)

    def apply_grad(hidden_ref, grad_ref, put):
        @pl.loop(0, PIX)
        def _(pixel):
            place = pl.ds(pl.multiple_of(pixel * views, 16), views)
            for block in range(C_MID // LANES):
                cols = slice(block * LANES, (block + 1) * LANES)
                grad = (
                    grad_ref[place, cols].astype(f32) * coef[0:1, cols]
                    - coef[1:2, cols]
                    - hidden_ref[place, cols].astype(f32) * coef[2:3, cols]
                )
                put(pixel, cols, grad.astype(bf16))

    apply_grad(hidden_two, slope_two, put_padded(padded_two))
    reduces[4].finish()
    column_places = [
        hidden_three.at[pl.ds(2 * rows, rows)],
        hidden_three.at[pl.ds(3 * rows, rows)],
        hidden_two,
        slope_two,
    ]
    column_loads = [feature_copy(block, column_places[block]) for block in range(BLOCKS)]
    for copy in column_loads:
        copy.start()
    reduces[2].core_add()

    def tap_grad(tap):
        down, across = tap // 3, tap % 3
        left = padded_one[pl.ds(down, SIDE), pl.ds(pl.multiple_of(across * views, 16), chunk), :]
        right = padded_two[1 : SIDE + 1, views : views + chunk, :]
        grad = dot_rows(left.reshape(rows, C_MID), right.reshape(rows, C_MID))
        stage_ref[pl.ds(pl.multiple_of(tap * C_MID, 16), C_MID), :] = grad.astype(bf16)

    two = reduces[1]
    pl.loop(0, 3)(tap_grad)
    two.core_start(0)
    reduces[2].first_add()
    reduces[3].second_add()
    pl.loop(3, 5)(tap_grad)
    two.core_start(1)
    two.core_add(0)
    reduces[2].second_add()
    pl.loop(5, 7)(tap_grad)
    two.core_start(2)
    two.core_add(1)
    two.first_add(0)
    reduces[3].finish()

    def second_back(first, count):
        right = jnp.concatenate([weights[1][tap * C_MID : (tap + 1) * C_MID, :] for tap in range(9)], axis=1)
        at = image_rows(first, count)
        upstream = dot_cols(patch(padded_two, first, count, True), right) * slope_one[at, :].astype(f32)
        slope_one[at, :] = upstream.astype(bf16)
        count_in(slice(0, C_MID), upstream, hidden_one[at, :].astype(f32))

    @pl.loop(0, 3)
    def _(index):
        second_back(2 * index, 2)
        at_place(index, 0, lambda: two.core_add(2), reduces[2].finish, lambda: two.second_add(0))
        at_place(index, 1, lambda: two.first_add(1))
        at_place(index, 2, lambda: two.first_add(2), lambda: two.second_add(1))

    second_back(6, 1)
    sums = row_sums[0:1, :C_MID], row_sums[1:2, :C_MID]
    sum_one_back = Sum(8)
    sum_one_back.start(sums[0], xhat_sum(0, *sums))

    @pl.loop(7, 9)
    def _(tap):
        tap_grad(tap)

        @pl.when(tap == 7)
        def _():
            sum_one_back.middle()

    two.core_start(3)
    two.second_add(2)
    grad_coefs(0, sum_one_back.finish(), row_total)

    def put_one(pixel, cols, value):
        act_two[pl.ds(pl.multiple_of(pixel * views, 16), views), cols] = value

    apply_grad(hidden_one, slope_one, put_one)
    two.core_add(3)

    def block_grad(block):
        column_loads[block].wait()
        grad = dot_rows(column_places[block][...], act_two[...])
        mem.g1[block] = grad.astype(bf16).reshape(plan.x, -1, C_MID)

    one = reduces[0]
    block_grad(0)
    one.core_start(0)
    two.first_add(3)
    block_grad(1)
    one.core_start(1)
    one.core_add(0)
    two.second_add(3)
    block_grad(2)
    one.core_start(2)
    one.core_add(1)
    one.first_add(0)
    block_grad(3)
    one.core_start(3)
    one.core_add(2)
    one.first_add(1)
    one.second_add(0)
    two.finish()

    first_loads(slope_hbm)
    sum_last = Sum(9)

    @pl.loop(0, pieces)
    def _(index):
        block = index // CHUNKS
        weight = weights[0][block].reshape(C_MID, C_MID)
        back = dot_cols(act_two[span(lax.rem(index, CHUNKS)), :], weight)
        piece_copy(slope_hbm, index, True).wait()
        cols = pl.ds(pl.multiple_of(block * C_MID, LANES), C_MID)
        for pixel in range(SIDE):
            at = stage_rows(index, pixel, views)
            summed = stage_ref[at, :].astype(f32) * pool_slope[:, cols]
            stage_ref[at, :] = (summed + back[pixel * views : (pixel + 1) * views]).astype(bf16)
        save(outs.features_grad, index)
        next_load(slope_hbm, index)
        at_place(index, 2, lambda: one.core_add(3), lambda: one.first_add(2), lambda: one.second_add(1))
        at_place(index, 8, lambda: one.first_add(3), lambda: one.second_add(2))
        at_place(index, 13, lambda: one.second_add(3))
        at_place(index, 20, one.finish, lambda: sum_last.start(mem.squares[...], mem.squares[...]))
        at_place(index, 24, sum_last.middle)

    last_saves(outs.features_grad)
    squares = mem.squares[...]
    if plan.inside:
        squares = sum_last.finish()[0:1]
    norm_grads = outs.norm_grad[...]
    scalars = outs.scalars
    norm_squares = column_sums(norm_grads * norm_grads)
    for place in range(norm_squares.shape[1] // LANES):
        squares = squares + norm_squares[:, place * LANES : (place + 1) * LANES]
    scalars[...] = jnp.zeros_like(scalars)
    scalars[0:1, :] = jnp.broadcast_to(jnp.sum(objective_row, axis=1, keepdims=True) / image_total, (1, LANES))
    scalars[1:2, :] = jnp.broadcast_to(jnp.sum(squares, axis=1, keepdims=True), (1, LANES))
    if not plan.inside:
        stores = [
            pltpu.make_async_copy(gradients[which], outs.grads[which], mem.bulk_send.at[which])
            for which in range(5)
        ]
        for store in stores:
            store.start()
        for store in stores:
            store.wait()


def weight_shapes():
    return (
        (4, 2, 256, C_MID),
        (9 * C_MID, C_MID),
        (BLOCKS, 4, 2, 64, C_MID),
        (4, 2, 256, P_HID),
        (4, 2, P_OUT, P_OUT),
    )


def run_kernel(plan, features, order, shards, norm):
    rows, views = plan.rows, plan.views
    in_vmem = pl.BlockSpec(memory_space=pltpu.VMEM)
    anywhere = pl.BlockSpec(memory_space=pl.ANY)
    shapes = weight_shapes()
    operands = [features, order, norm, *shards]
    in_specs = [anywhere, in_vmem, in_vmem] + [in_vmem if plan.inside else anywhere] * 5
    results = [
        ((rows, C_IN), bf16, anywhere),
        ((rows, C_IN), bf16, anywhere),
        ((2, norm_width()), f32, in_vmem),
        ((8, LANES), f32, in_vmem),
    ]
    for which, shard in enumerate(shards):
        if plan.inside:
            results.append((shard.shape, f32, in_vmem))
        else:
            results.append((shapes[which], bf16, anywhere))
    dma = pltpu.SemaphoreType.DMA

    def sum_room(width):
        return SumRoom(
            pltpu.VMEM((plan.dp, 2, width), f32),
            pltpu.VMEM((plan.fsdp, 2, width), f32),
            dma((plan.dp,)),
            dma((plan.dp,)),
            dma((plan.fsdp,)),
            dma((plan.fsdp,)),
        )

    def matrix_room():
        size = plan.embed_rows
        return MatrixRoom(
            pltpu.VMEM((plan.dp, size, P_OUT), f32),
            pltpu.VMEM((plan.dp, size, P_OUT), f32),
            pltpu.VMEM((plan.fsdp, size, P_OUT), f32),
            pltpu.VMEM((plan.dp, size, P_OUT), f32),
            dma((plan.dp,)),
            dma((plan.dp,)),
            dma((plan.fsdp,)),
            dma((plan.fsdp,)),
            dma((plan.dp,)),
            dma((plan.dp,)),
        )

    scratch = Mem(
        w=[pltpu.VMEM(shape, bf16) for shape in shapes],
        g1=pltpu.VMEM(shapes[0], bf16),
        row_sums=pltpu.VMEM((2, C_IN), f32),
        r3=pltpu.VMEM(shapes[2], bf16),
        r4=pltpu.VMEM(shapes[3], bf16),
        r5=pltpu.VMEM(shapes[4], bf16),
        stage=pltpu.VMEM((max(SLOTS * plan.chunk, 9 * C_MID), C_MID), bf16),
        stage_sem=dma((2, SLOTS)),
        column_sem=dma((BLOCKS,)),
        h1=pltpu.VMEM((rows, C_MID), bf16),
        d1=pltpu.VMEM((rows, C_MID), bf16),
        h2=pltpu.VMEM((rows, C_MID), bf16),
        d2=pltpu.VMEM((rows, C_MID), bf16),
        a2=pltpu.VMEM((rows, C_MID), bf16),
        h3=pltpu.VMEM((BLOCKS * rows, C_MID), bf16),
        pad1=pltpu.VMEM((SIDE + 2, (SIDE + 2) * views, C_MID), bf16),
        pad2=pltpu.VMEM((SIDE + 2, (SIDE + 2) * views, C_MID), bf16),
        pool=pltpu.VMEM((views, C_IN), f32),
        pool_slope=pltpu.VMEM((views, C_IN), f32),
        pool_bend=pltpu.VMEM((views, C_IN), f32),
        pooled=pltpu.VMEM((views, C_IN), bf16),
        proj_act=pltpu.VMEM((views, P_HID), bf16),
        proj_slope=pltpu.VMEM((views, P_HID), f32),
        proj_hidden=pltpu.VMEM((views, P_HID), f32),
        coef=pltpu.VMEM((8, C_IN), f32),
        stats=pltpu.VMEM((2, norm_width()), f32),
        norm=pltpu.VMEM((2, norm_width()), f32),
        norm_tiles=pltpu.VMEM((plan.dp, plan.fsdp, 2, LANES), f32),
        norm_s0=dma((plan.dp,)),
        norm_r0=dma((plan.dp,)),
        norm_s1=dma((plan.fsdp,)),
        norm_r1=dma((plan.fsdp,)),
        bulk_send=dma((300,)),
        bulk_recv=dma((300,)),
        mats=[matrix_room(), matrix_room()],
        sums=[
            sum_room(width)
            for width in (C_MID, C_MID, C_IN // 2, C_IN // 2, P_HID, C_IN, LANES)
        ],
        squares=pltpu.VMEM((1, LANES), f32),
    )
    values = pl.pallas_call(
        lambda *refs: kernel(plan, *refs),
        out_shape=[jax.ShapeDtypeStruct(shape, kind) for shape, kind, _ in results],
        in_specs=in_specs,
        out_specs=[spec for _, _, spec in results],
        scratch_shapes=[scratch],
        compiler_params=pltpu.CompilerParams(
            collective_id=1, has_side_effects=True, vmem_limit_bytes=63 * 2**20
        ),
        name="train_step",
    )(*operands)
    return Outs(*values[:4], values[4:])


def norm_width():
    return 2 * C_MID + C_IN + P_HID


def adam_update(weight, moment_one, moment_two, gradient, step_rate, weight_decay):
    first_new = beta_first * moment_one + (1.0 - beta_first) * gradient
    second_new = beta_second * moment_two + (1.0 - beta_second) * gradient * gradient
    first_hat = first_new / (1.0 - beta_first**STEP)
    second_hat = second_new / (1.0 - beta_second**STEP)
    weight_new = weight - step_rate * (
        first_hat / (jnp.sqrt(second_hat) + adam_epsilon) + weight_decay * weight
    )
    return (weight_new, first_new, second_new)


def finish_kernel(rates, decays, *refs):
    count = len(rates)
    low, factor = refs[0], refs[1]
    given, results = refs[2 : 2 + 4 * count], refs[2 + 4 * count :]
    results[0][...] = low[...].astype(f32)

    @pl.when(pl.program_id(0) == 0)
    def _():
        scale = factor[0, 0]
        for place in range(count):
            weight, first, second, grad = (given[part * count + place][...] for part in range(4))
            updated = adam_update(weight, first, second, grad * scale, rates[place], decays[place])
            for part in range(3):
                results[1 + part * count + place][...] = updated[part]


def finish(features_grad, factor, masters, firsts, seconds, grads, rates, decays):
    rows = features_grad.shape[0]
    arrays = [*masters, *firsts, *seconds, *grads]

    def fixed(shape):
        return pl.BlockSpec(shape, lambda index: (0, 0))

    step = rows // CHUNKS
    moving = pl.BlockSpec((step, C_IN), lambda index: (index, 0))
    outputs = [*masters] * 3
    values = pl.pallas_call(
        lambda *refs: finish_kernel(rates, decays, *refs),
        grid=(CHUNKS,),
        in_specs=[moving, pl.BlockSpec(memory_space=pltpu.SMEM)] + [fixed(array.shape) for array in arrays],
        out_specs=[moving] + [fixed(array.shape) for array in outputs],
        out_shape=[jax.ShapeDtypeStruct((rows, C_IN), f32)]
        + [jax.ShapeDtypeStruct(array.shape, f32) for array in outputs],
        compiler_params=pltpu.CompilerParams(vmem_limit_bytes=48 * 2**20),
        name="finish",
    )(features_grad, factor, *arrays)
    count = len(masters)
    return values[0], values[1 : 1 + count], values[1 + count : 1 + 2 * count], values[1 + 2 * count :]


def gather_full(weight):
    outer = lax.all_gather(weight.astype(bf16), FSDP, axis=0, tiled=True)
    return lax.all_gather(outer, DP, axis=1, tiled=True)


def scatter_full(gradient):
    inner = lax.psum_scatter(gradient.astype(f32), DP, scatter_dimension=1, tiled=True)
    return lax.psum_scatter(inner, FSDP, scatter_dimension=0, tiled=True)


def body(features, view_order, *state):
    masters, firsts, seconds = state[:6], state[6:12], state[12:18]
    dp_size, fsdp_size = lax.axis_size(DP), lax.axis_size(FSDP)
    views = features.shape[0]
    inside = dp_size == 4 and fsdp_size == 8
    plan = Plan(dp_size, fsdp_size, views, inside)
    pixels = jnp.swapaxes(features, 0, 1).reshape(-1, C_IN)
    norm_params = masters[5]
    shapes = weight_shapes()
    if inside:
        shards = list(masters[:4]) + [masters[4].T]
        norm = norm_params
    else:
        full = [gather_full(weight) for weight in masters[:5]]
        shards = [
            full[0].reshape(shapes[0]),
            full[1],
            full[2].reshape(C_MID, BLOCKS, C_MID).swapaxes(0, 1).reshape(shapes[2]),
            full[3].reshape(shapes[3]),
            full[4].reshape(4, 2, P_OUT, P_OUT).swapaxes(2, 3),
        ]
        norm = lax.all_gather(norm_params.astype(bf16), (DP, FSDP), axis=1, tiled=True).astype(f32)
    got = run_kernel(plan, pixels, view_order, shards, norm)
    grads = list(got.grads)
    squares = got.scalars[1, 0]
    turned = [list(group) for group in (masters, firsts, seconds)]
    if inside:
        owned = grads
        for group in turned:
            group[4] = group[4].T
    else:
        whole_grads = [
            grads[0].reshape(C_IN, C_MID),
            grads[1],
            grads[2].reshape(BLOCKS, C_MID, C_MID).swapaxes(0, 1).reshape(C_MID, C_IN),
            grads[3].reshape(C_IN, P_HID),
            grads[4].swapaxes(2, 3).reshape(P_HID, P_OUT),
        ]
        owned = [scatter_full(gradient) for gradient in whole_grads]
        squares = squares + lax.psum(sum(jnp.sum(grad * grad) for grad in owned), (DP, FSDP))
    width = norm_params.shape[1]
    owner = lax.axis_index((DP, FSDP))
    owned.append(lax.dynamic_slice_in_dim(got.norm_grad, owner * width, width, 1))
    grad_norm = jnp.sqrt(squares)
    factor = clip_level / jnp.maximum(grad_norm, clip_level)
    step_rates = (
        C_IN ** (-0.5),
        (9 * C_MID) ** (-0.5),
        C_MID ** (-0.5),
        C_IN ** (-0.5),
        P_HID ** (-0.5),
        norm_rate,
    )
    decays = (decay_rate, decay_rate, decay_rate, decay_rate, decay_rate, 0.0)
    input_grad, *updates = finish(
        got.features_grad, factor.reshape(1, 1), *turned, owned, step_rates, decays
    )
    if inside:
        updates = [[*group[:4], group[4].T, group[5]] for group in updates]
    return (
        got.scalars[0, 0],
        jnp.swapaxes(input_grad.reshape(PIX, views, C_IN), 0, 1),
        grad_norm,
        *updates[0],
        *updates[1],
        *updates[2],
    )


def solution(mesh):
    views = P((DP, FSDP), None, None)
    split = P(FSDP, DP)
    norm = P(None, (DP, FSDP))
    params = (split,) * 5 + (norm,)
    return jax.shard_map(
        body,
        mesh=mesh,
        in_specs=(views, P((DP, FSDP), None)) + params * 3,
        out_specs=(P(), views, P()) + params * 3,
        check_vma=False,
    )
```

```python
from typing import Any, NamedTuple

import jax
import jax.numpy as jnp
from jax import lax
from jax.experimental import pallas as pl
from jax.experimental.pallas import tpu as pltpu
from jax.sharding import PartitionSpec as P

C_IN = 2048
C_MID = 512
P_HID = 1024
P_OUT = 128
SIDE = 7
STEP = 10
PIX = 49
LANES = 128
BLOCKS = C_IN // C_MID
CHUNKS = SIDE
SLOTS = 6


highest = lax.Precision.HIGHEST
bf16 = jnp.bfloat16
f32 = jnp.float32
norm_epsilon = 1e-05
ridge_term = 0.01
clip_level = 0.1
beta_first = 0.9
beta_second = 0.999
adam_epsilon = 1e-08
decay_rate = 0.05
norm_rate = 0.5
bell_scale = 0.3989422804014327
root_half = 0.5**0.5
bell_rate = -0.7213475204444817
DP, FSDP = "dp", "fsdp"


def gelu_pair(values):
    below = 0.5 + 0.5 * lax.erf(values * root_half)
    bell = jnp.exp2(values * values * bell_rate)
    return values * below, below + values * bell * bell_scale


def dot(left, right):
    return jnp.dot(left, right, preferred_element_type=f32)


def dot_cols(left, right):
    return lax.dot_general(left, right, (((1,), (1,)), ((), ())), preferred_element_type=f32)


def dot_rows(left, right):
    return lax.dot_general(left, right, (((0,), (0,)), ((), ())), preferred_element_type=f32)


def exact_cols(left, right):
    return lax.dot_general(
        left, right, (((1,), (1,)), ((), ())), precision=highest, preferred_element_type=f32
    )


def exact_rows(left, right):
    return lax.dot_general(
        left, right, (((0,), (0,)), ((), ())), precision=highest, preferred_element_type=f32
    )


def exact_dot(left, right):
    return jnp.dot(left, right, precision=highest, preferred_element_type=f32)


def inverse_factors(matrices):
    row_top = lax.broadcasted_iota(jnp.int32, (8, P_OUT), 0)
    row_all = lax.broadcasted_iota(jnp.int32, (P_OUT, P_OUT), 0)
    col_all = lax.broadcasted_iota(jnp.int32, (P_OUT, P_OUT), 1)

    def one_step(place, left, right):
        scale = lax.rsqrt(left[place : place + 1, place : place + 1])
        left_row = left[place : place + 1, :] * scale
        right_row = right[place : place + 1, :] * scale
        column = left[:, place : place + 1] * scale
        left = left - column * left_row
        right = right - column * right_row
        here = row_top == place
        left = jnp.concatenate([jnp.where(here, 0.0, left[:8]), left[8:]], axis=0)
        right = jnp.concatenate(
            [jnp.where(here, jnp.broadcast_to(right_row, (8, P_OUT)), right[:8]), right[8:]], axis=0
        )
        return left, right

    def panel(_, pairs):
        pairs = list(pairs)
        for place in range(8):
            for which in range(len(pairs)):
                pairs[which] = one_step(place, *pairs[which])
        return tuple(
            (
                pltpu.roll(jnp.concatenate([left[8:], left[:8]], axis=0), P_OUT - 8, 1),
                jnp.concatenate([right[8:], right[:8]], axis=0),
            )
            for left, right in pairs
        )

    start = tuple((matrix, (row_all == col_all).astype(f32)) for matrix in matrices)
    done = lax.fori_loop(0, P_OUT // 8, panel, start)
    return [right for _, right in done]


def pack_pair(first, second):
    row = lax.broadcasted_iota(jnp.int32, (P_OUT, P_OUT), 0)
    col = lax.broadcasted_iota(jnp.int32, (P_OUT, P_OUT), 1)
    packed = jnp.where(row >= col, first, second.T)
    diagonal = jnp.sum(jnp.where(row == col, second, 0.0), axis=0, keepdims=True)
    return packed, diagonal


def unpack_pair(packed, diagonal):
    row = lax.broadcasted_iota(jnp.int32, (P_OUT, P_OUT), 0)
    col = lax.broadcasted_iota(jnp.int32, (P_OUT, P_OUT), 1)
    turned = packed.T
    first = jnp.where(row >= col, packed, turned)
    second = jnp.where(row < col, packed, jnp.where(row == col, diagonal, turned))
    return first, second


class Ins(NamedTuple):
    features: Any
    order: Any
    norm: Any
    shards: Any


class Outs(NamedTuple):
    slope: Any
    features_grad: Any
    norm_grad: Any
    scalars: Any
    grads: Any


class SumRoom(NamedTuple):
    dp: Any
    fsdp: Any
    s0: Any
    r0: Any
    s1: Any
    r1: Any


class MatrixRoom(NamedTuple):
    pack: Any
    dp: Any
    fsdp: Any
    all: Any
    s0: Any
    r0: Any
    s1: Any
    r1: Any
    s2: Any
    r2: Any


class Mem(NamedTuple):
    w: Any
    g1: Any
    row_sums: Any
    r3: Any
    r4: Any
    r5: Any
    stage: Any
    stage_sem: Any
    column_sem: Any
    h1: Any
    d1: Any
    h2: Any
    d2: Any
    a2: Any
    h3: Any
    pad1: Any
    pad2: Any
    pool: Any
    pool_slope: Any
    pool_bend: Any
    pooled: Any
    proj_act: Any
    proj_slope: Any
    proj_hidden: Any
    coef: Any
    stats: Any
    norm: Any
    norm_tiles: Any
    norm_s0: Any
    norm_r0: Any
    norm_s1: Any
    norm_r1: Any
    bulk_send: Any
    bulk_recv: Any
    mats: Any
    sums: Any
    squares: Any


class Plan:
    def __init__(self, dp_size, fsdp_size, views, inside):
        self.dp = dp_size
        self.fsdp = fsdp_size
        self.devices = dp_size * fsdp_size
        self.views = views
        self.rows = views * PIX
        self.chunk = views * SIDE
        self.inside = inside
        self.z = 4
        self.x = 2
        self.half = (128, 288, 32, 128, 16)
        self.width = (128, 128, 512, 256, 128)
        piece = P_OUT + 8
        self.embed_rows = -(-piece // (8 * dp_size)) * 8


def kernel(plan, *refs):
    ins, outs, mem = Ins(*refs[:3], refs[3:8]), Outs(*refs[8:12], refs[12:17]), refs[17]
    views, chunk, rows = plan.views, plan.chunk, plan.rows
    row_total = float(rows * plan.devices)
    view_total = float(views * plan.devices)
    image_total = float(views * plan.devices // 2)
    dp_me, fsdp_me = lax.axis_index(DP), lax.axis_index(FSDP)
    y_me, c_me = dp_me // 2, dp_me % 2
    z_me, x_me = fsdp_me // 2, fsdp_me % 2
    y_other, c_other, x_other = 1 - y_me, 1 - c_me, 1 - x_me

    barrier = pltpu.get_barrier_semaphore()

    @pl.loop(1, plan.dp)
    def _(step):
        pl.semaphore_signal(
            barrier, 1, device_id={DP: lax.rem(dp_me + step, plan.dp)}, device_id_type=pl.DeviceIdType.MESH
        )

    @pl.loop(1, plan.fsdp)
    def _(step):
        pl.semaphore_signal(
            barrier, 1, device_id={FSDP: lax.rem(fsdp_me + step, plan.fsdp)}, device_id_type=pl.DeviceIdType.MESH
        )

    pl.semaphore_wait(barrier, plan.dp + plan.fsdp - 2)

    def share(axis, size, me, source_of, slots, send, recv):
        def outgoing(step):
            partner = lax.rem(me + step, size)
            return pltpu.make_async_remote_copy(
                src_ref=source_of(partner),
                dst_ref=slots.at[me],
                send_sem=send.at[step],
                recv_sem=recv.at[me],
                device_id={axis: partner},
                device_id_type=pl.DeviceIdType.MESH,
            )

        def incoming(step):
            source = lax.rem(me + step, size)
            return pltpu.make_async_remote_copy(
                src_ref=slots.at[source],
                dst_ref=slots.at[source],
                send_sem=send.at[step],
                recv_sem=recv.at[source],
                device_id={axis: source},
                device_id_type=pl.DeviceIdType.MESH,
            )

        def start():
            pl.loop(1, size)(lambda step: outgoing(step).start())

        def wait():
            pl.loop(1, size)(lambda step: incoming(step).wait_recv())
            pl.loop(1, size)(lambda step: outgoing(step).wait_send())

        return start, wait

    def add_slots(slots, size):
        total = slots[0]
        for place in range(1, size):
            total = total + slots[place]
        return total

    class Sum:
        def __init__(self, which):
            part = mem.sums[(0, 1, 2, 3, 4, 4, 5, 0, 1, 6)[which]]
            self.dp_slots, self.fsdp_slots = part.dp, part.fsdp
            self.dp_copy = share(
                DP, plan.dp, dp_me, lambda _: self.dp_slots.at[dp_me], self.dp_slots, part.s0, part.r0
            )
            self.fsdp_copy = share(
                FSDP, plan.fsdp, fsdp_me, lambda _: self.fsdp_slots.at[fsdp_me], self.fsdp_slots, part.s1, part.r1
            )

        def start(self, *values):
            for place, value in enumerate(values):
                self.dp_slots[dp_me, place : place + 1, :] = value
            self.dp_copy[0]()

        def middle(self):
            self.dp_copy[1]()
            self.fsdp_slots[fsdp_me] = add_slots(self.dp_slots, plan.dp)
            self.fsdp_copy[0]()

        def finish(self):
            self.fsdp_copy[1]()
            return add_slots(self.fsdp_slots, plan.fsdp)

        def all(self, *values):
            self.start(*values)
            self.middle()
            return self.finish()

    def sum_matrix(which, matrix, extra):
        part = mem.mats[which]
        size = plan.embed_rows
        pack = part.pack
        flat = jnp.concatenate(
            [matrix] + extra + [jnp.zeros((size * plan.dp - P_OUT - len(extra), P_OUT), f32)], axis=0
        )
        for place in range(plan.dp):
            pack[place] = flat[place * size : (place + 1) * size]
        start, wait = share(DP, plan.dp, dp_me, lambda to: pack.at[to], part.dp, part.s0, part.r0)
        start()
        part.dp[dp_me] = pack[dp_me]
        wait()
        part.fsdp[fsdp_me] = add_slots(part.dp, plan.dp)
        start, wait = share(
            FSDP, plan.fsdp, fsdp_me, lambda _: part.fsdp.at[fsdp_me], part.fsdp, part.s1, part.r1
        )
        start()
        wait()
        part.all[dp_me] = add_slots(part.fsdp, plan.fsdp)
        start, wait = share(
            DP, plan.dp, dp_me, lambda _: part.all.at[dp_me], part.all, part.s2, part.r2
        )
        start()
        wait()
        total = jnp.concatenate([part.all[place] for place in range(plan.dp)], axis=0)
        return total[:P_OUT], [total[P_OUT + place : P_OUT + place + 1] for place in range(len(extra))]

    weights = mem.w
    everything = slice(None)

    def row_span(which, half):
        if isinstance(half, tuple):
            return half
        size = plan.half[which]
        if half is None:
            return 0, 2 * size
        return half * size, size

    def column_span(which, dp_index):
        width = plan.width[which]
        return pl.ds(pl.multiple_of(dp_index * width, width), width)

    def places(which, z_index, x_index, dp_index, half, flat=True):
        start, size = row_span(which, half)
        if which == 1 and flat:
            z_list = range(plan.z) if z_index is None else [z_index]
            x_list = range(plan.x) if x_index is None else [x_index]
            return [
                (
                    pl.ds(pl.multiple_of((z_one * plan.x + x_one) * 576 + start, 16), size),
                    column_span(which, dp_index),
                )
                for z_one in z_list
                for x_one in x_list
            ]
        z_one = everything if z_index is None else z_index
        x_one = everything if x_index is None else x_index
        if which == 2:
            return [(dp_index, z_one, x_one, pl.ds(start, size), everything)]
        if which == 4:
            return [(z_one, x_one, pl.ds(pl.multiple_of(dp_index * 32 + start, 16), size), everything)]
        return [(z_one, x_one, pl.ds(start, size), column_span(which, dp_index))]

    recv_parts = {
        1: lambda index: mem.h3.at[index],
        0: lambda index: mem.r4.at[index],
        2: lambda index: mem.r3.at[index],
        3: lambda index: mem.r4.at[index],
        4: lambda index: mem.r5.at[index],
    }

    counter = [0]

    class Batch:
        def __init__(self, sources, targets, landings, axis, partner):
            base = counter[0]
            counter[0] += len(sources)
            send, recv = mem.bulk_send, mem.bulk_recv
            self.out = [
                pltpu.make_async_remote_copy(
                    src_ref=source,
                    dst_ref=target,
                    send_sem=send.at[base + place],
                    recv_sem=recv.at[base + place],
                    device_id={axis: partner},
                    device_id_type=pl.DeviceIdType.MESH,
                )
                for place, (source, target) in enumerate(zip(sources, targets))
            ]
            self.come = [
                pltpu.make_async_remote_copy(
                    src_ref=landing,
                    dst_ref=landing,
                    send_sem=send.at[base + place],
                    recv_sem=recv.at[base + place],
                    device_id={axis: partner},
                    device_id_type=pl.DeviceIdType.MESH,
                )
                for place, landing in enumerate(landings)
            ]

        def start(self):
            for copy in self.out:
                copy.start()

        def arrive(self):
            for copy in self.come:
                copy.wait_recv()

        def leave(self):
            for copy in self.out:
                copy.wait_send()

    class LineBatch:
        def __init__(self, source_of, target_of, landing_of):
            base = counter[0]
            counter[0] += plan.z
            send, recv = mem.bulk_send, mem.bulk_recv
            self.out, self.come = [], []
            for step in range(1, plan.z):
                z_to = (z_me + step) % plan.z
                self.out.append(
                    pltpu.make_async_remote_copy(
                        src_ref=source_of(z_to),
                        dst_ref=target_of(z_to),
                        send_sem=send.at[base + step],
                        recv_sem=recv.at[base + z_me],
                        device_id={FSDP: z_to * plan.x + x_me},
                        device_id_type=pl.DeviceIdType.MESH,
                    )
                )
                self.come.append(
                    pltpu.make_async_remote_copy(
                        src_ref=landing_of(z_to),
                        dst_ref=landing_of(z_to),
                        send_sem=send.at[base + step],
                        recv_sem=recv.at[base + z_to],
                        device_id={FSDP: z_to * plan.x + x_me},
                        device_id_type=pl.DeviceIdType.MESH,
                    )
                )

        start, arrive, leave = Batch.start, Batch.arrive, Batch.leave

    def pick(ref, indexes):
        return [ref.at[index] for index in indexes]

    def own_dp(y_index, c_index):
        return y_index * 2 + c_index

    x_partner = z_me * plan.x + x_other
    y_partner = own_dp(y_other, c_me)
    c_partner = own_dp(y_me, c_other)
    dp_far = own_dp(y_other, c_other)

    class Gather:
        def __init__(self, which, start, size):
            ref = weights[which]
            self.which, self.rows = which, (start, size)
            both, low, high = (start, size), (start, size // 2), (start + size // 2, size // 2)

            def at(*index):
                return pick(ref, places(which, *index, False))

            own = at(z_me, x_me, dp_me, both)[0]
            self.line = LineBatch(
                lambda _: own, lambda _: own, lambda z_from: at(z_from, x_me, dp_me, both)[0]
            )
            sent, come = at(None, x_me, dp_me, low), at(None, x_other, dp_me, low)
            x_first = Batch(sent, sent, come, FSDP, x_partner)
            sent, come = at(None, x_me, dp_me, high), at(None, x_me, y_partner, high)
            y_first = Batch(sent, sent, come, DP, y_partner)
            sent, come = at(None, None, dp_me, low), at(None, None, y_partner, low)
            y_second = Batch(sent, sent, come, DP, y_partner)
            sent = at(None, x_me, dp_me, high) + at(None, x_me, y_partner, high)
            come = at(None, x_other, dp_me, high) + at(None, x_other, y_partner, high)
            x_second = Batch(sent, sent, come, FSDP, x_partner)
            sent = at(None, None, dp_me, both) + at(None, None, y_partner, both)
            come = at(None, None, c_partner, both) + at(None, None, dp_far, both)
            core = Batch(sent, sent, come, DP, c_partner)
            self.stages = ((self.line,), (x_first, y_first), (y_second, x_second), (core,))

        def put_own(self):
            index = places(self.which, z_me, x_me, dp_me, self.rows, False)[0]
            shard = ins.shards[self.which][self.rows[0] : self.rows[0] + self.rows[1], :]
            weights[self.which][index] = shard.astype(bf16)

        def start(self, stage):
            for batch in self.stages[stage]:
                batch.start()

        def arrive(self, stage):
            for batch in self.stages[stage]:
                batch.arrive()

        def leave(self):
            for stage in self.stages:
                for batch in stage:
                    batch.leave()

    class Piece:
        def __init__(self, which, ref, room, z_index):
            def at(*index):
                return pick(ref, places(which, z_index, *index))

            def land(*index):
                return [room(index_one) for index_one in places(which, z_index, *index)]

            self.z = z_index
            self.core = Batch(
                at(None, c_partner, None) + at(None, dp_far, None),
                land(None, c_partner, None) + land(None, dp_far, None),
                land(None, dp_me, None) + land(None, y_partner, None),
                DP,
                c_partner,
            )
            self.y_first = Batch(
                at(None, y_partner, 0), land(None, dp_far, 0), land(None, c_partner, 0), DP, y_partner
            )
            self.x_first = Batch(
                at(x_other, dp_me, 1) + at(x_other, y_partner, 1),
                land(x_other, c_partner, 1) + land(x_other, dp_far, 1),
                land(x_me, c_partner, 1) + land(x_me, dp_far, 1),
                FSDP,
                x_partner,
            )
            self.x_second = Batch(
                at(x_other, dp_me, 0), land(x_other, dp_far, 0), land(x_me, dp_far, 0), FSDP, x_partner
            )
            self.y_second = Batch(
                at(x_me, y_partner, 1), land(x_other, dp_far, 1), land(x_other, c_partner, 1), DP, y_partner
            )

    class Reduce:
        def __init__(self, which, ref, cut):
            self.which, self.ref, self.room = which, ref, recv_parts[which]
            self.pieces = [
                Piece(which, ref, self.room, z_index) for z_index in (range(plan.z) if cut else [None])
            ]
            self.base = counter[0]
            counter[0] += plan.z

        def line_copy(self, z_to):
            return pltpu.make_async_remote_copy(
                src_ref=self.ref.at[places(self.which, z_to, x_me, dp_me, None)[0]],
                dst_ref=self.room(places(self.which, z_me, x_other, dp_far, None)[0]),
                send_sem=mem.bulk_send.at[self.base + z_to],
                recv_sem=mem.bulk_recv.at[self.base + z_me],
                device_id={FSDP: z_to * plan.x + x_me},
                device_id_type=pl.DeviceIdType.MESH,
            )

        def line_room(self, z_from):
            return self.room(places(self.which, z_from, x_other, dp_far, None)[0])

        def add(self, z_index, pairs):
            def one(z_one):
                for here, there in pairs:
                    for x_step in range(plan.x) if here[0] is None else [None]:
                        x_here = x_step if here[0] is None else here[0]
                        x_there = x_step if there[0] is None else there[0]
                        index = places(self.which, z_one, x_here, *here[1:])[0]
                        other = places(self.which, z_one, x_there, *there[1:])[0]
                        total = self.ref[index].astype(f32) + self.room(other)[...].astype(f32)
                        self.ref[index] = total.astype(bf16)

            if z_index is None:
                pl.loop(0, plan.z)(one)
            else:
                one(z_index)

        def core_start(self, place=0):
            if plan.inside:
                self.pieces[place].core.start()

        def core_add(self, place=0):
            if plan.inside:
                piece = self.pieces[place]
                piece.core.arrive()
                self.add(piece.z, [((None, dp_me, None),) * 2, ((None, y_partner, None),) * 2])
                piece.y_first.start()
                piece.x_first.start()

        def first_add(self, place=0):
            if plan.inside:
                piece = self.pieces[place]
                piece.y_first.arrive()
                self.add(piece.z, [((None, dp_me, 0), (None, c_partner, 0))])
                piece.x_second.start()
                piece.x_first.arrive()
                self.add(
                    piece.z, [((x_me, dp_me, 1), (x_me, c_partner, 1)), ((x_me, y_partner, 1), (x_me, dp_far, 1))]
                )
                piece.y_second.start()

        def second_add(self, place=0):
            if plan.inside:
                piece = self.pieces[place]
                piece.x_second.arrive()
                piece.y_second.arrive()
                self.add(
                    piece.z, [((x_me, dp_me, 0), (x_me, dp_far, 0)), ((x_me, dp_me, 1), (x_other, c_partner, 1))]
                )
                if piece.z is None:
                    for step in range(1, plan.z):
                        self.line_copy((z_me + step) % plan.z).start()
                else:

                    @pl.when(z_me != piece.z)
                    def _():
                        self.line_copy(piece.z).start()

        def finish(self):
            if not plan.inside:
                return
            total = self.ref[places(self.which, z_me, x_me, dp_me, None)[0]].astype(f32)
            for step in range(1, plan.z):
                z_from = (z_me + step) % plan.z
                room = self.line_room(z_from)
                pltpu.make_async_remote_copy(
                    src_ref=room,
                    dst_ref=room,
                    send_sem=mem.bulk_send.at[self.base + z_from],
                    recv_sem=mem.bulk_recv.at[self.base + z_from],
                    device_id={FSDP: z_from * plan.x + x_me},
                    device_id_type=pl.DeviceIdType.MESH,
                ).wait_recv()
                total = total + room[...].astype(f32)
            outs.grads[self.which][...] = total
            squares = jnp.sum(total * total, axis=0, keepdims=True)
            folded = squares[:, :LANES]
            for place in range(1, squares.shape[1] // LANES):
                folded = folded + squares[:, place * LANES : (place + 1) * LANES]
            mem.squares[...] += folded
            for step in range(1, plan.z):
                self.line_copy((z_me + step) % plan.z).wait_send()
            for piece in self.pieces:
                for batch in (piece.core, piece.y_first, piece.x_first, piece.x_second, piece.y_second):
                    batch.leave()

    gathers, steps = [], []
    if plan.inside:
        for which, cuts in enumerate((2, 3, 1, 2, 1)):
            size = 2 * plan.half[which] // cuts
            gathers += [Gather(which, cut * size, size) for cut in range(cuts)]

    def line_step(place):
        gathers[place].arrive(0)
        gathers[place].start(1)
        if place + 1 < len(gathers):
            gathers[place + 1].start(0)

    def first_step(place):
        gathers[place].arrive(1)
        gathers[place].start(2)

    def second_step(place):
        gathers[place].arrive(2)
        gathers[place].start(3)

    for place in range(len(gathers)):
        steps.append((line_step, place))
        if place > 0:
            steps.append((second_step, place - 1))
        steps.append((first_step, place))
    if plan.inside:
        steps.append((second_step, len(gathers) - 1))

    def take(count):
        taken, steps[:] = steps[:count], steps[count:]
        return [lambda one=one: one[0](one[1]) for one in taken]

    def advance(count):
        for move in take(count):
            move()

    def cores_arrive(which):
        for one in gathers:
            if one.which == which:
                one.arrive(3)

    gradients = [mem.g1, mem.stage.at[pl.ds(0, 9 * C_MID)], weights[2], weights[3], weights[4]]
    reduces = [Reduce(which, gradients[which], which < 4) for which in range(5)]
    mem.squares[...] = jnp.zeros((1, LANES), f32)

    if plan.inside:
        gathers[0].put_own()
        gathers[0].start(0)
        for one in gathers[1:]:
            one.put_own()
        tiles = mem.norm_tiles
        tiles[dp_me, fsdp_me] = ins.norm[...].astype(bf16).astype(f32)
        norm_dp = share(
            DP, plan.dp, dp_me, lambda _: tiles.at[dp_me, fsdp_me], tiles.at[:, fsdp_me], mem.norm_s0, mem.norm_r0
        )
        norm_dp[0]()
    else:
        loads = [
            pltpu.make_async_copy(ins.shards[which], weights[which], mem.bulk_send.at[which])
            for which in range(5)
        ]
        for load in loads:
            load.start()

    stage_ref, stage_sem = mem.stage, mem.stage_sem
    pieces = BLOCKS * CHUNKS

    def stage_rows(index, pixel=0, count=chunk):
        return pl.ds(pl.multiple_of(lax.rem(index, SLOTS) * chunk + pixel * views, 16), count)

    def hidden_rows(index, pixel=0, count=chunk):
        return pl.ds(pl.multiple_of(index * chunk + pixel * views, 16), count)

    def piece_copy(array, index, into):
        block, place = index // CHUNKS, lax.rem(index, CHUNKS)
        outer = array.at[
            pl.ds(pl.multiple_of(place * chunk, 16), chunk), pl.ds(pl.multiple_of(block * C_MID, LANES), C_MID)
        ]
        inner = stage_ref.at[stage_rows(index)]
        source, target = (outer, inner) if into else (inner, outer)
        return pltpu.make_async_copy(source, target, stage_sem.at[0 if into else 1, lax.rem(index, SLOTS)])

    def first_loads(array):
        for index in range(3):
            piece_copy(array, index, True).start()

    def next_load(array, index):
        @pl.when(index + 3 < pieces)
        def _():
            piece_copy(array, index + 3, True).start()

    def save(array, index):
        piece_copy(array, index, False).start()

        @pl.when(index >= 2)
        def _():
            piece_copy(array, index - 2, False).wait()

    def last_saves(array):
        for index in (pieces - 2, pieces - 1):
            piece_copy(array, index, False).wait()

    def piece_columns(index, part):
        return pl.ds(pl.multiple_of(index // CHUNKS * C_MID + part * LANES, LANES), LANES)

    features, slope_hbm = ins.features, outs.slope
    hidden_three = mem.h3

    def feature_copy(block, target):
        return pltpu.make_async_copy(
            features.at[:, pl.ds(block * C_MID, C_MID)], target, mem.column_sem.at[block]
        )

    feature_loads = [
        feature_copy(block, hidden_three.at[pl.ds(block * rows, rows)]) for block in range(BLOCKS)
    ]
    for copy in feature_loads:
        copy.start()
    first_loads(features)

    padded_one, padded_two = mem.pad1, mem.pad2
    for padded in (padded_one, padded_two):
        for edge in (0, SIDE + 1):
            padded[edge] = jnp.zeros((padded.shape[1], C_MID), bf16)
        for edge in (0, SIDE + 1):
            padded[:, pl.ds(edge * views, views), :] = jnp.zeros((SIDE + 2, views, C_MID), bf16)

    if plan.inside:
        norm_dp[1]()
        norm_out = []
        norm_in = []
        for step in range(1, plan.fsdp):
            partner = (fsdp_me + step) % plan.fsdp
            norm_out.append(
                pltpu.make_async_remote_copy(
                    src_ref=tiles.at[:, fsdp_me],
                    dst_ref=tiles.at[:, fsdp_me],
                    send_sem=mem.norm_s1.at[step],
                    recv_sem=mem.norm_r1.at[fsdp_me],
                    device_id={FSDP: partner},
                    device_id_type=pl.DeviceIdType.MESH,
                )
            )
            norm_in.append(
                pltpu.make_async_remote_copy(
                    src_ref=tiles.at[:, partner],
                    dst_ref=tiles.at[:, partner],
                    send_sem=mem.norm_s1.at[step],
                    recv_sem=mem.norm_r1.at[partner],
                    device_id={FSDP: partner},
                    device_id_type=pl.DeviceIdType.MESH,
                )
            )
        for copy in norm_out:
            copy.start()
        advance(7)
        for copy in norm_in:
            copy.wait_recv()
        for copy in norm_out:
            copy.wait_send()
        norm_all = mem.norm
        for dp_one in range(plan.dp):
            for fsdp_one in range(plan.fsdp):
                start = (dp_one * plan.fsdp + fsdp_one) * LANES
                norm_all[:, start : start + LANES] = tiles[dp_one, fsdp_one]
    else:
        for copy in loads:
            copy.wait()
        norm_all = mem.norm
        norm_all[...] = ins.norm[...]

    starts = (0, C_MID, 2 * C_MID, 2 * C_MID + C_IN, 2 * C_MID + C_IN + P_HID)

    def gain(layer):
        return norm_all[0:1, starts[layer] : starts[layer + 1]]

    coef, stats = mem.coef, mem.stats

    def norm_coefs(layer, totals, count, low=0):
        width = totals.shape[1]
        here, there = slice(low, low + width), slice(starts[layer] + low, starts[layer] + low + width)
        mean = totals[0:1] / count
        scaling = lax.rsqrt(totals[1:2] / count - mean * mean + norm_epsilon)
        slope = scaling * norm_all[0:1, there]
        stats[0:1, there] = mean
        stats[1:2, there] = scaling
        coef[0:1, here] = slope
        coef[1:2, here] = norm_all[1:2, there] - mean * slope

    def grad_coefs(layer, totals, count):
        width = starts[layer + 1] - starts[layer]
        mean = stats[0:1, starts[layer] : starts[layer + 1]]
        scaling = stats[1:2, starts[layer] : starts[layer + 1]]
        outs.norm_grad[0:1, starts[layer] : starts[layer + 1]] = totals[1:2]
        outs.norm_grad[1:2, starts[layer] : starts[layer + 1]] = totals[0:1]
        slope = scaling * gain(layer)
        bend = slope * scaling * totals[1:2] / count
        coef[0:1, :width] = slope
        coef[1:2, :width] = slope * totals[0:1] / count - mean * bend
        coef[2:3, :width] = bend

    def xhat_sum(layer, plain, product):
        mean = stats[0:1, starts[layer] : starts[layer + 1]]
        scaling = stats[1:2, starts[layer] : starts[layer + 1]]
        return scaling * (product - mean * plain)

    zero_row = jnp.zeros((1, C_MID), f32)

    def at_place(index, place, *moves):
        if plan.inside:

            @pl.when(index == place)
            def _():
                for move in moves:
                    move()

    def column_sums(value):
        return jnp.sum(value, axis=0, keepdims=True)

    def whole(which):
        value = weights[which][...]
        return value.reshape(-1, value.shape[-1])

    row_sums = mem.row_sums

    def clear_sums():
        row_sums[...] = jnp.zeros_like(row_sums)

    def count_in(cols, value, other):
        row_sums[0:1, cols] += column_sums(value)
        row_sums[1:2, cols] += column_sums(value * other)

    def own_columns(side):
        core = (c_me + side) % 2
        return [
            pl.ds(pl.multiple_of(half * (C_MID // 2) + core * LANES, LANES), LANES) for half in range(2)
        ]

    hidden_one, slope_one = mem.h1, mem.d1
    hidden_two, slope_two = mem.h2, mem.d2
    act_two = mem.a2
    long = rows // 3

    def span(index):
        return pl.ds(pl.multiple_of(index * chunk, 16), chunk)

    def long_rows(block, index):
        return pl.ds(pl.multiple_of(block * rows + index * long, 16), long)

    def put_sides(ref, at, sides, hidden):
        for place, cols in enumerate(sides):
            part = hidden[:, place * LANES : (place + 1) * LANES]
            ref[at, cols] = part.astype(bf16)
            count_in(cols, part, part)

    for copy in feature_loads:
        copy.wait()
    clear_sums()

    @pl.loop(0, 2)
    def _(side):
        sides = own_columns(side)

        @pl.loop(0, 3)
        def _(index):
            left = jnp.concatenate([hidden_three[long_rows(block, index), :] for block in range(BLOCKS)], axis=1)
            right = jnp.concatenate([weights[0][:, :, :, cols].reshape(C_IN, LANES) for cols in sides], axis=1)
            put_sides(hidden_one, long_rows(0, index), sides, dot(left, right))

            at_place(side * 3 + index, 1, *take(1))
            at_place(side * 3 + index, 3, *take(1))

        at_place(side, 0, lambda: cores_arrive(0))

    sum_one = Sum(0)
    sum_one.start(row_sums[0:1, :C_MID], row_sums[1:2, :C_MID])
    advance(1)
    sum_one.middle()
    advance(1)
    clear_sums()
    norm_coefs(0, sum_one.finish(), row_total)

    def activate(hidden_ref, slope_ref, put):
        @pl.loop(0, PIX)
        def _(pixel):
            place = pl.ds(pl.multiple_of(pixel * views, 16), views)
            for block in range(C_MID // LANES):
                cols = slice(block * LANES, (block + 1) * LANES)
                out = hidden_ref[place, cols].astype(f32) * coef[0:1, cols] + coef[1:2, cols]
                value, slope = gelu_pair(out)
                slope_ref[place, cols] = slope.astype(bf16)
                put(pixel, cols, value.astype(bf16))

    def put_padded(padded):
        def put(pixel, cols, value):
            padded[pixel // SIDE + 1, pl.ds(pl.multiple_of((pixel % SIDE + 1) * views, 16), views), cols] = value

        return put

    activate(hidden_one, slope_one, put_padded(padded_one))
    advance(5)

    def patch(padded, first, count, flip):
        found = []
        for vertical in range(3):
            for lateral in range(3):
                down, across = (2 - vertical, 2 - lateral) if flip else (vertical, lateral)
                piece = padded[pl.ds(first + down, count), across * views : across * views + chunk, :]
                found.append(piece.reshape(count * chunk, C_MID))
        return jnp.concatenate(found, axis=1)

    def image_rows(first, count):
        return pl.ds(pl.multiple_of(first * chunk, 16), count * chunk)

    def second_part(sides, first, count):
        right = jnp.concatenate([weights[1][:, :, :, cols].reshape(9 * C_MID, LANES) for cols in sides], axis=1)
        hidden = dot(patch(padded_one, first, count, False), right)
        put_sides(hidden_two, image_rows(first, count), sides, hidden)

    @pl.loop(0, 2)
    def _(side):
        sides = own_columns(side)

        @pl.loop(0, 3)
        def _(index):
            second_part(sides, 2 * index, 2)
            for place in range(6):
                at_place(side * 3 + index, place, *take(1))

        second_part(sides, 6, 1)
        at_place(side, 0, lambda: cores_arrive(1))

    sum_two = Sum(1)
    sum_two.start(row_sums[0:1, :C_MID], row_sums[1:2, :C_MID])
    sum_two.middle()
    advance(1)
    clear_sums()
    norm_coefs(1, sum_two.finish(), row_total)

    def put_rows(pixel, cols, value):
        act_two[pl.ds(pl.multiple_of(pixel * views, 16), views), cols] = value

    activate(hidden_two, slope_two, put_rows)
    advance(1)
    cores_arrive(2)

    def weight_three(block):
        return weights[2][block].reshape(C_MID, C_MID)

    sums_low, sums_high = Sum(2), Sum(3)
    half_width = C_IN // 2

    @pl.loop(0, BLOCKS)
    def _(block):
        cols = pl.ds(pl.multiple_of(block * C_MID, LANES), C_MID)

        @pl.loop(0, 3)
        def _(index):
            hidden = dot(act_two[long_rows(0, index), :], weight_three(block))
            hidden_three[long_rows(block, index), :] = hidden.astype(bf16)
            count_in(cols, hidden, hidden)

        for place in range(3):
            at_place(block, place, *take(1))

        @pl.when(block == 1)
        def _():
            sums_low.start(row_sums[0:1, :half_width], row_sums[1:2, :half_width])

        @pl.when(block == 2)
        def _():
            sums_low.middle()

    sums_high.start(row_sums[0:1, half_width:], row_sums[1:2, half_width:])
    norm_coefs(2, sums_low.finish(), row_total)

    pool, pool_slope, pool_bend = mem.pool, mem.pool_slope, mem.pool_bend
    for ref in (pool, pool_slope, pool_bend):
        ref[...] = jnp.zeros_like(ref)

    @pl.loop(0, pieces)
    def _(index):
        piece_copy(features, index, True).wait()

        @pl.loop(0, C_MID // LANES)
        def _(part):
            inner = pl.ds(pl.multiple_of(part * LANES, LANES), LANES)
            cols = piece_columns(index, part)
            slope_row, shift_row = coef[0:1, cols], coef[1:2, cols]
            kept = (pool[:, cols], pool_slope[:, cols], pool_bend[:, cols])
            for pixel in range(SIDE):
                stage_at, hidden_at = stage_rows(index, pixel, views), hidden_rows(index, pixel, views)
                hidden = hidden_three[hidden_at, inner].astype(f32)
                total = hidden * slope_row + shift_row + stage_ref[stage_at, inner].astype(f32)
                value, slope = gelu_pair(total)
                stage_ref[stage_at, inner] = slope.astype(bf16)
                kept = (kept[0] + value, kept[1] + slope, kept[2] + slope * hidden)
            pool[:, cols], pool_slope[:, cols], pool_bend[:, cols] = kept

        save(slope_hbm, index)
        next_load(features, index)

        @pl.when(index == 2)
        def _():
            sums_high.middle()

        @pl.when(index == pieces // 2 - 1)
        def _():
            norm_coefs(2, sums_high.finish(), row_total, half_width)

    last_saves(slope_hbm)
    cores_arrive(3)
    cores_arrive(4)
    for one in gathers:
        one.leave()

    pooled = (pool[...] * (1.0 / PIX)).astype(bf16)
    mem.pooled[...] = pooled
    proj_hidden = dot(pooled, whole(3))
    sum_four = Sum(4)
    totals = sum_four.all(column_sums(proj_hidden), column_sums(proj_hidden * proj_hidden))
    first_loads(slope_hbm)
    norm_coefs(3, totals, view_total)
    value, slope = gelu_pair(proj_hidden * coef[0:1, :P_HID] + coef[1:2, :P_HID])
    proj_act = value.astype(bf16)
    mem.proj_act[...] = proj_act
    mem.proj_slope[...] = slope
    mem.proj_hidden[...] = proj_hidden

    def weight_five(block):
        return weights[4][block // plan.x, block % plan.x]

    parts = P_HID // P_OUT
    embedding = jnp.zeros((views, P_OUT), f32)
    for block in range(parts):
        embedding = embedding + dot_cols(proj_act[:, block * P_OUT : (block + 1) * P_OUT], weight_five(block))

    images = views // 2
    order = jnp.broadcast_to(ins.order[...], (images, views))
    image_row = lax.broadcasted_iota(jnp.int32, (images, views), 0)
    selectors = [(order == 2 * image_row + which).astype(f32) for which in range(2)]
    embeds = [exact_dot(selector, embedding) for selector in selectors]
    moments = [exact_rows(embed, embed) for embed in embeds]
    packed, diagonal = pack_pair(*moments)
    packed, extra = sum_matrix(0, packed, [diagonal] + [column_sums(embed) for embed in embeds])
    moments = unpack_pair(packed, extra[0])
    eye = (
        lax.broadcasted_iota(jnp.int32, (P_OUT, P_OUT), 0) == lax.broadcasted_iota(jnp.int32, (P_OUT, P_OUT), 1)
    ).astype(f32)
    centred, covariances = [], []
    for which in range(2):
        mean = extra[1 + which] / image_total
        centred.append(embeds[which] - mean)
        covariances.append(moments[which] / image_total - exact_rows(mean, mean) + ridge_term * eye)
    inverses = inverse_factors(covariances)
    whitened = [exact_cols(centred[which], inverses[which]) for which in range(2)]
    scalings = [
        lax.rsqrt(jnp.mean(white * white, axis=1, keepdims=True) + norm_epsilon) for white in whitened
    ]
    units = [white * scaling for white, scaling in zip(whitened, scalings)]
    difference = units[0] - units[1]
    objective_row = column_sums(difference * difference) * (1.0 / P_OUT)
    unit_grads = [difference * (2.0 / P_OUT), difference * (-2.0 / P_OUT)]
    white_grads = []
    for which in range(2):
        inner = jnp.mean(whitened[which] * unit_grads[which], axis=1, keepdims=True)
        white_grads.append(
            scalings[which] * unit_grads[which] - whitened[which] * (scalings[which] ** 3 * inner)
        )
    directs = [exact_dot(white_grads[which], inverses[which]) for which in range(2)]
    products = [exact_rows(white_grads[which], whitened[which]) for which in range(2)]
    packed, diagonal = pack_pair(*products)
    packed, extra = sum_matrix(
        1, packed, [diagonal] + [column_sums(grad) for grad in white_grads] + [objective_row]
    )
    products = unpack_pair(packed, extra[0])
    embed_grad = jnp.zeros((views, P_OUT), f32)
    for which in range(2):
        symmetric = exact_rows(inverses[which], exact_dot(products[which], inverses[which]))
        mean_grad = exact_dot(extra[1 + which], inverses[which])
        grad = directs[which] - (exact_dot(centred[which], symmetric) + mean_grad) / image_total
        embed_grad = embed_grad + exact_rows(selectors[which], grad)
    objective_row = extra[3]
    embed_low = embed_grad.astype(bf16)

    proj_act, proj_hidden = mem.proj_act[...], mem.proj_hidden[...]
    act_grad = jnp.concatenate([dot(embed_low, weight_five(block)) for block in range(parts)], axis=1)
    upstream = act_grad * mem.proj_slope[...]
    plain = column_sums(upstream)
    sum_four_back = Sum(5)
    sum_four_back.start(plain, xhat_sum(3, plain, column_sums(upstream * proj_hidden)))
    for block in range(parts):
        weights[4][block // plan.x, block % plan.x] = dot_rows(
            embed_low, proj_act[:, block * P_OUT : (block + 1) * P_OUT]
        ).astype(bf16)
    sum_four_back.middle()
    reduces[4].core_start()
    grad_coefs(3, sum_four_back.finish(), view_total)
    four_low = (
        upstream * coef[0:1, :P_HID] - coef[1:2, :P_HID] - proj_hidden * coef[2:3, :P_HID]
    ).astype(bf16)
    pool_grad = dot_cols(four_low, whole(3)) * (1.0 / PIX)
    plain = column_sums(pool_grad * pool_slope[...])
    sum_three_back = Sum(6)
    sum_three_back.start(plain, xhat_sum(2, plain, column_sums(pool_grad * pool_bend[...])))
    grad_four = dot_rows(mem.pooled[...], four_low).astype(bf16)
    weights[3][...] = grad_four.reshape(weights[3].shape)
    sum_three_back.middle()
    four, three, two, one = reduces[3], reduces[2], reduces[1], reduces[0]
    for place in range(plan.z):
        four.core_start(place)
    grad_coefs(2, sum_three_back.finish(), row_total)
    pool[...] = pool_grad * coef[0:1, :]
    pool_slope[...] = pool_grad

    clear_sums()

    @pl.loop(0, pieces)
    def _(index):
        piece_copy(slope_hbm, index, True).wait()
        next_load(slope_hbm, index)

        @pl.loop(0, C_MID // LANES)
        def _(part):
            inner = pl.ds(pl.multiple_of(part * LANES, LANES), LANES)
            cols = piece_columns(index, part)
            spread, shift_row, bend_row = pool[:, cols], coef[1:2, cols], coef[2:3, cols]
            for pixel in range(SIDE):
                hidden_at = hidden_rows(index, pixel, views)
                hidden = hidden_three[hidden_at, inner].astype(f32)
                slope = stage_ref[stage_rows(index, pixel, views), inner].astype(f32)
                hidden_three[hidden_at, inner] = (slope * spread - shift_row - hidden * bend_row).astype(bf16)

        at_place(index, 3, reduces[4].core_add, lambda: four.core_add(0))
        at_place(index, 11, lambda: four.core_add(1), reduces[4].first_add)
        at_place(index, 20, lambda: four.first_add(0), lambda: four.core_add(2))

    @pl.loop(0, 3)
    def _(index):
        at = long_rows(0, index)
        left = jnp.concatenate([hidden_three[long_rows(block, index), :] for block in range(BLOCKS)], axis=1)
        right = jnp.concatenate([weight_three(block) for block in range(BLOCKS)], axis=1)
        upstream = dot_cols(left, right) * slope_two[at, :].astype(f32)
        slope_two[at, :] = upstream.astype(bf16)
        count_in(slice(0, C_MID), upstream, hidden_two[at, :].astype(f32))
        at_place(index, 0, lambda: four.first_add(1), lambda: four.second_add(0), reduces[4].second_add)
        at_place(index, 1, lambda: four.core_add(3))
        at_place(index, 2, lambda: four.first_add(2), lambda: four.second_add(1))

    sums = row_sums[0:1, :C_MID], row_sums[1:2, :C_MID]
    sum_two_back = Sum(7)
    sum_two_back.start(sums[0], xhat_sum(1, *sums))

    @pl.loop(0, BLOCKS)
    def _(block):
        three = hidden_three[pl.ds(pl.multiple_of(block * rows, 16), rows), :]
        grad = dot_rows(act_two[...], three)
        weights[2][block] = grad.astype(bf16).reshape(plan.z, plan.x, -1, C_MID)

        @pl.when(block == 1)
        def _():
            sum_two_back.middle()

        at_place(block, 0, lambda: four.first_add(3))
        at_place(block, 2, lambda: four.second_add(2))
        at_place(block, 3, lambda: four.second_add(3))

    for place in range(plan.z):
        three.core_start(place)
    clear_sums()
    grad_coefs(1, sum_two_back.finish(), row_total)

    def apply_grad(hidden_ref, grad_ref, put):
        @pl.loop(0, PIX)
        def _(pixel):
            place = pl.ds(pl.multiple_of(pixel * views, 16), views)
            for block in range(C_MID // LANES):
                cols = slice(block * LANES, (block + 1) * LANES)
                grad = (
                    grad_ref[place, cols].astype(f32) * coef[0:1, cols]
                    - coef[1:2, cols]
                    - hidden_ref[place, cols].astype(f32) * coef[2:3, cols]
                )
                put(pixel, cols, grad.astype(bf16))

    apply_grad(hidden_two, slope_two, put_padded(padded_two))
    reduces[4].finish()
    column_places = [
        hidden_three.at[pl.ds(2 * rows, rows)],
        hidden_three.at[pl.ds(3 * rows, rows)],
        hidden_two,
        slope_two,
    ]
    column_loads = [feature_copy(block, column_places[block]) for block in range(BLOCKS)]
    for copy in column_loads:
        copy.start()
    three.core_add(0)
    three.core_add(1)

    def tap_grad(tap):
        down, across = tap // 3, tap % 3
        left = padded_one[pl.ds(down, SIDE), pl.ds(pl.multiple_of(across * views, 16), chunk), :]
        right = padded_two[1 : SIDE + 1, views : views + chunk, :]
        grad = dot_rows(left.reshape(rows, C_MID), right.reshape(rows, C_MID))
        stage_ref[pl.ds(pl.multiple_of(tap * C_MID, 16), C_MID), :] = grad.astype(bf16)

    pl.loop(0, 3)(tap_grad)
    two.core_start(0)
    three.first_add(0)
    three.core_add(2)
    three.core_add(3)
    pl.loop(3, 5)(tap_grad)
    two.core_start(1)
    two.core_add(0)
    three.first_add(1)
    three.second_add(0)
    pl.loop(5, 7)(tap_grad)
    two.core_start(2)
    three.first_add(2)
    three.first_add(3)
    two.core_add(1)
    three.second_add(1)
    four.finish()

    def second_back(first, count):
        flat = weights[1][...].reshape(9 * C_MID, C_MID)
        right = jnp.concatenate([flat[tap * C_MID : (tap + 1) * C_MID, :] for tap in range(9)], axis=1)
        at = image_rows(first, count)
        upstream = dot_cols(patch(padded_two, first, count, True), right) * slope_one[at, :].astype(f32)
        slope_one[at, :] = upstream.astype(bf16)
        count_in(slice(0, C_MID), upstream, hidden_one[at, :].astype(f32))

    @pl.loop(0, 3)
    def _(index):
        second_back(2 * index, 2)
        at_place(
            index, 0, lambda: two.first_add(0), lambda: two.core_add(2), lambda: three.second_add(2), lambda: three.second_add(3)
        )
        at_place(index, 1, lambda: two.first_add(1), three.finish, lambda: two.second_add(0))
        at_place(index, 2, lambda: two.first_add(2), lambda: two.second_add(1))

    second_back(6, 1)
    sums = row_sums[0:1, :C_MID], row_sums[1:2, :C_MID]
    sum_one_back = Sum(8)
    sum_one_back.start(sums[0], xhat_sum(0, *sums))

    @pl.loop(7, 9)
    def _(tap):
        tap_grad(tap)

        @pl.when(tap == 7)
        def _():
            sum_one_back.middle()

    two.core_start(3)
    two.second_add(2)
    grad_coefs(0, sum_one_back.finish(), row_total)

    def put_one(pixel, cols, value):
        act_two[pl.ds(pl.multiple_of(pixel * views, 16), views), cols] = value

    apply_grad(hidden_one, slope_one, put_one)
    two.core_add(3)

    def block_grad(block):
        column_loads[block].wait()
        grad = dot_rows(column_places[block][...], act_two[...])
        mem.g1[block] = grad.astype(bf16).reshape(plan.x, -1, C_MID)

    block_grad(0)
    one.core_start(0)
    two.first_add(3)
    block_grad(1)
    one.core_start(1)
    one.core_add(0)
    two.second_add(3)
    block_grad(2)
    one.core_start(2)
    one.core_add(1)
    one.first_add(0)
    block_grad(3)
    one.core_start(3)
    one.core_add(2)
    one.first_add(1)
    one.second_add(0)
    two.finish()

    first_loads(slope_hbm)
    sum_last = Sum(9)

    @pl.loop(0, pieces)
    def _(index):
        block = index // CHUNKS
        weight = weights[0][block].reshape(C_MID, C_MID)
        back = dot_cols(act_two[span(lax.rem(index, CHUNKS)), :], weight)
        piece_copy(slope_hbm, index, True).wait()
        cols = pl.ds(pl.multiple_of(block * C_MID, LANES), C_MID)
        for pixel in range(SIDE):
            at = stage_rows(index, pixel, views)
            summed = stage_ref[at, :].astype(f32) * pool_slope[:, cols]
            stage_ref[at, :] = (summed + back[pixel * views : (pixel + 1) * views]).astype(bf16)
        save(outs.features_grad, index)
        next_load(slope_hbm, index)
        at_place(index, 2, lambda: one.core_add(3), lambda: one.first_add(2), lambda: one.second_add(1))
        at_place(index, 8, lambda: one.first_add(3), lambda: one.second_add(2))
        at_place(index, 13, lambda: one.second_add(3))
        at_place(index, 20, one.finish, lambda: sum_last.start(mem.squares[...], mem.squares[...]))
        at_place(index, 24, sum_last.middle)

    last_saves(outs.features_grad)
    squares = mem.squares[...]
    if plan.inside:
        squares = sum_last.finish()[0:1]
    norm_grads = outs.norm_grad[...]
    scalars = outs.scalars
    norm_squares = column_sums(norm_grads * norm_grads)
    for place in range(norm_squares.shape[1] // LANES):
        squares = squares + norm_squares[:, place * LANES : (place + 1) * LANES]
    scalars[...] = jnp.zeros_like(scalars)
    scalars[0:1, :] = jnp.broadcast_to(jnp.sum(objective_row, axis=1, keepdims=True) / image_total, (1, LANES))
    scalars[1:2, :] = jnp.broadcast_to(jnp.sum(squares, axis=1, keepdims=True), (1, LANES))
    if not plan.inside:
        stores = [
            pltpu.make_async_copy(gradients[which], outs.grads[which], mem.bulk_send.at[which])
            for which in range(5)
        ]
        for store in stores:
            store.start()
        for store in stores:
            store.wait()


def weight_shapes():
    return (
        (4, 2, 256, C_MID),
        (4, 2, 576, C_MID),
        (BLOCKS, 4, 2, 64, C_MID),
        (4, 2, 256, P_HID),
        (4, 2, P_OUT, P_OUT),
    )


def run_kernel(plan, features, order, shards, norm):
    rows, views = plan.rows, plan.views
    in_vmem = pl.BlockSpec(memory_space=pltpu.VMEM)
    anywhere = pl.BlockSpec(memory_space=pl.ANY)
    shapes = weight_shapes()
    operands = [features, order, norm, *shards]
    in_specs = [anywhere, in_vmem, in_vmem] + [in_vmem if plan.inside else anywhere] * 5
    results = [
        ((rows, C_IN), bf16, anywhere),
        ((rows, C_IN), bf16, anywhere),
        ((2, norm_width()), f32, in_vmem),
        ((8, LANES), f32, in_vmem),
    ]
    for which, shard in enumerate(shards):
        if plan.inside:
            results.append((shard.shape, f32, in_vmem))
        else:
            results.append(((9 * C_MID, C_MID) if which == 1 else shapes[which], bf16, anywhere))
    dma = pltpu.SemaphoreType.DMA

    def sum_room(width):
        return SumRoom(
            pltpu.VMEM((plan.dp, 2, width), f32),
            pltpu.VMEM((plan.fsdp, 2, width), f32),
            dma((plan.dp,)),
            dma((plan.dp,)),
            dma((plan.fsdp,)),
            dma((plan.fsdp,)),
        )

    def matrix_room():
        size = plan.embed_rows
        return MatrixRoom(
            pltpu.VMEM((plan.dp, size, P_OUT), f32),
            pltpu.VMEM((plan.dp, size, P_OUT), f32),
            pltpu.VMEM((plan.fsdp, size, P_OUT), f32),
            pltpu.VMEM((plan.dp, size, P_OUT), f32),
            dma((plan.dp,)),
            dma((plan.dp,)),
            dma((plan.fsdp,)),
            dma((plan.fsdp,)),
            dma((plan.dp,)),
            dma((plan.dp,)),
        )

    scratch = Mem(
        w=[pltpu.VMEM(shape, bf16) for shape in shapes],
        g1=pltpu.VMEM(shapes[0], bf16),
        row_sums=pltpu.VMEM((2, C_IN), f32),
        r3=pltpu.VMEM(shapes[2], bf16),
        r4=pltpu.VMEM(shapes[3], bf16),
        r5=pltpu.VMEM(shapes[4], bf16),
        stage=pltpu.VMEM((max(SLOTS * plan.chunk, 9 * C_MID), C_MID), bf16),
        stage_sem=dma((2, SLOTS)),
        column_sem=dma((BLOCKS,)),
        h1=pltpu.VMEM((rows, C_MID), bf16),
        d1=pltpu.VMEM((rows, C_MID), bf16),
        h2=pltpu.VMEM((rows, C_MID), bf16),
        d2=pltpu.VMEM((rows, C_MID), bf16),
        a2=pltpu.VMEM((rows, C_MID), bf16),
        h3=pltpu.VMEM((BLOCKS * rows, C_MID), bf16),
        pad1=pltpu.VMEM((SIDE + 2, (SIDE + 2) * views, C_MID), bf16),
        pad2=pltpu.VMEM((SIDE + 2, (SIDE + 2) * views, C_MID), bf16),
        pool=pltpu.VMEM((views, C_IN), f32),
        pool_slope=pltpu.VMEM((views, C_IN), f32),
        pool_bend=pltpu.VMEM((views, C_IN), f32),
        pooled=pltpu.VMEM((views, C_IN), bf16),
        proj_act=pltpu.VMEM((views, P_HID), bf16),
        proj_slope=pltpu.VMEM((views, P_HID), f32),
        proj_hidden=pltpu.VMEM((views, P_HID), f32),
        coef=pltpu.VMEM((8, C_IN), f32),
        stats=pltpu.VMEM((2, norm_width()), f32),
        norm=pltpu.VMEM((2, norm_width()), f32),
        norm_tiles=pltpu.VMEM((plan.dp, plan.fsdp, 2, LANES), f32),
        norm_s0=dma((plan.dp,)),
        norm_r0=dma((plan.dp,)),
        norm_s1=dma((plan.fsdp,)),
        norm_r1=dma((plan.fsdp,)),
        bulk_send=dma((300,)),
        bulk_recv=dma((300,)),
        mats=[matrix_room(), matrix_room()],
        sums=[
            sum_room(width)
            for width in (C_MID, C_MID, C_IN // 2, C_IN // 2, P_HID, C_IN, LANES)
        ],
        squares=pltpu.VMEM((1, LANES), f32),
    )
    values = pl.pallas_call(
        lambda *refs: kernel(plan, *refs),
        out_shape=[jax.ShapeDtypeStruct(shape, kind) for shape, kind, _ in results],
        in_specs=in_specs,
        out_specs=[spec for _, _, spec in results],
        scratch_shapes=[scratch],
        compiler_params=pltpu.CompilerParams(
            collective_id=1, has_side_effects=True, vmem_limit_bytes=63 * 2**20
        ),
        name="train_step",
    )(*operands)
    return Outs(*values[:4], values[4:])


def norm_width():
    return 2 * C_MID + C_IN + P_HID


def adam_update(weight, moment_one, moment_two, gradient, step_rate, weight_decay):
    first_new = beta_first * moment_one + (1.0 - beta_first) * gradient
    second_new = beta_second * moment_two + (1.0 - beta_second) * gradient * gradient
    first_hat = first_new / (1.0 - beta_first**STEP)
    second_hat = second_new / (1.0 - beta_second**STEP)
    weight_new = weight - step_rate * (
        first_hat / (jnp.sqrt(second_hat) + adam_epsilon) + weight_decay * weight
    )
    return (weight_new, first_new, second_new)


def finish_kernel(rates, decays, *refs):
    count = len(rates)
    low, factor = refs[0], refs[1]
    given, results = refs[2 : 2 + 4 * count], refs[2 + 4 * count :]
    results[0][...] = low[...].astype(f32)

    @pl.when(pl.program_id(0) == 0)
    def _():
        scale = factor[0, 0]
        for place in range(count):
            weight, first, second, grad = (given[part * count + place][...] for part in range(4))
            updated = adam_update(weight, first, second, grad * scale, rates[place], decays[place])
            for part in range(3):
                results[1 + part * count + place][...] = updated[part]


def finish(features_grad, factor, masters, firsts, seconds, grads, rates, decays):
    rows = features_grad.shape[0]
    arrays = [*masters, *firsts, *seconds, *grads]

    def fixed(shape):
        return pl.BlockSpec(shape, lambda index: (0, 0))

    step = rows // CHUNKS
    moving = pl.BlockSpec((step, C_IN), lambda index: (index, 0))
    outputs = [*masters] * 3
    values = pl.pallas_call(
        lambda *refs: finish_kernel(rates, decays, *refs),
        grid=(CHUNKS,),
        in_specs=[moving, pl.BlockSpec(memory_space=pltpu.SMEM)] + [fixed(array.shape) for array in arrays],
        out_specs=[moving] + [fixed(array.shape) for array in outputs],
        out_shape=[jax.ShapeDtypeStruct((rows, C_IN), f32)]
        + [jax.ShapeDtypeStruct(array.shape, f32) for array in outputs],
        compiler_params=pltpu.CompilerParams(vmem_limit_bytes=62 * 2**20),
        name="finish",
    )(features_grad, factor, *arrays)
    count = len(masters)
    return values[0], values[1 : 1 + count], values[1 + count : 1 + 2 * count], values[1 + 2 * count :]


def gather_full(weight):
    outer = lax.all_gather(weight.astype(bf16), FSDP, axis=0, tiled=True)
    return lax.all_gather(outer, DP, axis=1, tiled=True)


def scatter_full(gradient):
    inner = lax.psum_scatter(gradient.astype(f32), DP, scatter_dimension=1, tiled=True)
    return lax.psum_scatter(inner, FSDP, scatter_dimension=0, tiled=True)


def body(features, view_order, *state):
    masters, firsts, seconds = state[:6], state[6:12], state[12:18]
    dp_size, fsdp_size = lax.axis_size(DP), lax.axis_size(FSDP)
    views = features.shape[0]
    inside = dp_size == 4 and fsdp_size == 8
    plan = Plan(dp_size, fsdp_size, views, inside)
    pixels = jnp.swapaxes(features, 0, 1).reshape(-1, C_IN)
    norm_params = masters[5]
    shapes = weight_shapes()
    if inside:
        shards = list(masters[:4]) + [masters[4].T]
        norm = norm_params
    else:
        full = [gather_full(weight) for weight in masters[:5]]
        shards = [
            full[0].reshape(shapes[0]),
            full[1].reshape(shapes[1]),
            full[2].reshape(C_MID, BLOCKS, C_MID).swapaxes(0, 1).reshape(shapes[2]),
            full[3].reshape(shapes[3]),
            full[4].reshape(4, 2, P_OUT, P_OUT).swapaxes(2, 3),
        ]
        norm = lax.all_gather(norm_params.astype(bf16), (DP, FSDP), axis=1, tiled=True).astype(f32)
    got = run_kernel(plan, pixels, view_order, shards, norm)
    grads = list(got.grads)
    squares = got.scalars[1, 0]
    turned = [list(group) for group in (masters, firsts, seconds)]
    if inside:
        owned = grads
        for group in turned:
            group[4] = group[4].T
    else:
        whole_grads = [
            grads[0].reshape(C_IN, C_MID),
            grads[1],
            grads[2].reshape(BLOCKS, C_MID, C_MID).swapaxes(0, 1).reshape(C_MID, C_IN),
            grads[3].reshape(C_IN, P_HID),
            grads[4].swapaxes(2, 3).reshape(P_HID, P_OUT),
        ]
        owned = [scatter_full(gradient) for gradient in whole_grads]
        squares = squares + lax.psum(sum(jnp.sum(grad * grad) for grad in owned), (DP, FSDP))
    width = norm_params.shape[1]
    owner = lax.axis_index((DP, FSDP))
    owned.append(lax.dynamic_slice_in_dim(got.norm_grad, owner * width, width, 1))
    grad_norm = jnp.sqrt(squares)
    factor = clip_level / jnp.maximum(grad_norm, clip_level)
    step_rates = (
        C_IN ** (-0.5),
        (9 * C_MID) ** (-0.5),
        C_MID ** (-0.5),
        C_IN ** (-0.5),
        P_HID ** (-0.5),
        norm_rate,
    )
    decays = (decay_rate, decay_rate, decay_rate, decay_rate, decay_rate, 0.0)
    input_grad, *updates = finish(
        got.features_grad, factor.reshape(1, 1), *turned, owned, step_rates, decays
    )
    if inside:
        updates = [[*group[:4], group[4].T, group[5]] for group in updates]
    return (
        got.scalars[0, 0],
        jnp.swapaxes(input_grad.reshape(PIX, views, C_IN), 0, 1),
        grad_norm,
        *updates[0],
        *updates[1],
        *updates[2],
    )


def solution(mesh):
    views = P((DP, FSDP), None, None)
    split = P(FSDP, DP)
    norm = P(None, (DP, FSDP))
    params = (split,) * 5 + (norm,)
    return jax.shard_map(
        body,
        mesh=mesh,
        in_specs=(views, P((DP, FSDP), None)) + params * 3,
        out_specs=(P(), views, P()) + params * 3,
        check_vma=False,
    )
```

```python
from typing import Any, NamedTuple

import jax
import jax.numpy as jnp
from jax import lax
from jax.experimental import pallas as pl
from jax.experimental.pallas import tpu as pltpu
from jax.sharding import PartitionSpec as P

C_IN = 2048
C_MID = 512
P_HID = 1024
P_OUT = 128
SIDE = 7
STEP = 10
PIX = 49
LANES = 128
BLOCKS = C_IN // C_MID
CHUNKS = SIDE
SLOTS = 6
LAST_SUM = 23


highest = lax.Precision.HIGHEST
bf16 = jnp.bfloat16
f32 = jnp.float32
norm_epsilon = 1e-05
ridge_term = 0.01
clip_level = 0.1
beta_first = 0.9
beta_second = 0.999
adam_epsilon = 1e-08
decay_rate = 0.05
norm_rate = 0.5
bell_scale = 0.3989422804014327
root_half = 0.5**0.5
bell_rate = -0.7213475204444817
DP, FSDP = "dp", "fsdp"


def gelu_pair(values):
    below = 0.5 + 0.5 * lax.erf(values * root_half)
    bell = jnp.exp2(values * values * bell_rate)
    return values * below, below + values * bell * bell_scale


def dot(left, right):
    return jnp.dot(left, right, preferred_element_type=f32)


def dot_cols(left, right):
    return lax.dot_general(left, right, (((1,), (1,)), ((), ())), preferred_element_type=f32)


def dot_rows(left, right):
    return lax.dot_general(left, right, (((0,), (0,)), ((), ())), preferred_element_type=f32)


def exact_cols(left, right):
    return lax.dot_general(
        left, right, (((1,), (1,)), ((), ())), precision=highest, preferred_element_type=f32
    )


def exact_rows(left, right):
    return lax.dot_general(
        left, right, (((0,), (0,)), ((), ())), precision=highest, preferred_element_type=f32
    )


def exact_dot(left, right):
    return jnp.dot(left, right, precision=highest, preferred_element_type=f32)


def inverse_factors(matrices):
    row_top = lax.broadcasted_iota(jnp.int32, (8, P_OUT), 0)
    row_all = lax.broadcasted_iota(jnp.int32, (P_OUT, P_OUT), 0)
    col_all = lax.broadcasted_iota(jnp.int32, (P_OUT, P_OUT), 1)

    def one_step(place, left, right):
        scale = lax.rsqrt(left[place : place + 1, place : place + 1])
        left_row = left[place : place + 1, :] * scale
        right_row = right[place : place + 1, :] * scale
        column = left[:, place : place + 1] * scale
        left = left - column * left_row
        right = right - column * right_row
        here = row_top == place
        left = jnp.concatenate([jnp.where(here, 0.0, left[:8]), left[8:]], axis=0)
        right = jnp.concatenate(
            [jnp.where(here, jnp.broadcast_to(right_row, (8, P_OUT)), right[:8]), right[8:]], axis=0
        )
        return left, right

    def panel(_, pairs):
        pairs = list(pairs)
        for place in range(8):
            for which in range(len(pairs)):
                pairs[which] = one_step(place, *pairs[which])
        return tuple(
            (
                pltpu.roll(jnp.concatenate([left[8:], left[:8]], axis=0), P_OUT - 8, 1),
                jnp.concatenate([right[8:], right[:8]], axis=0),
            )
            for left, right in pairs
        )

    pairs = tuple((matrix, (row_all == col_all).astype(f32)) for matrix in matrices)
    done = [[] for _ in matrices]
    size = P_OUT // 4
    for _ in range(4):
        pairs = lax.fori_loop(0, size // 8, panel, pairs)
        for found, (_, right) in zip(done, pairs):
            found.append(right[-size:])
        pairs = tuple((left[:-size], right[:-size]) for left, right in pairs)
    return [jnp.concatenate(found, axis=0) for found in done]


def pack_pair(first, second):
    row = lax.broadcasted_iota(jnp.int32, (P_OUT, P_OUT), 0)
    col = lax.broadcasted_iota(jnp.int32, (P_OUT, P_OUT), 1)
    packed = jnp.where(row >= col, first, second.T)
    diagonal = jnp.sum(jnp.where(row == col, second, 0.0), axis=0, keepdims=True)
    return packed, diagonal


def unpack_pair(packed, diagonal):
    row = lax.broadcasted_iota(jnp.int32, (P_OUT, P_OUT), 0)
    col = lax.broadcasted_iota(jnp.int32, (P_OUT, P_OUT), 1)
    turned = packed.T
    first = jnp.where(row >= col, packed, turned)
    second = jnp.where(row < col, packed, jnp.where(row == col, diagonal, turned))
    return first, second


GATHER_AT = {
    (0, 1): 1,
    (0, 3): 1,
    (1, 0): 1,
    (3, 0): 1,
    (3, 2): 1,
    (3, 3): 1,
    (3, 6): 1,
    (5, 1): 1,
    (5, 4): 1,
    (6, 0): 2,
    (9, 4): 1,
    (9, 11): 1,
    (10, 0): 1,
    (10, 7): 1,
    (10, 15): 2,
    (10, 21): 1,
    (21, 0): 9,
}
REDUCE_AT = {
    (11, 0): ((4, 0, 0),),
    (11, 6): ((3, 2, 0),),
    (11, 7): ((3, 3, 0),),
    (11, 13): ((3, 0, 0),),
    (11, 17): ((3, 1, 1),),
    (11, 21): ((4, 0, 1),),
    (11, 25): ((3, 2, 1),),
    (12, 2): ((3, 3, 1), (3, 1, 2)),
    (13, 2): ((3, 0, 1),),
    (13, 3): ((2, 0, 0),),
    (14, 1): ((3, 2, 2),),
    (14, 2): ((3, 3, 2),),
    (14, 4): ((3, 1, 3), (2, 2, 0)),
    (14, 6): ((2, 3, 0), (2, 1, 0)),
    (15, 0): ((2, 0, 1),),
    (15, 1): ((3, 0, 2),),
    (15, 2): ((4, 0, 2),),
    (15, 3): ((2, 3, 1),),
    (15, 4): ((1, 1, 0),),
    (15, 5): ((1, 0, 0), (2, 2, 1), (2, 1, 1)),
    (15, 6): ((3, 3, 3), (3, 2, 3)),
    (16, 0): ((2, 0, 2), (2, 2, 2), (1, 1, 1), (1, 2, 0)),
    (16, 1): ((3, 0, 3), (2, 1, 2), (1, 0, 1)),
    (16, 2): ((2, 3, 2),),
    (16, 3): ((3, 9, 4), (2, 0, 3), (1, 2, 1)),
    (17, 0): ((2, 1, 3),),
    (17, 1): ((1, 3, 0), (1, 0, 2), (2, 3, 3), (2, 2, 3)),
    (18, 0): ((1, 1, 2),),
    (18, 4): ((4, 0, 3),),
    (18, 5): ((1, 3, 1),),
    (19, 0): ((2, 9, 4), (1, 0, 3), (1, 1, 3), (1, 2, 2)),
    (19, 1): ((0, 1, 0), (0, 0, 0), (1, 3, 2)),
    (19, 2): ((1, 2, 3), (0, 1, 1), (0, 2, 0)),
    (19, 3): ((0, 0, 1),),
    (20, 0): ((0, 3, 0),),
    (20, 2): ((0, 2, 1),),
    (20, 4): ((0, 1, 2), (1, 3, 3)),
    (20, 6): ((0, 3, 1),),
    (20, 8): ((0, 2, 2),),
    (20, 10): ((0, 0, 2), (0, 1, 3)),
    (20, 12): ((4, 9, 4),),
    (20, 13): ((0, 3, 2),),
    (20, 14): ((0, 2, 3),),
    (20, 17): ((0, 0, 3), (1, 9, 4)),
    (20, 18): ((0, 3, 3),),
    (20, 22): ((0, 9, 4),),
    (23, 0): ((3, 1, 0),),
}


class Ins(NamedTuple):
    features: Any
    order: Any
    norm: Any
    shards: Any


class Outs(NamedTuple):
    slope: Any
    features_grad: Any
    norm_grad: Any
    scalars: Any
    grads: Any


class SumRoom(NamedTuple):
    dp: Any
    fsdp: Any
    s0: Any
    r0: Any
    s1: Any
    r1: Any


class MatrixRoom(NamedTuple):
    pack: Any
    dp: Any
    fsdp: Any
    all: Any
    s0: Any
    r0: Any
    s1: Any
    r1: Any
    s2: Any
    r2: Any


class Mem(NamedTuple):
    w: Any
    g1: Any
    row_sums: Any
    r3: Any
    r4: Any
    r5: Any
    stage: Any
    stage_sem: Any
    column_sem: Any
    h1: Any
    d1: Any
    h2: Any
    d2: Any
    a2: Any
    h3: Any
    pad1: Any
    pad2: Any
    pool: Any
    pool_slope: Any
    pool_bend: Any
    pooled: Any
    proj_act: Any
    proj_slope: Any
    proj_hidden: Any
    coef: Any
    stats: Any
    norm: Any
    norm_grads: Any
    norm_tiles: Any
    norm_s0: Any
    norm_r0: Any
    norm_s1: Any
    norm_r1: Any
    bulk_send: Any
    bulk_recv: Any
    mats: Any
    sums: Any
    squares: Any


class Plan:
    def __init__(self, dp_size, fsdp_size, views, inside):
        self.dp = dp_size
        self.fsdp = fsdp_size
        self.devices = dp_size * fsdp_size
        self.views = views
        self.rows = views * PIX
        self.chunk = views * SIDE
        self.inside = inside
        self.z = 4
        self.x = 2
        self.half = (128, 288, 32, 128, 16)
        self.width = (128, 128, 512, 256, 128)
        piece = P_OUT + 8
        self.embed_rows = -(-piece // (8 * dp_size)) * 8


def kernel(plan, *refs):
    ins, outs, mem = Ins(*refs[:3], refs[3:8]), Outs(*refs[8:12], refs[12:17]), refs[17]
    views, chunk, rows = plan.views, plan.chunk, plan.rows
    row_total = float(rows * plan.devices)
    view_total = float(views * plan.devices)
    image_total = float(views * plan.devices // 2)
    dp_me, fsdp_me = lax.axis_index(DP), lax.axis_index(FSDP)
    y_me, c_me = dp_me // 2, dp_me % 2
    z_me, x_me = fsdp_me // 2, fsdp_me % 2
    y_other, c_other, x_other = 1 - y_me, 1 - c_me, 1 - x_me

    barrier = pltpu.get_barrier_semaphore()

    @pl.loop(1, plan.dp)
    def _(step):
        pl.semaphore_signal(
            barrier, 1, device_id={DP: lax.rem(dp_me + step, plan.dp)}, device_id_type=pl.DeviceIdType.MESH
        )

    @pl.loop(1, plan.fsdp)
    def _(step):
        pl.semaphore_signal(
            barrier, 1, device_id={FSDP: lax.rem(fsdp_me + step, plan.fsdp)}, device_id_type=pl.DeviceIdType.MESH
        )

    pl.semaphore_wait(barrier, plan.dp + plan.fsdp - 2)

    def share(axis, size, me, source_of, slots, send, recv):
        def outgoing(step):
            partner = lax.rem(me + step, size)
            return pltpu.make_async_remote_copy(
                src_ref=source_of(partner),
                dst_ref=slots.at[me],
                send_sem=send.at[step],
                recv_sem=recv.at[me],
                device_id={axis: partner},
                device_id_type=pl.DeviceIdType.MESH,
            )

        def incoming(step):
            source = lax.rem(me + step, size)
            return pltpu.make_async_remote_copy(
                src_ref=slots.at[source],
                dst_ref=slots.at[source],
                send_sem=send.at[step],
                recv_sem=recv.at[source],
                device_id={axis: source},
                device_id_type=pl.DeviceIdType.MESH,
            )

        def start():
            pl.loop(1, size)(lambda step: outgoing(step).start())

        def wait():
            pl.loop(1, size)(lambda step: incoming(step).wait_recv())
            pl.loop(1, size)(lambda step: outgoing(step).wait_send())

        return start, wait

    def add_slots(slots, size):
        total = slots[0]
        for place in range(1, size):
            total = total + slots[place]
        return total

    class Sum:
        def __init__(self, which):
            part = mem.sums[(0, 1, 2, 3, 4, 4, 5, 0, 1, 6)[which]]
            self.dp_slots, self.fsdp_slots = part.dp, part.fsdp
            self.dp_copy = share(
                DP, plan.dp, dp_me, lambda _: self.dp_slots.at[dp_me], self.dp_slots, part.s0, part.r0
            )
            self.fsdp_copy = share(
                FSDP, plan.fsdp, fsdp_me, lambda _: self.fsdp_slots.at[fsdp_me], self.fsdp_slots, part.s1, part.r1
            )

        def start(self, *values):
            for place, value in enumerate(values):
                self.dp_slots[dp_me, place : place + 1, :] = value
            self.dp_copy[0]()

        def middle(self):
            self.dp_copy[1]()
            self.fsdp_slots[fsdp_me] = add_slots(self.dp_slots, plan.dp)
            self.fsdp_copy[0]()

        def finish(self):
            self.fsdp_copy[1]()
            return add_slots(self.fsdp_slots, plan.fsdp)

        def all(self, *values):
            self.start(*values)
            self.middle()
            return self.finish()

    def sum_matrix(which, matrix, extra):
        part = mem.mats[which]
        size = plan.embed_rows
        pack = part.pack
        flat = jnp.concatenate(
            [matrix] + extra + [jnp.zeros((size * plan.dp - P_OUT - len(extra), P_OUT), f32)], axis=0
        )
        for place in range(plan.dp):
            pack[place] = flat[place * size : (place + 1) * size]
        start, wait = share(DP, plan.dp, dp_me, lambda to: pack.at[to], part.dp, part.s0, part.r0)
        start()
        part.dp[dp_me] = pack[dp_me]
        wait()
        part.fsdp[fsdp_me] = add_slots(part.dp, plan.dp)
        start, wait = share(
            FSDP, plan.fsdp, fsdp_me, lambda _: part.fsdp.at[fsdp_me], part.fsdp, part.s1, part.r1
        )
        start()
        wait()
        part.all[dp_me] = add_slots(part.fsdp, plan.fsdp)
        start, wait = share(
            DP, plan.dp, dp_me, lambda _: part.all.at[dp_me], part.all, part.s2, part.r2
        )
        start()
        wait()
        total = jnp.concatenate([part.all[place] for place in range(plan.dp)], axis=0)
        return total[:P_OUT], [total[P_OUT + place : P_OUT + place + 1] for place in range(len(extra))]

    weights = mem.w
    everything = slice(None)

    def row_span(which, half):
        if isinstance(half, tuple):
            return half
        size = plan.half[which]
        if half is None:
            return 0, 2 * size
        return half * size, size

    def column_span(which, dp_index):
        width = plan.width[which]
        return pl.ds(pl.multiple_of(dp_index * width, width), width)

    def places(which, z_index, x_index, dp_index, half, flat=True):
        start, size = row_span(which, half)
        if which == 1 and flat:
            z_list = range(plan.z) if z_index is None else [z_index]
            x_list = range(plan.x) if x_index is None else [x_index]
            return [
                (
                    pl.ds(pl.multiple_of((z_one * plan.x + x_one) * 576 + start, 16), size),
                    column_span(which, dp_index),
                )
                for z_one in z_list
                for x_one in x_list
            ]
        z_one = everything if z_index is None else z_index
        x_one = everything if x_index is None else x_index
        if which == 2:
            return [(dp_index, z_one, x_one, pl.ds(start, size), everything)]
        if which == 4:
            return [(z_one, x_one, pl.ds(pl.multiple_of(dp_index * 32 + start, 16), size), everything)]
        return [(z_one, x_one, pl.ds(start, size), column_span(which, dp_index))]

    recv_parts = {
        1: lambda index: mem.h3.at[index],
        0: lambda index: mem.r4.at[index],
        2: lambda index: mem.r3.at[index],
        3: lambda index: mem.r4.at[index],
        4: lambda index: mem.r5.at[index],
    }

    counter = [0]

    class Batch:
        def __init__(self, sources, targets, landings, axis, partner):
            base = counter[0]
            counter[0] += len(sources)
            send, recv = mem.bulk_send, mem.bulk_recv
            self.out = [
                pltpu.make_async_remote_copy(
                    src_ref=source,
                    dst_ref=target,
                    send_sem=send.at[base + place],
                    recv_sem=recv.at[base + place],
                    device_id={axis: partner},
                    device_id_type=pl.DeviceIdType.MESH,
                )
                for place, (source, target) in enumerate(zip(sources, targets))
            ]
            self.come = [
                pltpu.make_async_remote_copy(
                    src_ref=landing,
                    dst_ref=landing,
                    send_sem=send.at[base + place],
                    recv_sem=recv.at[base + place],
                    device_id={axis: partner},
                    device_id_type=pl.DeviceIdType.MESH,
                )
                for place, landing in enumerate(landings)
            ]

        def start(self):
            for copy in self.out:
                copy.start()

        def arrive(self):
            for copy in self.come:
                copy.wait_recv()

        def leave(self):
            for copy in self.out:
                copy.wait_send()

    class LineBatch:
        def __init__(self, source_of, target_of, landing_of):
            base = counter[0]
            counter[0] += plan.z
            send, recv = mem.bulk_send, mem.bulk_recv
            self.out, self.come = [], []
            for step in range(1, plan.z):
                z_to = (z_me + step) % plan.z
                self.out.append(
                    pltpu.make_async_remote_copy(
                        src_ref=source_of(z_to),
                        dst_ref=target_of(z_to),
                        send_sem=send.at[base + step],
                        recv_sem=recv.at[base + z_me],
                        device_id={FSDP: z_to * plan.x + x_me},
                        device_id_type=pl.DeviceIdType.MESH,
                    )
                )
                self.come.append(
                    pltpu.make_async_remote_copy(
                        src_ref=landing_of(z_to),
                        dst_ref=landing_of(z_to),
                        send_sem=send.at[base + step],
                        recv_sem=recv.at[base + z_to],
                        device_id={FSDP: z_to * plan.x + x_me},
                        device_id_type=pl.DeviceIdType.MESH,
                    )
                )

        start, arrive, leave = Batch.start, Batch.arrive, Batch.leave

    def pick(ref, indexes):
        return [ref.at[index] for index in indexes]

    def own_dp(y_index, c_index):
        return y_index * 2 + c_index

    x_partner = z_me * plan.x + x_other
    y_partner = own_dp(y_other, c_me)
    c_partner = own_dp(y_me, c_other)
    dp_far = own_dp(y_other, c_other)

    class Gather:
        def __init__(self, which, start, size):
            ref = weights[which]
            self.which, self.rows = which, (start, size)
            both, low, high = (start, size), (start, size // 2), (start + size // 2, size // 2)

            def at(*index):
                return pick(ref, places(which, *index, False))

            own = at(z_me, x_me, dp_me, both)[0]
            self.line = LineBatch(
                lambda _: own, lambda _: own, lambda z_from: at(z_from, x_me, dp_me, both)[0]
            )
            sent, come = at(None, x_me, dp_me, low), at(None, x_other, dp_me, low)
            x_first = Batch(sent, sent, come, FSDP, x_partner)
            sent, come = at(None, x_me, dp_me, high), at(None, x_me, y_partner, high)
            y_first = Batch(sent, sent, come, DP, y_partner)
            sent, come = at(None, None, dp_me, low), at(None, None, y_partner, low)
            y_second = Batch(sent, sent, come, DP, y_partner)
            sent = at(None, x_me, dp_me, high) + at(None, x_me, y_partner, high)
            come = at(None, x_other, dp_me, high) + at(None, x_other, y_partner, high)
            x_second = Batch(sent, sent, come, FSDP, x_partner)
            sent = at(None, None, dp_me, both) + at(None, None, y_partner, both)
            come = at(None, None, c_partner, both) + at(None, None, dp_far, both)
            core = Batch(sent, sent, come, DP, c_partner)
            self.stages = ((self.line,), (x_first, y_first), (y_second, x_second), (core,))

        def put_own(self):
            index = places(self.which, z_me, x_me, dp_me, self.rows, False)[0]
            shard = ins.shards[self.which][self.rows[0] : self.rows[0] + self.rows[1], :]
            weights[self.which][index] = shard.astype(bf16)

        def start(self, stage):
            for batch in self.stages[stage]:
                batch.start()

        def arrive(self, stage):
            for batch in self.stages[stage]:
                batch.arrive()

        def leave(self):
            for stage in self.stages:
                for batch in stage:
                    batch.leave()

    class Piece:
        def __init__(self, which, ref, room, z_index):
            def at(*index):
                return pick(ref, places(which, z_index, *index))

            def land(*index):
                return [room(index_one) for index_one in places(which, z_index, *index)]

            self.z = z_index
            self.core = Batch(
                at(None, c_partner, None) + at(None, dp_far, None),
                land(None, c_partner, None) + land(None, dp_far, None),
                land(None, dp_me, None) + land(None, y_partner, None),
                DP,
                c_partner,
            )
            self.y_first = Batch(
                at(None, y_partner, 0), land(None, dp_far, 0), land(None, c_partner, 0), DP, y_partner
            )
            self.x_first = Batch(
                at(x_other, dp_me, 1) + at(x_other, y_partner, 1),
                land(x_other, c_partner, 1) + land(x_other, dp_far, 1),
                land(x_me, c_partner, 1) + land(x_me, dp_far, 1),
                FSDP,
                x_partner,
            )
            self.x_second = Batch(
                at(x_other, dp_me, 0), land(x_other, dp_far, 0), land(x_me, dp_far, 0), FSDP, x_partner
            )
            self.y_second = Batch(
                at(x_me, y_partner, 1), land(x_other, dp_far, 1), land(x_other, c_partner, 1), DP, y_partner
            )

    class Reduce:
        def __init__(self, which, ref, cut):
            self.which, self.ref, self.room = which, ref, recv_parts[which]
            self.pieces = [
                Piece(which, ref, self.room, z_index) for z_index in (range(plan.z) if cut else [None])
            ]
            self.base = counter[0]
            counter[0] += plan.z

        def line_copy(self, z_to):
            return pltpu.make_async_remote_copy(
                src_ref=self.ref.at[places(self.which, z_to, x_me, dp_me, None)[0]],
                dst_ref=self.room(places(self.which, z_me, x_other, dp_far, None)[0]),
                send_sem=mem.bulk_send.at[self.base + z_to],
                recv_sem=mem.bulk_recv.at[self.base + z_me],
                device_id={FSDP: z_to * plan.x + x_me},
                device_id_type=pl.DeviceIdType.MESH,
            )

        def line_room(self, z_from):
            return self.room(places(self.which, z_from, x_other, dp_far, None)[0])

        def add(self, z_index, pairs):
            def one(z_one):
                for here, there in pairs:
                    for x_step in range(plan.x) if here[0] is None else [None]:
                        x_here = x_step if here[0] is None else here[0]
                        x_there = x_step if there[0] is None else there[0]
                        index = places(self.which, z_one, x_here, *here[1:])[0]
                        other = places(self.which, z_one, x_there, *there[1:])[0]
                        total = self.ref[index].astype(f32) + self.room(other)[...].astype(f32)
                        self.ref[index] = total.astype(bf16)

            if z_index is None:
                pl.loop(0, plan.z)(one)
            else:
                one(z_index)

        def core_start(self, place=0):
            if plan.inside:
                self.pieces[place].core.start()

        def core_add(self, place=0):
            if plan.inside:
                piece = self.pieces[place]
                piece.core.arrive()
                self.add(piece.z, [((None, dp_me, None),) * 2, ((None, y_partner, None),) * 2])
                piece.y_first.start()
                piece.x_first.start()

        def first_add(self, place=0):
            if plan.inside:
                piece = self.pieces[place]
                piece.y_first.arrive()
                self.add(piece.z, [((None, dp_me, 0), (None, c_partner, 0))])
                piece.x_second.start()
                piece.x_first.arrive()
                self.add(
                    piece.z, [((x_me, dp_me, 1), (x_me, c_partner, 1)), ((x_me, y_partner, 1), (x_me, dp_far, 1))]
                )
                piece.y_second.start()

        def second_add(self, place=0):
            if plan.inside:
                piece = self.pieces[place]
                piece.x_second.arrive()
                piece.y_second.arrive()
                self.add(
                    piece.z, [((x_me, dp_me, 0), (x_me, dp_far, 0)), ((x_me, dp_me, 1), (x_other, c_partner, 1))]
                )
                if piece.z is None:
                    for step in range(1, plan.z):
                        self.line_copy((z_me + step) % plan.z).start()
                else:

                    @pl.when(z_me != piece.z)
                    def _():
                        self.line_copy(piece.z).start()

        def finish(self):
            if not plan.inside:
                return
            total = self.ref[places(self.which, z_me, x_me, dp_me, None)[0]].astype(f32)
            for step in range(1, plan.z):
                z_from = (z_me + step) % plan.z
                room = self.line_room(z_from)
                pltpu.make_async_remote_copy(
                    src_ref=room,
                    dst_ref=room,
                    send_sem=mem.bulk_send.at[self.base + z_from],
                    recv_sem=mem.bulk_recv.at[self.base + z_from],
                    device_id={FSDP: z_from * plan.x + x_me},
                    device_id_type=pl.DeviceIdType.MESH,
                ).wait_recv()
                total = total + room[...].astype(f32)
            outs.grads[self.which][...] = total
            squares = jnp.sum(total * total, axis=0, keepdims=True)
            folded = squares[:, :LANES]
            for place in range(1, squares.shape[1] // LANES):
                folded = folded + squares[:, place * LANES : (place + 1) * LANES]
            mem.squares[...] += folded
            for step in range(1, plan.z):
                self.line_copy((z_me + step) % plan.z).wait_send()
            for piece in self.pieces:
                for batch in (piece.core, piece.y_first, piece.x_first, piece.x_second, piece.y_second):
                    batch.leave()

    gathers, steps = [], []
    if plan.inside:
        for which, cuts in enumerate((2, 3, 1, 2, 1)):
            size = 2 * plan.half[which] // cuts
            gathers += [Gather(which, cut * size, size) for cut in range(cuts)]

    def line_step(place):
        gathers[place].arrive(0)
        gathers[place].start(1)
        if place + 1 < len(gathers):
            gathers[place + 1].start(0)

    def first_step(place):
        gathers[place].arrive(1)
        gathers[place].start(2)

    def second_step(place):
        gathers[place].arrive(2)
        gathers[place].start(3)

    for place in range(len(gathers)):
        steps.append((line_step, place))
        if place > 0:
            steps.append((second_step, place - 1))
        steps.append((first_step, place))
    if plan.inside:
        steps.append((second_step, len(gathers) - 1))

    def take(count):
        taken, steps[:] = steps[:count], steps[count:]
        return [lambda one=one: one[0](one[1]) for one in taken]

    def moves(site, item):
        found = take(GATHER_AT.get((site, item), 0)) if plan.inside else []
        for which, piece, kind in REDUCE_AT.get((site, item), ()):
            one = reduces[which]
            found.append(
                one.finish
                if kind == 4
                else lambda one=one, kind=kind, piece=piece: (
                    one.core_start,
                    one.core_add,
                    one.first_add,
                    one.second_add,
                )[kind](piece)
            )
        return found

    def hook(site, item=0):
        for move in moves(site, item):
            move()

    def hook_in(site, index, count, first=0, stride=1):
        for item in range(count):
            found = moves(site, item)
            if found and plan.inside:

                @pl.when(index == first + item * stride)
                def _(found=found):
                    for move in found:
                        move()

    def cores_arrive(which):
        for one in gathers:
            if one.which == which:
                one.arrive(3)

    gradients = [mem.g1, mem.stage.at[pl.ds(0, 9 * C_MID)], weights[2], weights[3], weights[4]]
    reduces = [Reduce(which, gradients[which], which < 4) for which in range(5)]
    mem.squares[...] = jnp.zeros((1, LANES), f32)

    if plan.inside:
        gathers[0].put_own()
        gathers[0].start(0)
        for one in gathers[1:]:
            one.put_own()
        tiles = mem.norm_tiles
        tiles[dp_me, fsdp_me] = ins.norm[...].astype(bf16).astype(f32)
        norm_dp = share(
            DP, plan.dp, dp_me, lambda _: tiles.at[dp_me, fsdp_me], tiles.at[:, fsdp_me], mem.norm_s0, mem.norm_r0
        )
        norm_dp[0]()
    else:
        loads = [
            pltpu.make_async_copy(ins.shards[which], weights[which], mem.bulk_send.at[which])
            for which in range(5)
        ]
        for load in loads:
            load.start()

    pieces = BLOCKS * CHUNKS

    def hidden_rows(index, pixel=0, count=chunk):
        return pl.ds(pl.multiple_of(index * chunk + pixel * views, 16), count)

    class Ring:
        def __init__(self, ref, start):
            self.ref, self.base = ref, start

        def rows(self, index, pixel=0, count=chunk):
            return pl.ds(
                pl.multiple_of(self.base + lax.rem(index, SLOTS) * chunk + pixel * views, 16), count
            )

        def copy(self, array, index, into):
            block, place = index // CHUNKS, lax.rem(index, CHUNKS)
            outer = array.at[
                pl.ds(pl.multiple_of(place * chunk, 16), chunk),
                pl.ds(pl.multiple_of(block * C_MID, LANES), C_MID),
            ]
            inner = self.ref.at[self.rows(index)]
            source, target = (outer, inner) if into else (inner, outer)
            return pltpu.make_async_copy(
                source, target, mem.stage_sem.at[0 if into else 1, lax.rem(index, SLOTS)]
            )

        def first_loads(self, array):
            for index in range(3):
                self.copy(array, index, True).start()

        def next_load(self, array, index):
            @pl.when(index + 3 < pieces)
            def _():
                self.copy(array, index + 3, True).start()

        def save(self, array, index):
            self.copy(array, index, False).start()

            @pl.when(index >= 2)
            def _():
                self.copy(array, index - 2, False).wait()

        def last_saves(self, array):
            for index in (pieces - 2, pieces - 1):
                self.copy(array, index, False).wait()

    stage_ref = mem.stage
    stage = Ring(stage_ref, 0)

    def piece_columns(index, part):
        return pl.ds(pl.multiple_of(index // CHUNKS * C_MID + part * LANES, LANES), LANES)

    features, slope_hbm = ins.features, outs.slope
    hidden_three = mem.h3

    def feature_copy(block, target):
        return pltpu.make_async_copy(
            features.at[:, pl.ds(block * C_MID, C_MID)], target, mem.column_sem.at[block]
        )

    feature_loads = [
        feature_copy(block, hidden_three.at[pl.ds(block * rows, rows)]) for block in range(BLOCKS)
    ]
    for copy in feature_loads:
        copy.start()
    stage.first_loads(features)

    padded_one, padded_two = mem.pad1, mem.pad2
    for padded in (padded_one, padded_two):
        for edge in (0, SIDE + 1):
            padded[edge] = jnp.zeros((padded.shape[1], C_MID), bf16)
        for edge in (0, SIDE + 1):
            padded[:, pl.ds(edge * views, views), :] = jnp.zeros((SIDE + 2, views, C_MID), bf16)

    if plan.inside:
        norm_dp[1]()
        norm_out = []
        norm_in = []
        for step in range(1, plan.fsdp):
            partner = (fsdp_me + step) % plan.fsdp
            norm_out.append(
                pltpu.make_async_remote_copy(
                    src_ref=tiles.at[:, fsdp_me],
                    dst_ref=tiles.at[:, fsdp_me],
                    send_sem=mem.norm_s1.at[step],
                    recv_sem=mem.norm_r1.at[fsdp_me],
                    device_id={FSDP: partner},
                    device_id_type=pl.DeviceIdType.MESH,
                )
            )
            norm_in.append(
                pltpu.make_async_remote_copy(
                    src_ref=tiles.at[:, partner],
                    dst_ref=tiles.at[:, partner],
                    send_sem=mem.norm_s1.at[step],
                    recv_sem=mem.norm_r1.at[partner],
                    device_id={FSDP: partner},
                    device_id_type=pl.DeviceIdType.MESH,
                )
            )
        for copy in norm_out:
            copy.start()
        hook(21)
        for copy in norm_in:
            copy.wait_recv()
        for copy in norm_out:
            copy.wait_send()
        norm_all = mem.norm
        for dp_one in range(plan.dp):
            for fsdp_one in range(plan.fsdp):
                start = (dp_one * plan.fsdp + fsdp_one) * LANES
                norm_all[:, start : start + LANES] = tiles[dp_one, fsdp_one]
    else:
        for copy in loads:
            copy.wait()
        norm_all = mem.norm
        norm_all[...] = ins.norm[...]

    starts = (0, C_MID, 2 * C_MID, 2 * C_MID + C_IN, 2 * C_MID + C_IN + P_HID)

    def gain(layer):
        return norm_all[0:1, starts[layer] : starts[layer + 1]]

    coef, stats = mem.coef, mem.stats

    def norm_coefs(layer, totals, count, low=0):
        width = totals.shape[1]
        here, there = slice(low, low + width), slice(starts[layer] + low, starts[layer] + low + width)
        mean = totals[0:1] / count
        scaling = lax.rsqrt(totals[1:2] / count - mean * mean + norm_epsilon)
        slope = scaling * norm_all[0:1, there]
        stats[0:1, there] = mean
        stats[1:2, there] = scaling
        coef[0:1, here] = slope
        coef[1:2, here] = norm_all[1:2, there] - mean * slope

    def grad_coefs(layer, totals, count):
        width = starts[layer + 1] - starts[layer]
        mean = stats[0:1, starts[layer] : starts[layer + 1]]
        scaling = stats[1:2, starts[layer] : starts[layer + 1]]
        mem.norm_grads[0:1, starts[layer] : starts[layer + 1]] = totals[1:2]
        mem.norm_grads[1:2, starts[layer] : starts[layer + 1]] = totals[0:1]
        slope = scaling * gain(layer)
        bend = slope * scaling * totals[1:2] / count
        coef[0:1, :width] = slope
        coef[1:2, :width] = slope * totals[0:1] / count - mean * bend
        coef[2:3, :width] = bend

    def xhat_sum(layer, plain, product):
        mean = stats[0:1, starts[layer] : starts[layer + 1]]
        scaling = stats[1:2, starts[layer] : starts[layer + 1]]
        return scaling * (product - mean * plain)

    zero_row = jnp.zeros((1, C_MID), f32)

    def column_sums(value):
        return jnp.sum(value, axis=0, keepdims=True)

    def whole(which):
        value = weights[which][...]
        return value.reshape(-1, value.shape[-1])

    row_sums = mem.row_sums

    def clear_sums():
        row_sums[...] = jnp.zeros_like(row_sums)

    def count_in(cols, value, other):
        row_sums[0:1, cols] += column_sums(value)
        row_sums[1:2, cols] += column_sums(value * other)

    def own_columns(side):
        core = (c_me + side) % 2
        return [
            pl.ds(pl.multiple_of(half * (C_MID // 2) + core * LANES, LANES), LANES) for half in range(2)
        ]

    hidden_one, slope_one = mem.h1, mem.d1
    hidden_two, slope_two = mem.h2, mem.d2
    act_two = mem.a2
    long = rows // 3

    def span(index):
        return pl.ds(pl.multiple_of(index * chunk, 16), chunk)

    def long_rows(block, index):
        return pl.ds(pl.multiple_of(block * rows + index * long, 16), long)

    def put_sides(ref, at, sides, hidden):
        for place, cols in enumerate(sides):
            part = hidden[:, place * LANES : (place + 1) * LANES]
            ref[at, cols] = part.astype(bf16)
            count_in(cols, part, part)

    for copy in feature_loads:
        copy.wait()
    clear_sums()

    @pl.loop(0, 2)
    def _(side):
        sides = own_columns(side)

        @pl.loop(0, 3)
        def _(index):
            left = jnp.concatenate([hidden_three[long_rows(block, index), :] for block in range(BLOCKS)], axis=1)
            right = jnp.concatenate([weights[0][:, :, :, cols].reshape(C_IN, LANES) for cols in sides], axis=1)
            put_sides(hidden_one, long_rows(0, index), sides, dot(left, right))

            hook_in(0, side * 3 + index, 6)

        @pl.when(side == 0)
        def _():
            cores_arrive(0)

    sum_one = Sum(0)
    sum_one.start(row_sums[0:1, :C_MID], row_sums[1:2, :C_MID])
    hook(1)
    sum_one.middle()
    hook(2)
    clear_sums()
    norm_coefs(0, sum_one.finish(), row_total)

    def activate(hidden_ref, slope_ref, put, site):
        @pl.loop(0, PIX)
        def _(pixel):
            place = pl.ds(pl.multiple_of(pixel * views, 16), views)
            for block in range(C_MID // LANES):
                cols = slice(block * LANES, (block + 1) * LANES)
                out = hidden_ref[place, cols].astype(f32) * coef[0:1, cols] + coef[1:2, cols]
                value, slope = gelu_pair(out)
                slope_ref[place, cols] = slope.astype(bf16)
                put(pixel, cols, value.astype(bf16))
            hook_in(site, pixel, SIDE, SIDE - 1, SIDE)

    def put_padded(padded):
        def put(pixel, cols, value):
            padded[pixel // SIDE + 1, pl.ds(pl.multiple_of((pixel % SIDE + 1) * views, 16), views), cols] = value

        return put

    activate(hidden_one, slope_one, put_padded(padded_one), 3)
    hook(4)

    def patch(padded, first, count, flip):
        found = []
        for vertical in range(3):
            for lateral in range(3):
                down, across = (2 - vertical, 2 - lateral) if flip else (vertical, lateral)
                piece = padded[pl.ds(first + down, count), across * views : across * views + chunk, :]
                found.append(piece.reshape(count * chunk, C_MID))
        return jnp.concatenate(found, axis=1)

    def image_rows(first, count):
        return pl.ds(pl.multiple_of(first * chunk, 16), count * chunk)

    def second_part(sides, first, count):
        right = jnp.concatenate([weights[1][:, :, :, cols].reshape(9 * C_MID, LANES) for cols in sides], axis=1)
        hidden = dot(patch(padded_one, first, count, False), right)
        put_sides(hidden_two, image_rows(first, count), sides, hidden)

    @pl.loop(0, 2)
    def _(side):
        sides = own_columns(side)

        @pl.loop(0, 3)
        def _(index):
            second_part(sides, 2 * index, 2)
            hook_in(5, side * 4 + index, 8)

        second_part(sides, 6, 1)

        @pl.when(side == 0)
        def _():
            cores_arrive(1)

    sum_two = Sum(1)
    sum_two.start(row_sums[0:1, :C_MID], row_sums[1:2, :C_MID])
    hook(6)
    sum_two.middle()
    hook(7)
    clear_sums()
    norm_coefs(1, sum_two.finish(), row_total)

    def put_rows(pixel, cols, value):
        act_two[pl.ds(pl.multiple_of(pixel * views, 16), views), cols] = value

    activate(hidden_two, slope_two, put_rows, 8)
    cores_arrive(2)

    def weight_three(block):
        return weights[2][block].reshape(C_MID, C_MID)

    sums_low, sums_high = Sum(2), Sum(3)
    half_width = C_IN // 2

    @pl.loop(0, BLOCKS)
    def _(block):
        cols = pl.ds(pl.multiple_of(block * C_MID, LANES), C_MID)

        @pl.loop(0, 3)
        def _(index):
            hidden = dot(act_two[long_rows(0, index), :], weight_three(block))
            hidden_three[long_rows(block, index), :] = hidden.astype(bf16)
            count_in(cols, hidden, hidden)
            hook_in(9, block * 3 + index, 12)

        @pl.when(block == 1)
        def _():
            sums_low.start(row_sums[0:1, :half_width], row_sums[1:2, :half_width])

        @pl.when(block == 2)
        def _():
            sums_low.middle()

    sums_high.start(row_sums[0:1, half_width:], row_sums[1:2, half_width:])
    norm_coefs(2, sums_low.finish(), row_total)

    hook(22)

    pool, pool_slope, pool_bend = mem.pool, mem.pool_slope, mem.pool_bend
    for ref in (pool, pool_slope, pool_bend):
        ref[...] = jnp.zeros_like(ref)

    @pl.loop(0, pieces)
    def _(index):
        stage.copy(features, index, True).wait()

        @pl.loop(0, C_MID // LANES)
        def _(part):
            inner = pl.ds(pl.multiple_of(part * LANES, LANES), LANES)
            cols = piece_columns(index, part)
            slope_row, shift_row = coef[0:1, cols], coef[1:2, cols]
            kept = (pool[:, cols], pool_slope[:, cols], pool_bend[:, cols])
            for pixel in range(SIDE):
                stage_at, hidden_at = stage.rows(index, pixel, views), hidden_rows(index, pixel, views)
                hidden = hidden_three[hidden_at, inner].astype(f32)
                total = hidden * slope_row + shift_row + stage_ref[stage_at, inner].astype(f32)
                value, slope = gelu_pair(total)
                stage_ref[stage_at, inner] = slope.astype(bf16)
                kept = (kept[0] + value, kept[1] + slope, kept[2] + slope * hidden)
            pool[:, cols], pool_slope[:, cols], pool_bend[:, cols] = kept

        stage.save(slope_hbm, index)
        stage.next_load(features, index)

        @pl.when(index == 2)
        def _():
            sums_high.middle()

        @pl.when(index == pieces // 2 - 1)
        def _():
            norm_coefs(2, sums_high.finish(), row_total, half_width)

        hook_in(10, index, pieces)

    stage.last_saves(slope_hbm)
    cores_arrive(3)
    cores_arrive(4)
    for one in gathers:
        one.leave()

    pooled = (pool[...] * (1.0 / PIX)).astype(bf16)
    mem.pooled[...] = pooled
    proj_hidden = dot(pooled, whole(3))
    sum_four = Sum(4)
    totals = sum_four.all(column_sums(proj_hidden), column_sums(proj_hidden * proj_hidden))
    stage.first_loads(slope_hbm)
    norm_coefs(3, totals, view_total)
    value, slope = gelu_pair(proj_hidden * coef[0:1, :P_HID] + coef[1:2, :P_HID])
    proj_act = value.astype(bf16)
    mem.proj_act[...] = proj_act
    mem.proj_slope[...] = slope
    mem.proj_hidden[...] = proj_hidden

    def weight_five(block):
        return weights[4][block // plan.x, block % plan.x]

    parts = P_HID // P_OUT
    embedding = jnp.zeros((views, P_OUT), f32)
    for block in range(parts):
        embedding = embedding + dot_cols(proj_act[:, block * P_OUT : (block + 1) * P_OUT], weight_five(block))

    images = views // 2
    order = jnp.broadcast_to(ins.order[...], (images, views))
    image_row = lax.broadcasted_iota(jnp.int32, (images, views), 0)
    selectors = [(order == 2 * image_row + which).astype(f32) for which in range(2)]
    embeds = [exact_dot(selector, embedding) for selector in selectors]
    moments = [exact_rows(embed, embed) for embed in embeds]
    packed, diagonal = pack_pair(*moments)
    packed, extra = sum_matrix(0, packed, [diagonal] + [column_sums(embed) for embed in embeds])
    moments = unpack_pair(packed, extra[0])
    eye = (
        lax.broadcasted_iota(jnp.int32, (P_OUT, P_OUT), 0) == lax.broadcasted_iota(jnp.int32, (P_OUT, P_OUT), 1)
    ).astype(f32)
    centred, covariances = [], []
    for which in range(2):
        mean = extra[1 + which] / image_total
        centred.append(embeds[which] - mean)
        covariances.append(moments[which] / image_total - exact_rows(mean, mean) + ridge_term * eye)
    inverses = inverse_factors(covariances)
    whitened = [exact_cols(centred[which], inverses[which]) for which in range(2)]
    scalings = [
        lax.rsqrt(jnp.mean(white * white, axis=1, keepdims=True) + norm_epsilon) for white in whitened
    ]
    units = [white * scaling for white, scaling in zip(whitened, scalings)]
    difference = units[0] - units[1]
    objective_row = column_sums(difference * difference) * (1.0 / P_OUT)
    unit_grads = [difference * (2.0 / P_OUT), difference * (-2.0 / P_OUT)]
    white_grads = []
    for which in range(2):
        inner = jnp.mean(whitened[which] * unit_grads[which], axis=1, keepdims=True)
        white_grads.append(
            scalings[which] * unit_grads[which] - whitened[which] * (scalings[which] ** 3 * inner)
        )
    directs = [exact_dot(white_grads[which], inverses[which]) for which in range(2)]
    products = [exact_rows(white_grads[which], whitened[which]) for which in range(2)]
    packed, diagonal = pack_pair(*products)
    packed, extra = sum_matrix(
        1, packed, [diagonal] + [column_sums(grad) for grad in white_grads] + [objective_row]
    )
    products = unpack_pair(packed, extra[0])
    embed_grad = jnp.zeros((views, P_OUT), f32)
    for which in range(2):
        symmetric = exact_rows(inverses[which], exact_dot(products[which], inverses[which]))
        mean_grad = exact_dot(extra[1 + which], inverses[which])
        grad = directs[which] - (exact_dot(centred[which], symmetric) + mean_grad) / image_total
        embed_grad = embed_grad + exact_rows(selectors[which], grad)
    objective_row = extra[3]
    embed_low = embed_grad.astype(bf16)

    proj_act, proj_hidden = mem.proj_act[...], mem.proj_hidden[...]
    act_grad = jnp.concatenate([dot(embed_low, weight_five(block)) for block in range(parts)], axis=1)
    upstream = act_grad * mem.proj_slope[...]
    plain = column_sums(upstream)
    sum_four_back = Sum(5)
    sum_four_back.start(plain, xhat_sum(3, plain, column_sums(upstream * proj_hidden)))
    for block in range(parts):
        weights[4][block // plan.x, block % plan.x] = dot_rows(
            embed_low, proj_act[:, block * P_OUT : (block + 1) * P_OUT]
        ).astype(bf16)
    sum_four_back.middle()
    grad_coefs(3, sum_four_back.finish(), view_total)
    four_low = (
        upstream * coef[0:1, :P_HID] - coef[1:2, :P_HID] - proj_hidden * coef[2:3, :P_HID]
    ).astype(bf16)
    pool_grad = dot_cols(four_low, whole(3)) * (1.0 / PIX)
    plain = column_sums(pool_grad * pool_slope[...])
    sum_three_back = Sum(6)
    sum_three_back.start(plain, xhat_sum(2, plain, column_sums(pool_grad * pool_bend[...])))
    grad_four = dot_rows(mem.pooled[...], four_low).astype(bf16)
    weights[3][...] = grad_four.reshape(weights[3].shape)
    sum_three_back.middle()
    hook(23)
    grad_coefs(2, sum_three_back.finish(), row_total)
    pool[...] = pool_grad * coef[0:1, :]
    pool_slope[...] = pool_grad

    clear_sums()

    @pl.loop(0, pieces)
    def _(index):
        stage.copy(slope_hbm, index, True).wait()
        stage.next_load(slope_hbm, index)

        @pl.loop(0, C_MID // LANES)
        def _(part):
            inner = pl.ds(pl.multiple_of(part * LANES, LANES), LANES)
            cols = piece_columns(index, part)
            spread, shift_row, bend_row = pool[:, cols], coef[1:2, cols], coef[2:3, cols]
            for pixel in range(SIDE):
                hidden_at = hidden_rows(index, pixel, views)
                hidden = hidden_three[hidden_at, inner].astype(f32)
                slope = stage_ref[stage.rows(index, pixel, views), inner].astype(f32)
                hidden_three[hidden_at, inner] = (slope * spread - shift_row - hidden * bend_row).astype(bf16)

        hook_in(11, index, pieces)

    @pl.loop(0, 3)
    def _(index):
        at = long_rows(0, index)
        left = jnp.concatenate([hidden_three[long_rows(block, index), :] for block in range(BLOCKS)], axis=1)
        right = jnp.concatenate([weight_three(block) for block in range(BLOCKS)], axis=1)
        upstream = dot_cols(left, right) * slope_two[at, :].astype(f32)
        slope_two[at, :] = upstream.astype(bf16)
        count_in(slice(0, C_MID), upstream, hidden_two[at, :].astype(f32))
        hook_in(12, index, 3)

    sums = row_sums[0:1, :C_MID], row_sums[1:2, :C_MID]
    sum_two_back = Sum(7)
    sum_two_back.start(sums[0], xhat_sum(1, *sums))

    @pl.loop(0, BLOCKS)
    def _(block):
        three = hidden_three[pl.ds(pl.multiple_of(block * rows, 16), rows), :]
        grad = dot_rows(act_two[...], three)
        weights[2][block] = grad.astype(bf16).reshape(plan.z, plan.x, -1, C_MID)

        @pl.when(block == 1)
        def _():
            sum_two_back.middle()

        hook_in(13, block, BLOCKS)

    clear_sums()
    grad_coefs(1, sum_two_back.finish(), row_total)

    def apply_grad(hidden_ref, grad_ref, put, site):
        @pl.loop(0, PIX)
        def _(pixel):
            place = pl.ds(pl.multiple_of(pixel * views, 16), views)
            for block in range(C_MID // LANES):
                cols = slice(block * LANES, (block + 1) * LANES)
                grad = (
                    grad_ref[place, cols].astype(f32) * coef[0:1, cols]
                    - coef[1:2, cols]
                    - hidden_ref[place, cols].astype(f32) * coef[2:3, cols]
                )
                put(pixel, cols, grad.astype(bf16))
            hook_in(site, pixel, SIDE, SIDE - 1, SIDE)

    apply_grad(hidden_two, slope_two, put_padded(padded_two), 14)
    column_places = [
        hidden_three.at[pl.ds(2 * rows, rows)],
        hidden_three.at[pl.ds(3 * rows, rows)],
        hidden_two,
        slope_two,
    ]
    column_loads = [feature_copy(block, column_places[block]) for block in range(BLOCKS)]
    for copy in column_loads:
        copy.start()
    def tap_grad(tap):
        down, across = tap // 3, tap % 3
        left = padded_one[pl.ds(down, SIDE), pl.ds(pl.multiple_of(across * views, 16), chunk), :]
        right = padded_two[1 : SIDE + 1, views : views + chunk, :]
        grad = dot_rows(left.reshape(rows, C_MID), right.reshape(rows, C_MID))
        stage_ref[pl.ds(pl.multiple_of(tap * C_MID, 16), C_MID), :] = grad.astype(bf16)

    @pl.loop(0, 7)
    def _(tap):
        tap_grad(tap)
        hook_in(15, tap, 7)

    def second_back(first, count):
        flat = weights[1][...].reshape(9 * C_MID, C_MID)
        right = jnp.concatenate([flat[tap * C_MID : (tap + 1) * C_MID, :] for tap in range(9)], axis=1)
        at = image_rows(first, count)
        upstream = dot_cols(patch(padded_two, first, count, True), right) * slope_one[at, :].astype(f32)
        slope_one[at, :] = upstream.astype(bf16)
        count_in(slice(0, C_MID), upstream, hidden_one[at, :].astype(f32))

    @pl.loop(0, 3)
    def _(index):
        second_back(2 * index, 2)
        hook_in(16, index, 3)

    second_back(6, 1)
    hook(16, 3)
    sums = row_sums[0:1, :C_MID], row_sums[1:2, :C_MID]
    sum_one_back = Sum(8)
    sum_one_back.start(sums[0], xhat_sum(0, *sums))

    @pl.loop(7, 9)
    def _(tap):
        tap_grad(tap)

        @pl.when(tap == 7)
        def _():
            sum_one_back.middle()

        hook_in(17, tap, 2, 7)

    grad_coefs(0, sum_one_back.finish(), row_total)

    def put_one(pixel, cols, value):
        act_two[pl.ds(pl.multiple_of(pixel * views, 16), views), cols] = value

    apply_grad(hidden_one, slope_one, put_one, 18)

    def block_grad(block):
        column_loads[block].wait()
        grad = dot_rows(column_places[block][...], act_two[...])
        mem.g1[block] = grad.astype(bf16).reshape(plan.x, -1, C_MID)

    tail = Ring(hidden_three, 2 * rows)
    for block in range(BLOCKS):
        block_grad(block)
        hook(19, block)
        if block == 1:
            tail.first_loads(slope_hbm)

    sum_last = Sum(9)

    @pl.loop(0, pieces)
    def _(index):
        block = index // CHUNKS
        weight = weights[0][block].reshape(C_MID, C_MID)
        back = dot_cols(act_two[span(lax.rem(index, CHUNKS)), :], weight)
        tail.copy(slope_hbm, index, True).wait()
        cols = pl.ds(pl.multiple_of(block * C_MID, LANES), C_MID)
        for pixel in range(SIDE):
            at = tail.rows(index, pixel, views)
            summed = hidden_three[at, :].astype(f32) * pool_slope[:, cols]
            hidden_three[at, :] = (summed + back[pixel * views : (pixel + 1) * views]).astype(bf16)
        tail.save(outs.features_grad, index)
        tail.next_load(slope_hbm, index)
        hook_in(20, index, pieces)
        if plan.inside:

            @pl.when(index == LAST_SUM)
            def _():
                sum_last.start(mem.squares[...], mem.squares[...])

            @pl.when(index == LAST_SUM + 3)
            def _():
                sum_last.middle()

    tail.last_saves(outs.features_grad)
    squares = mem.squares[...]
    if plan.inside:
        squares = sum_last.finish()[0:1]
    norm_grads = mem.norm_grads[...]
    scalars = outs.scalars
    norm_squares = column_sums(norm_grads * norm_grads)
    for place in range(norm_squares.shape[1] // LANES):
        squares = squares + norm_squares[:, place * LANES : (place + 1) * LANES]
    scalars[...] = jnp.zeros_like(scalars)
    squares = jnp.sum(squares, axis=1, keepdims=True)
    norm = jnp.sqrt(squares)
    found = (jnp.sum(objective_row, axis=1, keepdims=True) / image_total, squares, norm, clip_factor(norm))
    for place, value in enumerate(found):
        scalars[place : place + 1, :] = jnp.broadcast_to(value, (1, LANES))
    if plan.inside:
        owner = (dp_me * plan.fsdp + fsdp_me) * LANES
        outs.norm_grad[...] = mem.norm_grads[:, pl.ds(pl.multiple_of(owner, LANES), LANES)]
    else:
        outs.norm_grad[...] = norm_grads
    if not plan.inside:
        stores = [
            pltpu.make_async_copy(gradients[which], outs.grads[which], mem.bulk_send.at[which])
            for which in range(5)
        ]
        for store in stores:
            store.start()
        for store in stores:
            store.wait()


def weight_shapes():
    return (
        (4, 2, 256, C_MID),
        (4, 2, 576, C_MID),
        (BLOCKS, 4, 2, 64, C_MID),
        (4, 2, 256, P_HID),
        (4, 2, P_OUT, P_OUT),
    )


def run_kernel(plan, features, order, shards, norm):
    rows, views = plan.rows, plan.views
    in_vmem = pl.BlockSpec(memory_space=pltpu.VMEM)
    anywhere = pl.BlockSpec(memory_space=pl.ANY)
    shapes = weight_shapes()
    operands = [features, order, norm, *shards]
    in_specs = [anywhere, in_vmem, in_vmem] + [in_vmem if plan.inside else anywhere] * 5
    results = [
        ((rows, C_IN), bf16, anywhere),
        ((rows, C_IN), bf16, anywhere),
        (norm.shape, f32, in_vmem),
        ((8, LANES), f32, in_vmem),
    ]
    for which, shard in enumerate(shards):
        if plan.inside:
            results.append((shard.shape, f32, in_vmem))
        else:
            results.append(((9 * C_MID, C_MID) if which == 1 else shapes[which], bf16, anywhere))
    dma = pltpu.SemaphoreType.DMA

    def sum_room(width):
        return SumRoom(
            pltpu.VMEM((plan.dp, 2, width), f32),
            pltpu.VMEM((plan.fsdp, 2, width), f32),
            dma((plan.dp,)),
            dma((plan.dp,)),
            dma((plan.fsdp,)),
            dma((plan.fsdp,)),
        )

    def matrix_room():
        size = plan.embed_rows
        return MatrixRoom(
            pltpu.VMEM((plan.dp, size, P_OUT), f32),
            pltpu.VMEM((plan.dp, size, P_OUT), f32),
            pltpu.VMEM((plan.fsdp, size, P_OUT), f32),
            pltpu.VMEM((plan.dp, size, P_OUT), f32),
            dma((plan.dp,)),
            dma((plan.dp,)),
            dma((plan.fsdp,)),
            dma((plan.fsdp,)),
            dma((plan.dp,)),
            dma((plan.dp,)),
        )

    scratch = Mem(
        w=[pltpu.VMEM(shape, bf16) for shape in shapes],
        g1=pltpu.VMEM(shapes[0], bf16),
        row_sums=pltpu.VMEM((2, C_IN), f32),
        r3=pltpu.VMEM(shapes[2], bf16),
        r4=pltpu.VMEM(shapes[3], bf16),
        r5=pltpu.VMEM(shapes[4], bf16),
        stage=pltpu.VMEM((max(SLOTS * plan.chunk, 9 * C_MID), C_MID), bf16),
        stage_sem=dma((2, SLOTS)),
        column_sem=dma((BLOCKS,)),
        h1=pltpu.VMEM((rows, C_MID), bf16),
        d1=pltpu.VMEM((rows, C_MID), bf16),
        h2=pltpu.VMEM((rows, C_MID), bf16),
        d2=pltpu.VMEM((rows, C_MID), bf16),
        a2=pltpu.VMEM((rows, C_MID), bf16),
        h3=pltpu.VMEM((BLOCKS * rows, C_MID), bf16),
        pad1=pltpu.VMEM((SIDE + 2, (SIDE + 2) * views, C_MID), bf16),
        pad2=pltpu.VMEM((SIDE + 2, (SIDE + 2) * views, C_MID), bf16),
        pool=pltpu.VMEM((views, C_IN), f32),
        pool_slope=pltpu.VMEM((views, C_IN), f32),
        pool_bend=pltpu.VMEM((views, C_IN), f32),
        pooled=pltpu.VMEM((views, C_IN), bf16),
        proj_act=pltpu.VMEM((views, P_HID), bf16),
        proj_slope=pltpu.VMEM((views, P_HID), f32),
        proj_hidden=pltpu.VMEM((views, P_HID), f32),
        coef=pltpu.VMEM((8, C_IN), f32),
        stats=pltpu.VMEM((2, norm_width()), f32),
        norm=pltpu.VMEM((2, norm_width()), f32),
        norm_grads=pltpu.VMEM((2, norm_width()), f32),
        norm_tiles=pltpu.VMEM((plan.dp, plan.fsdp, 2, LANES), f32),
        norm_s0=dma((plan.dp,)),
        norm_r0=dma((plan.dp,)),
        norm_s1=dma((plan.fsdp,)),
        norm_r1=dma((plan.fsdp,)),
        bulk_send=dma((300,)),
        bulk_recv=dma((300,)),
        mats=[matrix_room(), matrix_room()],
        sums=[
            sum_room(width)
            for width in (C_MID, C_MID, C_IN // 2, C_IN // 2, P_HID, C_IN, LANES)
        ],
        squares=pltpu.VMEM((1, LANES), f32),
    )
    values = pl.pallas_call(
        lambda *refs: kernel(plan, *refs),
        out_shape=[jax.ShapeDtypeStruct(shape, kind) for shape, kind, _ in results],
        in_specs=in_specs,
        out_specs=[spec for _, _, spec in results],
        scratch_shapes=[scratch],
        compiler_params=pltpu.CompilerParams(
            collective_id=1, has_side_effects=True, vmem_limit_bytes=63 * 2**20
        ),
        name="train_step",
    )(*operands)
    return Outs(*values[:4], values[4:])


def norm_width():
    return 2 * C_MID + C_IN + P_HID


def clip_factor(norm):
    return clip_level / jnp.maximum(norm, clip_level)


def adam_update(weight, moment_one, moment_two, gradient, step_rate, weight_decay):
    first_new = beta_first * moment_one + (1.0 - beta_first) * gradient
    second_new = beta_second * moment_two + (1.0 - beta_second) * gradient * gradient
    first_hat = first_new / (1.0 - beta_first**STEP)
    second_hat = second_new / (1.0 - beta_second**STEP)
    weight_new = weight - step_rate * (
        first_hat / (jnp.sqrt(second_hat) + adam_epsilon) + weight_decay * weight
    )
    return (weight_new, first_new, second_new)


def finish_kernel(rates, decays, *refs):
    count = len(rates)
    low, scalars = refs[0], refs[1]
    given, results = refs[2 : 2 + 4 * count], refs[2 + 4 * count :]
    results[0][...] = low[...].astype(f32)

    @pl.when(pl.program_id(0) == 0)
    def _():
        results[1][0, 0] = scalars[0, 0]
        results[2][0, 0] = scalars[2, 0]
        scale = scalars[3, 0]
        for place in range(count):
            weight, first, second, grad = (given[part * count + place][...] for part in range(4))
            updated = adam_update(weight, first, second, grad * scale, rates[place], decays[place])
            for part in range(3):
                results[3 + part * count + place][...] = updated[part]


def finish(features_grad, scalars, masters, firsts, seconds, grads, rates, decays):
    rows = features_grad.shape[0]
    arrays = [*masters, *firsts, *seconds, *grads]

    def fixed(shape):
        return pl.BlockSpec(shape, lambda index: (0, 0))

    steps = 2 * CHUNKS
    moving = pl.BlockSpec((rows // steps, C_IN), lambda index: (index, 0))
    single = pl.BlockSpec(memory_space=pltpu.SMEM)
    outputs = [*masters] * 3
    values = pl.pallas_call(
        lambda *refs: finish_kernel(rates, decays, *refs),
        grid=(steps,),
        in_specs=[moving, single] + [fixed(array.shape) for array in arrays],
        out_specs=[moving, single, single] + [fixed(array.shape) for array in outputs],
        out_shape=[jax.ShapeDtypeStruct((rows, C_IN), f32)]
        + [jax.ShapeDtypeStruct((1, 1), f32)] * 2
        + [jax.ShapeDtypeStruct(array.shape, f32) for array in outputs],
        compiler_params=pltpu.CompilerParams(vmem_limit_bytes=62 * 2**20),
        name="finish",
    )(features_grad, scalars, *arrays)
    count = len(masters)
    groups = [values[3 + part * count : 3 + (part + 1) * count] for part in range(3)]
    return values[0], values[1].reshape(()), values[2].reshape(()), *groups


def gather_full(weight):
    outer = lax.all_gather(weight.astype(bf16), FSDP, axis=0, tiled=True)
    return lax.all_gather(outer, DP, axis=1, tiled=True)


def scatter_full(gradient):
    inner = lax.psum_scatter(gradient.astype(f32), DP, scatter_dimension=1, tiled=True)
    return lax.psum_scatter(inner, FSDP, scatter_dimension=0, tiled=True)


def body(features, view_order, *state):
    masters, firsts, seconds = state[:6], state[6:12], state[12:18]
    dp_size, fsdp_size = lax.axis_size(DP), lax.axis_size(FSDP)
    views = features.shape[0]
    inside = dp_size == 4 and fsdp_size == 8
    plan = Plan(dp_size, fsdp_size, views, inside)
    pixels = jnp.swapaxes(features, 0, 1).reshape(-1, C_IN)
    norm_params = masters[5]
    shapes = weight_shapes()
    if inside:
        shards = list(masters[:4]) + [masters[4].T]
        norm = norm_params
    else:
        full = [gather_full(weight) for weight in masters[:5]]
        shards = [
            full[0].reshape(shapes[0]),
            full[1].reshape(shapes[1]),
            full[2].reshape(C_MID, BLOCKS, C_MID).swapaxes(0, 1).reshape(shapes[2]),
            full[3].reshape(shapes[3]),
            full[4].reshape(4, 2, P_OUT, P_OUT).swapaxes(2, 3),
        ]
        norm = lax.all_gather(norm_params.astype(bf16), (DP, FSDP), axis=1, tiled=True).astype(f32)
    got = run_kernel(plan, pixels, view_order, shards, norm)
    grads = list(got.grads)
    scalars = got.scalars
    turned = [list(group) for group in (masters, firsts, seconds)]
    if inside:
        owned = grads
        for group in turned:
            group[4] = group[4].T
    else:
        whole_grads = [
            grads[0].reshape(C_IN, C_MID),
            grads[1],
            grads[2].reshape(BLOCKS, C_MID, C_MID).swapaxes(0, 1).reshape(C_MID, C_IN),
            grads[3].reshape(C_IN, P_HID),
            grads[4].swapaxes(2, 3).reshape(P_HID, P_OUT),
        ]
        owned = [scatter_full(gradient) for gradient in whole_grads]
        squares = scalars[1, 0] + lax.psum(sum(jnp.sum(grad * grad) for grad in owned), (DP, FSDP))
        norm_value = jnp.sqrt(squares)
        scalars = scalars.at[2].set(norm_value).at[3].set(clip_factor(norm_value))
    width = norm_params.shape[1]
    if inside:
        owned.append(got.norm_grad)
    else:
        owner = lax.axis_index((DP, FSDP))
        owned.append(lax.dynamic_slice_in_dim(got.norm_grad, owner * width, width, 1))
    step_rates = (
        C_IN ** (-0.5),
        (9 * C_MID) ** (-0.5),
        C_MID ** (-0.5),
        C_IN ** (-0.5),
        P_HID ** (-0.5),
        norm_rate,
    )
    decays = (decay_rate, decay_rate, decay_rate, decay_rate, decay_rate, 0.0)
    input_grad, loss, grad_norm, *updates = finish(
        got.features_grad, scalars, *turned, owned, step_rates, decays
    )
    if inside:
        updates = [[*group[:4], group[4].T, group[5]] for group in updates]
    return (
        loss,
        jnp.swapaxes(input_grad.reshape(PIX, views, C_IN), 0, 1),
        grad_norm,
        *updates[0],
        *updates[1],
        *updates[2],
    )


def solution(mesh):
    views = P((DP, FSDP), None, None)
    split = P(FSDP, DP)
    norm = P(None, (DP, FSDP))
    params = (split,) * 5 + (norm,)
    return jax.shard_map(
        body,
        mesh=mesh,
        in_specs=(views, P((DP, FSDP), None)) + params * 3,
        out_specs=(P(), views, P()) + params * 3,
        check_vma=False,
    )
```

```python
from typing import Any, NamedTuple

import jax
import jax.numpy as jnp
from jax import lax
from jax.experimental import pallas as pl
from jax.experimental.pallas import tpu as pltpu
from jax.sharding import PartitionSpec as P

C_IN = 2048
C_MID = 512
P_HID = 1024
P_OUT = 128
SIDE = 7
STEP = 10
PIX = 49
LANES = 128
BLOCKS = C_IN // C_MID
CHUNKS = SIDE
SLOTS = 6
LAST_SUM = 23
COPIES = 360


highest = lax.Precision.HIGHEST
bf16 = jnp.bfloat16
f32 = jnp.float32
norm_epsilon = 1e-05
ridge_term = 0.01
clip_level = 0.1
beta_first = 0.9
beta_second = 0.999
adam_epsilon = 1e-08
decay_rate = 0.05
norm_rate = 0.5
bell_scale = 0.3989422804014327
root_half = 0.5**0.5
bell_rate = -0.7213475204444817
DP, FSDP = "dp", "fsdp"


def gelu_pair(values):
    below = 0.5 + 0.5 * lax.erf(values * root_half)
    bell = jnp.exp2(values * values * bell_rate)
    return values * below, below + values * bell * bell_scale


def dot(left, right):
    return jnp.dot(left, right, preferred_element_type=f32)


def dot_cols(left, right):
    return lax.dot_general(left, right, (((1,), (1,)), ((), ())), preferred_element_type=f32)


def dot_rows(left, right):
    return lax.dot_general(left, right, (((0,), (0,)), ((), ())), preferred_element_type=f32)


def exact_cols(left, right):
    return lax.dot_general(
        left, right, (((1,), (1,)), ((), ())), precision=highest, preferred_element_type=f32
    )


def exact_rows(left, right):
    return lax.dot_general(
        left, right, (((0,), (0,)), ((), ())), precision=highest, preferred_element_type=f32
    )


def exact_dot(left, right):
    return jnp.dot(left, right, precision=highest, preferred_element_type=f32)


def inverse_factors(matrices):
    row_top = lax.broadcasted_iota(jnp.int32, (8, P_OUT), 0)
    row_all = lax.broadcasted_iota(jnp.int32, (P_OUT, P_OUT), 0)
    col_all = lax.broadcasted_iota(jnp.int32, (P_OUT, P_OUT), 1)

    def one_step(place, left, right):
        scale = lax.rsqrt(left[place : place + 1, place : place + 1])
        left_row = left[place : place + 1, :] * scale
        right_row = right[place : place + 1, :] * scale
        column = left[:, place : place + 1] * scale
        left = left - column * left_row
        right = right - column * right_row
        here = row_top == place
        left = jnp.concatenate([jnp.where(here, 0.0, left[:8]), left[8:]], axis=0)
        right = jnp.concatenate(
            [jnp.where(here, jnp.broadcast_to(right_row, (8, P_OUT)), right[:8]), right[8:]], axis=0
        )
        return left, right

    def panel(_, pairs):
        pairs = list(pairs)
        for place in range(8):
            for which in range(len(pairs)):
                pairs[which] = one_step(place, *pairs[which])
        return tuple(
            (
                pltpu.roll(jnp.concatenate([left[8:], left[:8]], axis=0), P_OUT - 8, 1),
                jnp.concatenate([right[8:], right[:8]], axis=0),
            )
            for left, right in pairs
        )

    pairs = tuple((matrix, (row_all == col_all).astype(f32)) for matrix in matrices)
    done = [[] for _ in matrices]
    size = P_OUT // 4
    for _ in range(4):
        pairs = lax.fori_loop(0, size // 8, panel, pairs)
        for found, (_, right) in zip(done, pairs):
            found.append(right[-size:])
        pairs = tuple((left[:-size], right[:-size]) for left, right in pairs)
    return [jnp.concatenate(found, axis=0) for found in done]


def pack_pair(first, second):
    row = lax.broadcasted_iota(jnp.int32, (P_OUT, P_OUT), 0)
    col = lax.broadcasted_iota(jnp.int32, (P_OUT, P_OUT), 1)
    packed = jnp.where(row >= col, first, second.T)
    diagonal = jnp.sum(jnp.where(row == col, second, 0.0), axis=0, keepdims=True)
    return packed, diagonal


def unpack_pair(packed, diagonal):
    row = lax.broadcasted_iota(jnp.int32, (P_OUT, P_OUT), 0)
    col = lax.broadcasted_iota(jnp.int32, (P_OUT, P_OUT), 1)
    turned = packed.T
    first = jnp.where(row >= col, packed, turned)
    second = jnp.where(row < col, packed, jnp.where(row == col, diagonal, turned))
    return first, second


GATHER_AT = {
    (0, 1): 1,
    (0, 3): 1,
    (1, 0): 1,
    (2, 0): 1,
    (4, 0): 5,
    (5, 0): 1,
    (5, 1): 1,
    (5, 2): 1,
    (5, 4): 1,
    (5, 5): 1,
    (5, 6): 1,
    (7, 0): 1,
    (8, 6): 1,
    (9, 2): 1,
    (9, 5): 1,
    (9, 8): 1,
    (21, 0): 7,
}
REDUCE_AT = {
    (11, 3): ((4, 0, 1), (3, 0, 1)),
    (11, 11): ((3, 1, 1), (4, 0, 2)),
    (11, 20): ((3, 0, 2), (3, 2, 1)),
    (12, 0): ((3, 1, 2), (3, 0, 3), (4, 0, 3)),
    (12, 1): ((3, 3, 1),),
    (12, 2): ((3, 2, 2), (3, 1, 3)),
    (13, 0): ((3, 3, 2),),
    (13, 2): ((3, 2, 3),),
    (13, 3): ((3, 3, 3), (2, 0, 0), (2, 1, 0), (2, 2, 0), (2, 3, 0)),
    (14, 6): ((4, 9, 4), (2, 0, 1), (2, 1, 1)),
    (15, 2): ((1, 0, 0), (2, 0, 2), (2, 2, 1), (2, 3, 1)),
    (15, 4): ((1, 1, 0), (1, 0, 1), (2, 1, 2), (2, 0, 3)),
    (15, 6): ((1, 2, 0), (2, 2, 2), (2, 3, 2), (1, 1, 1), (2, 1, 3), (3, 9, 4)),
    (16, 0): ((1, 0, 2), (1, 2, 1), (2, 2, 3), (2, 3, 3)),
    (16, 1): ((1, 1, 2), (2, 9, 4), (1, 0, 3)),
    (16, 2): ((1, 2, 2), (1, 1, 3)),
    (17, 1): ((1, 3, 0), (1, 2, 3)),
    (18, 6): ((1, 3, 1),),
    (19, 0): ((0, 0, 0), (1, 3, 2)),
    (19, 1): ((0, 1, 0), (0, 0, 1), (1, 3, 3)),
    (19, 2): ((0, 2, 0), (0, 1, 1), (0, 0, 2)),
    (19, 3): ((0, 3, 0), (0, 2, 1), (0, 1, 2), (0, 0, 3), (1, 9, 4)),
    (20, 2): ((0, 3, 1), (0, 2, 2), (0, 1, 3)),
    (20, 8): ((0, 3, 2), (0, 2, 3)),
    (20, 13): ((0, 3, 3),),
    (20, 20): ((0, 9, 4),),
    (23, 0): ((4, 0, 0), (3, 0, 0), (3, 1, 0), (3, 2, 0), (3, 3, 0)),
}


class Ins(NamedTuple):
    features: Any
    order: Any
    norm: Any
    shards: Any


class Outs(NamedTuple):
    slope: Any
    features_grad: Any
    norm_grad: Any
    scalars: Any
    grads: Any


class SumRoom(NamedTuple):
    dp: Any
    fsdp: Any
    s0: Any
    r0: Any
    s1: Any
    r1: Any


class MatrixRoom(NamedTuple):
    pack: Any
    dp: Any
    fsdp: Any
    all: Any
    s0: Any
    r0: Any
    s1: Any
    r1: Any
    s2: Any
    r2: Any


class Mem(NamedTuple):
    w: Any
    g1: Any
    row_sums: Any
    r3: Any
    r4: Any
    r5: Any
    stage: Any
    stage_sem: Any
    column_sem: Any
    h1: Any
    d1: Any
    h2: Any
    d2: Any
    a2: Any
    h3: Any
    pad1: Any
    pad2: Any
    pool: Any
    pool_slope: Any
    pool_bend: Any
    pooled: Any
    proj_act: Any
    proj_slope: Any
    proj_hidden: Any
    coef: Any
    stats: Any
    norm: Any
    norm_grads: Any
    norm_tiles: Any
    norm_s0: Any
    norm_r0: Any
    norm_s1: Any
    norm_r1: Any
    bulk_send: Any
    bulk_recv: Any
    mats: Any
    sums: Any
    squares: Any


class Plan:
    def __init__(self, dp_size, fsdp_size, views, inside):
        self.dp = dp_size
        self.fsdp = fsdp_size
        self.devices = dp_size * fsdp_size
        self.views = views
        self.rows = views * PIX
        self.chunk = views * SIDE
        self.inside = inside
        self.z = 4
        self.x = 2
        self.half = (128, 288, 32, 128, 16)
        self.width = (128, 128, 512, 256, 128)
        piece = P_OUT + 8
        self.embed_rows = -(-piece // (8 * dp_size)) * 8


def kernel(plan, *refs):
    ins, outs, mem = Ins(*refs[:3], refs[3:8]), Outs(*refs[8:12], refs[12:17]), refs[17]
    views, chunk, rows = plan.views, plan.chunk, plan.rows
    row_total = float(rows * plan.devices)
    view_total = float(views * plan.devices)
    image_total = float(views * plan.devices // 2)
    dp_me, fsdp_me = lax.axis_index(DP), lax.axis_index(FSDP)
    y_me, c_me = dp_me // 2, dp_me % 2
    z_me, x_me = fsdp_me // 2, fsdp_me % 2
    y_other, c_other, x_other = 1 - y_me, 1 - c_me, 1 - x_me

    barrier = pltpu.get_barrier_semaphore()

    @pl.loop(1, plan.dp)
    def _(step):
        pl.semaphore_signal(
            barrier, 1, device_id={DP: lax.rem(dp_me + step, plan.dp)}, device_id_type=pl.DeviceIdType.MESH
        )

    @pl.loop(1, plan.fsdp)
    def _(step):
        pl.semaphore_signal(
            barrier, 1, device_id={FSDP: lax.rem(fsdp_me + step, plan.fsdp)}, device_id_type=pl.DeviceIdType.MESH
        )

    pl.semaphore_wait(barrier, plan.dp + plan.fsdp - 2)

    def share(axis, size, me, source_of, slots, send, recv):
        def outgoing(step):
            partner = lax.rem(me + step, size)
            return pltpu.make_async_remote_copy(
                src_ref=source_of(partner),
                dst_ref=slots.at[me],
                send_sem=send.at[step],
                recv_sem=recv.at[me],
                device_id={axis: partner},
                device_id_type=pl.DeviceIdType.MESH,
            )

        def incoming(step):
            source = lax.rem(me + step, size)
            return pltpu.make_async_remote_copy(
                src_ref=slots.at[source],
                dst_ref=slots.at[source],
                send_sem=send.at[step],
                recv_sem=recv.at[source],
                device_id={axis: source},
                device_id_type=pl.DeviceIdType.MESH,
            )

        def start():
            pl.loop(1, size)(lambda step: outgoing(step).start())

        def wait():
            pl.loop(1, size)(lambda step: incoming(step).wait_recv())
            pl.loop(1, size)(lambda step: outgoing(step).wait_send())

        return start, wait

    def add_slots(slots, size):
        total = slots[0]
        for place in range(1, size):
            total = total + slots[place]
        return total

    class Sum:
        def __init__(self, which):
            part = mem.sums[(0, 1, 2, 3, 4, 4, 5, 0, 1, 6)[which]]
            self.dp_slots, self.fsdp_slots = part.dp, part.fsdp
            self.dp_copy = share(
                DP, plan.dp, dp_me, lambda _: self.dp_slots.at[dp_me], self.dp_slots, part.s0, part.r0
            )
            self.fsdp_copy = share(
                FSDP, plan.fsdp, fsdp_me, lambda _: self.fsdp_slots.at[fsdp_me], self.fsdp_slots, part.s1, part.r1
            )

        def start(self, *values):
            for place, value in enumerate(values):
                self.dp_slots[dp_me, place : place + 1, :] = value
            self.dp_copy[0]()

        def middle(self):
            self.dp_copy[1]()
            self.fsdp_slots[fsdp_me] = add_slots(self.dp_slots, plan.dp)
            self.fsdp_copy[0]()

        def finish(self):
            self.fsdp_copy[1]()
            return add_slots(self.fsdp_slots, plan.fsdp)

        def all(self, *values):
            self.start(*values)
            self.middle()
            return self.finish()

    def sum_matrix(which, matrix, extra):
        part = mem.mats[which]
        size = plan.embed_rows
        pack = part.pack
        flat = jnp.concatenate(
            [matrix] + extra + [jnp.zeros((size * plan.dp - P_OUT - len(extra), P_OUT), f32)], axis=0
        )
        for place in range(plan.dp):
            pack[place] = flat[place * size : (place + 1) * size]
        start, wait = share(DP, plan.dp, dp_me, lambda to: pack.at[to], part.dp, part.s0, part.r0)
        start()
        part.dp[dp_me] = pack[dp_me]
        wait()
        part.fsdp[fsdp_me] = add_slots(part.dp, plan.dp)
        start, wait = share(
            FSDP, plan.fsdp, fsdp_me, lambda _: part.fsdp.at[fsdp_me], part.fsdp, part.s1, part.r1
        )
        start()
        wait()
        part.all[dp_me] = add_slots(part.fsdp, plan.fsdp)
        start, wait = share(
            DP, plan.dp, dp_me, lambda _: part.all.at[dp_me], part.all, part.s2, part.r2
        )
        start()
        wait()
        total = jnp.concatenate([part.all[place] for place in range(plan.dp)], axis=0)
        return total[:P_OUT], [total[P_OUT + place : P_OUT + place + 1] for place in range(len(extra))]

    weights = mem.w
    everything = slice(None)

    def row_span(which, half):
        if isinstance(half, tuple):
            return half
        size = plan.half[which]
        if half is None:
            return 0, 2 * size
        return half * size, size

    def column_span(which, dp_index):
        width = plan.width[which]
        return pl.ds(pl.multiple_of(dp_index * width, width), width)

    def places(which, z_index, x_index, dp_index, half, flat=True):
        start, size = row_span(which, half)
        if which == 1 and flat:
            z_list = range(plan.z) if z_index is None else [z_index]
            x_list = range(plan.x) if x_index is None else [x_index]
            return [
                (
                    pl.ds(pl.multiple_of((z_one * plan.x + x_one) * 576 + start, 16), size),
                    column_span(which, dp_index),
                )
                for z_one in z_list
                for x_one in x_list
            ]
        z_one = everything if z_index is None else z_index
        x_one = everything if x_index is None else x_index
        if which == 2:
            return [(dp_index, z_one, x_one, pl.ds(start, size), everything)]
        if which == 4:
            return [(z_one, x_one, pl.ds(pl.multiple_of(dp_index * 32 + start, 16), size), everything)]
        return [(z_one, x_one, pl.ds(start, size), column_span(which, dp_index))]

    recv_parts = {
        1: lambda index: mem.h3.at[index],
        0: lambda index: mem.r4.at[index],
        2: lambda index: mem.r3.at[index],
        3: lambda index: mem.r4.at[index],
        4: lambda index: mem.r5.at[index],
    }

    counter = [0]

    class Batch:
        def __init__(self, sources, targets, landings, axis, partner):
            base = counter[0]
            counter[0] += len(sources)
            send, recv = mem.bulk_send, mem.bulk_recv
            self.out = [
                pltpu.make_async_remote_copy(
                    src_ref=source,
                    dst_ref=target,
                    send_sem=send.at[base + place],
                    recv_sem=recv.at[base + place],
                    device_id={axis: partner},
                    device_id_type=pl.DeviceIdType.MESH,
                )
                for place, (source, target) in enumerate(zip(sources, targets))
            ]
            self.come = [
                pltpu.make_async_remote_copy(
                    src_ref=landing,
                    dst_ref=landing,
                    send_sem=send.at[base + place],
                    recv_sem=recv.at[base + place],
                    device_id={axis: partner},
                    device_id_type=pl.DeviceIdType.MESH,
                )
                for place, landing in enumerate(landings)
            ]

        def start(self):
            for copy in self.out:
                copy.start()

        def arrive(self):
            for copy in self.come:
                copy.wait_recv()

        def leave(self):
            for copy in self.out:
                copy.wait_send()

    class LineBatch:
        def __init__(self, source_of, target_of, landing_of):
            base = counter[0]
            counter[0] += plan.z
            send, recv = mem.bulk_send, mem.bulk_recv
            self.out, self.come = [], []
            for step in range(1, plan.z):
                z_to = (z_me + step) % plan.z
                self.out.append(
                    pltpu.make_async_remote_copy(
                        src_ref=source_of(z_to),
                        dst_ref=target_of(z_to),
                        send_sem=send.at[base + step],
                        recv_sem=recv.at[base + z_me],
                        device_id={FSDP: z_to * plan.x + x_me},
                        device_id_type=pl.DeviceIdType.MESH,
                    )
                )
                self.come.append(
                    pltpu.make_async_remote_copy(
                        src_ref=landing_of(z_to),
                        dst_ref=landing_of(z_to),
                        send_sem=send.at[base + step],
                        recv_sem=recv.at[base + z_to],
                        device_id={FSDP: z_to * plan.x + x_me},
                        device_id_type=pl.DeviceIdType.MESH,
                    )
                )

        start, arrive, leave = Batch.start, Batch.arrive, Batch.leave

    def pick(ref, indexes):
        return [ref.at[index] for index in indexes]

    def own_dp(y_index, c_index):
        return y_index * 2 + c_index

    x_partner = z_me * plan.x + x_other
    y_partner = own_dp(y_other, c_me)
    c_partner = own_dp(y_me, c_other)
    dp_far = own_dp(y_other, c_other)

    class Gather:
        def __init__(self, which, start, size):
            ref = weights[which]
            self.which, self.rows = which, (start, size)
            both, low, high = (start, size), (start, size // 2), (start + size // 2, size // 2)

            def at(z_index, *index):
                found = [slice(0, 2), slice(2, 4)] if z_index is None else [z_index]
                return [one for z_one in found for one in pick(ref, places(which, z_one, *index, False))]

            own = at(z_me, x_me, dp_me, both)[0]
            self.line = LineBatch(
                lambda _: own, lambda _: own, lambda z_from: at(z_from, x_me, dp_me, both)[0]
            )
            sent, come = at(None, x_me, dp_me, low), at(None, x_other, dp_me, low)
            x_first = Batch(sent, sent, come, FSDP, x_partner)
            sent, come = at(None, x_me, dp_me, high), at(None, x_me, y_partner, high)
            y_first = Batch(sent, sent, come, DP, y_partner)
            sent, come = at(None, None, dp_me, low), at(None, None, y_partner, low)
            y_second = Batch(sent, sent, come, DP, y_partner)
            sent = at(None, x_me, dp_me, high) + at(None, x_me, y_partner, high)
            come = at(None, x_other, dp_me, high) + at(None, x_other, y_partner, high)
            x_second = Batch(sent, sent, come, FSDP, x_partner)
            sent = at(None, None, dp_me, both) + at(None, None, y_partner, both)
            come = at(None, None, c_partner, both) + at(None, None, dp_far, both)
            core = Batch(sent, sent, come, DP, c_partner)
            self.stages = ((self.line,), (x_first, y_first), (y_second, x_second), (core,))

        def put_own(self):
            index = places(self.which, z_me, x_me, dp_me, self.rows, False)[0]
            shard = ins.shards[self.which][self.rows[0] : self.rows[0] + self.rows[1], :]
            weights[self.which][index] = shard.astype(bf16)

        def start(self, stage):
            for batch in self.stages[stage]:
                batch.start()

        def arrive(self, stage):
            for batch in self.stages[stage]:
                batch.arrive()

        def leave(self):
            for stage in self.stages:
                for batch in stage:
                    batch.leave()

    class Piece:
        def __init__(self, which, ref, room, z_index):
            def at(*index):
                return pick(ref, places(which, z_index, *index))

            def land(*index):
                return [room(index_one) for index_one in places(which, z_index, *index)]

            self.z = z_index
            self.core = Batch(
                at(None, c_partner, None) + at(None, dp_far, None),
                land(None, c_partner, None) + land(None, dp_far, None),
                land(None, dp_me, None) + land(None, y_partner, None),
                DP,
                c_partner,
            )
            self.y_first = Batch(
                at(None, y_partner, 0), land(None, dp_far, 0), land(None, c_partner, 0), DP, y_partner
            )
            self.x_first = Batch(
                at(x_other, dp_me, 1) + at(x_other, y_partner, 1),
                land(x_other, c_partner, 1) + land(x_other, dp_far, 1),
                land(x_me, c_partner, 1) + land(x_me, dp_far, 1),
                FSDP,
                x_partner,
            )
            self.x_second = Batch(
                at(x_other, dp_me, 0), land(x_other, dp_far, 0), land(x_me, dp_far, 0), FSDP, x_partner
            )
            self.y_second = Batch(
                at(x_me, y_partner, 1), land(x_other, dp_far, 1), land(x_other, c_partner, 1), DP, y_partner
            )

    class Reduce:
        def __init__(self, which, ref, cut):
            self.which, self.ref, self.room = which, ref, recv_parts[which]
            self.pieces = [
                Piece(which, ref, self.room, z_index) for z_index in (range(plan.z) if cut else [None])
            ]
            self.base = counter[0]
            counter[0] += plan.z

        def line_copy(self, z_to):
            return pltpu.make_async_remote_copy(
                src_ref=self.ref.at[places(self.which, z_to, x_me, dp_me, None)[0]],
                dst_ref=self.room(places(self.which, z_me, x_other, dp_far, None)[0]),
                send_sem=mem.bulk_send.at[self.base + z_to],
                recv_sem=mem.bulk_recv.at[self.base + z_me],
                device_id={FSDP: z_to * plan.x + x_me},
                device_id_type=pl.DeviceIdType.MESH,
            )

        def line_room(self, z_from):
            return self.room(places(self.which, z_from, x_other, dp_far, None)[0])

        def add(self, z_index, pairs):
            def one(z_one):
                for here, there in pairs:
                    for x_step in range(plan.x) if here[0] is None else [None]:
                        x_here = x_step if here[0] is None else here[0]
                        x_there = x_step if there[0] is None else there[0]
                        index = places(self.which, z_one, x_here, *here[1:])[0]
                        other = places(self.which, z_one, x_there, *there[1:])[0]
                        total = self.ref[index].astype(f32) + self.room(other)[...].astype(f32)
                        self.ref[index] = total.astype(bf16)

            if z_index is None:
                pl.loop(0, plan.z)(one)
            else:
                one(z_index)

        def core_start(self, place=0):
            if plan.inside:
                self.pieces[place].core.start()

        def core_add(self, place=0):
            if plan.inside:
                piece = self.pieces[place]
                piece.core.arrive()
                self.add(piece.z, [((None, dp_me, None),) * 2, ((None, y_partner, None),) * 2])
                piece.y_first.start()
                piece.x_first.start()

        def first_add(self, place=0):
            if plan.inside:
                piece = self.pieces[place]
                piece.y_first.arrive()
                self.add(piece.z, [((None, dp_me, 0), (None, c_partner, 0))])
                piece.x_second.start()
                piece.x_first.arrive()
                self.add(
                    piece.z, [((x_me, dp_me, 1), (x_me, c_partner, 1)), ((x_me, y_partner, 1), (x_me, dp_far, 1))]
                )
                piece.y_second.start()

        def second_add(self, place=0):
            if plan.inside:
                piece = self.pieces[place]
                piece.x_second.arrive()
                piece.y_second.arrive()
                self.add(
                    piece.z, [((x_me, dp_me, 0), (x_me, dp_far, 0)), ((x_me, dp_me, 1), (x_other, c_partner, 1))]
                )
                if piece.z is None:
                    for step in range(1, plan.z):
                        self.line_copy((z_me + step) % plan.z).start()
                else:

                    @pl.when(z_me != piece.z)
                    def _():
                        self.line_copy(piece.z).start()

        def finish(self):
            if not plan.inside:
                return
            total = self.ref[places(self.which, z_me, x_me, dp_me, None)[0]].astype(f32)
            for step in range(1, plan.z):
                z_from = (z_me + step) % plan.z
                room = self.line_room(z_from)
                pltpu.make_async_remote_copy(
                    src_ref=room,
                    dst_ref=room,
                    send_sem=mem.bulk_send.at[self.base + z_from],
                    recv_sem=mem.bulk_recv.at[self.base + z_from],
                    device_id={FSDP: z_from * plan.x + x_me},
                    device_id_type=pl.DeviceIdType.MESH,
                ).wait_recv()
                total = total + room[...].astype(f32)
            outs.grads[self.which][...] = total
            squares = jnp.sum(total * total, axis=0, keepdims=True)
            folded = squares[:, :LANES]
            for place in range(1, squares.shape[1] // LANES):
                folded = folded + squares[:, place * LANES : (place + 1) * LANES]
            mem.squares[...] += folded
            for step in range(1, plan.z):
                self.line_copy((z_me + step) % plan.z).wait_send()
            for piece in self.pieces:
                for batch in (piece.core, piece.y_first, piece.x_first, piece.x_second, piece.y_second):
                    batch.leave()

    gathers, steps = [], []
    if plan.inside:
        for which, cuts in enumerate((2, 3, 1, 2, 1)):
            size = 2 * plan.half[which] // cuts
            gathers += [Gather(which, cut * size, size) for cut in range(cuts)]

    def line_step(place):
        gathers[place].arrive(0)
        gathers[place].start(1)
        if place + 1 < len(gathers):
            gathers[place + 1].start(0)

    def first_step(place):
        gathers[place].arrive(1)
        gathers[place].start(2)

    def second_step(place):
        gathers[place].arrive(2)
        gathers[place].start(3)

    for place in range(len(gathers)):
        steps.append((line_step, place))
        if place > 0:
            steps.append((second_step, place - 1))
        steps.append((first_step, place))
    if plan.inside:
        steps.append((second_step, len(gathers) - 1))

    def take(count):
        taken, steps[:] = steps[:count], steps[count:]
        return [lambda one=one: one[0](one[1]) for one in taken]

    def moves(site, item):
        found = take(GATHER_AT.get((site, item), 0)) if plan.inside else []
        for which, piece, kind in REDUCE_AT.get((site, item), ()):
            one = reduces[which]
            found.append(
                one.finish
                if kind == 4
                else lambda one=one, kind=kind, piece=piece: (
                    one.core_start,
                    one.core_add,
                    one.first_add,
                    one.second_add,
                )[kind](piece)
            )
        return found

    def hook(site, item=0):
        for move in moves(site, item):
            move()

    def hook_in(site, index, count, first=0, stride=1):
        for item in range(count):
            found = moves(site, item)
            if found and plan.inside:

                @pl.when(index == first + item * stride)
                def _(found=found):
                    for move in found:
                        move()

    def cores_arrive(which):
        for one in gathers:
            if one.which == which:
                one.arrive(3)

    gradients = [mem.g1, mem.stage.at[pl.ds(0, 9 * C_MID)], weights[2], weights[3], weights[4]]
    reduces = [Reduce(which, gradients[which], which < 4) for which in range(5)]
    assert counter[0] <= COPIES
    mem.squares[...] = jnp.zeros((1, LANES), f32)

    if plan.inside:
        gathers[0].put_own()
        gathers[0].start(0)
        for one in gathers[1:]:
            one.put_own()
        tiles = mem.norm_tiles
        tiles[dp_me, fsdp_me] = ins.norm[...].astype(bf16).astype(f32)
        norm_dp = share(
            DP, plan.dp, dp_me, lambda _: tiles.at[dp_me, fsdp_me], tiles.at[:, fsdp_me], mem.norm_s0, mem.norm_r0
        )
        norm_dp[0]()
    else:
        loads = [
            pltpu.make_async_copy(ins.shards[which], weights[which], mem.bulk_send.at[which])
            for which in range(5)
        ]
        for load in loads:
            load.start()

    pieces = BLOCKS * CHUNKS

    def hidden_rows(index, pixel=0, count=chunk):
        return pl.ds(pl.multiple_of(index * chunk + pixel * views, 16), count)

    class Ring:
        def __init__(self, ref, start):
            self.ref, self.base = ref, start

        def rows(self, index, pixel=0, count=chunk):
            return pl.ds(
                pl.multiple_of(self.base + lax.rem(index, SLOTS) * chunk + pixel * views, 16), count
            )

        def copy(self, array, index, into):
            block, place = index // CHUNKS, lax.rem(index, CHUNKS)
            outer = array.at[
                pl.ds(pl.multiple_of(place * chunk, 16), chunk),
                pl.ds(pl.multiple_of(block * C_MID, LANES), C_MID),
            ]
            inner = self.ref.at[self.rows(index)]
            source, target = (outer, inner) if into else (inner, outer)
            return pltpu.make_async_copy(
                source, target, mem.stage_sem.at[0 if into else 1, lax.rem(index, SLOTS)]
            )

        def first_loads(self, array):
            for index in range(3):
                self.copy(array, index, True).start()

        def next_load(self, array, index):
            @pl.when(index + 3 < pieces)
            def _():
                self.copy(array, index + 3, True).start()

        def save(self, array, index):
            self.copy(array, index, False).start()

            @pl.when(index >= 2)
            def _():
                self.copy(array, index - 2, False).wait()

        def last_saves(self, array):
            for index in (pieces - 2, pieces - 1):
                self.copy(array, index, False).wait()

    stage_ref = mem.stage
    stage = Ring(stage_ref, 0)

    def piece_columns(index, part):
        return pl.ds(pl.multiple_of(index // CHUNKS * C_MID + part * LANES, LANES), LANES)

    features, slope_hbm = ins.features, outs.slope
    hidden_three = mem.h3

    def feature_copy(block, target):
        return pltpu.make_async_copy(
            features.at[:, pl.ds(block * C_MID, C_MID)], target, mem.column_sem.at[block]
        )

    feature_loads = [
        feature_copy(block, hidden_three.at[pl.ds(block * rows, rows)]) for block in range(BLOCKS)
    ]
    for copy in feature_loads:
        copy.start()
    stage.first_loads(features)

    padded_one, padded_two = mem.pad1, mem.pad2
    for padded in (padded_one, padded_two):
        for edge in (0, SIDE + 1):
            padded[edge] = jnp.zeros((padded.shape[1], C_MID), bf16)
        for edge in (0, SIDE + 1):
            padded[:, pl.ds(edge * views, views), :] = jnp.zeros((SIDE + 2, views, C_MID), bf16)

    if plan.inside:
        norm_dp[1]()
        norm_out = []
        norm_in = []
        for step in range(1, plan.fsdp):
            partner = (fsdp_me + step) % plan.fsdp
            norm_out.append(
                pltpu.make_async_remote_copy(
                    src_ref=tiles.at[:, fsdp_me],
                    dst_ref=tiles.at[:, fsdp_me],
                    send_sem=mem.norm_s1.at[step],
                    recv_sem=mem.norm_r1.at[fsdp_me],
                    device_id={FSDP: partner},
                    device_id_type=pl.DeviceIdType.MESH,
                )
            )
            norm_in.append(
                pltpu.make_async_remote_copy(
                    src_ref=tiles.at[:, partner],
                    dst_ref=tiles.at[:, partner],
                    send_sem=mem.norm_s1.at[step],
                    recv_sem=mem.norm_r1.at[partner],
                    device_id={FSDP: partner},
                    device_id_type=pl.DeviceIdType.MESH,
                )
            )
        for copy in norm_out:
            copy.start()
        hook(21)
        for copy in norm_in:
            copy.wait_recv()
        for copy in norm_out:
            copy.wait_send()
        norm_all = mem.norm
        for dp_one in range(plan.dp):
            for fsdp_one in range(plan.fsdp):
                start = (dp_one * plan.fsdp + fsdp_one) * LANES
                norm_all[:, start : start + LANES] = tiles[dp_one, fsdp_one]
    else:
        for copy in loads:
            copy.wait()
        norm_all = mem.norm
        norm_all[...] = ins.norm[...]

    starts = (0, C_MID, 2 * C_MID, 2 * C_MID + C_IN, 2 * C_MID + C_IN + P_HID)

    def gain(layer):
        return norm_all[0:1, starts[layer] : starts[layer + 1]]

    coef, stats = mem.coef, mem.stats

    def norm_coefs(layer, totals, count, low=0):
        width = totals.shape[1]
        here, there = slice(low, low + width), slice(starts[layer] + low, starts[layer] + low + width)
        mean = totals[0:1] / count
        scaling = lax.rsqrt(totals[1:2] / count - mean * mean + norm_epsilon)
        slope = scaling * norm_all[0:1, there]
        stats[0:1, there] = mean
        stats[1:2, there] = scaling
        coef[0:1, here] = slope
        coef[1:2, here] = norm_all[1:2, there] - mean * slope

    def grad_coefs(layer, totals, count):
        width = starts[layer + 1] - starts[layer]
        mean = stats[0:1, starts[layer] : starts[layer + 1]]
        scaling = stats[1:2, starts[layer] : starts[layer + 1]]
        mem.norm_grads[0:1, starts[layer] : starts[layer + 1]] = totals[1:2]
        mem.norm_grads[1:2, starts[layer] : starts[layer + 1]] = totals[0:1]
        slope = scaling * gain(layer)
        bend = slope * scaling * totals[1:2] / count
        coef[0:1, :width] = slope
        coef[1:2, :width] = slope * totals[0:1] / count - mean * bend
        coef[2:3, :width] = bend

    def xhat_sum(layer, plain, product):
        mean = stats[0:1, starts[layer] : starts[layer + 1]]
        scaling = stats[1:2, starts[layer] : starts[layer + 1]]
        return scaling * (product - mean * plain)

    zero_row = jnp.zeros((1, C_MID), f32)

    def column_sums(value):
        return jnp.sum(value, axis=0, keepdims=True)

    def whole(which):
        value = weights[which][...]
        return value.reshape(-1, value.shape[-1])

    row_sums = mem.row_sums

    def clear_sums():
        row_sums[...] = jnp.zeros_like(row_sums)

    def count_in(cols, value, other):
        row_sums[0:1, cols] += column_sums(value)
        row_sums[1:2, cols] += column_sums(value * other)

    def own_columns(side):
        core = (c_me + side) % 2
        return [
            pl.ds(pl.multiple_of(half * (C_MID // 2) + core * LANES, LANES), LANES) for half in range(2)
        ]

    hidden_one, slope_one = mem.h1, mem.d1
    hidden_two, slope_two = mem.h2, mem.d2
    act_two = mem.a2
    long = rows // 3

    def span(index):
        return pl.ds(pl.multiple_of(index * chunk, 16), chunk)

    def long_rows(block, index):
        return pl.ds(pl.multiple_of(block * rows + index * long, 16), long)

    def put_sides(ref, at, sides, hidden):
        for place, cols in enumerate(sides):
            part = hidden[:, place * LANES : (place + 1) * LANES]
            ref[at, cols] = part.astype(bf16)
            count_in(cols, part, part)

    for copy in feature_loads:
        copy.wait()
    clear_sums()

    @pl.loop(0, 2)
    def _(side):
        sides = own_columns(side)

        @pl.loop(0, 3)
        def _(index):
            left = jnp.concatenate([hidden_three[long_rows(block, index), :] for block in range(BLOCKS)], axis=1)
            right = jnp.concatenate([weights[0][:, :, :, cols].reshape(C_IN, LANES) for cols in sides], axis=1)
            put_sides(hidden_one, long_rows(0, index), sides, dot(left, right))

            hook_in(0, side * 3 + index, 6)

        @pl.when(side == 0)
        def _():
            cores_arrive(0)

    sum_one = Sum(0)
    sum_one.start(row_sums[0:1, :C_MID], row_sums[1:2, :C_MID])
    hook(1)
    sum_one.middle()
    hook(2)
    clear_sums()
    norm_coefs(0, sum_one.finish(), row_total)

    def activate(hidden_ref, slope_ref, put, site):
        @pl.loop(0, PIX)
        def _(pixel):
            place = pl.ds(pl.multiple_of(pixel * views, 16), views)
            for block in range(C_MID // LANES):
                cols = slice(block * LANES, (block + 1) * LANES)
                out = hidden_ref[place, cols].astype(f32) * coef[0:1, cols] + coef[1:2, cols]
                value, slope = gelu_pair(out)
                slope_ref[place, cols] = slope.astype(bf16)
                put(pixel, cols, value.astype(bf16))
            hook_in(site, pixel, SIDE, SIDE - 1, SIDE)

    def put_padded(padded):
        def put(pixel, cols, value):
            padded[pixel // SIDE + 1, pl.ds(pl.multiple_of((pixel % SIDE + 1) * views, 16), views), cols] = value

        return put

    activate(hidden_one, slope_one, put_padded(padded_one), 3)
    hook(4)

    def patch(padded, first, count, flip):
        found = []
        for vertical in range(3):
            for lateral in range(3):
                down, across = (2 - vertical, 2 - lateral) if flip else (vertical, lateral)
                piece = padded[pl.ds(first + down, count), across * views : across * views + chunk, :]
                found.append(piece.reshape(count * chunk, C_MID))
        return jnp.concatenate(found, axis=1)

    def image_rows(first, count):
        return pl.ds(pl.multiple_of(first * chunk, 16), count * chunk)

    def second_part(sides, first, count):
        right = jnp.concatenate([weights[1][:, :, :, cols].reshape(9 * C_MID, LANES) for cols in sides], axis=1)
        hidden = dot(patch(padded_one, first, count, False), right)
        put_sides(hidden_two, image_rows(first, count), sides, hidden)

    @pl.loop(0, 2)
    def _(side):
        sides = own_columns(side)

        @pl.loop(0, 3)
        def _(index):
            second_part(sides, 2 * index, 2)
            hook_in(5, side * 4 + index, 8)

        second_part(sides, 6, 1)

        @pl.when(side == 0)
        def _():
            cores_arrive(1)

    sum_two = Sum(1)
    sum_two.start(row_sums[0:1, :C_MID], row_sums[1:2, :C_MID])
    hook(6)
    sum_two.middle()
    hook(7)
    clear_sums()
    norm_coefs(1, sum_two.finish(), row_total)

    def put_rows(pixel, cols, value):
        act_two[pl.ds(pl.multiple_of(pixel * views, 16), views), cols] = value

    activate(hidden_two, slope_two, put_rows, 8)
    cores_arrive(2)

    def weight_three(block):
        return weights[2][block].reshape(C_MID, C_MID)

    sums_low, sums_high = Sum(2), Sum(3)
    half_width = C_IN // 2

    @pl.loop(0, BLOCKS)
    def _(block):
        cols = pl.ds(pl.multiple_of(block * C_MID, LANES), C_MID)

        @pl.loop(0, 3)
        def _(index):
            hidden = dot(act_two[long_rows(0, index), :], weight_three(block))
            hidden_three[long_rows(block, index), :] = hidden.astype(bf16)
            count_in(cols, hidden, hidden)
            hook_in(9, block * 3 + index, 12)

        @pl.when(block == 1)
        def _():
            sums_low.start(row_sums[0:1, :half_width], row_sums[1:2, :half_width])

        @pl.when(block == 2)
        def _():
            sums_low.middle()

    sums_high.start(row_sums[0:1, half_width:], row_sums[1:2, half_width:])
    norm_coefs(2, sums_low.finish(), row_total)

    hook(22)

    pool, pool_slope, pool_bend = mem.pool, mem.pool_slope, mem.pool_bend
    for ref in (pool, pool_slope, pool_bend):
        ref[...] = jnp.zeros_like(ref)

    @pl.loop(0, pieces)
    def _(index):
        stage.copy(features, index, True).wait()

        @pl.loop(0, C_MID // LANES)
        def _(part):
            inner = pl.ds(pl.multiple_of(part * LANES, LANES), LANES)
            cols = piece_columns(index, part)
            slope_row, shift_row = coef[0:1, cols], coef[1:2, cols]
            kept = (pool[:, cols], pool_slope[:, cols], pool_bend[:, cols])
            for pixel in range(SIDE):
                stage_at, hidden_at = stage.rows(index, pixel, views), hidden_rows(index, pixel, views)
                hidden = hidden_three[hidden_at, inner].astype(f32)
                total = hidden * slope_row + shift_row + stage_ref[stage_at, inner].astype(f32)
                value, slope = gelu_pair(total)
                stage_ref[stage_at, inner] = slope.astype(bf16)
                kept = (kept[0] + value, kept[1] + slope, kept[2] + slope * hidden)
            pool[:, cols], pool_slope[:, cols], pool_bend[:, cols] = kept

        stage.save(slope_hbm, index)
        stage.next_load(features, index)

        @pl.when(index == 2)
        def _():
            sums_high.middle()

        @pl.when(index == pieces // 2 - 1)
        def _():
            norm_coefs(2, sums_high.finish(), row_total, half_width)

        hook_in(10, index, pieces)

    stage.last_saves(slope_hbm)
    cores_arrive(3)
    cores_arrive(4)
    for one in gathers:
        one.leave()

    pooled = (pool[...] * (1.0 / PIX)).astype(bf16)
    mem.pooled[...] = pooled
    proj_hidden = dot(pooled, whole(3))
    sum_four = Sum(4)
    totals = sum_four.all(column_sums(proj_hidden), column_sums(proj_hidden * proj_hidden))
    stage.first_loads(slope_hbm)
    norm_coefs(3, totals, view_total)
    value, slope = gelu_pair(proj_hidden * coef[0:1, :P_HID] + coef[1:2, :P_HID])
    proj_act = value.astype(bf16)
    mem.proj_act[...] = proj_act
    mem.proj_slope[...] = slope
    mem.proj_hidden[...] = proj_hidden

    def weight_five(block):
        return weights[4][block // plan.x, block % plan.x]

    parts = P_HID // P_OUT
    embedding = jnp.zeros((views, P_OUT), f32)
    for block in range(parts):
        embedding = embedding + dot_cols(proj_act[:, block * P_OUT : (block + 1) * P_OUT], weight_five(block))

    images = views // 2
    order = jnp.broadcast_to(ins.order[...], (images, views))
    image_row = lax.broadcasted_iota(jnp.int32, (images, views), 0)
    selectors = [(order == 2 * image_row + which).astype(f32) for which in range(2)]
    embeds = [exact_dot(selector, embedding) for selector in selectors]
    moments = [exact_rows(embed, embed) for embed in embeds]
    packed, diagonal = pack_pair(*moments)
    packed, extra = sum_matrix(0, packed, [diagonal] + [column_sums(embed) for embed in embeds])
    moments = unpack_pair(packed, extra[0])
    eye = (
        lax.broadcasted_iota(jnp.int32, (P_OUT, P_OUT), 0) == lax.broadcasted_iota(jnp.int32, (P_OUT, P_OUT), 1)
    ).astype(f32)
    centred, covariances = [], []
    for which in range(2):
        mean = extra[1 + which] / image_total
        centred.append(embeds[which] - mean)
        covariances.append(moments[which] / image_total - exact_rows(mean, mean) + ridge_term * eye)
    inverses = inverse_factors(covariances)
    whitened = [exact_cols(centred[which], inverses[which]) for which in range(2)]
    scalings = [
        lax.rsqrt(jnp.mean(white * white, axis=1, keepdims=True) + norm_epsilon) for white in whitened
    ]
    units = [white * scaling for white, scaling in zip(whitened, scalings)]
    difference = units[0] - units[1]
    objective_row = column_sums(difference * difference) * (1.0 / P_OUT)
    unit_grads = [difference * (2.0 / P_OUT), difference * (-2.0 / P_OUT)]
    white_grads = []
    for which in range(2):
        inner = jnp.mean(whitened[which] * unit_grads[which], axis=1, keepdims=True)
        white_grads.append(
            scalings[which] * unit_grads[which] - whitened[which] * (scalings[which] ** 3 * inner)
        )
    directs = [exact_dot(white_grads[which], inverses[which]) for which in range(2)]
    products = [exact_rows(white_grads[which], whitened[which]) for which in range(2)]
    packed, diagonal = pack_pair(*products)
    packed, extra = sum_matrix(
        1, packed, [diagonal] + [column_sums(grad) for grad in white_grads] + [objective_row]
    )
    products = unpack_pair(packed, extra[0])
    embed_grad = jnp.zeros((views, P_OUT), f32)
    for which in range(2):
        symmetric = exact_rows(inverses[which], exact_dot(products[which], inverses[which]))
        mean_grad = exact_dot(extra[1 + which], inverses[which])
        grad = directs[which] - (exact_dot(centred[which], symmetric) + mean_grad) / image_total
        embed_grad = embed_grad + exact_rows(selectors[which], grad)
    objective_row = extra[3]
    embed_low = embed_grad.astype(bf16)

    proj_act, proj_hidden = mem.proj_act[...], mem.proj_hidden[...]
    act_grad = jnp.concatenate([dot(embed_low, weight_five(block)) for block in range(parts)], axis=1)
    upstream = act_grad * mem.proj_slope[...]
    plain = column_sums(upstream)
    sum_four_back = Sum(5)
    sum_four_back.start(plain, xhat_sum(3, plain, column_sums(upstream * proj_hidden)))
    for block in range(parts):
        weights[4][block // plan.x, block % plan.x] = dot_rows(
            embed_low, proj_act[:, block * P_OUT : (block + 1) * P_OUT]
        ).astype(bf16)
    sum_four_back.middle()
    grad_coefs(3, sum_four_back.finish(), view_total)
    four_low = (
        upstream * coef[0:1, :P_HID] - coef[1:2, :P_HID] - proj_hidden * coef[2:3, :P_HID]
    ).astype(bf16)
    pool_grad = dot_cols(four_low, whole(3)) * (1.0 / PIX)
    plain = column_sums(pool_grad * pool_slope[...])
    sum_three_back = Sum(6)
    sum_three_back.start(plain, xhat_sum(2, plain, column_sums(pool_grad * pool_bend[...])))
    grad_four = dot_rows(mem.pooled[...], four_low).astype(bf16)
    weights[3][...] = grad_four.reshape(weights[3].shape)
    sum_three_back.middle()
    hook(23)
    grad_coefs(2, sum_three_back.finish(), row_total)
    pool[...] = pool_grad * coef[0:1, :]
    pool_slope[...] = pool_grad

    clear_sums()

    @pl.loop(0, pieces)
    def _(index):
        stage.copy(slope_hbm, index, True).wait()
        stage.next_load(slope_hbm, index)

        @pl.loop(0, C_MID // LANES)
        def _(part):
            inner = pl.ds(pl.multiple_of(part * LANES, LANES), LANES)
            cols = piece_columns(index, part)
            spread, shift_row, bend_row = pool[:, cols], coef[1:2, cols], coef[2:3, cols]
            for pixel in range(SIDE):
                hidden_at = hidden_rows(index, pixel, views)
                hidden = hidden_three[hidden_at, inner].astype(f32)
                slope = stage_ref[stage.rows(index, pixel, views), inner].astype(f32)
                hidden_three[hidden_at, inner] = (slope * spread - shift_row - hidden * bend_row).astype(bf16)

        hook_in(11, index, pieces)

    @pl.loop(0, 3)
    def _(index):
        at = long_rows(0, index)
        left = jnp.concatenate([hidden_three[long_rows(block, index), :] for block in range(BLOCKS)], axis=1)
        right = jnp.concatenate([weight_three(block) for block in range(BLOCKS)], axis=1)
        upstream = dot_cols(left, right) * slope_two[at, :].astype(f32)
        slope_two[at, :] = upstream.astype(bf16)
        count_in(slice(0, C_MID), upstream, hidden_two[at, :].astype(f32))
        hook_in(12, index, 3)

    sums = row_sums[0:1, :C_MID], row_sums[1:2, :C_MID]
    sum_two_back = Sum(7)
    sum_two_back.start(sums[0], xhat_sum(1, *sums))

    @pl.loop(0, BLOCKS)
    def _(block):
        three = hidden_three[pl.ds(pl.multiple_of(block * rows, 16), rows), :]
        grad = dot_rows(act_two[...], three)
        weights[2][block] = grad.astype(bf16).reshape(plan.z, plan.x, -1, C_MID)

        @pl.when(block == 1)
        def _():
            sum_two_back.middle()

        hook_in(13, block, BLOCKS)

    clear_sums()
    grad_coefs(1, sum_two_back.finish(), row_total)

    def apply_grad(hidden_ref, grad_ref, put, site):
        @pl.loop(0, PIX)
        def _(pixel):
            place = pl.ds(pl.multiple_of(pixel * views, 16), views)
            for block in range(C_MID // LANES):
                cols = slice(block * LANES, (block + 1) * LANES)
                grad = (
                    grad_ref[place, cols].astype(f32) * coef[0:1, cols]
                    - coef[1:2, cols]
                    - hidden_ref[place, cols].astype(f32) * coef[2:3, cols]
                )
                put(pixel, cols, grad.astype(bf16))
            hook_in(site, pixel, SIDE, SIDE - 1, SIDE)

    apply_grad(hidden_two, slope_two, put_padded(padded_two), 14)
    column_places = [
        hidden_three.at[pl.ds(2 * rows, rows)],
        hidden_three.at[pl.ds(3 * rows, rows)],
        hidden_two,
        slope_two,
    ]
    column_loads = [feature_copy(block, column_places[block]) for block in range(BLOCKS)]
    for copy in column_loads:
        copy.start()
    def tap_grad(tap):
        down, across = tap // 3, tap % 3
        left = padded_one[pl.ds(down, SIDE), pl.ds(pl.multiple_of(across * views, 16), chunk), :]
        right = padded_two[1 : SIDE + 1, views : views + chunk, :]
        grad = dot_rows(left.reshape(rows, C_MID), right.reshape(rows, C_MID))
        stage_ref[pl.ds(pl.multiple_of(tap * C_MID, 16), C_MID), :] = grad.astype(bf16)

    @pl.loop(0, 7)
    def _(tap):
        tap_grad(tap)
        hook_in(15, tap, 7)

    def second_back(first, count):
        flat = weights[1][...].reshape(9 * C_MID, C_MID)
        right = jnp.concatenate([flat[tap * C_MID : (tap + 1) * C_MID, :] for tap in range(9)], axis=1)
        at = image_rows(first, count)
        upstream = dot_cols(patch(padded_two, first, count, True), right) * slope_one[at, :].astype(f32)
        slope_one[at, :] = upstream.astype(bf16)
        count_in(slice(0, C_MID), upstream, hidden_one[at, :].astype(f32))

    @pl.loop(0, 3)
    def _(index):
        second_back(2 * index, 2)
        hook_in(16, index, 3)

    second_back(6, 1)
    hook(16, 3)
    sums = row_sums[0:1, :C_MID], row_sums[1:2, :C_MID]
    sum_one_back = Sum(8)
    sum_one_back.start(sums[0], xhat_sum(0, *sums))

    @pl.loop(7, 9)
    def _(tap):
        tap_grad(tap)

        @pl.when(tap == 7)
        def _():
            sum_one_back.middle()

        hook_in(17, tap, 2, 7)

    grad_coefs(0, sum_one_back.finish(), row_total)

    def put_one(pixel, cols, value):
        act_two[pl.ds(pl.multiple_of(pixel * views, 16), views), cols] = value

    apply_grad(hidden_one, slope_one, put_one, 18)

    def block_grad(block):
        column_loads[block].wait()
        grad = dot_rows(column_places[block][...], act_two[...])
        mem.g1[block] = grad.astype(bf16).reshape(plan.x, -1, C_MID)

    tail = Ring(hidden_three, 2 * rows)
    for block in range(BLOCKS):
        block_grad(block)
        hook(19, block)
        if block == 1:
            tail.first_loads(slope_hbm)

    sum_last = Sum(9)

    @pl.loop(0, pieces)
    def _(index):
        block = index // CHUNKS
        weight = weights[0][block].reshape(C_MID, C_MID)
        back = dot_cols(act_two[span(lax.rem(index, CHUNKS)), :], weight)
        tail.copy(slope_hbm, index, True).wait()
        cols = pl.ds(pl.multiple_of(block * C_MID, LANES), C_MID)
        for pixel in range(SIDE):
            at = tail.rows(index, pixel, views)
            summed = hidden_three[at, :].astype(f32) * pool_slope[:, cols]
            hidden_three[at, :] = (summed + back[pixel * views : (pixel + 1) * views]).astype(bf16)
        tail.save(outs.features_grad, index)
        tail.next_load(slope_hbm, index)
        hook_in(20, index, pieces)
        if plan.inside:

            @pl.when(index == LAST_SUM)
            def _():
                sum_last.start(mem.squares[...], mem.squares[...])

            @pl.when(index == LAST_SUM + 3)
            def _():
                sum_last.middle()

    tail.last_saves(outs.features_grad)
    squares = mem.squares[...]
    if plan.inside:
        squares = sum_last.finish()[0:1]
    norm_grads = mem.norm_grads[...]
    scalars = outs.scalars
    norm_squares = column_sums(norm_grads * norm_grads)
    for place in range(norm_squares.shape[1] // LANES):
        squares = squares + norm_squares[:, place * LANES : (place + 1) * LANES]
    scalars[...] = jnp.zeros_like(scalars)
    squares = jnp.sum(squares, axis=1, keepdims=True)
    norm = jnp.sqrt(squares)
    found = (jnp.sum(objective_row, axis=1, keepdims=True) / image_total, squares, norm, clip_factor(norm))
    for place, value in enumerate(found):
        scalars[place : place + 1, :] = jnp.broadcast_to(value, (1, LANES))
    if plan.inside:
        owner = (dp_me * plan.fsdp + fsdp_me) * LANES
        outs.norm_grad[...] = mem.norm_grads[:, pl.ds(pl.multiple_of(owner, LANES), LANES)]
    else:
        outs.norm_grad[...] = norm_grads
    if not plan.inside:
        stores = [
            pltpu.make_async_copy(gradients[which], outs.grads[which], mem.bulk_send.at[which])
            for which in range(5)
        ]
        for store in stores:
            store.start()
        for store in stores:
            store.wait()


def weight_shapes():
    return (
        (4, 2, 256, C_MID),
        (4, 2, 576, C_MID),
        (BLOCKS, 4, 2, 64, C_MID),
        (4, 2, 256, P_HID),
        (4, 2, P_OUT, P_OUT),
    )


def run_kernel(plan, features, order, shards, norm):
    rows, views = plan.rows, plan.views
    in_vmem = pl.BlockSpec(memory_space=pltpu.VMEM)
    anywhere = pl.BlockSpec(memory_space=pl.ANY)
    shapes = weight_shapes()
    operands = [features, order, norm, *shards]
    in_specs = [anywhere, in_vmem, in_vmem] + [in_vmem if plan.inside else anywhere] * 5
    results = [
        ((rows, C_IN), bf16, anywhere),
        ((rows, C_IN), bf16, anywhere),
        (norm.shape, f32, in_vmem),
        ((8, LANES), f32, in_vmem),
    ]
    for which, shard in enumerate(shards):
        if plan.inside:
            results.append((shard.shape, f32, in_vmem))
        else:
            results.append(((9 * C_MID, C_MID) if which == 1 else shapes[which], bf16, anywhere))
    dma = pltpu.SemaphoreType.DMA

    def sum_room(width):
        return SumRoom(
            pltpu.VMEM((plan.dp, 2, width), f32),
            pltpu.VMEM((plan.fsdp, 2, width), f32),
            dma((plan.dp,)),
            dma((plan.dp,)),
            dma((plan.fsdp,)),
            dma((plan.fsdp,)),
        )

    def matrix_room():
        size = plan.embed_rows
        return MatrixRoom(
            pltpu.VMEM((plan.dp, size, P_OUT), f32),
            pltpu.VMEM((plan.dp, size, P_OUT), f32),
            pltpu.VMEM((plan.fsdp, size, P_OUT), f32),
            pltpu.VMEM((plan.dp, size, P_OUT), f32),
            dma((plan.dp,)),
            dma((plan.dp,)),
            dma((plan.fsdp,)),
            dma((plan.fsdp,)),
            dma((plan.dp,)),
            dma((plan.dp,)),
        )

    scratch = Mem(
        w=[pltpu.VMEM(shape, bf16) for shape in shapes],
        g1=pltpu.VMEM(shapes[0], bf16),
        row_sums=pltpu.VMEM((2, C_IN), f32),
        r3=pltpu.VMEM(shapes[2], bf16),
        r4=pltpu.VMEM(shapes[3], bf16),
        r5=pltpu.VMEM(shapes[4], bf16),
        stage=pltpu.VMEM((max(SLOTS * plan.chunk, 9 * C_MID), C_MID), bf16),
        stage_sem=dma((2, SLOTS)),
        column_sem=dma((BLOCKS,)),
        h1=pltpu.VMEM((rows, C_MID), bf16),
        d1=pltpu.VMEM((rows, C_MID), bf16),
        h2=pltpu.VMEM((rows, C_MID), bf16),
        d2=pltpu.VMEM((rows, C_MID), bf16),
        a2=pltpu.VMEM((rows, C_MID), bf16),
        h3=pltpu.VMEM((BLOCKS * rows, C_MID), bf16),
        pad1=pltpu.VMEM((SIDE + 2, (SIDE + 2) * views, C_MID), bf16),
        pad2=pltpu.VMEM((SIDE + 2, (SIDE + 2) * views, C_MID), bf16),
        pool=pltpu.VMEM((views, C_IN), f32),
        pool_slope=pltpu.VMEM((views, C_IN), f32),
        pool_bend=pltpu.VMEM((views, C_IN), f32),
        pooled=pltpu.VMEM((views, C_IN), bf16),
        proj_act=pltpu.VMEM((views, P_HID), bf16),
        proj_slope=pltpu.VMEM((views, P_HID), f32),
        proj_hidden=pltpu.VMEM((views, P_HID), f32),
        coef=pltpu.VMEM((8, C_IN), f32),
        stats=pltpu.VMEM((2, norm_width()), f32),
        norm=pltpu.VMEM((2, norm_width()), f32),
        norm_grads=pltpu.VMEM((2, norm_width()), f32),
        norm_tiles=pltpu.VMEM((plan.dp, plan.fsdp, 2, LANES), f32),
        norm_s0=dma((plan.dp,)),
        norm_r0=dma((plan.dp,)),
        norm_s1=dma((plan.fsdp,)),
        norm_r1=dma((plan.fsdp,)),
        bulk_send=dma((COPIES,)),
        bulk_recv=dma((COPIES,)),
        mats=[matrix_room(), matrix_room()],
        sums=[
            sum_room(width)
            for width in (C_MID, C_MID, C_IN // 2, C_IN // 2, P_HID, C_IN, LANES)
        ],
        squares=pltpu.VMEM((1, LANES), f32),
    )
    values = pl.pallas_call(
        lambda *refs: kernel(plan, *refs),
        out_shape=[jax.ShapeDtypeStruct(shape, kind) for shape, kind, _ in results],
        in_specs=in_specs,
        out_specs=[spec for _, _, spec in results],
        scratch_shapes=[scratch],
        compiler_params=pltpu.CompilerParams(
            collective_id=1, has_side_effects=True, vmem_limit_bytes=63 * 2**20
        ),
        name="train_step",
    )(*operands)
    return Outs(*values[:4], values[4:])


def norm_width():
    return 2 * C_MID + C_IN + P_HID


def clip_factor(norm):
    return clip_level / jnp.maximum(norm, clip_level)


def adam_update(weight, moment_one, moment_two, gradient, step_rate, weight_decay):
    first_new = beta_first * moment_one + (1.0 - beta_first) * gradient
    second_new = beta_second * moment_two + (1.0 - beta_second) * gradient * gradient
    first_hat = first_new / (1.0 - beta_first**STEP)
    second_hat = second_new / (1.0 - beta_second**STEP)
    weight_new = weight - step_rate * (
        first_hat / (jnp.sqrt(second_hat) + adam_epsilon) + weight_decay * weight
    )
    return (weight_new, first_new, second_new)


def finish_kernel(rates, decays, *refs):
    count = len(rates)
    low, scalars = refs[0], refs[1]
    refs = refs[2:]
    given, wide, loss, norm, updated = refs[: 4 * count], *refs[4 * count : 4 * count + 3], refs[4 * count + 3 : -2]
    rooms, sems = refs[-2], refs[-1]
    wide[...] = low[...].astype(f32)
    step = pl.program_id(0)

    def load(place):
        return pltpu.make_async_copy(given[place], rooms[place], sems.at[place])

    def store(place):
        return pltpu.make_async_copy(rooms[place], updated[place], sems.at[place])

    @pl.when(step == 0)
    def _():
        loss[0, 0] = scalars[0, 0]
        norm[0, 0] = scalars[2, 0]
        for place in range(4 * count):
            load(place).start()

    @pl.when(step == 2)
    def _():
        for place in range(4 * count):
            load(place).wait()
        for place in range(count):
            weight, first, second, grad = (rooms[part * count + place][...] for part in range(4))
            found = adam_update(weight, first, second, grad * scalars[3, 0], rates[place], decays[place])
            for part in range(3):
                rooms[part * count + place][...] = found[part]
        for place in range(3 * count):
            store(place).start()

    @pl.when(step == CHUNKS - 1)
    def _():
        for place in range(3 * count):
            store(place).wait()


def finish(features_grad, scalars, masters, firsts, seconds, grads, rates, decays):
    rows = features_grad.shape[0]
    arrays = [*masters, *firsts, *seconds, *grads]
    moving = pl.BlockSpec((rows // CHUNKS, C_IN), lambda index: (index, 0))
    single = pl.BlockSpec(memory_space=pltpu.SMEM)
    anywhere = pl.BlockSpec(memory_space=pl.ANY)
    count = len(masters)
    values = pl.pallas_call(
        lambda *refs: finish_kernel(rates, decays, *refs),
        grid=(CHUNKS,),
        in_specs=[moving, single] + [anywhere] * (4 * count),
        out_specs=[moving, single, single] + [anywhere] * (3 * count),
        out_shape=[jax.ShapeDtypeStruct((rows, C_IN), f32)]
        + [jax.ShapeDtypeStruct((1, 1), f32)] * 2
        + [jax.ShapeDtypeStruct(array.shape, f32) for array in arrays[: 3 * count]],
        scratch_shapes=[
            [pltpu.VMEM(array.shape, f32) for array in arrays],
            pltpu.SemaphoreType.DMA((4 * count,)),
        ],
        compiler_params=pltpu.CompilerParams(vmem_limit_bytes=62 * 2**20),
        name="finish",
    )(features_grad, scalars, *arrays)
    groups = [values[3 + part * count : 3 + (part + 1) * count] for part in range(3)]
    return values[0], values[1].reshape(()), values[2].reshape(()), *groups


def gather_full(weight):
    outer = lax.all_gather(weight.astype(bf16), FSDP, axis=0, tiled=True)
    return lax.all_gather(outer, DP, axis=1, tiled=True)


def scatter_full(gradient):
    inner = lax.psum_scatter(gradient.astype(f32), DP, scatter_dimension=1, tiled=True)
    return lax.psum_scatter(inner, FSDP, scatter_dimension=0, tiled=True)


def body(features, view_order, *state):
    masters, firsts, seconds = state[:6], state[6:12], state[12:18]
    dp_size, fsdp_size = lax.axis_size(DP), lax.axis_size(FSDP)
    views = features.shape[0]
    inside = dp_size == 4 and fsdp_size == 8
    plan = Plan(dp_size, fsdp_size, views, inside)
    pixels = jnp.swapaxes(features, 0, 1).reshape(-1, C_IN)
    norm_params = masters[5]
    shapes = weight_shapes()
    if inside:
        shards = list(masters[:4]) + [masters[4].T]
        norm = norm_params
    else:
        full = [gather_full(weight) for weight in masters[:5]]
        shards = [
            full[0].reshape(shapes[0]),
            full[1].reshape(shapes[1]),
            full[2].reshape(C_MID, BLOCKS, C_MID).swapaxes(0, 1).reshape(shapes[2]),
            full[3].reshape(shapes[3]),
            full[4].reshape(4, 2, P_OUT, P_OUT).swapaxes(2, 3),
        ]
        norm = lax.all_gather(norm_params.astype(bf16), (DP, FSDP), axis=1, tiled=True).astype(f32)
    got = run_kernel(plan, pixels, view_order, shards, norm)
    grads = list(got.grads)
    scalars = got.scalars
    turned = [list(group) for group in (masters, firsts, seconds)]
    if inside:
        owned = grads
        for group in turned:
            group[4] = group[4].T
    else:
        whole_grads = [
            grads[0].reshape(C_IN, C_MID),
            grads[1],
            grads[2].reshape(BLOCKS, C_MID, C_MID).swapaxes(0, 1).reshape(C_MID, C_IN),
            grads[3].reshape(C_IN, P_HID),
            grads[4].swapaxes(2, 3).reshape(P_HID, P_OUT),
        ]
        owned = [scatter_full(gradient) for gradient in whole_grads]
        squares = scalars[1, 0] + lax.psum(sum(jnp.sum(grad * grad) for grad in owned), (DP, FSDP))
        norm_value = jnp.sqrt(squares)
        scalars = scalars.at[2].set(norm_value).at[3].set(clip_factor(norm_value))
    width = norm_params.shape[1]
    if inside:
        owned.append(got.norm_grad)
    else:
        owner = lax.axis_index((DP, FSDP))
        owned.append(lax.dynamic_slice_in_dim(got.norm_grad, owner * width, width, 1))
    step_rates = (
        C_IN ** (-0.5),
        (9 * C_MID) ** (-0.5),
        C_MID ** (-0.5),
        C_IN ** (-0.5),
        P_HID ** (-0.5),
        norm_rate,
    )
    decays = (decay_rate, decay_rate, decay_rate, decay_rate, decay_rate, 0.0)
    input_grad, loss, grad_norm, *updates = finish(
        got.features_grad, scalars, *turned, owned, step_rates, decays
    )
    if inside:
        updates = [[*group[:4], group[4].T, group[5]] for group in updates]
    return (
        loss,
        jnp.swapaxes(input_grad.reshape(PIX, views, C_IN), 0, 1),
        grad_norm,
        *updates[0],
        *updates[1],
        *updates[2],
    )


def solution(mesh):
    views = P((DP, FSDP), None, None)
    split = P(FSDP, DP)
    norm = P(None, (DP, FSDP))
    params = (split,) * 5 + (norm,)
    return jax.shard_map(
        body,
        mesh=mesh,
        in_specs=(views, P((DP, FSDP), None)) + params * 3,
        out_specs=(P(), views, P()) + params * 3,
        check_vma=False,
    )
```

```python
from typing import Any, NamedTuple

import jax
import jax.numpy as jnp
from jax import lax
from jax.experimental import pallas as pl
from jax.experimental.pallas import tpu as pltpu
from jax.sharding import PartitionSpec as P

C_IN = 2048
C_MID = 512
P_HID = 1024
P_OUT = 128
SIDE = 7
STEP = 10
PIX = 49
LANES = 128
BLOCKS = C_IN // C_MID
CHUNKS = SIDE
SLOTS = 6
LAST_SUM = 23
COPIES = 360


highest = lax.Precision.HIGHEST
bf16 = jnp.bfloat16
f32 = jnp.float32
norm_epsilon = 1e-05
ridge_term = 0.01
clip_level = 0.1
beta_first = 0.9
beta_second = 0.999
adam_epsilon = 1e-08
decay_rate = 0.05
norm_rate = 0.5
bell_scale = 0.3989422804014327
root_half = 0.5**0.5
bell_rate = -0.7213475204444817
DP, FSDP = "dp", "fsdp"


def gelu_pair(values):
    below = 0.5 + 0.5 * lax.erf(values * root_half)
    bell = jnp.exp2(values * values * bell_rate)
    return values * below, below + values * bell * bell_scale


def dot(left, right):
    return jnp.dot(left, right, preferred_element_type=f32)


def dot_cols(left, right):
    return lax.dot_general(left, right, (((1,), (1,)), ((), ())), preferred_element_type=f32)


def dot_rows(left, right):
    return lax.dot_general(left, right, (((0,), (0,)), ((), ())), preferred_element_type=f32)


def exact_cols(left, right):
    return lax.dot_general(
        left, right, (((1,), (1,)), ((), ())), precision=highest, preferred_element_type=f32
    )


def exact_rows(left, right):
    return lax.dot_general(
        left, right, (((0,), (0,)), ((), ())), precision=highest, preferred_element_type=f32
    )


def exact_dot(left, right):
    return jnp.dot(left, right, precision=highest, preferred_element_type=f32)


def inverse_factors(matrices):
    row_top = lax.broadcasted_iota(jnp.int32, (8, P_OUT), 0)
    row_all = lax.broadcasted_iota(jnp.int32, (P_OUT, P_OUT), 0)
    col_all = lax.broadcasted_iota(jnp.int32, (P_OUT, P_OUT), 1)

    def one_step(place, left, right):
        scale = lax.rsqrt(left[place : place + 1, place : place + 1])
        left_row = left[place : place + 1, :] * scale
        right_row = right[place : place + 1, :] * scale
        column = left[:, place : place + 1] * scale
        left = left - column * left_row
        right = right - column * right_row
        here = row_top == place
        left = jnp.concatenate([jnp.where(here, 0.0, left[:8]), left[8:]], axis=0)
        right = jnp.concatenate(
            [jnp.where(here, jnp.broadcast_to(right_row, (8, P_OUT)), right[:8]), right[8:]], axis=0
        )
        return left, right

    def panel(_, pairs):
        pairs = list(pairs)
        for place in range(8):
            for which in range(len(pairs)):
                pairs[which] = one_step(place, *pairs[which])
        return tuple(
            (
                pltpu.roll(jnp.concatenate([left[8:], left[:8]], axis=0), P_OUT - 8, 1),
                jnp.concatenate([right[8:], right[:8]], axis=0),
            )
            for left, right in pairs
        )

    pairs = tuple((matrix, (row_all == col_all).astype(f32)) for matrix in matrices)
    done = [[] for _ in matrices]
    size = P_OUT // 4
    for _ in range(4):
        pairs = lax.fori_loop(0, size // 8, panel, pairs)
        for found, (_, right) in zip(done, pairs):
            found.append(right[-size:])
        pairs = tuple((left[:-size], right[:-size]) for left, right in pairs)
    return [jnp.concatenate(found, axis=0) for found in done]


def pack_pair(first, second):
    row = lax.broadcasted_iota(jnp.int32, (P_OUT, P_OUT), 0)
    col = lax.broadcasted_iota(jnp.int32, (P_OUT, P_OUT), 1)
    packed = jnp.where(row >= col, first, second.T)
    diagonal = jnp.sum(jnp.where(row == col, second, 0.0), axis=0, keepdims=True)
    return packed, diagonal


def unpack_pair(packed, diagonal):
    row = lax.broadcasted_iota(jnp.int32, (P_OUT, P_OUT), 0)
    col = lax.broadcasted_iota(jnp.int32, (P_OUT, P_OUT), 1)
    turned = packed.T
    first = jnp.where(row >= col, packed, turned)
    second = jnp.where(row < col, packed, jnp.where(row == col, diagonal, turned))
    return first, second


GATHER_AT = {
    (0, 1): 1,
    (0, 3): 1,
    (1, 0): 1,
    (2, 0): 1,
    (4, 0): 5,
    (5, 0): 1,
    (5, 1): 1,
    (5, 2): 1,
    (5, 4): 1,
    (5, 5): 1,
    (5, 6): 1,
    (7, 0): 1,
    (8, 6): 1,
    (9, 2): 1,
    (9, 5): 1,
    (9, 8): 1,
    (21, 0): 7,
}
REDUCE_AT = {
    (11, 3): ((4, 0, 1), (3, 0, 1)),
    (11, 11): ((3, 1, 1), (4, 0, 2)),
    (11, 20): ((3, 0, 2), (3, 2, 1)),
    (12, 0): ((3, 1, 2), (3, 0, 3), (4, 0, 3)),
    (12, 1): ((3, 3, 1),),
    (12, 2): ((3, 2, 2), (3, 1, 3)),
    (13, 0): ((3, 3, 2),),
    (13, 2): ((3, 2, 3),),
    (13, 3): ((3, 3, 3), (2, 0, 0), (2, 1, 0), (2, 2, 0), (2, 3, 0)),
    (14, 6): ((4, 9, 4), (2, 0, 1), (2, 1, 1)),
    (15, 2): ((1, 0, 0), (2, 0, 2), (2, 2, 1), (2, 3, 1)),
    (15, 4): ((1, 1, 0), (1, 0, 1), (2, 1, 2), (2, 0, 3)),
    (15, 6): ((1, 2, 0), (2, 2, 2), (2, 3, 2), (1, 1, 1), (2, 1, 3), (3, 9, 4)),
    (16, 0): ((1, 0, 2), (1, 2, 1), (2, 2, 3), (2, 3, 3)),
    (16, 1): ((1, 1, 2), (2, 9, 4), (1, 0, 3)),
    (16, 2): ((1, 2, 2), (1, 1, 3)),
    (17, 1): ((1, 3, 0), (1, 2, 3)),
    (18, 6): ((1, 3, 1),),
    (19, 0): ((0, 0, 0), (1, 3, 2)),
    (19, 1): ((0, 1, 0), (0, 0, 1), (1, 3, 3)),
    (19, 2): ((0, 2, 0), (0, 1, 1), (0, 0, 2)),
    (19, 3): ((0, 3, 0), (0, 2, 1), (0, 1, 2), (0, 0, 3), (1, 9, 4)),
    (20, 2): ((0, 3, 1), (0, 2, 2), (0, 1, 3)),
    (20, 8): ((0, 3, 2), (0, 2, 3)),
    (20, 13): ((0, 3, 3),),
    (20, 20): ((0, 9, 4),),
    (23, 0): ((4, 0, 0), (3, 0, 0), (3, 1, 0), (3, 2, 0), (3, 3, 0)),
}


class Ins(NamedTuple):
    features: Any
    order: Any
    norm: Any
    shards: Any


class Outs(NamedTuple):
    slope: Any
    features_grad: Any
    norm_grad: Any
    scalars: Any
    grads: Any


class SumRoom(NamedTuple):
    dp: Any
    fsdp: Any
    s0: Any
    r0: Any
    s1: Any
    r1: Any


class MatrixRoom(NamedTuple):
    pack: Any
    dp: Any
    fsdp: Any
    all: Any
    s0: Any
    r0: Any
    s1: Any
    r1: Any
    s2: Any
    r2: Any


class Mem(NamedTuple):
    w: Any
    g1: Any
    row_sums: Any
    r3: Any
    r4: Any
    r5: Any
    stage: Any
    stage_sem: Any
    column_sem: Any
    h1: Any
    d1: Any
    h2: Any
    d2: Any
    a2: Any
    h3: Any
    pad1: Any
    pad2: Any
    pool: Any
    pool_slope: Any
    pool_bend: Any
    pooled: Any
    proj_act: Any
    proj_slope: Any
    proj_hidden: Any
    coef: Any
    stats: Any
    norm: Any
    norm_grads: Any
    norm_tiles: Any
    norm_s0: Any
    norm_r0: Any
    norm_s1: Any
    norm_r1: Any
    bulk_send: Any
    bulk_recv: Any
    mats: Any
    sums: Any
    squares: Any


class Plan:
    def __init__(self, dp_size, fsdp_size, views, inside):
        self.dp = dp_size
        self.fsdp = fsdp_size
        self.devices = dp_size * fsdp_size
        self.views = views
        self.rows = views * PIX
        self.tall = -(-self.rows // C_MID) * C_MID
        self.chunk = views * SIDE
        self.inside = inside
        self.z = 4
        self.x = 2
        self.half = (128, 288, 32, 128, 16)
        self.width = (128, 128, 512, 256, 128)
        piece = P_OUT + 8
        self.embed_rows = -(-piece // (8 * dp_size)) * 8


def kernel(plan, *refs):
    ins, outs, mem = Ins(*refs[:3], refs[3:8]), Outs(*refs[8:12], refs[12:17]), refs[17]
    views, chunk, rows, tall = plan.views, plan.chunk, plan.rows, plan.tall
    row_total = float(rows * plan.devices)
    view_total = float(views * plan.devices)
    image_total = float(views * plan.devices // 2)
    dp_me, fsdp_me = lax.axis_index(DP), lax.axis_index(FSDP)
    y_me, c_me = dp_me // 2, dp_me % 2
    z_me, x_me = fsdp_me // 2, fsdp_me % 2
    y_other, c_other, x_other = 1 - y_me, 1 - c_me, 1 - x_me

    barrier = pltpu.get_barrier_semaphore()

    @pl.loop(1, plan.dp)
    def _(step):
        pl.semaphore_signal(
            barrier, 1, device_id={DP: lax.rem(dp_me + step, plan.dp)}, device_id_type=pl.DeviceIdType.MESH
        )

    @pl.loop(1, plan.fsdp)
    def _(step):
        pl.semaphore_signal(
            barrier, 1, device_id={FSDP: lax.rem(fsdp_me + step, plan.fsdp)}, device_id_type=pl.DeviceIdType.MESH
        )

    pl.semaphore_wait(barrier, plan.dp + plan.fsdp - 2)

    def share(axis, size, me, source_of, slots, send, recv):
        def outgoing(step):
            partner = lax.rem(me + step, size)
            return pltpu.make_async_remote_copy(
                src_ref=source_of(partner),
                dst_ref=slots.at[me],
                send_sem=send.at[step],
                recv_sem=recv.at[me],
                device_id={axis: partner},
                device_id_type=pl.DeviceIdType.MESH,
            )

        def incoming(step):
            source = lax.rem(me + step, size)
            return pltpu.make_async_remote_copy(
                src_ref=slots.at[source],
                dst_ref=slots.at[source],
                send_sem=send.at[step],
                recv_sem=recv.at[source],
                device_id={axis: source},
                device_id_type=pl.DeviceIdType.MESH,
            )

        def start():
            pl.loop(1, size)(lambda step: outgoing(step).start())

        def wait():
            pl.loop(1, size)(lambda step: incoming(step).wait_recv())
            pl.loop(1, size)(lambda step: outgoing(step).wait_send())

        return start, wait

    def add_slots(slots, size):
        total = slots[0]
        for place in range(1, size):
            total = total + slots[place]
        return total

    class Sum:
        def __init__(self, which):
            part = mem.sums[(0, 1, 2, 3, 4, 4, 5, 0, 1, 6)[which]]
            self.dp_slots, self.fsdp_slots = part.dp, part.fsdp
            self.dp_copy = share(
                DP, plan.dp, dp_me, lambda _: self.dp_slots.at[dp_me], self.dp_slots, part.s0, part.r0
            )
            self.fsdp_copy = share(
                FSDP, plan.fsdp, fsdp_me, lambda _: self.fsdp_slots.at[fsdp_me], self.fsdp_slots, part.s1, part.r1
            )

        def start(self, *values):
            for place, value in enumerate(values):
                self.dp_slots[dp_me, place : place + 1, :] = value
            self.dp_copy[0]()

        def middle(self):
            self.dp_copy[1]()
            self.fsdp_slots[fsdp_me] = add_slots(self.dp_slots, plan.dp)
            self.fsdp_copy[0]()

        def finish(self):
            self.fsdp_copy[1]()
            return add_slots(self.fsdp_slots, plan.fsdp)

        def all(self, *values):
            self.start(*values)
            self.middle()
            return self.finish()

    def sum_matrix(which, matrix, extra):
        part = mem.mats[which]
        size = plan.embed_rows
        pack = part.pack
        flat = jnp.concatenate(
            [matrix] + extra + [jnp.zeros((size * plan.dp - P_OUT - len(extra), P_OUT), f32)], axis=0
        )
        for place in range(plan.dp):
            pack[place] = flat[place * size : (place + 1) * size]
        start, wait = share(DP, plan.dp, dp_me, lambda to: pack.at[to], part.dp, part.s0, part.r0)
        start()
        part.dp[dp_me] = pack[dp_me]
        wait()
        part.fsdp[fsdp_me] = add_slots(part.dp, plan.dp)
        start, wait = share(
            FSDP, plan.fsdp, fsdp_me, lambda _: part.fsdp.at[fsdp_me], part.fsdp, part.s1, part.r1
        )
        start()
        wait()
        part.all[dp_me] = add_slots(part.fsdp, plan.fsdp)
        start, wait = share(
            DP, plan.dp, dp_me, lambda _: part.all.at[dp_me], part.all, part.s2, part.r2
        )
        start()
        wait()
        total = jnp.concatenate([part.all[place] for place in range(plan.dp)], axis=0)
        return total[:P_OUT], [total[P_OUT + place : P_OUT + place + 1] for place in range(len(extra))]

    weights = mem.w
    everything = slice(None)

    def row_span(which, half):
        if isinstance(half, tuple):
            return half
        size = plan.half[which]
        if half is None:
            return 0, 2 * size
        return half * size, size

    def column_span(which, dp_index):
        width = plan.width[which]
        return pl.ds(pl.multiple_of(dp_index * width, width), width)

    def places(which, z_index, x_index, dp_index, half, flat=True):
        start, size = row_span(which, half)
        if which == 1 and flat:
            z_list = range(plan.z) if z_index is None else [z_index]
            x_list = range(plan.x) if x_index is None else [x_index]
            return [
                (
                    pl.ds(pl.multiple_of((z_one * plan.x + x_one) * 576 + start, 16), size),
                    column_span(which, dp_index),
                )
                for z_one in z_list
                for x_one in x_list
            ]
        z_one = everything if z_index is None else z_index
        x_one = everything if x_index is None else x_index
        if which == 2:
            return [(dp_index, z_one, x_one, pl.ds(start, size), everything)]
        if which == 4:
            return [(z_one, x_one, pl.ds(pl.multiple_of(dp_index * 32 + start, 16), size), everything)]
        return [(z_one, x_one, pl.ds(start, size), column_span(which, dp_index))]

    recv_parts = {
        1: lambda index: mem.h3.at[index],
        0: lambda index: mem.r4.at[index],
        2: lambda index: mem.r3.at[index],
        3: lambda index: mem.r4.at[index],
        4: lambda index: mem.r5.at[index],
    }

    counter = [0]

    class Batch:
        def __init__(self, sources, targets, landings, axis, partner):
            base = counter[0]
            counter[0] += len(sources)
            send, recv = mem.bulk_send, mem.bulk_recv
            self.out = [
                pltpu.make_async_remote_copy(
                    src_ref=source,
                    dst_ref=target,
                    send_sem=send.at[base + place],
                    recv_sem=recv.at[base + place],
                    device_id={axis: partner},
                    device_id_type=pl.DeviceIdType.MESH,
                )
                for place, (source, target) in enumerate(zip(sources, targets))
            ]
            self.come = [
                pltpu.make_async_remote_copy(
                    src_ref=landing,
                    dst_ref=landing,
                    send_sem=send.at[base + place],
                    recv_sem=recv.at[base + place],
                    device_id={axis: partner},
                    device_id_type=pl.DeviceIdType.MESH,
                )
                for place, landing in enumerate(landings)
            ]

        def start(self):
            for copy in self.out:
                copy.start()

        def arrive(self):
            for copy in self.come:
                copy.wait_recv()

        def leave(self):
            for copy in self.out:
                copy.wait_send()

    class LineBatch:
        def __init__(self, source_of, target_of, landing_of):
            base = counter[0]
            counter[0] += plan.z
            send, recv = mem.bulk_send, mem.bulk_recv
            self.out, self.come = [], []
            for step in range(1, plan.z):
                z_to = (z_me + step) % plan.z
                self.out.append(
                    pltpu.make_async_remote_copy(
                        src_ref=source_of(z_to),
                        dst_ref=target_of(z_to),
                        send_sem=send.at[base + step],
                        recv_sem=recv.at[base + z_me],
                        device_id={FSDP: z_to * plan.x + x_me},
                        device_id_type=pl.DeviceIdType.MESH,
                    )
                )
                self.come.append(
                    pltpu.make_async_remote_copy(
                        src_ref=landing_of(z_to),
                        dst_ref=landing_of(z_to),
                        send_sem=send.at[base + step],
                        recv_sem=recv.at[base + z_to],
                        device_id={FSDP: z_to * plan.x + x_me},
                        device_id_type=pl.DeviceIdType.MESH,
                    )
                )

        start, arrive, leave = Batch.start, Batch.arrive, Batch.leave

    def pick(ref, indexes):
        return [ref.at[index] for index in indexes]

    def own_dp(y_index, c_index):
        return y_index * 2 + c_index

    x_partner = z_me * plan.x + x_other
    y_partner = own_dp(y_other, c_me)
    c_partner = own_dp(y_me, c_other)
    dp_far = own_dp(y_other, c_other)

    class Gather:
        def __init__(self, which, start, size):
            ref = weights[which]
            self.which, self.rows = which, (start, size)
            both, low, high = (start, size), (start, size // 2), (start + size // 2, size // 2)

            def at(*index):
                return pick(ref, places(which, *index, False))

            own = at(z_me, x_me, dp_me, both)[0]
            self.line = LineBatch(
                lambda _: own, lambda _: own, lambda z_from: at(z_from, x_me, dp_me, both)[0]
            )
            sent, come = at(None, x_me, dp_me, low), at(None, x_other, dp_me, low)
            x_first = Batch(sent, sent, come, FSDP, x_partner)
            sent, come = at(None, x_me, dp_me, high), at(None, x_me, y_partner, high)
            y_first = Batch(sent, sent, come, DP, y_partner)
            sent, come = at(None, None, dp_me, low), at(None, None, y_partner, low)
            y_second = Batch(sent, sent, come, DP, y_partner)
            sent = at(None, x_me, dp_me, high) + at(None, x_me, y_partner, high)
            come = at(None, x_other, dp_me, high) + at(None, x_other, y_partner, high)
            x_second = Batch(sent, sent, come, FSDP, x_partner)
            sent = at(None, None, dp_me, both) + at(None, None, y_partner, both)
            come = at(None, None, c_partner, both) + at(None, None, dp_far, both)
            core = Batch(sent, sent, come, DP, c_partner)
            self.stages = ((self.line,), (x_first, y_first), (y_second, x_second), (core,))

        def put_own(self):
            index = places(self.which, z_me, x_me, dp_me, self.rows, False)[0]
            shard = ins.shards[self.which][self.rows[0] : self.rows[0] + self.rows[1], :]
            weights[self.which][index] = shard.astype(bf16)

        def start(self, stage):
            for batch in self.stages[stage]:
                batch.start()

        def arrive(self, stage):
            for batch in self.stages[stage]:
                batch.arrive()

        def leave(self):
            for stage in self.stages:
                for batch in stage:
                    batch.leave()

    class Piece:
        def __init__(self, which, ref, room, z_index):
            def at(*index):
                return pick(ref, places(which, z_index, *index))

            def land(*index):
                return [room(index_one) for index_one in places(which, z_index, *index)]

            self.z = z_index
            self.core = Batch(
                at(None, c_partner, None) + at(None, dp_far, None),
                land(None, c_partner, None) + land(None, dp_far, None),
                land(None, dp_me, None) + land(None, y_partner, None),
                DP,
                c_partner,
            )
            self.y_first = Batch(
                at(None, y_partner, 0), land(None, dp_far, 0), land(None, c_partner, 0), DP, y_partner
            )
            self.x_first = Batch(
                at(x_other, dp_me, 1) + at(x_other, y_partner, 1),
                land(x_other, c_partner, 1) + land(x_other, dp_far, 1),
                land(x_me, c_partner, 1) + land(x_me, dp_far, 1),
                FSDP,
                x_partner,
            )
            self.x_second = Batch(
                at(x_other, dp_me, 0), land(x_other, dp_far, 0), land(x_me, dp_far, 0), FSDP, x_partner
            )
            self.y_second = Batch(
                at(x_me, y_partner, 1), land(x_other, dp_far, 1), land(x_other, c_partner, 1), DP, y_partner
            )

    class Reduce:
        def __init__(self, which, ref, cut):
            self.which, self.ref, self.room = which, ref, recv_parts[which]
            self.pieces = [
                Piece(which, ref, self.room, z_index) for z_index in (range(plan.z) if cut else [None])
            ]
            self.base = counter[0]
            counter[0] += plan.z

        def line_copy(self, z_to):
            return pltpu.make_async_remote_copy(
                src_ref=self.ref.at[places(self.which, z_to, x_me, dp_me, None)[0]],
                dst_ref=self.room(places(self.which, z_me, x_other, dp_far, None)[0]),
                send_sem=mem.bulk_send.at[self.base + z_to],
                recv_sem=mem.bulk_recv.at[self.base + z_me],
                device_id={FSDP: z_to * plan.x + x_me},
                device_id_type=pl.DeviceIdType.MESH,
            )

        def line_room(self, z_from):
            return self.room(places(self.which, z_from, x_other, dp_far, None)[0])

        def add(self, z_index, pairs):
            def one(z_one):
                for here, there in pairs:
                    for x_step in range(plan.x) if here[0] is None else [None]:
                        x_here = x_step if here[0] is None else here[0]
                        x_there = x_step if there[0] is None else there[0]
                        index = places(self.which, z_one, x_here, *here[1:])[0]
                        other = places(self.which, z_one, x_there, *there[1:])[0]
                        total = self.ref[index].astype(f32) + self.room(other)[...].astype(f32)
                        self.ref[index] = total.astype(bf16)

            if z_index is None:
                pl.loop(0, plan.z)(one)
            else:
                one(z_index)

        def core_start(self, place=0):
            if plan.inside:
                self.pieces[place].core.start()

        def core_add(self, place=0):
            if plan.inside:
                piece = self.pieces[place]
                piece.core.arrive()
                self.add(piece.z, [((None, dp_me, None),) * 2, ((None, y_partner, None),) * 2])
                piece.y_first.start()
                piece.x_first.start()

        def first_add(self, place=0):
            if plan.inside:
                piece = self.pieces[place]
                piece.y_first.arrive()
                self.add(piece.z, [((None, dp_me, 0), (None, c_partner, 0))])
                piece.x_second.start()
                piece.x_first.arrive()
                self.add(
                    piece.z, [((x_me, dp_me, 1), (x_me, c_partner, 1)), ((x_me, y_partner, 1), (x_me, dp_far, 1))]
                )
                piece.y_second.start()

        def second_add(self, place=0):
            if plan.inside:
                piece = self.pieces[place]
                piece.x_second.arrive()
                piece.y_second.arrive()
                self.add(
                    piece.z, [((x_me, dp_me, 0), (x_me, dp_far, 0)), ((x_me, dp_me, 1), (x_other, c_partner, 1))]
                )
                if piece.z is None:
                    for step in range(1, plan.z):
                        self.line_copy((z_me + step) % plan.z).start()
                else:

                    @pl.when(z_me != piece.z)
                    def _():
                        self.line_copy(piece.z).start()

        def finish(self):
            if not plan.inside:
                return
            total = self.ref[places(self.which, z_me, x_me, dp_me, None)[0]].astype(f32)
            for step in range(1, plan.z):
                z_from = (z_me + step) % plan.z
                room = self.line_room(z_from)
                pltpu.make_async_remote_copy(
                    src_ref=room,
                    dst_ref=room,
                    send_sem=mem.bulk_send.at[self.base + z_from],
                    recv_sem=mem.bulk_recv.at[self.base + z_from],
                    device_id={FSDP: z_from * plan.x + x_me},
                    device_id_type=pl.DeviceIdType.MESH,
                ).wait_recv()
                total = total + room[...].astype(f32)
            outs.grads[self.which][...] = total
            squares = jnp.sum(total * total, axis=0, keepdims=True)
            folded = squares[:, :LANES]
            for place in range(1, squares.shape[1] // LANES):
                folded = folded + squares[:, place * LANES : (place + 1) * LANES]
            mem.squares[...] += folded
            for step in range(1, plan.z):
                self.line_copy((z_me + step) % plan.z).wait_send()
            for piece in self.pieces:
                for batch in (piece.core, piece.y_first, piece.x_first, piece.x_second, piece.y_second):
                    batch.leave()

    gathers, steps = [], []
    if plan.inside:
        for which, cuts in enumerate((2, 3, 1, 2, 1)):
            size = 2 * plan.half[which] // cuts
            gathers += [Gather(which, cut * size, size) for cut in range(cuts)]

    def line_step(place):
        gathers[place].arrive(0)
        gathers[place].start(1)
        if place + 1 < len(gathers):
            gathers[place + 1].start(0)

    def first_step(place):
        gathers[place].arrive(1)
        gathers[place].start(2)

    def second_step(place):
        gathers[place].arrive(2)
        gathers[place].start(3)

    for place in range(len(gathers)):
        steps.append((line_step, place))
        if place > 0:
            steps.append((second_step, place - 1))
        steps.append((first_step, place))
    if plan.inside:
        steps.append((second_step, len(gathers) - 1))

    def take(count):
        taken, steps[:] = steps[:count], steps[count:]
        return [lambda one=one: one[0](one[1]) for one in taken]

    def moves(site, item):
        found = take(GATHER_AT.get((site, item), 0)) if plan.inside else []
        for which, piece, kind in REDUCE_AT.get((site, item), ()):
            one = reduces[which]
            found.append(
                one.finish
                if kind == 4
                else lambda one=one, kind=kind, piece=piece: (
                    one.core_start,
                    one.core_add,
                    one.first_add,
                    one.second_add,
                )[kind](piece)
            )
        return found

    def hook(site, item=0):
        for move in moves(site, item):
            move()

    def hook_in(site, index, count, first=0, stride=1):
        for item in range(count):
            found = moves(site, item)
            if found and plan.inside:

                @pl.when(index == first + item * stride)
                def _(found=found):
                    for move in found:
                        move()

    def cores_arrive(which):
        for one in gathers:
            if one.which == which:
                one.arrive(3)

    gradients = [mem.g1, mem.stage.at[pl.ds(0, 9 * C_MID)], weights[2], weights[3], weights[4]]
    reduces = [Reduce(which, gradients[which], which < 4) for which in range(5)]
    assert counter[0] <= COPIES
    mem.squares[...] = jnp.zeros((1, LANES), f32)

    if plan.inside:
        gathers[0].put_own()
        gathers[0].start(0)
        for one in gathers[1:]:
            one.put_own()
        tiles = mem.norm_tiles
        tiles[dp_me, fsdp_me] = ins.norm[...].astype(bf16).astype(f32)
        norm_dp = share(
            DP, plan.dp, dp_me, lambda _: tiles.at[dp_me, fsdp_me], tiles.at[:, fsdp_me], mem.norm_s0, mem.norm_r0
        )
        norm_dp[0]()
    else:
        loads = [
            pltpu.make_async_copy(ins.shards[which], weights[which], mem.bulk_send.at[which])
            for which in range(5)
        ]
        for load in loads:
            load.start()

    pieces = BLOCKS * CHUNKS

    def hidden_rows(index, pixel=0, count=chunk):
        return pl.ds(pl.multiple_of(index * chunk + pixel * views, 16), count)

    class Ring:
        def __init__(self, ref, start):
            self.ref, self.base = ref, start

        def rows(self, index, pixel=0, count=chunk):
            return pl.ds(
                pl.multiple_of(self.base + lax.rem(index, SLOTS) * chunk + pixel * views, 16), count
            )

        def copy(self, array, index, into):
            block, place = index // CHUNKS, lax.rem(index, CHUNKS)
            outer = array.at[
                pl.ds(pl.multiple_of(place * chunk, 16), chunk),
                pl.ds(pl.multiple_of(block * C_MID, LANES), C_MID),
            ]
            inner = self.ref.at[self.rows(index)]
            source, target = (outer, inner) if into else (inner, outer)
            return pltpu.make_async_copy(
                source, target, mem.stage_sem.at[0 if into else 1, lax.rem(index, SLOTS)]
            )

        def first_loads(self, array):
            for index in range(3):
                self.copy(array, index, True).start()

        def next_load(self, array, index):
            @pl.when(index + 3 < pieces)
            def _():
                self.copy(array, index + 3, True).start()

        def save(self, array, index):
            self.copy(array, index, False).start()

            @pl.when(index >= 2)
            def _():
                self.copy(array, index - 2, False).wait()

        def last_saves(self, array):
            for index in (pieces - 2, pieces - 1):
                self.copy(array, index, False).wait()

    stage_ref = mem.stage
    stage = Ring(stage_ref, 0)

    def piece_columns(index, part):
        return pl.ds(pl.multiple_of(index // CHUNKS * C_MID + part * LANES, LANES), LANES)

    features, slope_hbm = ins.features, outs.slope
    hidden_three = mem.h3

    def feature_copy(block, target):
        return pltpu.make_async_copy(
            features.at[:, pl.ds(block * C_MID, C_MID)], target, mem.column_sem.at[block]
        )

    feature_loads = [
        feature_copy(block, hidden_three.at[pl.ds(block * rows, rows)]) for block in range(BLOCKS)
    ]
    for copy in feature_loads:
        copy.start()
    stage.first_loads(features)

    padded_one, padded_two = mem.pad1, mem.pad2
    for padded in (padded_one, padded_two):
        for edge in (0, SIDE + 1):
            padded[edge] = jnp.zeros((padded.shape[1], C_MID), bf16)
        for edge in (0, SIDE + 1):
            padded[:, pl.ds(edge * views, views), :] = jnp.zeros((SIDE + 2, views, C_MID), bf16)
    rest = jnp.zeros((tall - rows, C_MID), bf16)
    for ref, end in ((mem.d1, rows), (mem.h2, rows), (mem.d2, rows), (mem.a2, rows), (hidden_three, BLOCKS * rows)):
        ref[end : end + tall - rows, :] = rest

    if plan.inside:
        norm_dp[1]()
        norm_out = []
        norm_in = []
        for step in range(1, plan.fsdp):
            partner = (fsdp_me + step) % plan.fsdp
            norm_out.append(
                pltpu.make_async_remote_copy(
                    src_ref=tiles.at[:, fsdp_me],
                    dst_ref=tiles.at[:, fsdp_me],
                    send_sem=mem.norm_s1.at[step],
                    recv_sem=mem.norm_r1.at[fsdp_me],
                    device_id={FSDP: partner},
                    device_id_type=pl.DeviceIdType.MESH,
                )
            )
            norm_in.append(
                pltpu.make_async_remote_copy(
                    src_ref=tiles.at[:, partner],
                    dst_ref=tiles.at[:, partner],
                    send_sem=mem.norm_s1.at[step],
                    recv_sem=mem.norm_r1.at[partner],
                    device_id={FSDP: partner},
                    device_id_type=pl.DeviceIdType.MESH,
                )
            )
        for copy in norm_out:
            copy.start()
        hook(21)
        for copy in norm_in:
            copy.wait_recv()
        for copy in norm_out:
            copy.wait_send()
        norm_all = mem.norm
        for dp_one in range(plan.dp):
            for fsdp_one in range(plan.fsdp):
                start = (dp_one * plan.fsdp + fsdp_one) * LANES
                norm_all[:, start : start + LANES] = tiles[dp_one, fsdp_one]
    else:
        for copy in loads:
            copy.wait()
        norm_all = mem.norm
        norm_all[...] = ins.norm[...]

    starts = (0, C_MID, 2 * C_MID, 2 * C_MID + C_IN, 2 * C_MID + C_IN + P_HID)

    def gain(layer):
        return norm_all[0:1, starts[layer] : starts[layer + 1]]

    coef, stats = mem.coef, mem.stats

    def norm_coefs(layer, totals, count, low=0):
        width = totals.shape[1]
        here, there = slice(low, low + width), slice(starts[layer] + low, starts[layer] + low + width)
        mean = totals[0:1] / count
        scaling = lax.rsqrt(totals[1:2] / count - mean * mean + norm_epsilon)
        slope = scaling * norm_all[0:1, there]
        stats[0:1, there] = mean
        stats[1:2, there] = scaling
        coef[0:1, here] = slope
        coef[1:2, here] = norm_all[1:2, there] - mean * slope

    def grad_coefs(layer, totals, count):
        width = starts[layer + 1] - starts[layer]
        mean = stats[0:1, starts[layer] : starts[layer + 1]]
        scaling = stats[1:2, starts[layer] : starts[layer + 1]]
        mem.norm_grads[0:1, starts[layer] : starts[layer + 1]] = totals[1:2]
        mem.norm_grads[1:2, starts[layer] : starts[layer + 1]] = totals[0:1]
        slope = scaling * gain(layer)
        bend = slope * scaling * totals[1:2] / count
        coef[0:1, :width] = slope
        coef[1:2, :width] = slope * totals[0:1] / count - mean * bend
        coef[2:3, :width] = bend

    def xhat_sum(layer, plain, product):
        mean = stats[0:1, starts[layer] : starts[layer + 1]]
        scaling = stats[1:2, starts[layer] : starts[layer + 1]]
        return scaling * (product - mean * plain)

    zero_row = jnp.zeros((1, C_MID), f32)

    def column_sums(value):
        return jnp.sum(value, axis=0, keepdims=True)

    def whole(which):
        value = weights[which][...]
        return value.reshape(-1, value.shape[-1])

    row_sums = mem.row_sums

    def clear_sums():
        row_sums[...] = jnp.zeros_like(row_sums)

    def count_in(cols, value, other):
        row_sums[0:1, cols] += column_sums(value)
        row_sums[1:2, cols] += column_sums(value * other)

    def own_columns(side):
        core = (c_me + side) % 2
        return [
            pl.ds(pl.multiple_of(half * (C_MID // 2) + core * LANES, LANES), LANES) for half in range(2)
        ]

    def turn_rows(ref):
        @pl.loop(0, tall // C_MID)
        def _(block):
            at = pl.ds(pl.multiple_of(block * C_MID, C_MID), C_MID)
            ref[at, :] = ref[at, :].T

    def turned(ref):
        return jnp.concatenate([ref[start : start + C_MID, :] for start in range(0, tall, C_MID)], axis=1)

    def sends_leave(which):
        for one in gathers:
            if one.which == which:
                one.leave()

    def turn_weight(which, block):
        ref = weights[which]
        if which == 1:
            groups = [block * 8 + group for group in range(8)]
            ats = [
                (group // 18, group // 9 % 2, pl.ds(pl.multiple_of(group % 9 * 64, 64), 64), everything)
                for group in groups
            ]
            value = jnp.concatenate([ref[at] for at in ats], axis=0).T
            for place, at in enumerate(ats):
                ref[at] = value[place * 64 : (place + 1) * 64, :]
        elif which == 3:
            for half in range(P_HID // C_MID):
                cols = slice(half * C_MID, (half + 1) * C_MID)
                value = ref[block, :, :, cols]
                ref[block, :, :, cols] = value.reshape(C_MID, C_MID).T.reshape(value.shape)
        else:
            value = ref[block]
            ref[block] = value.reshape(C_MID, C_MID).T.reshape(value.shape)

    hidden_one, slope_one = mem.h1, mem.d1
    hidden_two, slope_two = mem.h2, mem.d2
    act_two = mem.a2
    long = rows // 3

    def span(index):
        return pl.ds(pl.multiple_of(index * chunk, 16), chunk)

    def long_rows(block, index):
        return pl.ds(pl.multiple_of(block * rows + index * long, 16), long)

    def put_sides(ref, at, sides, hidden):
        for place, cols in enumerate(sides):
            part = hidden[:, place * LANES : (place + 1) * LANES]
            ref[at, cols] = part.astype(bf16)
            count_in(cols, part, part)

    for copy in feature_loads:
        copy.wait()
    clear_sums()

    @pl.loop(0, 2)
    def _(side):
        sides = own_columns(side)

        @pl.loop(0, 3)
        def _(index):
            left = jnp.concatenate([hidden_three[long_rows(block, index), :] for block in range(BLOCKS)], axis=1)
            right = jnp.concatenate([weights[0][:, :, :, cols].reshape(C_IN, LANES) for cols in sides], axis=1)
            put_sides(hidden_one, long_rows(0, index), sides, dot(left, right))

            hook_in(0, side * 3 + index, 6)

        @pl.when(side == 0)
        def _():
            cores_arrive(0)

    sum_one = Sum(0)
    sum_one.start(row_sums[0:1, :C_MID], row_sums[1:2, :C_MID])
    hook(1)
    sends_leave(0)
    pl.loop(0, 2)(lambda block: turn_weight(0, block))
    sum_one.middle()
    pl.loop(2, 4)(lambda block: turn_weight(0, block))
    hook(2)
    clear_sums()
    norm_coefs(0, sum_one.finish(), row_total)

    def activate(hidden_ref, slope_ref, put, site):
        @pl.loop(0, PIX)
        def _(pixel):
            place = pl.ds(pl.multiple_of(pixel * views, 16), views)
            for block in range(C_MID // LANES):
                cols = slice(block * LANES, (block + 1) * LANES)
                out = hidden_ref[place, cols].astype(f32) * coef[0:1, cols] + coef[1:2, cols]
                value, slope = gelu_pair(out)
                slope_ref[place, cols] = slope.astype(bf16)
                put(pixel, cols, value.astype(bf16))
            hook_in(site, pixel, SIDE, SIDE - 1, SIDE)

    def put_padded(padded):
        def put(pixel, cols, value):
            padded[pixel // SIDE + 1, pl.ds(pl.multiple_of((pixel % SIDE + 1) * views, 16), views), cols] = value

        return put

    activate(hidden_one, slope_one, put_padded(padded_one), 3)
    hook(4)

    def patch(padded, first, count, flip):
        found = []
        for vertical in range(3):
            for lateral in range(3):
                down, across = (2 - vertical, 2 - lateral) if flip else (vertical, lateral)
                piece = padded[pl.ds(first + down, count), across * views : across * views + chunk, :]
                found.append(piece.reshape(count * chunk, C_MID))
        return jnp.concatenate(found, axis=1)

    def image_rows(first, count):
        return pl.ds(pl.multiple_of(first * chunk, 16), count * chunk)

    def second_part(sides, first, count):
        right = jnp.concatenate([weights[1][:, :, :, cols].reshape(9 * C_MID, LANES) for cols in sides], axis=1)
        hidden = dot(patch(padded_one, first, count, False), right)
        put_sides(hidden_two, image_rows(first, count), sides, hidden)

    @pl.loop(0, 2)
    def _(side):
        sides = own_columns(side)

        @pl.loop(0, 3)
        def _(index):
            second_part(sides, 2 * index, 2)
            hook_in(5, side * 4 + index, 8)

        second_part(sides, 6, 1)

        @pl.when(side == 0)
        def _():
            cores_arrive(1)

    sum_two = Sum(1)
    sum_two.start(row_sums[0:1, :C_MID], row_sums[1:2, :C_MID])
    hook(6)
    sends_leave(1)
    pl.loop(0, 4)(lambda block: turn_weight(1, block))
    sum_two.middle()
    pl.loop(4, 9)(lambda block: turn_weight(1, block))
    hook(7)
    clear_sums()
    norm_coefs(1, sum_two.finish(), row_total)

    def put_rows(pixel, cols, value):
        act_two[pl.ds(pl.multiple_of(pixel * views, 16), views), cols] = value

    activate(hidden_two, slope_two, put_rows, 8)
    cores_arrive(2)

    def weight_three(block):
        return weights[2][block].reshape(C_MID, C_MID)

    sums_low, sums_high = Sum(2), Sum(3)
    half_width = C_IN // 2

    @pl.loop(0, BLOCKS)
    def _(block):
        cols = pl.ds(pl.multiple_of(block * C_MID, LANES), C_MID)

        @pl.loop(0, 3)
        def _(index):
            hidden = dot(act_two[long_rows(0, index), :], weight_three(block))
            hidden_three[long_rows(block, index), :] = hidden.astype(bf16)
            count_in(cols, hidden, hidden)
            hook_in(9, block * 3 + index, 12)

        @pl.when(block == 1)
        def _():
            sums_low.start(row_sums[0:1, :half_width], row_sums[1:2, :half_width])

        @pl.when(block == 2)
        def _():
            sums_low.middle()

    sums_high.start(row_sums[0:1, half_width:], row_sums[1:2, half_width:])
    norm_coefs(2, sums_low.finish(), row_total)

    hook(22)

    pool, pool_slope, pool_bend = mem.pool, mem.pool_slope, mem.pool_bend
    for ref in (pool, pool_slope, pool_bend):
        ref[...] = jnp.zeros_like(ref)

    @pl.loop(0, pieces)
    def _(index):
        stage.copy(features, index, True).wait()

        @pl.loop(0, C_MID // LANES)
        def _(part):
            inner = pl.ds(pl.multiple_of(part * LANES, LANES), LANES)
            cols = piece_columns(index, part)
            slope_row, shift_row = coef[0:1, cols], coef[1:2, cols]
            kept = (pool[:, cols], pool_slope[:, cols], pool_bend[:, cols])
            for pixel in range(SIDE):
                stage_at, hidden_at = stage.rows(index, pixel, views), hidden_rows(index, pixel, views)
                hidden = hidden_three[hidden_at, inner].astype(f32)
                total = hidden * slope_row + shift_row + stage_ref[stage_at, inner].astype(f32)
                value, slope = gelu_pair(total)
                stage_ref[stage_at, inner] = slope.astype(bf16)
                kept = (kept[0] + value, kept[1] + slope, kept[2] + slope * hidden)
            pool[:, cols], pool_slope[:, cols], pool_bend[:, cols] = kept

        stage.save(slope_hbm, index)
        stage.next_load(features, index)

        @pl.when(index == 2)
        def _():
            sums_high.middle()

        @pl.when(index == pieces // 2 - 1)
        def _():
            norm_coefs(2, sums_high.finish(), row_total, half_width)

        hook_in(10, index, pieces)

    stage.last_saves(slope_hbm)
    cores_arrive(3)
    cores_arrive(4)
    for which in range(2, 5):
        sends_leave(which)

    pooled = (pool[...] * (1.0 / PIX)).astype(bf16)
    mem.pooled[...] = pooled
    proj_hidden = dot(pooled, whole(3))
    sum_four = Sum(4)
    sum_four.start(column_sums(proj_hidden), column_sums(proj_hidden * proj_hidden))
    pl.loop(0, 2)(lambda block: turn_weight(3, block))
    sum_four.middle()
    pl.loop(2, 4)(lambda block: turn_weight(3, block))
    totals = sum_four.finish()
    stage.first_loads(slope_hbm)
    norm_coefs(3, totals, view_total)
    value, slope = gelu_pair(proj_hidden * coef[0:1, :P_HID] + coef[1:2, :P_HID])
    proj_act = value.astype(bf16)
    mem.proj_act[...] = proj_act
    mem.proj_slope[...] = slope
    mem.proj_hidden[...] = proj_hidden

    def weight_five(block):
        return weights[4][block // plan.x, block % plan.x]

    parts = P_HID // P_OUT
    embedding = jnp.zeros((views, P_OUT), f32)
    for block in range(parts):
        embedding = embedding + dot_cols(proj_act[:, block * P_OUT : (block + 1) * P_OUT], weight_five(block))

    images = views // 2
    order = jnp.broadcast_to(ins.order[...], (images, views))
    image_row = lax.broadcasted_iota(jnp.int32, (images, views), 0)
    selectors = [(order == 2 * image_row + which).astype(f32) for which in range(2)]
    embeds = [exact_dot(selector, embedding) for selector in selectors]
    moments = [exact_rows(embed, embed) for embed in embeds]
    packed, diagonal = pack_pair(*moments)
    packed, extra = sum_matrix(0, packed, [diagonal] + [column_sums(embed) for embed in embeds])
    moments = unpack_pair(packed, extra[0])
    eye = (
        lax.broadcasted_iota(jnp.int32, (P_OUT, P_OUT), 0) == lax.broadcasted_iota(jnp.int32, (P_OUT, P_OUT), 1)
    ).astype(f32)
    centred, covariances = [], []
    for which in range(2):
        mean = extra[1 + which] / image_total
        centred.append(embeds[which] - mean)
        covariances.append(moments[which] / image_total - exact_rows(mean, mean) + ridge_term * eye)
    inverses = inverse_factors(covariances)
    whitened = [exact_cols(centred[which], inverses[which]) for which in range(2)]
    scalings = [
        lax.rsqrt(jnp.mean(white * white, axis=1, keepdims=True) + norm_epsilon) for white in whitened
    ]
    units = [white * scaling for white, scaling in zip(whitened, scalings)]
    difference = units[0] - units[1]
    objective_row = column_sums(difference * difference) * (1.0 / P_OUT)
    unit_grads = [difference * (2.0 / P_OUT), difference * (-2.0 / P_OUT)]
    white_grads = []
    for which in range(2):
        inner = jnp.mean(whitened[which] * unit_grads[which], axis=1, keepdims=True)
        white_grads.append(
            scalings[which] * unit_grads[which] - whitened[which] * (scalings[which] ** 3 * inner)
        )
    directs = [exact_dot(white_grads[which], inverses[which]) for which in range(2)]
    products = [exact_rows(white_grads[which], whitened[which]) for which in range(2)]
    packed, diagonal = pack_pair(*products)
    packed, extra = sum_matrix(
        1, packed, [diagonal] + [column_sums(grad) for grad in white_grads] + [objective_row]
    )
    products = unpack_pair(packed, extra[0])
    embed_grad = jnp.zeros((views, P_OUT), f32)
    for which in range(2):
        symmetric = exact_rows(inverses[which], exact_dot(products[which], inverses[which]))
        mean_grad = exact_dot(extra[1 + which], inverses[which])
        grad = directs[which] - (exact_dot(centred[which], symmetric) + mean_grad) / image_total
        embed_grad = embed_grad + exact_rows(selectors[which], grad)
    objective_row = extra[3]
    embed_low = embed_grad.astype(bf16)

    proj_act, proj_hidden = mem.proj_act[...], mem.proj_hidden[...]
    act_grad = jnp.concatenate([dot(embed_low, weight_five(block)) for block in range(parts)], axis=1)
    upstream = act_grad * mem.proj_slope[...]
    plain = column_sums(upstream)
    sum_four_back = Sum(5)
    sum_four_back.start(plain, xhat_sum(3, plain, column_sums(upstream * proj_hidden)))
    for block in range(parts):
        weights[4][block // plan.x, block % plan.x] = dot_rows(
            embed_low, proj_act[:, block * P_OUT : (block + 1) * P_OUT]
        ).astype(bf16)
    pl.loop(0, 4)(lambda block: turn_weight(2, block))
    sum_four_back.middle()
    turn_rows(act_two)
    grad_coefs(3, sum_four_back.finish(), view_total)
    four_low = (
        upstream * coef[0:1, :P_HID] - coef[1:2, :P_HID] - proj_hidden * coef[2:3, :P_HID]
    ).astype(bf16)
    @pl.loop(0, BLOCKS)
    def _(block):
        cols = pl.ds(pl.multiple_of(block * C_MID, LANES), C_MID)
        right = jnp.concatenate(
            [
                weights[3][block, :, :, half * C_MID : (half + 1) * C_MID].reshape(C_MID, C_MID)
                for half in range(P_HID // C_MID)
            ],
            axis=0,
        )
        grad = dot(four_low, right) * (1.0 / PIX)
        row_sums[0:1, cols] = column_sums(grad * pool_slope[:, cols])
        row_sums[1:2, cols] = column_sums(grad * pool_bend[:, cols])
        pool_slope[:, cols] = grad

    plain = row_sums[0:1, :]
    sum_three_back = Sum(6)
    sum_three_back.start(plain, xhat_sum(2, plain, row_sums[1:2, :]))
    grad_four = dot_rows(mem.pooled[...], four_low).astype(bf16)
    weights[3][...] = grad_four.reshape(weights[3].shape)
    sum_three_back.middle()
    hook(23)
    grad_coefs(2, sum_three_back.finish(), row_total)
    pool[...] = pool_slope[...] * coef[0:1, :]

    clear_sums()

    @pl.loop(0, pieces)
    def _(index):
        stage.copy(slope_hbm, index, True).wait()
        stage.next_load(slope_hbm, index)

        @pl.loop(0, C_MID // LANES)
        def _(part):
            inner = pl.ds(pl.multiple_of(part * LANES, LANES), LANES)
            cols = piece_columns(index, part)
            spread, shift_row, bend_row = pool[:, cols], coef[1:2, cols], coef[2:3, cols]
            for pixel in range(SIDE):
                hidden_at = hidden_rows(index, pixel, views)
                hidden = hidden_three[hidden_at, inner].astype(f32)
                slope = stage_ref[stage.rows(index, pixel, views), inner].astype(f32)
                hidden_three[hidden_at, inner] = (slope * spread - shift_row - hidden * bend_row).astype(bf16)

        hook_in(11, index, pieces)

    @pl.loop(0, 3)
    def _(index):
        at = long_rows(0, index)
        left = jnp.concatenate([hidden_three[long_rows(block, index), :] for block in range(BLOCKS)], axis=1)
        upstream = dot(left, weights[2][...].reshape(C_IN, C_MID)) * slope_two[at, :].astype(f32)
        slope_two[at, :] = upstream.astype(bf16)
        count_in(slice(0, C_MID), upstream, hidden_two[at, :].astype(f32))
        hook_in(12, index, 3)

    sums = row_sums[0:1, :C_MID], row_sums[1:2, :C_MID]
    sum_two_back = Sum(7)
    sum_two_back.start(sums[0], xhat_sum(1, *sums))

    @pl.loop(0, BLOCKS)
    def _(block):
        grad = dot(turned(act_two), hidden_three[pl.ds(pl.multiple_of(block * rows, 16), tall), :])
        weights[2][block] = grad.astype(bf16).reshape(plan.z, plan.x, -1, C_MID)

        @pl.when(block == 1)
        def _():
            sum_two_back.middle()

        hook_in(13, block, BLOCKS)

    clear_sums()
    grad_coefs(1, sum_two_back.finish(), row_total)

    def apply_grad(hidden_ref, grad_ref, put, site):
        @pl.loop(0, PIX)
        def _(pixel):
            place = pl.ds(pl.multiple_of(pixel * views, 16), views)
            for block in range(C_MID // LANES):
                cols = slice(block * LANES, (block + 1) * LANES)
                grad = (
                    grad_ref[place, cols].astype(f32) * coef[0:1, cols]
                    - coef[1:2, cols]
                    - hidden_ref[place, cols].astype(f32) * coef[2:3, cols]
                )
                put(pixel, cols, grad.astype(bf16))
            hook_in(site, pixel, SIDE, SIDE - 1, SIDE)

    def put_two(pixel, cols, value):
        put_padded(padded_two)(pixel, cols, value)
        slope_two[pl.ds(pl.multiple_of(pixel * views, 16), views), cols] = value

    apply_grad(hidden_two, slope_two, put_two, 14)
    turn_rows(slope_two)
    column_places = [
        hidden_three.at[pl.ds(2 * rows, rows)],
        hidden_three.at[pl.ds(3 * rows, rows)],
        hidden_two.at[pl.ds(0, rows)],
        hidden_three.at[pl.ds(2 * rows, rows)],
    ]
    column_loads = [feature_copy(block, column_places[block]) for block in range(BLOCKS)]
    for copy in column_loads[:3]:
        copy.start()
    def tap_grad(tap):
        down, across = tap // 3, tap % 3
        left = padded_one[pl.ds(down, SIDE), pl.ds(pl.multiple_of(across * views, 16), chunk), :]
        right = jnp.concatenate([left.reshape(rows, C_MID), jnp.zeros((tall - rows, C_MID), bf16)], axis=0)
        grad = dot(turned(slope_two), right).astype(bf16).T
        stage_ref[pl.ds(pl.multiple_of(tap * C_MID, 16), C_MID), :] = grad

    @pl.loop(0, 7)
    def _(tap):
        tap_grad(tap)
        hook_in(15, tap, 7)

    def second_back(first, count):
        at = image_rows(first, count)
        upstream = dot(patch(padded_two, first, count, True), weights[1][...].reshape(9 * C_MID, C_MID))
        upstream = upstream * slope_one[at, :].astype(f32)
        slope_one[at, :] = upstream.astype(bf16)
        count_in(slice(0, C_MID), upstream, hidden_one[at, :].astype(f32))

    @pl.loop(0, 3)
    def _(index):
        second_back(2 * index, 2)
        hook_in(16, index, 3)

    second_back(6, 1)
    hook(16, 3)
    sums = row_sums[0:1, :C_MID], row_sums[1:2, :C_MID]
    sum_one_back = Sum(8)
    sum_one_back.start(sums[0], xhat_sum(0, *sums))

    @pl.loop(7, 9)
    def _(tap):
        tap_grad(tap)

        @pl.when(tap == 7)
        def _():
            sum_one_back.middle()

        hook_in(17, tap, 2, 7)

    grad_coefs(0, sum_one_back.finish(), row_total)

    def put_one(pixel, cols, value):
        put_rows(pixel, cols, value)
        slope_one[pl.ds(pl.multiple_of(pixel * views, 16), views), cols] = value

    apply_grad(hidden_one, slope_one, put_one, 18)
    turn_rows(slope_one)

    def block_grad(block):
        if block != 1:
            column_loads[block].wait()
        start = 3 * rows if block == 1 else 2 * rows
        right = hidden_two[...] if block == 2 else hidden_three[start : start + tall, :]
        grad = dot(turned(slope_one), right).astype(bf16).T
        mem.g1[block] = grad.reshape(plan.x, -1, C_MID)

    column_loads[1].wait()
    tail = Ring(hidden_two, 0)
    for block in range(BLOCKS):
        block_grad(block)
        if block == 0:
            column_loads[3].start()
        hook(19, block)
        if block == 2:
            tail.first_loads(slope_hbm)

    sum_last = Sum(9)

    @pl.loop(0, pieces)
    def _(index):
        block = index // CHUNKS
        back = dot(act_two[span(lax.rem(index, CHUNKS)), :], weights[0][block].reshape(C_MID, C_MID))
        tail.copy(slope_hbm, index, True).wait()
        cols = pl.ds(pl.multiple_of(block * C_MID, LANES), C_MID)
        for pixel in range(SIDE):
            at = tail.rows(index, pixel, views)
            summed = hidden_two[at, :].astype(f32) * pool_slope[:, cols]
            hidden_two[at, :] = (summed + back[pixel * views : (pixel + 1) * views]).astype(bf16)
        tail.save(outs.features_grad, index)
        tail.next_load(slope_hbm, index)
        hook_in(20, index, pieces)
        if plan.inside:

            @pl.when(index == LAST_SUM)
            def _():
                sum_last.start(mem.squares[...], mem.squares[...])

            @pl.when(index == LAST_SUM + 3)
            def _():
                sum_last.middle()

    tail.last_saves(outs.features_grad)
    squares = mem.squares[...]
    if plan.inside:
        squares = sum_last.finish()[0:1]
    norm_grads = mem.norm_grads[...]
    scalars = outs.scalars
    norm_squares = column_sums(norm_grads * norm_grads)
    for place in range(norm_squares.shape[1] // LANES):
        squares = squares + norm_squares[:, place * LANES : (place + 1) * LANES]
    scalars[...] = jnp.zeros_like(scalars)
    squares = jnp.sum(squares, axis=1, keepdims=True)
    norm = jnp.sqrt(squares)
    found = (jnp.sum(objective_row, axis=1, keepdims=True) / image_total, squares, norm, clip_factor(norm))
    for place, value in enumerate(found):
        scalars[place : place + 1, :] = jnp.broadcast_to(value, (1, LANES))
    if plan.inside:
        owner = (dp_me * plan.fsdp + fsdp_me) * LANES
        outs.norm_grad[...] = mem.norm_grads[:, pl.ds(pl.multiple_of(owner, LANES), LANES)]
    else:
        outs.norm_grad[...] = norm_grads
    if not plan.inside:
        stores = [
            pltpu.make_async_copy(gradients[which], outs.grads[which], mem.bulk_send.at[which])
            for which in range(5)
        ]
        for store in stores:
            store.start()
        for store in stores:
            store.wait()


def weight_shapes():
    return (
        (4, 2, 256, C_MID),
        (4, 2, 576, C_MID),
        (BLOCKS, 4, 2, 64, C_MID),
        (4, 2, 256, P_HID),
        (4, 2, P_OUT, P_OUT),
    )


def run_kernel(plan, features, order, shards, norm):
    rows, views = plan.rows, plan.views
    in_vmem = pl.BlockSpec(memory_space=pltpu.VMEM)
    anywhere = pl.BlockSpec(memory_space=pl.ANY)
    shapes = weight_shapes()
    operands = [features, order, norm, *shards]
    in_specs = [anywhere, in_vmem, in_vmem] + [in_vmem if plan.inside else anywhere] * 5
    results = [
        ((rows, C_IN), bf16, anywhere),
        ((rows, C_IN), bf16, anywhere),
        (norm.shape, f32, in_vmem),
        ((8, LANES), f32, in_vmem),
    ]
    for which, shard in enumerate(shards):
        if plan.inside:
            results.append((shard.shape, f32, in_vmem))
        else:
            results.append(((9 * C_MID, C_MID) if which == 1 else shapes[which], bf16, anywhere))
    dma = pltpu.SemaphoreType.DMA

    def sum_room(width):
        return SumRoom(
            pltpu.VMEM((plan.dp, 2, width), f32),
            pltpu.VMEM((plan.fsdp, 2, width), f32),
            dma((plan.dp,)),
            dma((plan.dp,)),
            dma((plan.fsdp,)),
            dma((plan.fsdp,)),
        )

    def matrix_room():
        size = plan.embed_rows
        return MatrixRoom(
            pltpu.VMEM((plan.dp, size, P_OUT), f32),
            pltpu.VMEM((plan.dp, size, P_OUT), f32),
            pltpu.VMEM((plan.fsdp, size, P_OUT), f32),
            pltpu.VMEM((plan.dp, size, P_OUT), f32),
            dma((plan.dp,)),
            dma((plan.dp,)),
            dma((plan.fsdp,)),
            dma((plan.fsdp,)),
            dma((plan.dp,)),
            dma((plan.dp,)),
        )

    scratch = Mem(
        w=[pltpu.VMEM(shape, bf16) for shape in shapes],
        g1=pltpu.VMEM(shapes[0], bf16),
        row_sums=pltpu.VMEM((2, C_IN), f32),
        r3=pltpu.VMEM(shapes[2], bf16),
        r4=pltpu.VMEM(shapes[3], bf16),
        r5=pltpu.VMEM(shapes[4], bf16),
        stage=pltpu.VMEM((max(SLOTS * plan.chunk, 9 * C_MID), C_MID), bf16),
        stage_sem=dma((2, SLOTS)),
        column_sem=dma((BLOCKS,)),
        h1=pltpu.VMEM((rows, C_MID), bf16),
        d1=pltpu.VMEM((plan.tall, C_MID), bf16),
        h2=pltpu.VMEM((plan.tall, C_MID), bf16),
        d2=pltpu.VMEM((plan.tall, C_MID), bf16),
        a2=pltpu.VMEM((plan.tall, C_MID), bf16),
        h3=pltpu.VMEM((3 * rows + plan.tall, C_MID), bf16),
        pad1=pltpu.VMEM((SIDE + 2, (SIDE + 2) * views, C_MID), bf16),
        pad2=pltpu.VMEM((SIDE + 2, (SIDE + 2) * views, C_MID), bf16),
        pool=pltpu.VMEM((views, C_IN), f32),
        pool_slope=pltpu.VMEM((views, C_IN), f32),
        pool_bend=pltpu.VMEM((views, C_IN), f32),
        pooled=pltpu.VMEM((views, C_IN), bf16),
        proj_act=pltpu.VMEM((views, P_HID), bf16),
        proj_slope=pltpu.VMEM((views, P_HID), f32),
        proj_hidden=pltpu.VMEM((views, P_HID), f32),
        coef=pltpu.VMEM((8, C_IN), f32),
        stats=pltpu.VMEM((2, norm_width()), f32),
        norm=pltpu.VMEM((2, norm_width()), f32),
        norm_grads=pltpu.VMEM((2, norm_width()), f32),
        norm_tiles=pltpu.VMEM((plan.dp, plan.fsdp, 2, LANES), f32),
        norm_s0=dma((plan.dp,)),
        norm_r0=dma((plan.dp,)),
        norm_s1=dma((plan.fsdp,)),
        norm_r1=dma((plan.fsdp,)),
        bulk_send=dma((COPIES,)),
        bulk_recv=dma((COPIES,)),
        mats=[matrix_room(), matrix_room()],
        sums=[
            sum_room(width)
            for width in (C_MID, C_MID, C_IN // 2, C_IN // 2, P_HID, C_IN, LANES)
        ],
        squares=pltpu.VMEM((1, LANES), f32),
    )
    values = pl.pallas_call(
        lambda *refs: kernel(plan, *refs),
        out_shape=[jax.ShapeDtypeStruct(shape, kind) for shape, kind, _ in results],
        in_specs=in_specs,
        out_specs=[spec for _, _, spec in results],
        scratch_shapes=[scratch],
        compiler_params=pltpu.CompilerParams(
            collective_id=1, has_side_effects=True, vmem_limit_bytes=63 * 2**20
        ),
        name="train_step",
    )(*operands)
    return Outs(*values[:4], values[4:])


def norm_width():
    return 2 * C_MID + C_IN + P_HID


def clip_factor(norm):
    return clip_level / jnp.maximum(norm, clip_level)


def adam_update(weight, moment_one, moment_two, gradient, step_rate, weight_decay):
    first_new = beta_first * moment_one + (1.0 - beta_first) * gradient
    second_new = beta_second * moment_two + (1.0 - beta_second) * gradient * gradient
    first_hat = first_new / (1.0 - beta_first**STEP)
    second_hat = second_new / (1.0 - beta_second**STEP)
    weight_new = weight - step_rate * (
        first_hat / (jnp.sqrt(second_hat) + adam_epsilon) + weight_decay * weight
    )
    return (weight_new, first_new, second_new)


def finish_kernel(rates, decays, *refs):
    count = len(rates)
    low, scalars = refs[0], refs[1]
    refs = refs[2:]
    given, wide, loss, norm, updated = refs[: 4 * count], *refs[4 * count : 4 * count + 3], refs[4 * count + 3 : -2]
    rooms, sems = refs[-2], refs[-1]
    wide[...] = low[...].astype(f32)
    step = pl.program_id(0)

    def load(place):
        return pltpu.make_async_copy(given[place], rooms[place], sems.at[place])

    def store(place):
        return pltpu.make_async_copy(rooms[place], updated[place], sems.at[place])

    @pl.when(step == 0)
    def _():
        loss[0, 0] = scalars[0, 0]
        norm[0, 0] = scalars[2, 0]
        for place in range(4 * count):
            load(place).start()

    @pl.when(step == 2)
    def _():
        for place in range(4 * count):
            load(place).wait()
        for place in range(count):
            weight, first, second, grad = (rooms[part * count + place][...] for part in range(4))
            found = adam_update(weight, first, second, grad * scalars[3, 0], rates[place], decays[place])
            for part in range(3):
                rooms[part * count + place][...] = found[part]
        for place in range(3 * count):
            store(place).start()

    @pl.when(step == CHUNKS - 1)
    def _():
        for place in range(3 * count):
            store(place).wait()


def finish(features_grad, scalars, masters, firsts, seconds, grads, rates, decays):
    rows = features_grad.shape[0]
    arrays = [*masters, *firsts, *seconds, *grads]
    moving = pl.BlockSpec((rows // CHUNKS, C_IN), lambda index: (index, 0))
    single = pl.BlockSpec(memory_space=pltpu.SMEM)
    anywhere = pl.BlockSpec(memory_space=pl.ANY)
    count = len(masters)
    values = pl.pallas_call(
        lambda *refs: finish_kernel(rates, decays, *refs),
        grid=(CHUNKS,),
        in_specs=[moving, single] + [anywhere] * (4 * count),
        out_specs=[moving, single, single] + [anywhere] * (3 * count),
        out_shape=[jax.ShapeDtypeStruct((rows, C_IN), f32)]
        + [jax.ShapeDtypeStruct((1, 1), f32)] * 2
        + [jax.ShapeDtypeStruct(array.shape, f32) for array in arrays[: 3 * count]],
        scratch_shapes=[
            [pltpu.VMEM(array.shape, f32) for array in arrays],
            pltpu.SemaphoreType.DMA((4 * count,)),
        ],
        compiler_params=pltpu.CompilerParams(vmem_limit_bytes=62 * 2**20),
        name="finish",
    )(features_grad, scalars, *arrays)
    groups = [values[3 + part * count : 3 + (part + 1) * count] for part in range(3)]
    return values[0], values[1].reshape(()), values[2].reshape(()), *groups


def gather_full(weight):
    outer = lax.all_gather(weight.astype(bf16), FSDP, axis=0, tiled=True)
    return lax.all_gather(outer, DP, axis=1, tiled=True)


def scatter_full(gradient):
    inner = lax.psum_scatter(gradient.astype(f32), DP, scatter_dimension=1, tiled=True)
    return lax.psum_scatter(inner, FSDP, scatter_dimension=0, tiled=True)


def body(features, view_order, *state):
    masters, firsts, seconds = state[:6], state[6:12], state[12:18]
    dp_size, fsdp_size = lax.axis_size(DP), lax.axis_size(FSDP)
    views = features.shape[0]
    inside = dp_size == 4 and fsdp_size == 8
    plan = Plan(dp_size, fsdp_size, views, inside)
    pixels = jnp.swapaxes(features, 0, 1).reshape(-1, C_IN)
    norm_params = masters[5]
    shapes = weight_shapes()
    if inside:
        shards = list(masters[:4]) + [masters[4].T]
        norm = norm_params
    else:
        full = [gather_full(weight) for weight in masters[:5]]
        shards = [
            full[0].reshape(shapes[0]),
            full[1].reshape(shapes[1]),
            full[2].reshape(C_MID, BLOCKS, C_MID).swapaxes(0, 1).reshape(shapes[2]),
            full[3].reshape(shapes[3]),
            full[4].reshape(4, 2, P_OUT, P_OUT).swapaxes(2, 3),
        ]
        norm = lax.all_gather(norm_params.astype(bf16), (DP, FSDP), axis=1, tiled=True).astype(f32)
    got = run_kernel(plan, pixels, view_order, shards, norm)
    grads = list(got.grads)
    scalars = got.scalars
    turned = [list(group) for group in (masters, firsts, seconds)]
    if inside:
        owned = grads
        for group in turned:
            group[4] = group[4].T
    else:
        whole_grads = [
            grads[0].reshape(C_IN, C_MID),
            grads[1],
            grads[2].reshape(BLOCKS, C_MID, C_MID).swapaxes(0, 1).reshape(C_MID, C_IN),
            grads[3].reshape(C_IN, P_HID),
            grads[4].swapaxes(2, 3).reshape(P_HID, P_OUT),
        ]
        owned = [scatter_full(gradient) for gradient in whole_grads]
        squares = scalars[1, 0] + lax.psum(sum(jnp.sum(grad * grad) for grad in owned), (DP, FSDP))
        norm_value = jnp.sqrt(squares)
        scalars = scalars.at[2].set(norm_value).at[3].set(clip_factor(norm_value))
    width = norm_params.shape[1]
    if inside:
        owned.append(got.norm_grad)
    else:
        owner = lax.axis_index((DP, FSDP))
        owned.append(lax.dynamic_slice_in_dim(got.norm_grad, owner * width, width, 1))
    step_rates = (
        C_IN ** (-0.5),
        (9 * C_MID) ** (-0.5),
        C_MID ** (-0.5),
        C_IN ** (-0.5),
        P_HID ** (-0.5),
        norm_rate,
    )
    decays = (decay_rate, decay_rate, decay_rate, decay_rate, decay_rate, 0.0)
    input_grad, loss, grad_norm, *updates = finish(
        got.features_grad, scalars, *turned, owned, step_rates, decays
    )
    if inside:
        updates = [[*group[:4], group[4].T, group[5]] for group in updates]
    return (
        loss,
        jnp.swapaxes(input_grad.reshape(PIX, views, C_IN), 0, 1),
        grad_norm,
        *updates[0],
        *updates[1],
        *updates[2],
    )


def solution(mesh):
    views = P((DP, FSDP), None, None)
    split = P(FSDP, DP)
    norm = P(None, (DP, FSDP))
    params = (split,) * 5 + (norm,)
    return jax.shard_map(
        body,
        mesh=mesh,
        in_specs=(views, P((DP, FSDP), None)) + params * 3,
        out_specs=(P(), views, P()) + params * 3,
        check_vma=False,
    )
```

```python
from typing import Any, NamedTuple

import jax
import jax.numpy as jnp
from jax import lax
from jax.experimental import pallas as pl
from jax.experimental.pallas import tpu as pltpu
from jax.sharding import PartitionSpec as P

C_IN = 2048
C_MID = 512
P_HID = 1024
P_OUT = 128
SIDE = 7
STEP = 10
PIX = 49
LANES = 128
BLOCKS = C_IN // C_MID
CHUNKS = SIDE
SLOTS = 7
AHEAD = SLOTS - 2
LAST_SUM = 23
COPIES = 360


highest = lax.Precision.HIGHEST
bf16 = jnp.bfloat16
f32 = jnp.float32
norm_epsilon = 1e-05
ridge_term = 0.01
clip_level = 0.1
beta_first = 0.9
beta_second = 0.999
adam_epsilon = 1e-08
decay_rate = 0.05
norm_rate = 0.5
bell_scale = 0.3989422804014327
root_half = 0.5**0.5
bell_rate = -0.7213475204444817
DP, FSDP = "dp", "fsdp"


def gelu_pair(values):
    below = 0.5 + 0.5 * lax.erf(values * root_half)
    bell = jnp.exp2(values * values * bell_rate)
    return values * below, below + values * bell * bell_scale


def dot(left, right):
    return jnp.dot(left, right, preferred_element_type=f32)


def dot_cols(left, right):
    return lax.dot_general(left, right, (((1,), (1,)), ((), ())), preferred_element_type=f32)


def dot_rows(left, right):
    return lax.dot_general(left, right, (((0,), (0,)), ((), ())), preferred_element_type=f32)


def exact_cols(left, right):
    return lax.dot_general(
        left, right, (((1,), (1,)), ((), ())), precision=highest, preferred_element_type=f32
    )


def exact_rows(left, right):
    return lax.dot_general(
        left, right, (((0,), (0,)), ((), ())), precision=highest, preferred_element_type=f32
    )


def exact_dot(left, right):
    return jnp.dot(left, right, precision=highest, preferred_element_type=f32)


def inverse_factors(matrices):
    row_top = lax.broadcasted_iota(jnp.int32, (8, P_OUT), 0)
    row_all = lax.broadcasted_iota(jnp.int32, (P_OUT, P_OUT), 0)
    col_all = lax.broadcasted_iota(jnp.int32, (P_OUT, P_OUT), 1)

    def one_step(place, left, right):
        scale = lax.rsqrt(left[place : place + 1, place : place + 1])
        left_row = left[place : place + 1, :] * scale
        right_row = right[place : place + 1, :] * scale
        column = left[:, place : place + 1] * scale
        left = left - column * left_row
        right = right - column * right_row
        here = row_top == place
        left = jnp.concatenate([jnp.where(here, 0.0, left[:8]), left[8:]], axis=0)
        right = jnp.concatenate(
            [jnp.where(here, jnp.broadcast_to(right_row, (8, P_OUT)), right[:8]), right[8:]], axis=0
        )
        return left, right

    def panel(_, pairs):
        pairs = list(pairs)
        for place in range(8):
            for which in range(len(pairs)):
                pairs[which] = one_step(place, *pairs[which])
        return tuple(
            (
                pltpu.roll(jnp.concatenate([left[8:], left[:8]], axis=0), P_OUT - 8, 1),
                jnp.concatenate([right[8:], right[:8]], axis=0),
            )
            for left, right in pairs
        )

    pairs = tuple((matrix, (row_all == col_all).astype(f32)) for matrix in matrices)
    return [right for _, right in lax.fori_loop(0, P_OUT // 8, panel, pairs)]


def pack_pair(first, second):
    row = lax.broadcasted_iota(jnp.int32, (P_OUT, P_OUT), 0)
    col = lax.broadcasted_iota(jnp.int32, (P_OUT, P_OUT), 1)
    packed = jnp.where(row >= col, first, second.T)
    diagonal = jnp.sum(jnp.where(row == col, second, 0.0), axis=0, keepdims=True)
    return packed, diagonal


def unpack_pair(packed, diagonal):
    row = lax.broadcasted_iota(jnp.int32, (P_OUT, P_OUT), 0)
    col = lax.broadcasted_iota(jnp.int32, (P_OUT, P_OUT), 1)
    turned = packed.T
    first = jnp.where(row >= col, packed, turned)
    second = jnp.where(row < col, packed, jnp.where(row == col, diagonal, turned))
    return first, second


GATHER_AT = {
    (0, 1): 1,
    (0, 3): 1,
    (1, 0): 1,
    (2, 0): 1,
    (4, 0): 5,
    (5, 0): 1,
    (5, 1): 1,
    (5, 2): 1,
    (5, 4): 1,
    (5, 5): 1,
    (5, 6): 1,
    (7, 0): 1,
    (8, 6): 1,
    (9, 2): 1,
    (9, 5): 1,
    (9, 8): 1,
    (21, 0): 7,
}
REDUCE_AT = {
    (11, 3): ((4, 0, 1), (3, 0, 1)),
    (11, 11): ((3, 1, 1), (4, 0, 2)),
    (11, 20): ((3, 0, 2), (3, 2, 1)),
    (12, 0): ((3, 1, 2), (3, 0, 3), (4, 0, 3)),
    (12, 1): ((3, 3, 1),),
    (12, 2): ((3, 2, 2), (3, 1, 3)),
    (13, 0): ((3, 3, 2),),
    (13, 2): ((3, 2, 3),),
    (13, 3): ((3, 3, 3), (2, 0, 0), (2, 1, 0), (2, 2, 0), (2, 3, 0)),
    (14, 6): ((4, 9, 4), (2, 0, 1), (2, 1, 1)),
    (15, 2): ((1, 0, 0), (2, 0, 2), (2, 2, 1), (2, 3, 1)),
    (15, 4): ((1, 1, 0), (1, 0, 1), (2, 1, 2), (2, 0, 3)),
    (15, 6): ((1, 2, 0), (2, 2, 2), (2, 3, 2), (1, 1, 1), (2, 1, 3), (3, 9, 4)),
    (16, 0): ((1, 0, 2), (1, 2, 1), (2, 2, 3), (2, 3, 3)),
    (16, 1): ((1, 1, 2), (2, 9, 4), (1, 0, 3)),
    (16, 2): ((1, 2, 2), (1, 1, 3)),
    (17, 1): ((1, 3, 0), (1, 2, 3)),
    (18, 6): ((1, 3, 1),),
    (19, 0): ((0, 0, 0), (1, 3, 2)),
    (19, 1): ((0, 1, 0), (0, 0, 1), (1, 3, 3)),
    (19, 2): ((0, 2, 0), (0, 1, 1), (0, 0, 2)),
    (19, 3): ((0, 3, 0), (0, 2, 1), (0, 1, 2), (0, 0, 3), (1, 9, 4)),
    (20, 2): ((0, 3, 1), (0, 2, 2), (0, 1, 3)),
    (20, 8): ((0, 3, 2), (0, 2, 3)),
    (20, 13): ((0, 3, 3),),
    (20, 20): ((0, 9, 4),),
    (23, 0): ((4, 0, 0), (3, 0, 0), (3, 1, 0), (3, 2, 0), (3, 3, 0)),
}


class Ins(NamedTuple):
    features: Any
    order: Any
    norm: Any
    shards: Any


class Outs(NamedTuple):
    slope: Any
    features_grad: Any
    norm_grad: Any
    scalars: Any
    grads: Any


class SumRoom(NamedTuple):
    dp: Any
    fsdp: Any
    s0: Any
    r0: Any
    s1: Any
    r1: Any


class MatrixRoom(NamedTuple):
    pack: Any
    dp: Any
    fsdp: Any
    all: Any
    s0: Any
    r0: Any
    s1: Any
    r1: Any
    s2: Any
    r2: Any


class Mem(NamedTuple):
    w: Any
    g1: Any
    row_sums: Any
    r3: Any
    r4: Any
    r5: Any
    stage: Any
    stage_sem: Any
    column_sem: Any
    h1: Any
    d1: Any
    h2: Any
    d2: Any
    a2: Any
    h3: Any
    pad1: Any
    pad2: Any
    pool: Any
    pool_slope: Any
    pool_bend: Any
    pooled: Any
    proj_act: Any
    proj_slope: Any
    proj_hidden: Any
    coef: Any
    stats: Any
    norm: Any
    norm_grads: Any
    norm_tiles: Any
    norm_s0: Any
    norm_r0: Any
    norm_s1: Any
    norm_r1: Any
    bulk_send: Any
    bulk_recv: Any
    mats: Any
    sums: Any
    squares: Any


class Plan:
    def __init__(self, dp_size, fsdp_size, views, inside):
        self.dp = dp_size
        self.fsdp = fsdp_size
        self.devices = dp_size * fsdp_size
        self.views = views
        self.rows = views * PIX
        self.tall = -(-self.rows // C_MID) * C_MID
        self.chunk = views * SIDE
        self.inside = inside
        self.z = 4
        self.x = 2
        self.half = (128, 288, 32, 128, 16)
        self.width = (128, 128, 512, 256, 128)
        piece = P_OUT + 8
        self.embed_rows = -(-piece // (8 * dp_size)) * 8


def kernel(plan, *refs):
    ins, outs, mem = Ins(*refs[:3], refs[3:8]), Outs(*refs[8:12], refs[12:17]), refs[17]
    views, chunk, rows, tall = plan.views, plan.chunk, plan.rows, plan.tall
    row_total = float(rows * plan.devices)
    view_total = float(views * plan.devices)
    image_total = float(views * plan.devices // 2)
    dp_me, fsdp_me = lax.axis_index(DP), lax.axis_index(FSDP)
    y_me, c_me = dp_me // 2, dp_me % 2
    z_me, x_me = fsdp_me // 2, fsdp_me % 2
    y_other, c_other, x_other = 1 - y_me, 1 - c_me, 1 - x_me

    barrier = pltpu.get_barrier_semaphore()

    @pl.loop(1, plan.dp)
    def _(step):
        pl.semaphore_signal(
            barrier, 1, device_id={DP: lax.rem(dp_me + step, plan.dp)}, device_id_type=pl.DeviceIdType.MESH
        )

    @pl.loop(1, plan.fsdp)
    def _(step):
        pl.semaphore_signal(
            barrier, 1, device_id={FSDP: lax.rem(fsdp_me + step, plan.fsdp)}, device_id_type=pl.DeviceIdType.MESH
        )

    pl.semaphore_wait(barrier, plan.dp + plan.fsdp - 2)

    def share(axis, size, me, source_of, slots, send, recv):
        def outgoing(step):
            partner = lax.rem(me + step, size)
            return pltpu.make_async_remote_copy(
                src_ref=source_of(partner),
                dst_ref=slots.at[me],
                send_sem=send.at[step],
                recv_sem=recv.at[me],
                device_id={axis: partner},
                device_id_type=pl.DeviceIdType.MESH,
            )

        def incoming(step):
            source = lax.rem(me + step, size)
            return pltpu.make_async_remote_copy(
                src_ref=slots.at[source],
                dst_ref=slots.at[source],
                send_sem=send.at[step],
                recv_sem=recv.at[source],
                device_id={axis: source},
                device_id_type=pl.DeviceIdType.MESH,
            )

        def start():
            pl.loop(1, size)(lambda step: outgoing(step).start())

        def wait():
            pl.loop(1, size)(lambda step: incoming(step).wait_recv())
            pl.loop(1, size)(lambda step: outgoing(step).wait_send())

        return start, wait

    def add_slots(slots, size):
        total = slots[0]
        for place in range(1, size):
            total = total + slots[place]
        return total

    class Sum:
        def __init__(self, which):
            part = mem.sums[(0, 1, 2, 3, 4, 4, 5, 0, 1, 6)[which]]
            self.dp_slots, self.fsdp_slots = part.dp, part.fsdp
            self.dp_copy = share(
                DP, plan.dp, dp_me, lambda _: self.dp_slots.at[dp_me], self.dp_slots, part.s0, part.r0
            )
            self.fsdp_copy = share(
                FSDP, plan.fsdp, fsdp_me, lambda _: self.fsdp_slots.at[fsdp_me], self.fsdp_slots, part.s1, part.r1
            )

        def start(self, *values):
            for place, value in enumerate(values):
                self.dp_slots[dp_me, place : place + 1, :] = value
            self.dp_copy[0]()

        def middle(self):
            self.dp_copy[1]()
            self.fsdp_slots[fsdp_me] = add_slots(self.dp_slots, plan.dp)
            self.fsdp_copy[0]()

        def finish(self):
            self.fsdp_copy[1]()
            return add_slots(self.fsdp_slots, plan.fsdp)

        def all(self, *values):
            self.start(*values)
            self.middle()
            return self.finish()

    def sum_matrix(which, matrix, extra):
        part = mem.mats[which]
        size = plan.embed_rows
        pack = part.pack
        flat = jnp.concatenate(
            [matrix] + extra + [jnp.zeros((size * plan.dp - P_OUT - len(extra), P_OUT), f32)], axis=0
        )
        for place in range(plan.dp):
            pack[place] = flat[place * size : (place + 1) * size]
        start, wait = share(DP, plan.dp, dp_me, lambda to: pack.at[to], part.dp, part.s0, part.r0)
        start()
        part.dp[dp_me] = pack[dp_me]
        wait()
        part.fsdp[fsdp_me] = add_slots(part.dp, plan.dp)
        start, wait = share(
            FSDP, plan.fsdp, fsdp_me, lambda _: part.fsdp.at[fsdp_me], part.fsdp, part.s1, part.r1
        )
        start()
        wait()
        part.all[dp_me] = add_slots(part.fsdp, plan.fsdp)
        start, wait = share(
            DP, plan.dp, dp_me, lambda _: part.all.at[dp_me], part.all, part.s2, part.r2
        )
        start()
        wait()
        total = jnp.concatenate([part.all[place] for place in range(plan.dp)], axis=0)
        return total[:P_OUT], [total[P_OUT + place : P_OUT + place + 1] for place in range(len(extra))]

    weights = mem.w
    everything = slice(None)

    def row_span(which, half):
        if isinstance(half, tuple):
            return half
        size = plan.half[which]
        if half is None:
            return 0, 2 * size
        return half * size, size

    def aligned(start, size):
        return pl.ds(start if isinstance(start, int) else pl.multiple_of(start, 16), size)

    def column_span(which, dp_index):
        width = plan.width[which]
        return pl.ds(pl.multiple_of(dp_index * width, width), width)

    def places(which, z_index, x_index, dp_index, half, flat=True):
        start, size = row_span(which, half)
        if which == 1 and flat:
            z_list = range(plan.z) if z_index is None else [z_index]
            x_list = range(plan.x) if x_index is None else [x_index]
            return [
                (
                    pl.ds(pl.multiple_of((z_one * plan.x + x_one) * 576 + start, 16), size),
                    column_span(which, dp_index),
                )
                for z_one in z_list
                for x_one in x_list
            ]
        z_one = everything if z_index is None else z_index
        x_one = everything if x_index is None else x_index
        if which == 2:
            return [(dp_index, z_one, x_one, aligned(start, size), everything)]
        if which == 4:
            return [(z_one, x_one, pl.ds(pl.multiple_of(dp_index * 32 + start, 16), size), everything)]
        return [(z_one, x_one, aligned(start, size), column_span(which, dp_index))]

    recv_parts = {
        1: lambda index: mem.h3.at[index],
        0: lambda index: mem.r4.at[index],
        2: lambda index: mem.r3.at[index],
        3: lambda index: mem.r4.at[index],
        4: lambda index: mem.r5.at[index],
    }

    counter = [0]

    class Batch:
        def __init__(self, sources, targets, landings, axis, partner):
            base = counter[0]
            counter[0] += len(sources)
            send, recv = mem.bulk_send, mem.bulk_recv
            self.out = [
                pltpu.make_async_remote_copy(
                    src_ref=source,
                    dst_ref=target,
                    send_sem=send.at[base + place],
                    recv_sem=recv.at[base + place],
                    device_id={axis: partner},
                    device_id_type=pl.DeviceIdType.MESH,
                )
                for place, (source, target) in enumerate(zip(sources, targets))
            ]
            self.come = [
                pltpu.make_async_remote_copy(
                    src_ref=landing,
                    dst_ref=landing,
                    send_sem=send.at[base + place],
                    recv_sem=recv.at[base + place],
                    device_id={axis: partner},
                    device_id_type=pl.DeviceIdType.MESH,
                )
                for place, landing in enumerate(landings)
            ]

        def start(self):
            for copy in self.out:
                copy.start()

        def arrive(self):
            for copy in self.come:
                copy.wait_recv()

        def leave(self):
            for copy in self.out:
                copy.wait_send()

    class LineBatch:
        def __init__(self, source_of, target_of, landing_of):
            base = counter[0]
            counter[0] += plan.z
            send, recv = mem.bulk_send, mem.bulk_recv
            self.out, self.come = [], []
            for step in range(1, plan.z):
                z_to = (z_me + step) % plan.z
                self.out.append(
                    pltpu.make_async_remote_copy(
                        src_ref=source_of(z_to),
                        dst_ref=target_of(z_to),
                        send_sem=send.at[base + step],
                        recv_sem=recv.at[base + z_me],
                        device_id={FSDP: z_to * plan.x + x_me},
                        device_id_type=pl.DeviceIdType.MESH,
                    )
                )
                self.come.append(
                    pltpu.make_async_remote_copy(
                        src_ref=landing_of(z_to),
                        dst_ref=landing_of(z_to),
                        send_sem=send.at[base + step],
                        recv_sem=recv.at[base + z_to],
                        device_id={FSDP: z_to * plan.x + x_me},
                        device_id_type=pl.DeviceIdType.MESH,
                    )
                )

        start, arrive, leave = Batch.start, Batch.arrive, Batch.leave

    def pick(ref, indexes):
        return [ref.at[index] for index in indexes]

    def own_dp(y_index, c_index):
        return y_index * 2 + c_index

    x_partner = z_me * plan.x + x_other
    y_partner = own_dp(y_other, c_me)
    c_partner = own_dp(y_me, c_other)
    dp_far = own_dp(y_other, c_other)

    class Gather:
        def __init__(self, which, start, size):
            ref = weights[which]
            self.which, self.rows = which, (start, size)
            both, low, high = (start, size), (start, size // 2), (start + size // 2, size // 2)

            def at(*index):
                return pick(ref, places(which, *index, False))

            own = at(z_me, x_me, dp_me, both)[0]
            self.line = LineBatch(
                lambda _: own, lambda _: own, lambda z_from: at(z_from, x_me, dp_me, both)[0]
            )
            sent, come = at(None, x_me, dp_me, low), at(None, x_other, dp_me, low)
            x_first = Batch(sent, sent, come, FSDP, x_partner)
            sent, come = at(None, x_me, dp_me, high), at(None, x_me, y_partner, high)
            y_first = Batch(sent, sent, come, DP, y_partner)
            sent, come = at(None, None, dp_me, low), at(None, None, y_partner, low)
            y_second = Batch(sent, sent, come, DP, y_partner)
            sent = at(None, x_me, dp_me, high) + at(None, x_me, y_partner, high)
            come = at(None, x_other, dp_me, high) + at(None, x_other, y_partner, high)
            x_second = Batch(sent, sent, come, FSDP, x_partner)
            sent = at(None, None, dp_me, both) + at(None, None, y_partner, both)
            come = at(None, None, c_partner, both) + at(None, None, dp_far, both)
            core = Batch(sent, sent, come, DP, c_partner)
            self.stages = ((self.line,), (x_first, y_first), (y_second, x_second), (core,))

        def put_own(self):
            index = places(self.which, z_me, x_me, dp_me, self.rows, False)[0]
            shard = ins.shards[self.which][self.rows[0] : self.rows[0] + self.rows[1], :]
            weights[self.which][index] = shard.astype(bf16)

        def start(self, stage):
            for batch in self.stages[stage]:
                batch.start()

        def arrive(self, stage):
            for batch in self.stages[stage]:
                batch.arrive()

        def leave(self):
            for stage in self.stages:
                for batch in stage:
                    batch.leave()

    class Piece:
        def __init__(self, which, ref, room, z_index):
            def at(*index):
                return pick(ref, places(which, z_index, *index))

            def land(*index):
                return [room(index_one) for index_one in places(which, z_index, *index)]

            self.z = z_index
            self.core = Batch(
                at(None, c_partner, None) + at(None, dp_far, None),
                land(None, c_partner, None) + land(None, dp_far, None),
                land(None, dp_me, None) + land(None, y_partner, None),
                DP,
                c_partner,
            )
            self.y_first = Batch(
                at(None, y_partner, 0), land(None, dp_far, 0), land(None, c_partner, 0), DP, y_partner
            )
            self.x_first = Batch(
                at(x_other, dp_me, 1) + at(x_other, y_partner, 1),
                land(x_other, c_partner, 1) + land(x_other, dp_far, 1),
                land(x_me, c_partner, 1) + land(x_me, dp_far, 1),
                FSDP,
                x_partner,
            )
            self.x_second = Batch(
                at(x_other, dp_me, 0), land(x_other, dp_far, 0), land(x_me, dp_far, 0), FSDP, x_partner
            )
            self.y_second = Batch(
                at(x_me, y_partner, 1), land(x_other, dp_far, 1), land(x_other, c_partner, 1), DP, y_partner
            )

    class Reduce:
        def __init__(self, which, ref, cut):
            self.which, self.ref, self.room = which, ref, recv_parts[which]
            self.pieces = [
                Piece(which, ref, self.room, z_index) for z_index in (range(plan.z) if cut else [None])
            ]
            self.base = counter[0]
            counter[0] += plan.z

        def line_copy(self, z_to):
            return pltpu.make_async_remote_copy(
                src_ref=self.ref.at[places(self.which, z_to, x_me, dp_me, None)[0]],
                dst_ref=self.room(places(self.which, z_me, x_other, dp_far, None)[0]),
                send_sem=mem.bulk_send.at[self.base + z_to],
                recv_sem=mem.bulk_recv.at[self.base + z_me],
                device_id={FSDP: z_to * plan.x + x_me},
                device_id_type=pl.DeviceIdType.MESH,
            )

        def line_room(self, z_from):
            return self.room(places(self.which, z_from, x_other, dp_far, None)[0])

        def add(self, z_index, pairs):
            step = min(32, row_span(self.which, pairs[0][0][2])[1])

            def one(z_one, offset):
                for here, there in pairs:
                    rows_here = (row_span(self.which, here[2])[0] + offset, step)
                    rows_there = (row_span(self.which, there[2])[0] + offset, step)
                    for x_step in range(plan.x) if here[0] is None else [None]:
                        x_here = x_step if here[0] is None else here[0]
                        x_there = x_step if there[0] is None else there[0]
                        index = places(self.which, z_one, x_here, here[1], rows_here)[0]
                        other = places(self.which, z_one, x_there, there[1], rows_there)[0]
                        total = self.ref[index].astype(f32) + self.room(other)[...].astype(f32)
                        self.ref[index] = total.astype(bf16)

            @pl.loop(0, row_span(self.which, pairs[0][0][2])[1] // step)
            def _(part):
                if z_index is None:
                    pl.loop(0, plan.z)(lambda z_one: one(z_one, part * step))
                else:
                    one(z_index, part * step)

        def core_start(self, place=0):
            if plan.inside:
                self.pieces[place].core.start()

        def core_add(self, place=0):
            if plan.inside:
                piece = self.pieces[place]
                piece.core.arrive()
                self.add(piece.z, [((None, dp_me, None),) * 2, ((None, y_partner, None),) * 2])
                piece.y_first.start()
                piece.x_first.start()

        def first_add(self, place=0):
            if plan.inside:
                piece = self.pieces[place]
                piece.y_first.arrive()
                self.add(piece.z, [((None, dp_me, 0), (None, c_partner, 0))])
                piece.x_second.start()
                piece.x_first.arrive()
                self.add(
                    piece.z, [((x_me, dp_me, 1), (x_me, c_partner, 1)), ((x_me, y_partner, 1), (x_me, dp_far, 1))]
                )
                piece.y_second.start()

        def second_add(self, place=0):
            if plan.inside:
                piece = self.pieces[place]
                piece.x_second.arrive()
                piece.y_second.arrive()
                self.add(
                    piece.z, [((x_me, dp_me, 0), (x_me, dp_far, 0)), ((x_me, dp_me, 1), (x_other, c_partner, 1))]
                )
                if piece.z is None:
                    for step in range(1, plan.z):
                        self.line_copy((z_me + step) % plan.z).start()
                else:

                    @pl.when(z_me != piece.z)
                    def _():
                        self.line_copy(piece.z).start()

        def finish(self):
            if not plan.inside:
                return
            total = self.ref[places(self.which, z_me, x_me, dp_me, None)[0]].astype(f32)
            for step in range(1, plan.z):
                z_from = (z_me + step) % plan.z
                room = self.line_room(z_from)
                pltpu.make_async_remote_copy(
                    src_ref=room,
                    dst_ref=room,
                    send_sem=mem.bulk_send.at[self.base + z_from],
                    recv_sem=mem.bulk_recv.at[self.base + z_from],
                    device_id={FSDP: z_from * plan.x + x_me},
                    device_id_type=pl.DeviceIdType.MESH,
                ).wait_recv()
                total = total + room[...].astype(f32)
            outs.grads[self.which][...] = total
            squares = jnp.sum(total * total, axis=0, keepdims=True)
            folded = squares[:, :LANES]
            for place in range(1, squares.shape[1] // LANES):
                folded = folded + squares[:, place * LANES : (place + 1) * LANES]
            mem.squares[...] += folded
            for step in range(1, plan.z):
                self.line_copy((z_me + step) % plan.z).wait_send()
            for piece in self.pieces:
                for batch in (piece.core, piece.y_first, piece.x_first, piece.x_second, piece.y_second):
                    batch.leave()

    gathers, steps = [], []
    if plan.inside:
        for which, cuts in enumerate((2, 3, 1, 2, 1)):
            size = 2 * plan.half[which] // cuts
            gathers += [Gather(which, cut * size, size) for cut in range(cuts)]

    def line_step(place):
        gathers[place].arrive(0)
        gathers[place].start(1)
        if place + 1 < len(gathers):
            gathers[place + 1].start(0)

    def first_step(place):
        gathers[place].arrive(1)
        gathers[place].start(2)

    def second_step(place):
        gathers[place].arrive(2)
        gathers[place].start(3)

    for place in range(len(gathers)):
        steps.append((line_step, place))
        if place > 0:
            steps.append((second_step, place - 1))
        steps.append((first_step, place))
    if plan.inside:
        steps.append((second_step, len(gathers) - 1))

    def take(count):
        taken, steps[:] = steps[:count], steps[count:]
        return [lambda one=one: one[0](one[1]) for one in taken]

    def moves(site, item):
        found = take(GATHER_AT.get((site, item), 0)) if plan.inside else []
        for which, piece, kind in REDUCE_AT.get((site, item), ()):
            one = reduces[which]
            found.append(
                one.finish
                if kind == 4
                else lambda one=one, kind=kind, piece=piece: (
                    one.core_start,
                    one.core_add,
                    one.first_add,
                    one.second_add,
                )[kind](piece)
            )
        return found

    def hook(site, item=0):
        for move in moves(site, item):
            move()

    def hook_in(site, index, count, first=0, stride=1):
        for item in range(count):
            found = moves(site, item)
            if found and plan.inside:

                @pl.when(index == first + item * stride)
                def _(found=found):
                    for move in found:
                        move()

    def cores_arrive(which):
        for one in gathers:
            if one.which == which:
                one.arrive(3)

    gradients = [mem.g1, mem.stage.at[pl.ds(0, 9 * C_MID)], weights[2], weights[3], weights[4]]
    reduces = [Reduce(which, gradients[which], which < 4) for which in range(5)]
    assert counter[0] <= COPIES
    mem.squares[...] = jnp.zeros((1, LANES), f32)

    if plan.inside:
        gathers[0].put_own()
        gathers[0].start(0)
        for one in gathers[1:]:
            one.put_own()
        tiles = mem.norm_tiles
        tiles[dp_me, fsdp_me] = ins.norm[...].astype(bf16).astype(f32)
        norm_dp = share(
            DP, plan.dp, dp_me, lambda _: tiles.at[dp_me, fsdp_me], tiles.at[:, fsdp_me], mem.norm_s0, mem.norm_r0
        )
        norm_dp[0]()
    else:
        loads = [
            pltpu.make_async_copy(ins.shards[which], weights[which], mem.bulk_send.at[which])
            for which in range(5)
        ]
        for load in loads:
            load.start()

    pieces = BLOCKS * CHUNKS

    def hidden_rows(index, pixel=0, count=chunk):
        return pl.ds(pl.multiple_of(index * chunk + pixel * views, 16), count)

    class Ring:
        def __init__(self, ref, start):
            self.ref, self.base = ref, start

        def rows(self, index, pixel=0, count=chunk):
            return pl.ds(
                pl.multiple_of(self.base + lax.rem(index, SLOTS) * chunk + pixel * views, 16), count
            )

        def copy(self, array, index, into):
            block, place = index // CHUNKS, lax.rem(index, CHUNKS)
            outer = array.at[
                pl.ds(pl.multiple_of(place * chunk, 16), chunk),
                pl.ds(pl.multiple_of(block * C_MID, LANES), C_MID),
            ]
            inner = self.ref.at[self.rows(index)]
            source, target = (outer, inner) if into else (inner, outer)
            return pltpu.make_async_copy(
                source, target, mem.stage_sem.at[0 if into else 1, lax.rem(index, SLOTS)]
            )

        def first_loads(self, array):
            for index in range(AHEAD):
                self.copy(array, index, True).start()

        def next_load(self, array, index):
            @pl.when(index + AHEAD < pieces)
            def _():
                self.copy(array, index + AHEAD, True).start()

        def save(self, array, index):
            self.copy(array, index, False).start()

            @pl.when(index >= 1)
            def _():
                self.copy(array, index - 1, False).wait()

        def last_saves(self, array):
            self.copy(array, pieces - 1, False).wait()

    stage_ref = mem.stage
    stage = Ring(stage_ref, 0)

    def piece_columns(index, part):
        return pl.ds(pl.multiple_of(index // CHUNKS * C_MID + part * LANES, LANES), LANES)

    features, slope_hbm = ins.features, outs.slope
    hidden_three = mem.h3

    def feature_copy(block, target):
        return pltpu.make_async_copy(
            features.at[:, pl.ds(block * C_MID, C_MID)], target, mem.column_sem.at[block]
        )

    feature_loads = [
        feature_copy(block, hidden_three.at[pl.ds(block * rows, rows)]) for block in range(BLOCKS)
    ]
    for copy in feature_loads:
        copy.start()
    stage.first_loads(features)

    padded_one, padded_two = mem.pad1, mem.pad2
    for padded in (padded_one, padded_two):
        for edge in (0, SIDE + 1):
            padded[edge] = jnp.zeros((padded.shape[1], C_MID), bf16)
        for edge in (0, SIDE + 1):
            padded[:, pl.ds(edge * views, views), :] = jnp.zeros((SIDE + 2, views, C_MID), bf16)
    rest = jnp.zeros((tall - rows, C_MID), bf16)
    for ref, end in ((mem.d1, rows), (mem.h2, rows), (mem.d2, rows), (mem.a2, rows), (hidden_three, BLOCKS * rows)):
        ref[end : end + tall - rows, :] = rest

    if plan.inside:
        norm_dp[1]()
        norm_out = []
        norm_in = []
        for step in range(1, plan.fsdp):
            partner = (fsdp_me + step) % plan.fsdp
            norm_out.append(
                pltpu.make_async_remote_copy(
                    src_ref=tiles.at[:, fsdp_me],
                    dst_ref=tiles.at[:, fsdp_me],
                    send_sem=mem.norm_s1.at[step],
                    recv_sem=mem.norm_r1.at[fsdp_me],
                    device_id={FSDP: partner},
                    device_id_type=pl.DeviceIdType.MESH,
                )
            )
            norm_in.append(
                pltpu.make_async_remote_copy(
                    src_ref=tiles.at[:, partner],
                    dst_ref=tiles.at[:, partner],
                    send_sem=mem.norm_s1.at[step],
                    recv_sem=mem.norm_r1.at[partner],
                    device_id={FSDP: partner},
                    device_id_type=pl.DeviceIdType.MESH,
                )
            )
        for copy in norm_out:
            copy.start()
        hook(21)
        for copy in norm_in:
            copy.wait_recv()
        for copy in norm_out:
            copy.wait_send()
        norm_all = mem.norm
        for dp_one in range(plan.dp):
            for fsdp_one in range(plan.fsdp):
                start = (dp_one * plan.fsdp + fsdp_one) * LANES
                norm_all[:, start : start + LANES] = tiles[dp_one, fsdp_one]
    else:
        for copy in loads:
            copy.wait()
        norm_all = mem.norm
        norm_all[...] = ins.norm[...]

    starts = (0, C_MID, 2 * C_MID, 2 * C_MID + C_IN, 2 * C_MID + C_IN + P_HID)

    def gain(layer):
        return norm_all[0:1, starts[layer] : starts[layer + 1]]

    coef, stats = mem.coef, mem.stats

    def norm_coefs(layer, totals, count, low=0):
        width = totals.shape[1]
        here, there = slice(low, low + width), slice(starts[layer] + low, starts[layer] + low + width)
        mean = totals[0:1] / count
        scaling = lax.rsqrt(totals[1:2] / count - mean * mean + norm_epsilon)
        slope = scaling * norm_all[0:1, there]
        stats[0:1, there] = mean
        stats[1:2, there] = scaling
        coef[0:1, here] = slope
        coef[1:2, here] = norm_all[1:2, there] - mean * slope

    def grad_coefs(layer, totals, count):
        width = starts[layer + 1] - starts[layer]
        mean = stats[0:1, starts[layer] : starts[layer + 1]]
        scaling = stats[1:2, starts[layer] : starts[layer + 1]]
        mem.norm_grads[0:1, starts[layer] : starts[layer + 1]] = totals[1:2]
        mem.norm_grads[1:2, starts[layer] : starts[layer + 1]] = totals[0:1]
        slope = scaling * gain(layer)
        bend = slope * scaling * totals[1:2] / count
        coef[0:1, :width] = slope
        coef[1:2, :width] = slope * totals[0:1] / count - mean * bend
        coef[2:3, :width] = bend

    def xhat_sum(layer, plain, product):
        mean = stats[0:1, starts[layer] : starts[layer + 1]]
        scaling = stats[1:2, starts[layer] : starts[layer + 1]]
        return scaling * (product - mean * plain)

    zero_row = jnp.zeros((1, C_MID), f32)

    def column_sums(value):
        return jnp.sum(value, axis=0, keepdims=True)

    def whole(which):
        value = weights[which][...]
        return value.reshape(-1, value.shape[-1])

    row_sums = mem.row_sums

    def clear_sums():
        row_sums[...] = jnp.zeros_like(row_sums)

    def count_in(cols, value, other):
        row_sums[0:1, cols] += column_sums(value)
        row_sums[1:2, cols] += column_sums(value * other)

    def own_columns(side):
        core = (c_me + side) % 2
        return [
            pl.ds(pl.multiple_of(half * (C_MID // 2) + core * LANES, LANES), LANES) for half in range(2)
        ]

    def turn_rows(ref):
        @pl.loop(0, tall // C_MID)
        def _(block):
            at = pl.ds(pl.multiple_of(block * C_MID, C_MID), C_MID)
            ref[at, :] = ref[at, :].T

    def turned(ref):
        return jnp.concatenate([ref[start : start + C_MID, :] for start in range(0, tall, C_MID)], axis=1)

    def sends_leave(which):
        for one in gathers:
            if one.which == which:
                one.leave()

    def turn_weight(which, block):
        ref = weights[which]
        if which == 1:
            groups = [block * 8 + group for group in range(8)]
            ats = [
                (group // 18, group // 9 % 2, pl.ds(pl.multiple_of(group % 9 * 64, 64), 64), everything)
                for group in groups
            ]
            value = jnp.concatenate([ref[at] for at in ats], axis=0).T
            for place, at in enumerate(ats):
                ref[at] = value[place * 64 : (place + 1) * 64, :]
        elif which == 3:
            for half in range(P_HID // C_MID):
                cols = slice(half * C_MID, (half + 1) * C_MID)
                value = ref[block, :, :, cols]
                ref[block, :, :, cols] = value.reshape(C_MID, C_MID).T.reshape(value.shape)
        else:
            value = ref[block]
            ref[block] = value.reshape(C_MID, C_MID).T.reshape(value.shape)

    hidden_one, slope_one = mem.h1, mem.d1
    hidden_two, slope_two = mem.h2, mem.d2
    act_two = mem.a2
    def span(index):
        return pl.ds(pl.multiple_of(index * chunk, 16), chunk)

    def block_rows(block, index):
        return pl.ds(pl.multiple_of(block * rows + index * chunk, 16), chunk)

    def put_sides(ref, at, sides, hidden):
        for place, cols in enumerate(sides):
            part = hidden[:, place * LANES : (place + 1) * LANES]
            ref[at, cols] = part.astype(bf16)
            count_in(cols, part, part)

    for copy in feature_loads:
        copy.wait()
    clear_sums()

    @pl.loop(0, 2)
    def _(side):
        sides = own_columns(side)

        @pl.loop(0, CHUNKS)
        def _(index):
            left = jnp.concatenate([hidden_three[block_rows(block, index), :] for block in range(BLOCKS)], axis=1)
            right = jnp.concatenate([weights[0][:, :, :, cols].reshape(C_IN, LANES) for cols in sides], axis=1)
            put_sides(hidden_one, block_rows(0, index), sides, dot(left, right))
            hook_in(0, side * CHUNKS + index, 6, 1, 2)

        @pl.when(side == 0)
        def _():
            cores_arrive(0)

    sum_one = Sum(0)
    sum_one.start(row_sums[0:1, :C_MID], row_sums[1:2, :C_MID])
    hook(1)
    sends_leave(0)
    pl.loop(0, 2)(lambda block: turn_weight(0, block))
    sum_one.middle()
    pl.loop(2, 4)(lambda block: turn_weight(0, block))
    hook(2)
    clear_sums()
    norm_coefs(0, sum_one.finish(), row_total)

    def activate(hidden_ref, slope_ref, put, site):
        @pl.loop(0, PIX)
        def _(pixel):
            place = pl.ds(pl.multiple_of(pixel * views, 16), views)
            for block in range(C_MID // LANES):
                cols = slice(block * LANES, (block + 1) * LANES)
                out = hidden_ref[place, cols].astype(f32) * coef[0:1, cols] + coef[1:2, cols]
                value, slope = gelu_pair(out)
                slope_ref[place, cols] = slope.astype(bf16)
                put(pixel, cols, value.astype(bf16))
            hook_in(site, pixel, SIDE, SIDE - 1, SIDE)

    def put_padded(padded):
        def put(pixel, cols, value):
            padded[pixel // SIDE + 1, pl.ds(pl.multiple_of((pixel % SIDE + 1) * views, 16), views), cols] = value

        return put

    activate(hidden_one, slope_one, put_padded(padded_one), 3)
    hook(4)

    def patch(padded, first, count, flip):
        found = []
        for vertical in range(3):
            for lateral in range(3):
                down, across = (2 - vertical, 2 - lateral) if flip else (vertical, lateral)
                piece = padded[pl.ds(first + down, count), across * views : across * views + chunk, :]
                found.append(piece.reshape(count * chunk, C_MID))
        return jnp.concatenate(found, axis=1)

    def image_rows(first, count):
        return pl.ds(pl.multiple_of(first * chunk, 16), count * chunk)

    def second_part(sides, first, count):
        right = jnp.concatenate([weights[1][:, :, :, cols].reshape(9 * C_MID, LANES) for cols in sides], axis=1)
        hidden = dot(patch(padded_one, first, count, False), right)
        put_sides(hidden_two, image_rows(first, count), sides, hidden)

    @pl.loop(0, 2)
    def _(side):
        sides = own_columns(side)

        @pl.loop(0, CHUNKS)
        def _(index):
            second_part(sides, index, 1)
            hook_in(5, side * 8 + index, 8, 1, 2)

        @pl.when(side == 0)
        def _():
            cores_arrive(1)

    sum_two = Sum(1)
    sum_two.start(row_sums[0:1, :C_MID], row_sums[1:2, :C_MID])
    hook(6)
    sends_leave(1)
    pl.loop(0, 4)(lambda block: turn_weight(1, block))
    sum_two.middle()
    pl.loop(4, 9)(lambda block: turn_weight(1, block))
    hook(7)
    clear_sums()
    norm_coefs(1, sum_two.finish(), row_total)

    def put_rows(pixel, cols, value):
        act_two[pl.ds(pl.multiple_of(pixel * views, 16), views), cols] = value

    activate(hidden_two, slope_two, put_rows, 8)
    cores_arrive(2)

    def weight_three(block):
        return weights[2][block].reshape(C_MID, C_MID)

    sums_low, sums_high = Sum(2), Sum(3)
    half_width = C_IN // 2

    @pl.loop(0, BLOCKS)
    def _(block):
        cols = pl.ds(pl.multiple_of(block * C_MID, LANES), C_MID)

        @pl.loop(0, CHUNKS)
        def _(index):
            hidden = dot(act_two[block_rows(0, index), :], weight_three(block))
            hidden_three[block_rows(block, index), :] = hidden.astype(bf16)
            count_in(cols, hidden, hidden)
            hook_in(9, block * 8 + index, 12, 2, 2)

        @pl.when(block == 1)
        def _():
            sums_low.start(row_sums[0:1, :half_width], row_sums[1:2, :half_width])

        @pl.when(block == 2)
        def _():
            sums_low.middle()

    sums_high.start(row_sums[0:1, half_width:], row_sums[1:2, half_width:])
    norm_coefs(2, sums_low.finish(), row_total)

    hook(22)

    pool, pool_slope, pool_bend = mem.pool, mem.pool_slope, mem.pool_bend
    for ref in (pool, pool_slope, pool_bend):
        ref[...] = jnp.zeros_like(ref)

    @pl.loop(0, pieces)
    def _(index):
        stage.copy(features, index, True).wait()

        @pl.loop(0, C_MID // LANES)
        def _(part):
            inner = pl.ds(pl.multiple_of(part * LANES, LANES), LANES)
            cols = piece_columns(index, part)
            slope_row, shift_row = coef[0:1, cols], coef[1:2, cols]
            kept = (pool[:, cols], pool_slope[:, cols], pool_bend[:, cols])
            for pixel in range(SIDE):
                stage_at, hidden_at = stage.rows(index, pixel, views), hidden_rows(index, pixel, views)
                hidden = hidden_three[hidden_at, inner].astype(f32)
                total = hidden * slope_row + shift_row + stage_ref[stage_at, inner].astype(f32)
                value, slope = gelu_pair(total)
                stage_ref[stage_at, inner] = slope.astype(bf16)
                kept = (kept[0] + value, kept[1] + slope, kept[2] + slope * hidden)
            pool[:, cols], pool_slope[:, cols], pool_bend[:, cols] = kept

        stage.save(slope_hbm, index)
        stage.next_load(features, index)

        @pl.when(index == 2)
        def _():
            sums_high.middle()

        @pl.when(index == pieces // 2 - 1)
        def _():
            norm_coefs(2, sums_high.finish(), row_total, half_width)

        hook_in(10, index, pieces)

    stage.last_saves(slope_hbm)
    cores_arrive(3)
    cores_arrive(4)
    for which in range(2, 5):
        sends_leave(which)

    pooled = (pool[...] * (1.0 / PIX)).astype(bf16)
    mem.pooled[...] = pooled

    @pl.loop(0, P_HID // C_MID)
    def _(half):
        cols = pl.ds(pl.multiple_of(half * C_MID, LANES), C_MID)
        mem.proj_hidden[:, cols] = dot(mem.pooled[...], weights[3][:, :, :, cols].reshape(C_IN, C_MID))

    proj_hidden = mem.proj_hidden[...]
    sum_four = Sum(4)
    sum_four.start(column_sums(proj_hidden), column_sums(proj_hidden * proj_hidden))
    pl.loop(0, 2)(lambda block: turn_weight(3, block))
    sum_four.middle()
    pl.loop(2, 4)(lambda block: turn_weight(3, block))
    totals = sum_four.finish()
    stage.first_loads(slope_hbm)
    norm_coefs(3, totals, view_total)
    value, slope = gelu_pair(proj_hidden * coef[0:1, :P_HID] + coef[1:2, :P_HID])
    proj_act = value.astype(bf16)
    mem.proj_act[...] = proj_act
    mem.proj_slope[...] = slope

    def weight_five(block):
        return weights[4][block // plan.x, block % plan.x]

    parts = P_HID // P_OUT
    embedding = jnp.zeros((views, P_OUT), f32)
    for block in range(parts):
        embedding = embedding + dot_cols(proj_act[:, block * P_OUT : (block + 1) * P_OUT], weight_five(block))

    images = views // 2
    order = jnp.broadcast_to(ins.order[...], (images, views))
    image_row = lax.broadcasted_iota(jnp.int32, (images, views), 0)
    selectors = [(order == 2 * image_row + which).astype(f32) for which in range(2)]
    embeds = [exact_dot(selector, embedding) for selector in selectors]
    moments = [exact_rows(embed, embed) for embed in embeds]
    packed, diagonal = pack_pair(*moments)
    packed, extra = sum_matrix(0, packed, [diagonal] + [column_sums(embed) for embed in embeds])
    moments = unpack_pair(packed, extra[0])
    eye = (
        lax.broadcasted_iota(jnp.int32, (P_OUT, P_OUT), 0) == lax.broadcasted_iota(jnp.int32, (P_OUT, P_OUT), 1)
    ).astype(f32)
    centred, covariances = [], []
    for which in range(2):
        mean = extra[1 + which] / image_total
        centred.append(embeds[which] - mean)
        covariances.append(moments[which] / image_total - exact_rows(mean, mean) + ridge_term * eye)
    inverses = inverse_factors(covariances)
    whitened = [exact_cols(centred[which], inverses[which]) for which in range(2)]
    scalings = [
        lax.rsqrt(jnp.mean(white * white, axis=1, keepdims=True) + norm_epsilon) for white in whitened
    ]
    units = [white * scaling for white, scaling in zip(whitened, scalings)]
    difference = units[0] - units[1]
    objective_row = column_sums(difference * difference) * (1.0 / P_OUT)
    unit_grads = [difference * (2.0 / P_OUT), difference * (-2.0 / P_OUT)]
    white_grads = []
    for which in range(2):
        inner = jnp.mean(whitened[which] * unit_grads[which], axis=1, keepdims=True)
        white_grads.append(
            scalings[which] * unit_grads[which] - whitened[which] * (scalings[which] ** 3 * inner)
        )
    directs = [exact_dot(white_grads[which], inverses[which]) for which in range(2)]
    products = [exact_rows(white_grads[which], whitened[which]) for which in range(2)]
    packed, diagonal = pack_pair(*products)
    packed, extra = sum_matrix(
        1, packed, [diagonal] + [column_sums(grad) for grad in white_grads] + [objective_row]
    )
    products = unpack_pair(packed, extra[0])
    embed_grad = jnp.zeros((views, P_OUT), f32)
    for which in range(2):
        symmetric = exact_rows(inverses[which], exact_dot(products[which], inverses[which]))
        mean_grad = exact_dot(extra[1 + which], inverses[which])
        grad = directs[which] - (exact_dot(centred[which], symmetric) + mean_grad) / image_total
        embed_grad = embed_grad + exact_rows(selectors[which], grad)
    objective_row = extra[3]
    embed_low = embed_grad.astype(bf16)

    proj_act, proj_hidden = mem.proj_act[...], mem.proj_hidden[...]
    act_grad = jnp.concatenate([dot(embed_low, weight_five(block)) for block in range(parts)], axis=1)
    upstream = act_grad * mem.proj_slope[...]
    plain = column_sums(upstream)
    sum_four_back = Sum(5)
    sum_four_back.start(plain, xhat_sum(3, plain, column_sums(upstream * proj_hidden)))
    for block in range(parts):
        weights[4][block // plan.x, block % plan.x] = dot_rows(
            embed_low, proj_act[:, block * P_OUT : (block + 1) * P_OUT]
        ).astype(bf16)
    pl.loop(0, 4)(lambda block: turn_weight(2, block))
    sum_four_back.middle()
    turn_rows(act_two)
    grad_coefs(3, sum_four_back.finish(), view_total)
    four_low = (
        upstream * coef[0:1, :P_HID] - coef[1:2, :P_HID] - proj_hidden * coef[2:3, :P_HID]
    ).astype(bf16)
    @pl.loop(0, BLOCKS)
    def _(block):
        cols = pl.ds(pl.multiple_of(block * C_MID, LANES), C_MID)
        right = jnp.concatenate(
            [
                weights[3][block, :, :, half * C_MID : (half + 1) * C_MID].reshape(C_MID, C_MID)
                for half in range(P_HID // C_MID)
            ],
            axis=0,
        )
        grad = dot(four_low, right) * (1.0 / PIX)
        row_sums[0:1, cols] = column_sums(grad * pool_slope[:, cols])
        row_sums[1:2, cols] = column_sums(grad * pool_bend[:, cols])
        pool_slope[:, cols] = grad

    plain = row_sums[0:1, :]
    sum_three_back = Sum(6)
    sum_three_back.start(plain, xhat_sum(2, plain, row_sums[1:2, :]))

    @pl.loop(0, BLOCKS)
    def _(block):
        left = mem.pooled[:, pl.ds(pl.multiple_of(block * C_MID, LANES), C_MID)]
        weights[3][block] = dot_rows(left, four_low).astype(bf16).reshape(plan.x, -1, P_HID)

    sum_three_back.middle()
    hook(23)
    grad_coefs(2, sum_three_back.finish(), row_total)
    pool[...] = pool_slope[...] * coef[0:1, :]

    clear_sums()

    @pl.loop(0, pieces)
    def _(index):
        stage.copy(slope_hbm, index, True).wait()
        stage.next_load(slope_hbm, index)

        @pl.loop(0, C_MID // LANES)
        def _(part):
            inner = pl.ds(pl.multiple_of(part * LANES, LANES), LANES)
            cols = piece_columns(index, part)
            spread, shift_row, bend_row = pool[:, cols], coef[1:2, cols], coef[2:3, cols]
            for pixel in range(SIDE):
                hidden_at = hidden_rows(index, pixel, views)
                hidden = hidden_three[hidden_at, inner].astype(f32)
                slope = stage_ref[stage.rows(index, pixel, views), inner].astype(f32)
                hidden_three[hidden_at, inner] = (slope * spread - shift_row - hidden * bend_row).astype(bf16)

        hook_in(11, index, pieces)

    @pl.loop(0, CHUNKS)
    def _(index):
        at = block_rows(0, index)
        left = jnp.concatenate([hidden_three[block_rows(block, index), :] for block in range(BLOCKS)], axis=1)
        upstream = dot(left, weights[2][...].reshape(C_IN, C_MID)) * slope_two[at, :].astype(f32)
        slope_two[at, :] = upstream.astype(bf16)
        count_in(slice(0, C_MID), upstream, hidden_two[at, :].astype(f32))
        hook_in(12, index, 3, 2, 2)

    sums = row_sums[0:1, :C_MID], row_sums[1:2, :C_MID]
    sum_two_back = Sum(7)
    sum_two_back.start(sums[0], xhat_sum(1, *sums))

    @pl.loop(0, BLOCKS)
    def _(block):
        grad = dot(turned(act_two), hidden_three[pl.ds(pl.multiple_of(block * rows, 16), tall), :])
        weights[2][block] = grad.astype(bf16).reshape(plan.z, plan.x, -1, C_MID)

        @pl.when(block == 1)
        def _():
            sum_two_back.middle()

        hook_in(13, block, BLOCKS)

    clear_sums()
    grad_coefs(1, sum_two_back.finish(), row_total)

    def apply_grad(hidden_ref, grad_ref, put, site):
        @pl.loop(0, PIX)
        def _(pixel):
            place = pl.ds(pl.multiple_of(pixel * views, 16), views)
            for block in range(C_MID // LANES):
                cols = slice(block * LANES, (block + 1) * LANES)
                grad = (
                    grad_ref[place, cols].astype(f32) * coef[0:1, cols]
                    - coef[1:2, cols]
                    - hidden_ref[place, cols].astype(f32) * coef[2:3, cols]
                )
                put(pixel, cols, grad.astype(bf16))
            hook_in(site, pixel, SIDE, SIDE - 1, SIDE)

    def put_two(pixel, cols, value):
        put_padded(padded_two)(pixel, cols, value)
        slope_two[pl.ds(pl.multiple_of(pixel * views, 16), views), cols] = value

    apply_grad(hidden_two, slope_two, put_two, 14)
    turn_rows(slope_two)
    def column_copy(block):
        return pltpu.make_async_copy(
            features.at[:, pl.ds(pl.multiple_of(block * C_MID, LANES), C_MID)],
            hidden_three.at[pl.ds(pl.multiple_of((2 + block % 2) * rows, 16), rows)],
            mem.column_sem.at[block],
        )

    column_copy(0).start()
    column_copy(1).start()

    def tap_grad(tap):
        down, across = tap // 3, tap % 3
        left = padded_one[pl.ds(down, SIDE), pl.ds(pl.multiple_of(across * views, 16), chunk), :]
        right = jnp.concatenate([left.reshape(rows, C_MID), jnp.zeros((tall - rows, C_MID), bf16)], axis=0)
        grad = dot(turned(slope_two), right).astype(bf16).T
        stage_ref[pl.ds(pl.multiple_of(tap * C_MID, 16), C_MID), :] = grad

    @pl.loop(0, 7)
    def _(tap):
        tap_grad(tap)
        hook_in(15, tap, 7)

    def second_back(first, count):
        at = image_rows(first, count)
        upstream = dot(patch(padded_two, first, count, True), weights[1][...].reshape(9 * C_MID, C_MID))
        upstream = upstream * slope_one[at, :].astype(f32)
        slope_one[at, :] = upstream.astype(bf16)
        count_in(slice(0, C_MID), upstream, hidden_one[at, :].astype(f32))

    @pl.loop(0, CHUNKS)
    def _(index):
        second_back(index, 1)
        hook_in(16, index, 3, 1, 2)

    hook(16, 3)
    sums = row_sums[0:1, :C_MID], row_sums[1:2, :C_MID]
    sum_one_back = Sum(8)
    sum_one_back.start(sums[0], xhat_sum(0, *sums))

    @pl.loop(7, 9)
    def _(tap):
        tap_grad(tap)

        @pl.when(tap == 7)
        def _():
            sum_one_back.middle()

        hook_in(17, tap, 2, 7)

    grad_coefs(0, sum_one_back.finish(), row_total)

    def put_one(pixel, cols, value):
        put_rows(pixel, cols, value)
        slope_one[pl.ds(pl.multiple_of(pixel * views, 16), views), cols] = value

    apply_grad(hidden_one, slope_one, put_one, 18)
    turn_rows(slope_one)

    tail = Ring(hidden_two, 0)
    tail.first_loads(slope_hbm)

    @pl.loop(0, BLOCKS)
    def _(block):
        column_copy(block).wait()
        found = hidden_three[pl.ds(pl.multiple_of((2 + block % 2) * rows, 16), rows), :]
        right = jnp.concatenate([found, jnp.zeros((tall - rows, C_MID), bf16)], axis=0)
        grad = dot(turned(slope_one), right).astype(bf16).T
        mem.g1[block] = grad.reshape(plan.x, -1, C_MID)

        @pl.when(block + 2 < BLOCKS)
        def _():
            column_copy(block + 2).start()

        hook_in(19, block, BLOCKS)

    sum_last = Sum(9)

    @pl.loop(0, pieces)
    def _(index):
        block = index // CHUNKS
        back = dot(act_two[span(lax.rem(index, CHUNKS)), :], weights[0][block].reshape(C_MID, C_MID))
        tail.copy(slope_hbm, index, True).wait()
        cols = pl.ds(pl.multiple_of(block * C_MID, LANES), C_MID)
        for pixel in range(SIDE):
            at = tail.rows(index, pixel, views)
            summed = hidden_two[at, :].astype(f32) * pool_slope[:, cols]
            hidden_two[at, :] = (summed + back[pixel * views : (pixel + 1) * views]).astype(bf16)
        tail.save(outs.features_grad, index)
        tail.next_load(slope_hbm, index)
        hook_in(20, index, pieces)
        if plan.inside:

            @pl.when(index == LAST_SUM)
            def _():
                sum_last.start(mem.squares[...], mem.squares[...])

            @pl.when(index == LAST_SUM + 3)
            def _():
                sum_last.middle()

    tail.last_saves(outs.features_grad)
    squares = mem.squares[...]
    if plan.inside:
        squares = sum_last.finish()[0:1]
    norm_grads = mem.norm_grads[...]
    scalars = outs.scalars
    norm_squares = column_sums(norm_grads * norm_grads)
    for place in range(norm_squares.shape[1] // LANES):
        squares = squares + norm_squares[:, place * LANES : (place + 1) * LANES]
    scalars[...] = jnp.zeros_like(scalars)
    squares = jnp.sum(squares, axis=1, keepdims=True)
    norm = jnp.sqrt(squares)
    found = (jnp.sum(objective_row, axis=1, keepdims=True) / image_total, squares, norm, clip_factor(norm))
    for place, value in enumerate(found):
        scalars[place : place + 1, :] = jnp.broadcast_to(value, (1, LANES))
    if plan.inside:
        owner = (dp_me * plan.fsdp + fsdp_me) * LANES
        outs.norm_grad[...] = mem.norm_grads[:, pl.ds(pl.multiple_of(owner, LANES), LANES)]
    else:
        outs.norm_grad[...] = norm_grads
    if not plan.inside:
        stores = [
            pltpu.make_async_copy(gradients[which], outs.grads[which], mem.bulk_send.at[which])
            for which in range(5)
        ]
        for store in stores:
            store.start()
        for store in stores:
            store.wait()


def weight_shapes():
    return (
        (4, 2, 256, C_MID),
        (4, 2, 576, C_MID),
        (BLOCKS, 4, 2, 64, C_MID),
        (4, 2, 256, P_HID),
        (4, 2, P_OUT, P_OUT),
    )


def run_kernel(plan, features, order, shards, norm):
    rows, views = plan.rows, plan.views
    in_vmem = pl.BlockSpec(memory_space=pltpu.VMEM)
    anywhere = pl.BlockSpec(memory_space=pl.ANY)
    shapes = weight_shapes()
    operands = [features, order, norm, *shards]
    in_specs = [anywhere, in_vmem, in_vmem] + [in_vmem if plan.inside else anywhere] * 5
    results = [
        ((rows, C_IN), bf16, anywhere),
        ((rows, C_IN), bf16, anywhere),
        (norm.shape, f32, in_vmem),
        ((8, LANES), f32, in_vmem),
    ]
    for which, shard in enumerate(shards):
        if plan.inside:
            results.append((shard.shape, f32, in_vmem))
        else:
            results.append(((9 * C_MID, C_MID) if which == 1 else shapes[which], bf16, anywhere))
    dma = pltpu.SemaphoreType.DMA

    def sum_room(width):
        return SumRoom(
            pltpu.VMEM((plan.dp, 2, width), f32),
            pltpu.VMEM((plan.fsdp, 2, width), f32),
            dma((plan.dp,)),
            dma((plan.dp,)),
            dma((plan.fsdp,)),
            dma((plan.fsdp,)),
        )

    def matrix_room():
        size = plan.embed_rows
        return MatrixRoom(
            pltpu.VMEM((plan.dp, size, P_OUT), f32),
            pltpu.VMEM((plan.dp, size, P_OUT), f32),
            pltpu.VMEM((plan.fsdp, size, P_OUT), f32),
            pltpu.VMEM((plan.dp, size, P_OUT), f32),
            dma((plan.dp,)),
            dma((plan.dp,)),
            dma((plan.fsdp,)),
            dma((plan.fsdp,)),
            dma((plan.dp,)),
            dma((plan.dp,)),
        )

    scratch = Mem(
        w=[pltpu.VMEM(shape, bf16) for shape in shapes],
        g1=pltpu.VMEM(shapes[0], bf16),
        row_sums=pltpu.VMEM((2, C_IN), f32),
        r3=pltpu.VMEM(shapes[2], bf16),
        r4=pltpu.VMEM(shapes[3], bf16),
        r5=pltpu.VMEM(shapes[4], bf16),
        stage=pltpu.VMEM((max(SLOTS * plan.chunk, 9 * C_MID), C_MID), bf16),
        stage_sem=dma((2, SLOTS)),
        column_sem=dma((BLOCKS,)),
        h1=pltpu.VMEM((rows, C_MID), bf16),
        d1=pltpu.VMEM((plan.tall, C_MID), bf16),
        h2=pltpu.VMEM((plan.tall, C_MID), bf16),
        d2=pltpu.VMEM((plan.tall, C_MID), bf16),
        a2=pltpu.VMEM((plan.tall, C_MID), bf16),
        h3=pltpu.VMEM((3 * rows + plan.tall, C_MID), bf16),
        pad1=pltpu.VMEM((SIDE + 2, (SIDE + 2) * views, C_MID), bf16),
        pad2=pltpu.VMEM((SIDE + 2, (SIDE + 2) * views, C_MID), bf16),
        pool=pltpu.VMEM((views, C_IN), f32),
        pool_slope=pltpu.VMEM((views, C_IN), f32),
        pool_bend=pltpu.VMEM((views, C_IN), f32),
        pooled=pltpu.VMEM((views, C_IN), bf16),
        proj_act=pltpu.VMEM((views, P_HID), bf16),
        proj_slope=pltpu.VMEM((views, P_HID), f32),
        proj_hidden=pltpu.VMEM((views, P_HID), f32),
        coef=pltpu.VMEM((8, C_IN), f32),
        stats=pltpu.VMEM((2, norm_width()), f32),
        norm=pltpu.VMEM((2, norm_width()), f32),
        norm_grads=pltpu.VMEM((2, norm_width()), f32),
        norm_tiles=pltpu.VMEM((plan.dp, plan.fsdp, 2, LANES), f32),
        norm_s0=dma((plan.dp,)),
        norm_r0=dma((plan.dp,)),
        norm_s1=dma((plan.fsdp,)),
        norm_r1=dma((plan.fsdp,)),
        bulk_send=dma((COPIES,)),
        bulk_recv=dma((COPIES,)),
        mats=[matrix_room(), matrix_room()],
        sums=[
            sum_room(width)
            for width in (C_MID, C_MID, C_IN // 2, C_IN // 2, P_HID, C_IN, LANES)
        ],
        squares=pltpu.VMEM((1, LANES), f32),
    )
    values = pl.pallas_call(
        lambda *refs: kernel(plan, *refs),
        out_shape=[jax.ShapeDtypeStruct(shape, kind) for shape, kind, _ in results],
        in_specs=in_specs,
        out_specs=[spec for _, _, spec in results],
        scratch_shapes=[scratch],
        compiler_params=pltpu.CompilerParams(
            collective_id=1, has_side_effects=True, vmem_limit_bytes=63 * 2**20
        ),
        name="train_step",
    )(*operands)
    return Outs(*values[:4], values[4:])


def norm_width():
    return 2 * C_MID + C_IN + P_HID


def clip_factor(norm):
    return clip_level / jnp.maximum(norm, clip_level)


def adam_update(weight, moment_one, moment_two, gradient, step_rate, weight_decay):
    first_new = beta_first * moment_one + (1.0 - beta_first) * gradient
    second_new = beta_second * moment_two + (1.0 - beta_second) * gradient * gradient
    first_hat = first_new / (1.0 - beta_first**STEP)
    second_hat = second_new / (1.0 - beta_second**STEP)
    weight_new = weight - step_rate * (
        first_hat / (jnp.sqrt(second_hat) + adam_epsilon) + weight_decay * weight
    )
    return (weight_new, first_new, second_new)


def finish_kernel(rates, decays, *refs):
    count = len(rates)
    low, scalars = refs[0], refs[1]
    refs = refs[2:]
    given, wide, loss, norm, updated = refs[: 4 * count], *refs[4 * count : 4 * count + 3], refs[4 * count + 3 : -2]
    rooms, sems = refs[-2], refs[-1]

    @pl.loop(0, low.shape[0] // 16)
    def _(part):
        at = pl.ds(pl.multiple_of(part * 16, 16), 16)
        wide[at, :] = low[at, :].astype(f32)

    step = pl.program_id(0)

    def load(place):
        return pltpu.make_async_copy(given[place], rooms[place], sems.at[place])

    def store(place):
        return pltpu.make_async_copy(rooms[place], updated[place], sems.at[place])

    @pl.when(step == 0)
    def _():
        loss[0, 0] = scalars[0, 0]
        norm[0, 0] = scalars[2, 0]
        for place in range(4 * count):
            load(place).start()

    @pl.when(step == 2)
    def _():
        for place in range(4 * count):
            load(place).wait()
        for place in range(count):
            rows = rooms[place].shape[0]
            tile = 16 if rows % 16 == 0 else rows

            @pl.loop(0, rows // tile)
            def _(index, place=place, tile=tile):
                at = pl.ds(pl.multiple_of(index * tile, tile), tile)
                weight, first, second, grad = (rooms[part * count + place][at, :] for part in range(4))
                found = adam_update(weight, first, second, grad * scalars[3, 0], rates[place], decays[place])
                for part in range(3):
                    rooms[part * count + place][at, :] = found[part]

        for place in range(3 * count):
            store(place).start()

    @pl.when(step == CHUNKS - 1)
    def _():
        for place in range(3 * count):
            store(place).wait()


def finish(features_grad, scalars, masters, firsts, seconds, grads, rates, decays):
    rows = features_grad.shape[0]
    arrays = [*masters, *firsts, *seconds, *grads]
    moving = pl.BlockSpec((rows // CHUNKS, C_IN), lambda index: (index, 0))
    single = pl.BlockSpec(memory_space=pltpu.SMEM)
    anywhere = pl.BlockSpec(memory_space=pl.ANY)
    count = len(masters)
    values = pl.pallas_call(
        lambda *refs: finish_kernel(rates, decays, *refs),
        grid=(CHUNKS,),
        in_specs=[moving, single] + [anywhere] * (4 * count),
        out_specs=[moving, single, single] + [anywhere] * (3 * count),
        out_shape=[jax.ShapeDtypeStruct((rows, C_IN), f32)]
        + [jax.ShapeDtypeStruct((1, 1), f32)] * 2
        + [jax.ShapeDtypeStruct(array.shape, f32) for array in arrays[: 3 * count]],
        scratch_shapes=[
            [pltpu.VMEM(array.shape, f32) for array in arrays],
            pltpu.SemaphoreType.DMA((4 * count,)),
        ],
        compiler_params=pltpu.CompilerParams(vmem_limit_bytes=62 * 2**20),
        name="finish",
    )(features_grad, scalars, *arrays)
    groups = [values[3 + part * count : 3 + (part + 1) * count] for part in range(3)]
    return values[0], values[1].reshape(()), values[2].reshape(()), *groups


def gather_full(weight):
    outer = lax.all_gather(weight.astype(bf16), FSDP, axis=0, tiled=True)
    return lax.all_gather(outer, DP, axis=1, tiled=True)


def scatter_full(gradient):
    inner = lax.psum_scatter(gradient.astype(f32), DP, scatter_dimension=1, tiled=True)
    return lax.psum_scatter(inner, FSDP, scatter_dimension=0, tiled=True)


def body(features, view_order, *state):
    masters, firsts, seconds = state[:6], state[6:12], state[12:18]
    dp_size, fsdp_size = lax.axis_size(DP), lax.axis_size(FSDP)
    views = features.shape[0]
    inside = dp_size == 4 and fsdp_size == 8
    plan = Plan(dp_size, fsdp_size, views, inside)
    pixels = jnp.swapaxes(features, 0, 1).reshape(-1, C_IN)
    norm_params = masters[5]
    shapes = weight_shapes()
    if inside:
        shards = list(masters[:4]) + [masters[4].T]
        norm = norm_params
    else:
        full = [gather_full(weight) for weight in masters[:5]]
        shards = [
            full[0].reshape(shapes[0]),
            full[1].reshape(shapes[1]),
            full[2].reshape(C_MID, BLOCKS, C_MID).swapaxes(0, 1).reshape(shapes[2]),
            full[3].reshape(shapes[3]),
            full[4].reshape(4, 2, P_OUT, P_OUT).swapaxes(2, 3),
        ]
        norm = lax.all_gather(norm_params.astype(bf16), (DP, FSDP), axis=1, tiled=True).astype(f32)
    got = run_kernel(plan, pixels, view_order, shards, norm)
    grads = list(got.grads)
    scalars = got.scalars
    turned = [list(group) for group in (masters, firsts, seconds)]
    if inside:
        owned = grads
        for group in turned:
            group[4] = group[4].T
    else:
        whole_grads = [
            grads[0].reshape(C_IN, C_MID),
            grads[1],
            grads[2].reshape(BLOCKS, C_MID, C_MID).swapaxes(0, 1).reshape(C_MID, C_IN),
            grads[3].reshape(C_IN, P_HID),
            grads[4].swapaxes(2, 3).reshape(P_HID, P_OUT),
        ]
        owned = [scatter_full(gradient) for gradient in whole_grads]
        squares = scalars[1, 0] + lax.psum(sum(jnp.sum(grad * grad) for grad in owned), (DP, FSDP))
        norm_value = jnp.sqrt(squares)
        scalars = scalars.at[2].set(norm_value).at[3].set(clip_factor(norm_value))
    width = norm_params.shape[1]
    if inside:
        owned.append(got.norm_grad)
    else:
        owner = lax.axis_index((DP, FSDP))
        owned.append(lax.dynamic_slice_in_dim(got.norm_grad, owner * width, width, 1))
    step_rates = (
        C_IN ** (-0.5),
        (9 * C_MID) ** (-0.5),
        C_MID ** (-0.5),
        C_IN ** (-0.5),
        P_HID ** (-0.5),
        norm_rate,
    )
    decays = (decay_rate, decay_rate, decay_rate, decay_rate, decay_rate, 0.0)
    input_grad, loss, grad_norm, *updates = finish(
        got.features_grad, scalars, *turned, owned, step_rates, decays
    )
    if inside:
        updates = [[*group[:4], group[4].T, group[5]] for group in updates]
    return (
        loss,
        jnp.swapaxes(input_grad.reshape(PIX, views, C_IN), 0, 1),
        grad_norm,
        *updates[0],
        *updates[1],
        *updates[2],
    )


def solution(mesh):
    views = P((DP, FSDP), None, None)
    split = P(FSDP, DP)
    norm = P(None, (DP, FSDP))
    params = (split,) * 5 + (norm,)
    return jax.shard_map(
        body,
        mesh=mesh,
        in_specs=(views, P((DP, FSDP), None)) + params * 3,
        out_specs=(P(), views, P()) + params * 3,
        check_vma=False,
    )
```

```python
from typing import Any, NamedTuple

import jax
import jax.numpy as jnp
from jax import lax
from jax.experimental import pallas as pl
from jax.experimental.pallas import tpu as pltpu
from jax.sharding import PartitionSpec as P

C_IN = 2048
C_MID = 512
P_HID = 1024
P_OUT = 128
SIDE = 7
STEP = 10
PIX = 49
LANES = 128
BLOCKS = C_IN // C_MID
CHUNKS = SIDE
SLOTS = 7
AHEAD = SLOTS - 2
LAST_SUM = 23
COPIES = 360


highest = lax.Precision.HIGHEST
bf16 = jnp.bfloat16
f32 = jnp.float32
norm_epsilon = 1e-05
ridge_term = 0.01
clip_level = 0.1
beta_first = 0.9
beta_second = 0.999
adam_epsilon = 1e-08
decay_rate = 0.05
norm_rate = 0.5
bell_scale = 0.3989422804014327
root_half = 0.5**0.5
bell_rate = -0.7213475204444817
DP, FSDP = "dp", "fsdp"


def gelu_pair(values):
    below = 0.5 + 0.5 * lax.erf(values * root_half)
    bell = jnp.exp2(values * values * bell_rate)
    return values * below, below + values * bell * bell_scale


def dot(left, right):
    return jnp.dot(left, right, preferred_element_type=f32)


def dot_cols(left, right):
    return lax.dot_general(left, right, (((1,), (1,)), ((), ())), preferred_element_type=f32)


def dot_rows(left, right):
    return lax.dot_general(left, right, (((0,), (0,)), ((), ())), preferred_element_type=f32)


def exact_cols(left, right):
    return lax.dot_general(
        left, right, (((1,), (1,)), ((), ())), precision=highest, preferred_element_type=f32
    )


def exact_rows(left, right):
    return lax.dot_general(
        left, right, (((0,), (0,)), ((), ())), precision=highest, preferred_element_type=f32
    )


def exact_dot(left, right):
    return jnp.dot(left, right, precision=highest, preferred_element_type=f32)


def inverse_factors(matrices):
    row_top = lax.broadcasted_iota(jnp.int32, (8, P_OUT), 0)
    row_all = lax.broadcasted_iota(jnp.int32, (P_OUT, P_OUT), 0)
    col_all = lax.broadcasted_iota(jnp.int32, (P_OUT, P_OUT), 1)

    def one_step(place, left, right):
        scale = lax.rsqrt(left[place : place + 1, place : place + 1])
        left_row = left[place : place + 1, :] * scale
        right_row = right[place : place + 1, :] * scale
        column = left[:, place : place + 1] * scale
        left = left - column * left_row
        right = right - column * right_row
        here = row_top == place
        left = jnp.concatenate([jnp.where(here, 0.0, left[:8]), left[8:]], axis=0)
        right = jnp.concatenate(
            [jnp.where(here, jnp.broadcast_to(right_row, (8, P_OUT)), right[:8]), right[8:]], axis=0
        )
        return left, right

    def panel(_, pairs):
        pairs = list(pairs)
        for place in range(8):
            for which in range(len(pairs)):
                pairs[which] = one_step(place, *pairs[which])
        return tuple(
            (
                pltpu.roll(jnp.concatenate([left[8:], left[:8]], axis=0), P_OUT - 8, 1),
                jnp.concatenate([right[8:], right[:8]], axis=0),
            )
            for left, right in pairs
        )

    pairs = tuple((matrix, (row_all == col_all).astype(f32)) for matrix in matrices)
    return [right for _, right in lax.fori_loop(0, P_OUT // 8, panel, pairs)]


def pack_pair(first, second):
    row = lax.broadcasted_iota(jnp.int32, (P_OUT, P_OUT), 0)
    col = lax.broadcasted_iota(jnp.int32, (P_OUT, P_OUT), 1)
    packed = jnp.where(row >= col, first, second.T)
    diagonal = jnp.sum(jnp.where(row == col, second, 0.0), axis=0, keepdims=True)
    return packed, diagonal


def unpack_pair(packed, diagonal):
    row = lax.broadcasted_iota(jnp.int32, (P_OUT, P_OUT), 0)
    col = lax.broadcasted_iota(jnp.int32, (P_OUT, P_OUT), 1)
    turned = packed.T
    first = jnp.where(row >= col, packed, turned)
    second = jnp.where(row < col, packed, jnp.where(row == col, diagonal, turned))
    return first, second


GATHER_AT = {
    (0, 0): 1,
    (0, 2): 1,
    (0, 4): 1,
    (0, 5): 2,
    (3, 0): 1,
    (3, 3): 1,
    (3, 6): 2,
    (5, 0): 1,
    (5, 1): 2,
    (5, 2): 1,
    (5, 3): 2,
    (8, 1): 1,
    (8, 6): 1,
    (9, 2): 1,
    (9, 5): 1,
    (9, 8): 1,
    (21, 0): 7,
}
REDUCE_AT = {
    (11, 4): ((4, 0, 1), (3, 0, 1)),
    (11, 10): ((3, 1, 1), (4, 0, 2)),
    (11, 17): ((3, 2, 1),),
    (11, 22): ((3, 0, 2),),
    (12, 0): ((3, 1, 2), (3, 3, 1), (4, 0, 3)),
    (12, 1): ((3, 0, 3),),
    (12, 2): ((3, 2, 2), (3, 1, 3)),
    (13, 1): ((3, 3, 2),),
    (13, 2): ((3, 2, 3),),
    (13, 3): ((3, 3, 3), (2, 0, 0), (2, 1, 0), (2, 2, 0), (2, 3, 0)),
    (14, 6): ((4, 9, 4), (2, 0, 1), (2, 1, 1)),
    (15, 1): ((2, 2, 1),),
    (15, 2): ((1, 0, 0), (2, 0, 2), (2, 3, 1)),
    (15, 3): ((2, 1, 2),),
    (15, 4): ((1, 1, 0), (1, 0, 1), (2, 0, 3)),
    (15, 5): ((2, 2, 2), (2, 1, 3)),
    (15, 6): ((1, 2, 0), (2, 3, 2), (1, 1, 1), (3, 9, 4)),
    (16, 0): ((1, 0, 2), (1, 2, 1), (2, 2, 3), (2, 3, 3)),
    (16, 1): ((1, 1, 2), (2, 9, 4), (1, 0, 3)),
    (16, 2): ((1, 2, 2), (1, 1, 3)),
    (17, 1): ((1, 3, 0),),
    (18, 2): ((1, 2, 3),),
    (18, 6): ((1, 3, 1),),
    (19, 0): ((0, 0, 0), (1, 3, 2)),
    (19, 1): ((0, 1, 0), (0, 0, 1), (1, 3, 3)),
    (19, 2): ((0, 2, 0), (0, 1, 1), (0, 0, 2)),
    (19, 3): ((0, 3, 0), (0, 2, 1), (0, 1, 2), (0, 0, 3)),
    (20, 2): ((0, 3, 1), (0, 2, 2), (0, 1, 3)),
    (20, 7): ((0, 3, 2), (0, 2, 3)),
    (20, 12): ((0, 3, 3), (1, 9, 4)),
    (20, 19): ((0, 9, 4),),
    (23, 0): ((4, 0, 0), (3, 0, 0), (3, 1, 0), (3, 2, 0), (3, 3, 0)),
}


class Ins(NamedTuple):
    features: Any
    order: Any
    norm: Any
    shards: Any


class Outs(NamedTuple):
    slope: Any
    features_grad: Any
    norm_grad: Any
    scalars: Any
    grads: Any


class SumRoom(NamedTuple):
    dp: Any
    fsdp: Any
    s0: Any
    r0: Any
    s1: Any
    r1: Any


class MatrixRoom(NamedTuple):
    pack: Any
    dp: Any
    fsdp: Any
    all: Any
    s0: Any
    r0: Any
    s1: Any
    r1: Any
    s2: Any
    r2: Any


class Mem(NamedTuple):
    w: Any
    g1: Any
    row_sums: Any
    r3: Any
    r4: Any
    r5: Any
    stage: Any
    stage_sem: Any
    column_sem: Any
    h1: Any
    d1: Any
    h2: Any
    d2: Any
    a2: Any
    h3: Any
    pad1: Any
    pad2: Any
    pool: Any
    pool_slope: Any
    pool_bend: Any
    pooled: Any
    proj_act: Any
    proj_slope: Any
    proj_hidden: Any
    coef: Any
    stats: Any
    norm: Any
    norm_grads: Any
    norm_tiles: Any
    norm_s0: Any
    norm_r0: Any
    norm_s1: Any
    norm_r1: Any
    bulk_send: Any
    bulk_recv: Any
    mats: Any
    sums: Any
    squares: Any


class Plan:
    def __init__(self, dp_size, fsdp_size, views, inside):
        self.dp = dp_size
        self.fsdp = fsdp_size
        self.devices = dp_size * fsdp_size
        self.views = views
        self.rows = views * PIX
        self.tall = -(-self.rows // C_MID) * C_MID
        self.chunk = views * SIDE
        self.inside = inside
        self.z = 4
        self.x = 2
        self.half = (128, 288, 32, 128, 16)
        self.width = (128, 128, 512, 256, 128)
        piece = P_OUT + 8
        self.embed_rows = -(-piece // (8 * dp_size)) * 8


def kernel(plan, *refs):
    ins, outs, mem = Ins(*refs[:3], refs[3:8]), Outs(*refs[8:12], refs[12:17]), refs[17]
    views, chunk, rows, tall = plan.views, plan.chunk, plan.rows, plan.tall
    row_total = float(rows * plan.devices)
    view_total = float(views * plan.devices)
    image_total = float(views * plan.devices // 2)
    dp_me, fsdp_me = lax.axis_index(DP), lax.axis_index(FSDP)
    y_me, c_me = dp_me // 2, dp_me % 2
    z_me, x_me = fsdp_me // 2, fsdp_me % 2
    y_other, c_other, x_other = 1 - y_me, 1 - c_me, 1 - x_me

    barrier = pltpu.get_barrier_semaphore()

    @pl.loop(1, plan.dp)
    def _(step):
        pl.semaphore_signal(
            barrier, 1, device_id={DP: lax.rem(dp_me + step, plan.dp)}, device_id_type=pl.DeviceIdType.MESH
        )

    @pl.loop(1, plan.fsdp)
    def _(step):
        pl.semaphore_signal(
            barrier, 1, device_id={FSDP: lax.rem(fsdp_me + step, plan.fsdp)}, device_id_type=pl.DeviceIdType.MESH
        )

    pl.semaphore_wait(barrier, plan.dp + plan.fsdp - 2)

    def share(axis, size, me, source_of, slots, send, recv):
        def outgoing(step):
            partner = lax.rem(me + step, size)
            return pltpu.make_async_remote_copy(
                src_ref=source_of(partner),
                dst_ref=slots.at[me],
                send_sem=send.at[step],
                recv_sem=recv.at[me],
                device_id={axis: partner},
                device_id_type=pl.DeviceIdType.MESH,
            )

        def incoming(step):
            source = lax.rem(me + step, size)
            return pltpu.make_async_remote_copy(
                src_ref=slots.at[source],
                dst_ref=slots.at[source],
                send_sem=send.at[step],
                recv_sem=recv.at[source],
                device_id={axis: source},
                device_id_type=pl.DeviceIdType.MESH,
            )

        def start():
            pl.loop(1, size)(lambda step: outgoing(step).start())

        def wait():
            pl.loop(1, size)(lambda step: incoming(step).wait_recv())
            pl.loop(1, size)(lambda step: outgoing(step).wait_send())

        return start, wait

    def add_slots(slots, size):
        total = slots[0]
        for place in range(1, size):
            total = total + slots[place]
        return total

    class Sum:
        def __init__(self, which):
            part = mem.sums[(0, 1, 2, 3, 4, 4, 5, 0, 1, 6)[which]]
            self.dp_slots, self.fsdp_slots = part.dp, part.fsdp
            self.dp_copy = share(
                DP, plan.dp, dp_me, lambda _: self.dp_slots.at[dp_me], self.dp_slots, part.s0, part.r0
            )
            self.fsdp_copy = share(
                FSDP, plan.fsdp, fsdp_me, lambda _: self.fsdp_slots.at[fsdp_me], self.fsdp_slots, part.s1, part.r1
            )

        def start(self, *values):
            for place, value in enumerate(values):
                self.dp_slots[dp_me, place : place + 1, :] = value
            self.dp_copy[0]()

        def middle(self):
            self.dp_copy[1]()
            self.fsdp_slots[fsdp_me] = add_slots(self.dp_slots, plan.dp)
            self.fsdp_copy[0]()

        def finish(self):
            self.fsdp_copy[1]()
            return add_slots(self.fsdp_slots, plan.fsdp)

        def all(self, *values):
            self.start(*values)
            self.middle()
            return self.finish()

    def sum_matrix(which, matrix, extra):
        part = mem.mats[which]
        size = plan.embed_rows
        pack = part.pack
        flat = jnp.concatenate(
            [matrix] + extra + [jnp.zeros((size * plan.dp - P_OUT - len(extra), P_OUT), f32)], axis=0
        )
        for place in range(plan.dp):
            pack[place] = flat[place * size : (place + 1) * size]
        start, wait = share(DP, plan.dp, dp_me, lambda to: pack.at[to], part.dp, part.s0, part.r0)
        start()
        part.dp[dp_me] = pack[dp_me]
        wait()
        part.fsdp[fsdp_me] = add_slots(part.dp, plan.dp)
        start, wait = share(
            FSDP, plan.fsdp, fsdp_me, lambda _: part.fsdp.at[fsdp_me], part.fsdp, part.s1, part.r1
        )
        start()
        wait()
        part.all[dp_me] = add_slots(part.fsdp, plan.fsdp)
        start, wait = share(
            DP, plan.dp, dp_me, lambda _: part.all.at[dp_me], part.all, part.s2, part.r2
        )
        start()
        wait()
        total = jnp.concatenate([part.all[place] for place in range(plan.dp)], axis=0)
        return total[:P_OUT], [total[P_OUT + place : P_OUT + place + 1] for place in range(len(extra))]

    weights = mem.w
    everything = slice(None)

    def row_span(which, half):
        if isinstance(half, tuple):
            return half
        size = plan.half[which]
        if half is None:
            return 0, 2 * size
        return half * size, size

    def column_span(which, dp_index):
        width = plan.width[which]
        return pl.ds(pl.multiple_of(dp_index * width, width), width)

    def places(which, z_index, x_index, dp_index, half, flat=True):
        start, size = row_span(which, half)
        if which == 1 and flat:
            z_list = range(plan.z) if z_index is None else [z_index]
            x_list = range(plan.x) if x_index is None else [x_index]
            return [
                (
                    pl.ds(pl.multiple_of((z_one * plan.x + x_one) * 576 + start, 16), size),
                    column_span(which, dp_index),
                )
                for z_one in z_list
                for x_one in x_list
            ]
        z_one = everything if z_index is None else z_index
        x_one = everything if x_index is None else x_index
        if which == 2:
            return [(dp_index, z_one, x_one, pl.ds(start, size), everything)]
        if which == 4:
            return [(z_one, x_one, pl.ds(pl.multiple_of(dp_index * 32 + start, 16), size), everything)]
        return [(z_one, x_one, pl.ds(start, size), column_span(which, dp_index))]

    recv_parts = {
        1: lambda index: mem.h3.at[index],
        0: lambda index: mem.r4.at[index],
        2: lambda index: mem.r3.at[index],
        3: lambda index: mem.r4.at[index],
        4: lambda index: mem.r5.at[index],
    }

    counter = [0]

    class Batch:
        def __init__(self, sources, targets, landings, axis, partner):
            base = counter[0]
            counter[0] += len(sources)
            send, recv = mem.bulk_send, mem.bulk_recv
            self.out = [
                pltpu.make_async_remote_copy(
                    src_ref=source,
                    dst_ref=target,
                    send_sem=send.at[base + place],
                    recv_sem=recv.at[base + place],
                    device_id={axis: partner},
                    device_id_type=pl.DeviceIdType.MESH,
                )
                for place, (source, target) in enumerate(zip(sources, targets))
            ]
            self.come = [
                pltpu.make_async_remote_copy(
                    src_ref=landing,
                    dst_ref=landing,
                    send_sem=send.at[base + place],
                    recv_sem=recv.at[base + place],
                    device_id={axis: partner},
                    device_id_type=pl.DeviceIdType.MESH,
                )
                for place, landing in enumerate(landings)
            ]

        def start(self):
            for copy in self.out:
                copy.start()

        def arrive(self):
            for copy in self.come:
                copy.wait_recv()

        def leave(self):
            for copy in self.out:
                copy.wait_send()

    class LineBatch:
        def __init__(self, source_of, target_of, landing_of):
            base = counter[0]
            counter[0] += plan.z
            send, recv = mem.bulk_send, mem.bulk_recv
            self.out, self.come = [], []
            for step in range(1, plan.z):
                z_to = (z_me + step) % plan.z
                self.out.append(
                    pltpu.make_async_remote_copy(
                        src_ref=source_of(z_to),
                        dst_ref=target_of(z_to),
                        send_sem=send.at[base + step],
                        recv_sem=recv.at[base + z_me],
                        device_id={FSDP: z_to * plan.x + x_me},
                        device_id_type=pl.DeviceIdType.MESH,
                    )
                )
                self.come.append(
                    pltpu.make_async_remote_copy(
                        src_ref=landing_of(z_to),
                        dst_ref=landing_of(z_to),
                        send_sem=send.at[base + step],
                        recv_sem=recv.at[base + z_to],
                        device_id={FSDP: z_to * plan.x + x_me},
                        device_id_type=pl.DeviceIdType.MESH,
                    )
                )

        start, arrive, leave = Batch.start, Batch.arrive, Batch.leave

    def pick(ref, indexes):
        return [ref.at[index] for index in indexes]

    def own_dp(y_index, c_index):
        return y_index * 2 + c_index

    x_partner = z_me * plan.x + x_other
    y_partner = own_dp(y_other, c_me)
    c_partner = own_dp(y_me, c_other)
    dp_far = own_dp(y_other, c_other)

    class Gather:
        def __init__(self, which, start, size):
            ref = weights[which]
            self.which, self.rows = which, (start, size)
            both, low, high = (start, size), (start, size // 2), (start + size // 2, size // 2)

            def at(*index):
                return pick(ref, places(which, *index, False))

            own = at(z_me, x_me, dp_me, both)[0]
            self.line = LineBatch(
                lambda _: own, lambda _: own, lambda z_from: at(z_from, x_me, dp_me, both)[0]
            )
            sent, come = at(None, x_me, dp_me, low), at(None, x_other, dp_me, low)
            x_first = Batch(sent, sent, come, FSDP, x_partner)
            sent, come = at(None, x_me, dp_me, high), at(None, x_me, y_partner, high)
            y_first = Batch(sent, sent, come, DP, y_partner)
            sent, come = at(None, None, dp_me, low), at(None, None, y_partner, low)
            y_second = Batch(sent, sent, come, DP, y_partner)
            sent = at(None, x_me, dp_me, high) + at(None, x_me, y_partner, high)
            come = at(None, x_other, dp_me, high) + at(None, x_other, y_partner, high)
            x_second = Batch(sent, sent, come, FSDP, x_partner)
            sent = at(None, None, dp_me, both) + at(None, None, y_partner, both)
            come = at(None, None, c_partner, both) + at(None, None, dp_far, both)
            core = Batch(sent, sent, come, DP, c_partner)
            self.stages = ((self.line,), (x_first, y_first), (y_second, x_second), (core,))

        def put_own(self):
            index = places(self.which, z_me, x_me, dp_me, self.rows, False)[0]
            shard = ins.shards[self.which][self.rows[0] : self.rows[0] + self.rows[1], :]
            weights[self.which][index] = shard.astype(bf16)

        def start(self, stage):
            for batch in self.stages[stage]:
                batch.start()

        def arrive(self, stage):
            for batch in self.stages[stage]:
                batch.arrive()

        def leave(self):
            for stage in self.stages:
                for batch in stage:
                    batch.leave()

    class Piece:
        def __init__(self, which, ref, room, z_index):
            def at(*index):
                return pick(ref, places(which, z_index, *index))

            def land(*index):
                return [room(index_one) for index_one in places(which, z_index, *index)]

            self.z = z_index
            self.core = Batch(
                at(None, c_partner, None) + at(None, dp_far, None),
                land(None, c_partner, None) + land(None, dp_far, None),
                land(None, dp_me, None) + land(None, y_partner, None),
                DP,
                c_partner,
            )
            self.y_first = Batch(
                at(None, y_partner, 0), land(None, dp_far, 0), land(None, c_partner, 0), DP, y_partner
            )
            self.x_first = Batch(
                at(x_other, dp_me, 1) + at(x_other, y_partner, 1),
                land(x_other, c_partner, 1) + land(x_other, dp_far, 1),
                land(x_me, c_partner, 1) + land(x_me, dp_far, 1),
                FSDP,
                x_partner,
            )
            self.x_second = Batch(
                at(x_other, dp_me, 0), land(x_other, dp_far, 0), land(x_me, dp_far, 0), FSDP, x_partner
            )
            self.y_second = Batch(
                at(x_me, y_partner, 1), land(x_other, dp_far, 1), land(x_other, c_partner, 1), DP, y_partner
            )

    class Reduce:
        def __init__(self, which, ref, cut):
            self.which, self.ref, self.room = which, ref, recv_parts[which]
            self.pieces = [
                Piece(which, ref, self.room, z_index) for z_index in (range(plan.z) if cut else [None])
            ]
            self.base = counter[0]
            counter[0] += plan.z

        def line_copy(self, z_to):
            return pltpu.make_async_remote_copy(
                src_ref=self.ref.at[places(self.which, z_to, x_me, dp_me, None)[0]],
                dst_ref=self.room(places(self.which, z_me, x_other, dp_far, None)[0]),
                send_sem=mem.bulk_send.at[self.base + z_to],
                recv_sem=mem.bulk_recv.at[self.base + z_me],
                device_id={FSDP: z_to * plan.x + x_me},
                device_id_type=pl.DeviceIdType.MESH,
            )

        def line_room(self, z_from):
            return self.room(places(self.which, z_from, x_other, dp_far, None)[0])

        def add(self, z_index, pairs):
            def one(z_one):
                for here, there in pairs:
                    for x_step in range(plan.x) if here[0] is None else [None]:
                        x_here = x_step if here[0] is None else here[0]
                        x_there = x_step if there[0] is None else there[0]
                        index = places(self.which, z_one, x_here, *here[1:])[0]
                        other = places(self.which, z_one, x_there, *there[1:])[0]
                        total = self.ref[index].astype(f32) + self.room(other)[...].astype(f32)
                        self.ref[index] = total.astype(bf16)

            if z_index is None:
                pl.loop(0, plan.z)(one)
            else:
                one(z_index)

        def core_start(self, place=0):
            if plan.inside:
                self.pieces[place].core.start()

        def core_add(self, place=0):
            if plan.inside:
                piece = self.pieces[place]
                piece.core.arrive()
                self.add(piece.z, [((None, dp_me, None),) * 2, ((None, y_partner, None),) * 2])
                piece.y_first.start()
                piece.x_first.start()

        def first_add(self, place=0):
            if plan.inside:
                piece = self.pieces[place]
                piece.y_first.arrive()
                self.add(piece.z, [((None, dp_me, 0), (None, c_partner, 0))])
                piece.x_second.start()
                piece.x_first.arrive()
                self.add(
                    piece.z, [((x_me, dp_me, 1), (x_me, c_partner, 1)), ((x_me, y_partner, 1), (x_me, dp_far, 1))]
                )
                piece.y_second.start()

        def second_add(self, place=0):
            if plan.inside:
                piece = self.pieces[place]
                piece.x_second.arrive()
                piece.y_second.arrive()
                self.add(
                    piece.z, [((x_me, dp_me, 0), (x_me, dp_far, 0)), ((x_me, dp_me, 1), (x_other, c_partner, 1))]
                )
                if piece.z is None:
                    for step in range(1, plan.z):
                        self.line_copy((z_me + step) % plan.z).start()
                else:

                    @pl.when(z_me != piece.z)
                    def _():
                        self.line_copy(piece.z).start()

        def finish(self):
            if not plan.inside:
                return
            total = self.ref[places(self.which, z_me, x_me, dp_me, None)[0]].astype(f32)
            for step in range(1, plan.z):
                z_from = (z_me + step) % plan.z
                room = self.line_room(z_from)
                pltpu.make_async_remote_copy(
                    src_ref=room,
                    dst_ref=room,
                    send_sem=mem.bulk_send.at[self.base + z_from],
                    recv_sem=mem.bulk_recv.at[self.base + z_from],
                    device_id={FSDP: z_from * plan.x + x_me},
                    device_id_type=pl.DeviceIdType.MESH,
                ).wait_recv()
                total = total + room[...].astype(f32)
            outs.grads[self.which][...] = total
            squares = jnp.sum(total * total, axis=0, keepdims=True)
            folded = squares[:, :LANES]
            for place in range(1, squares.shape[1] // LANES):
                folded = folded + squares[:, place * LANES : (place + 1) * LANES]
            mem.squares[...] += folded
            for step in range(1, plan.z):
                self.line_copy((z_me + step) % plan.z).wait_send()
            for piece in self.pieces:
                for batch in (piece.core, piece.y_first, piece.x_first, piece.x_second, piece.y_second):
                    batch.leave()

    gathers, steps = [], []
    if plan.inside:
        for which, cuts in enumerate((2, 3, 1, 2, 1)):
            size = 2 * plan.half[which] // cuts
            gathers += [Gather(which, cut * size, size) for cut in range(cuts)]

    def line_step(place):
        gathers[place].arrive(0)
        gathers[place].start(1)
        if place + 1 < len(gathers):
            gathers[place + 1].start(0)

    def first_step(place):
        gathers[place].arrive(1)
        gathers[place].start(2)

    def second_step(place):
        gathers[place].arrive(2)
        gathers[place].start(3)

    for place in range(len(gathers)):
        steps.append((line_step, place))
        if place > 0:
            steps.append((second_step, place - 1))
        steps.append((first_step, place))
    if plan.inside:
        steps.append((second_step, len(gathers) - 1))

    def take(count):
        taken, steps[:] = steps[:count], steps[count:]
        return [lambda one=one: one[0](one[1]) for one in taken]

    def moves(site, item):
        found = take(GATHER_AT.get((site, item), 0)) if plan.inside else []
        for which, piece, kind in REDUCE_AT.get((site, item), ()):
            one = reduces[which]
            found.append(
                one.finish
                if kind == 4
                else lambda one=one, kind=kind, piece=piece: (
                    one.core_start,
                    one.core_add,
                    one.first_add,
                    one.second_add,
                )[kind](piece)
            )
        return found

    def hook(site, item=0):
        for move in moves(site, item):
            move()

    def hook_in(site, index, count, first=0, stride=1):
        for item in range(count):
            found = moves(site, item)
            if found and plan.inside:

                @pl.when(index == first + item * stride)
                def _(found=found):
                    for move in found:
                        move()

    def when_at(index, choices):
        for item, found in enumerate(choices):
            if found and plan.inside:

                @pl.when(index == item)
                def _(found=found):
                    for move in found:
                        move()

    def cores_arrive(which):
        for one in gathers:
            if one.which == which:
                one.arrive(3)

    gradients = [mem.g1, mem.stage.at[pl.ds(0, 9 * C_MID)], weights[2], weights[3], weights[4]]
    reduces = [Reduce(which, gradients[which], which < 4) for which in range(5)]
    assert counter[0] <= COPIES
    mem.squares[...] = jnp.zeros((1, LANES), f32)

    if plan.inside:
        gathers[0].put_own()
        gathers[0].start(0)
        for one in gathers[1:]:
            one.put_own()
        tiles = mem.norm_tiles
        tiles[dp_me, fsdp_me] = ins.norm[...].astype(bf16).astype(f32)
        norm_dp = share(
            DP, plan.dp, dp_me, lambda _: tiles.at[dp_me, fsdp_me], tiles.at[:, fsdp_me], mem.norm_s0, mem.norm_r0
        )
        norm_dp[0]()
    else:
        loads = [
            pltpu.make_async_copy(ins.shards[which], weights[which], mem.bulk_send.at[which])
            for which in range(5)
        ]
        for load in loads:
            load.start()

    pieces = BLOCKS * CHUNKS

    def hidden_rows(index, pixel=0, count=chunk):
        return pl.ds(pl.multiple_of(index * chunk + pixel * views, 16), count)

    class Ring:
        def __init__(self, ref, start):
            self.ref, self.base = ref, start

        def rows(self, index, pixel=0, count=chunk):
            return pl.ds(
                pl.multiple_of(self.base + lax.rem(index, SLOTS) * chunk + pixel * views, 16), count
            )

        def copy(self, array, index, into):
            block, place = index // CHUNKS, lax.rem(index, CHUNKS)
            outer = array.at[
                pl.ds(pl.multiple_of(place * chunk, 16), chunk),
                pl.ds(pl.multiple_of(block * C_MID, LANES), C_MID),
            ]
            inner = self.ref.at[self.rows(index)]
            source, target = (outer, inner) if into else (inner, outer)
            return pltpu.make_async_copy(
                source, target, mem.stage_sem.at[0 if into else 1, lax.rem(index, SLOTS)]
            )

        def first_loads(self, array):
            for index in range(AHEAD):
                self.copy(array, index, True).start()

        def next_load(self, array, index):
            @pl.when(index + AHEAD < pieces)
            def _():
                self.copy(array, index + AHEAD, True).start()

        def save(self, array, index):
            self.copy(array, index, False).start()

            @pl.when(index >= 1)
            def _():
                self.copy(array, index - 1, False).wait()

        def last_saves(self, array):
            self.copy(array, pieces - 1, False).wait()

    stage_ref = mem.stage
    stage = Ring(stage_ref, 0)

    def piece_columns(index, part):
        return pl.ds(pl.multiple_of(index // CHUNKS * C_MID + part * LANES, LANES), LANES)

    features, slope_hbm = ins.features, outs.slope
    hidden_three = mem.h3

    def feature_copy(block, target):
        return pltpu.make_async_copy(
            features.at[:, pl.ds(block * C_MID, C_MID)], target, mem.column_sem.at[block]
        )

    feature_loads = [
        feature_copy(block, hidden_three.at[pl.ds(block * rows, rows)]) for block in range(BLOCKS)
    ]
    for copy in feature_loads:
        copy.start()
    stage.first_loads(features)

    padded_one, padded_two = mem.pad1, mem.pad2
    for padded in (padded_one, padded_two):
        for edge in (0, SIDE + 1):
            padded[edge] = jnp.zeros((padded.shape[1], C_MID), bf16)
        for edge in (0, SIDE + 1):
            padded[:, pl.ds(edge * views, views), :] = jnp.zeros((SIDE + 2, views, C_MID), bf16)
    rest = jnp.zeros((tall - rows, C_MID), bf16)
    for ref, end in ((mem.d1, rows), (mem.h2, rows), (mem.d2, rows), (mem.a2, rows), (hidden_three, BLOCKS * rows)):
        ref[end : end + tall - rows, :] = rest

    if plan.inside:
        norm_dp[1]()
        norm_out = []
        norm_in = []
        for step in range(1, plan.fsdp):
            partner = (fsdp_me + step) % plan.fsdp
            norm_out.append(
                pltpu.make_async_remote_copy(
                    src_ref=tiles.at[:, fsdp_me],
                    dst_ref=tiles.at[:, fsdp_me],
                    send_sem=mem.norm_s1.at[step],
                    recv_sem=mem.norm_r1.at[fsdp_me],
                    device_id={FSDP: partner},
                    device_id_type=pl.DeviceIdType.MESH,
                )
            )
            norm_in.append(
                pltpu.make_async_remote_copy(
                    src_ref=tiles.at[:, partner],
                    dst_ref=tiles.at[:, partner],
                    send_sem=mem.norm_s1.at[step],
                    recv_sem=mem.norm_r1.at[partner],
                    device_id={FSDP: partner},
                    device_id_type=pl.DeviceIdType.MESH,
                )
            )
        for copy in norm_out:
            copy.start()
        hook(21)
        for copy in norm_in:
            copy.wait_recv()
        for copy in norm_out:
            copy.wait_send()
        norm_all = mem.norm
        for dp_one in range(plan.dp):
            for fsdp_one in range(plan.fsdp):
                start = (dp_one * plan.fsdp + fsdp_one) * LANES
                norm_all[:, start : start + LANES] = tiles[dp_one, fsdp_one]
    else:
        for copy in loads:
            copy.wait()
        norm_all = mem.norm
        norm_all[...] = ins.norm[...]

    starts = (0, C_MID, 2 * C_MID, 2 * C_MID + C_IN, 2 * C_MID + C_IN + P_HID)

    def gain(layer):
        return norm_all[0:1, starts[layer] : starts[layer + 1]]

    coef, stats = mem.coef, mem.stats

    def norm_coefs(layer, totals, count, low=0):
        width = totals.shape[1]
        here, there = slice(low, low + width), slice(starts[layer] + low, starts[layer] + low + width)
        mean = totals[0:1] / count
        scaling = lax.rsqrt(totals[1:2] / count - mean * mean + norm_epsilon)
        slope = scaling * norm_all[0:1, there]
        stats[0:1, there] = mean
        stats[1:2, there] = scaling
        coef[0:1, here] = slope
        coef[1:2, here] = norm_all[1:2, there] - mean * slope

    def grad_coefs(layer, totals, count):
        width = starts[layer + 1] - starts[layer]
        mean = stats[0:1, starts[layer] : starts[layer + 1]]
        scaling = stats[1:2, starts[layer] : starts[layer + 1]]
        mem.norm_grads[0:1, starts[layer] : starts[layer + 1]] = totals[1:2]
        mem.norm_grads[1:2, starts[layer] : starts[layer + 1]] = totals[0:1]
        slope = scaling * gain(layer)
        bend = slope * scaling * totals[1:2] / count
        coef[0:1, :width] = slope
        coef[1:2, :width] = slope * totals[0:1] / count - mean * bend
        coef[2:3, :width] = bend

    def xhat_sum(layer, plain, product):
        mean = stats[0:1, starts[layer] : starts[layer + 1]]
        scaling = stats[1:2, starts[layer] : starts[layer + 1]]
        return scaling * (product - mean * plain)

    zero_row = jnp.zeros((1, C_MID), f32)

    def column_sums(value):
        return jnp.sum(value, axis=0, keepdims=True)

    def whole(which):
        value = weights[which][...]
        return value.reshape(-1, value.shape[-1])

    row_sums = mem.row_sums

    def clear_sums():
        row_sums[...] = jnp.zeros_like(row_sums)

    def count_in(cols, value, other):
        row_sums[0:1, cols] += column_sums(value)
        row_sums[1:2, cols] += column_sums(value * other)

    def own_columns(side):
        core = (c_me + side) % 2
        return [
            pl.ds(pl.multiple_of(half * (C_MID // 2) + core * LANES, LANES), LANES) for half in range(2)
        ]

    def turn_rows(ref):
        @pl.loop(0, tall // C_MID)
        def _(block):
            at = pl.ds(pl.multiple_of(block * C_MID, C_MID), C_MID)
            ref[at, :] = ref[at, :].T

    def turned(ref):
        return jnp.concatenate([ref[start : start + C_MID, :] for start in range(0, tall, C_MID)], axis=1)

    def sends_leave(which):
        for one in gathers:
            if one.which == which:
                one.leave()

    def turn_weight(which, block):
        ref = weights[which]
        if which == 1:
            groups = [block * 8 + group for group in range(8)]
            ats = [
                (group // 18, group // 9 % 2, pl.ds(pl.multiple_of(group % 9 * 64, 64), 64), everything)
                for group in groups
            ]
            value = jnp.concatenate([ref[at] for at in ats], axis=0).T
            for place, at in enumerate(ats):
                ref[at] = value[place * 64 : (place + 1) * 64, :]
        elif which == 3:
            for half in range(P_HID // C_MID):
                cols = slice(half * C_MID, (half + 1) * C_MID)
                value = ref[block, :, :, cols]
                ref[block, :, :, cols] = value.reshape(C_MID, C_MID).T.reshape(value.shape)
        else:
            value = ref[block]
            ref[block] = value.reshape(C_MID, C_MID).T.reshape(value.shape)

    hidden_one, slope_one = mem.h1, mem.d1
    hidden_two, slope_two = mem.h2, mem.d2
    act_two = mem.a2
    long = rows // 3

    def span(index):
        return pl.ds(pl.multiple_of(index * chunk, 16), chunk)

    def long_rows(block, index):
        return pl.ds(pl.multiple_of(block * rows + index * long, 16), long)

    def put_sides(ref, at, sides, hidden):
        for place, cols in enumerate(sides):
            part = hidden[:, place * LANES : (place + 1) * LANES]
            ref[at, cols] = part.astype(bf16)
            count_in(cols, part, part)

    for copy in feature_loads:
        copy.wait()
    clear_sums()

    @pl.loop(0, 2)
    def _(side):
        sides = own_columns(side)

        @pl.loop(0, 3)
        def _(index):
            left = jnp.concatenate([hidden_three[long_rows(block, index), :] for block in range(BLOCKS)], axis=1)
            right = jnp.concatenate([weights[0][:, :, :, cols].reshape(C_IN, LANES) for cols in sides], axis=1)
            put_sides(hidden_one, long_rows(0, index), sides, dot(left, right))

            hook_in(0, side * 3 + index, 6)

        @pl.when(side == 0)
        def _():
            cores_arrive(0)

    sum_one = Sum(0)
    sum_one.start(row_sums[0:1, :C_MID], row_sums[1:2, :C_MID])
    hook(1)
    sends_leave(0)
    pl.loop(0, 2)(lambda block: turn_weight(0, block))
    sum_one.middle()
    pl.loop(2, 4)(lambda block: turn_weight(0, block))
    hook(2)
    clear_sums()
    norm_coefs(0, sum_one.finish(), row_total)

    def activate(hidden_ref, slope_ref, put, site):
        @pl.loop(0, PIX)
        def _(pixel):
            place = pl.ds(pl.multiple_of(pixel * views, 16), views)
            for block in range(C_MID // LANES):
                cols = slice(block * LANES, (block + 1) * LANES)
                out = hidden_ref[place, cols].astype(f32) * coef[0:1, cols] + coef[1:2, cols]
                value, slope = gelu_pair(out)
                slope_ref[place, cols] = slope.astype(bf16)
                put(pixel, cols, value.astype(bf16))
            hook_in(site, pixel, SIDE, SIDE - 1, SIDE)

    def put_padded(padded):
        def put(pixel, cols, value):
            padded[pixel // SIDE + 1, pl.ds(pl.multiple_of((pixel % SIDE + 1) * views, 16), views), cols] = value

        return put

    activate(hidden_one, slope_one, put_padded(padded_one), 3)
    hook(4)

    def patch(padded, first, count, flip):
        found = []
        for vertical in range(3):
            for lateral in range(3):
                down, across = (2 - vertical, 2 - lateral) if flip else (vertical, lateral)
                piece = padded[pl.ds(first + down, count), across * views : across * views + chunk, :]
                found.append(piece.reshape(count * chunk, C_MID))
        return jnp.concatenate(found, axis=1)

    def image_rows(first, count):
        return pl.ds(pl.multiple_of(first * chunk, 16), count * chunk)

    def second_part(sides, first, count):
        right = jnp.concatenate([weights[1][:, :, :, cols].reshape(9 * C_MID, LANES) for cols in sides], axis=1)
        hidden = dot(patch(padded_one, first, count, False), right)
        put_sides(hidden_two, image_rows(first, count), sides, hidden)

    found = [moves(5, item) for item in range(4)]

    @pl.loop(0, 2)
    def _(side):
        sides = own_columns(side)

        second_part(sides, 0, 4)
        when_at(side, (found[0], found[2]))
        second_part(sides, 4, 3)
        when_at(side, (found[1], found[3]))

        @pl.when(side == 0)
        def _():
            cores_arrive(1)

    sum_two = Sum(1)
    sum_two.start(row_sums[0:1, :C_MID], row_sums[1:2, :C_MID])
    hook(6)
    sends_leave(1)
    pl.loop(0, 4)(lambda block: turn_weight(1, block))
    sum_two.middle()
    pl.loop(4, 9)(lambda block: turn_weight(1, block))
    hook(7)
    clear_sums()
    norm_coefs(1, sum_two.finish(), row_total)

    def put_rows(pixel, cols, value):
        act_two[pl.ds(pl.multiple_of(pixel * views, 16), views), cols] = value

    activate(hidden_two, slope_two, put_rows, 8)
    cores_arrive(2)

    def weight_three(block):
        return weights[2][block].reshape(C_MID, C_MID)

    sums_low, sums_high = Sum(2), Sum(3)
    half_width = C_IN // 2

    @pl.loop(0, BLOCKS)
    def _(block):
        cols = pl.ds(pl.multiple_of(block * C_MID, LANES), C_MID)

        @pl.loop(0, 3)
        def _(index):
            hidden = dot(act_two[long_rows(0, index), :], weight_three(block))
            hidden_three[long_rows(block, index), :] = hidden.astype(bf16)
            count_in(cols, hidden, hidden)
            hook_in(9, block * 3 + index, 12)

        @pl.when(block == 1)
        def _():
            sums_low.start(row_sums[0:1, :half_width], row_sums[1:2, :half_width])

        @pl.when(block == 2)
        def _():
            sums_low.middle()

    sums_high.start(row_sums[0:1, half_width:], row_sums[1:2, half_width:])
    norm_coefs(2, sums_low.finish(), row_total)

    hook(22)

    pool, pool_slope, pool_bend = mem.pool, mem.pool_slope, mem.pool_bend
    for ref in (pool, pool_slope, pool_bend):
        ref[...] = jnp.zeros_like(ref)

    @pl.loop(0, pieces)
    def _(index):
        stage.copy(features, index, True).wait()

        @pl.loop(0, C_MID // LANES)
        def _(part):
            inner = pl.ds(pl.multiple_of(part * LANES, LANES), LANES)
            cols = piece_columns(index, part)
            slope_row, shift_row = coef[0:1, cols], coef[1:2, cols]
            kept = (pool[:, cols], pool_slope[:, cols], pool_bend[:, cols])
            slopes = []
            for pixel in range(SIDE):
                stage_at, hidden_at = stage.rows(index, pixel, views), hidden_rows(index, pixel, views)
                hidden = hidden_three[hidden_at, inner].astype(f32)
                total = hidden * slope_row + shift_row + stage_ref[stage_at, inner].astype(f32)
                value, slope = gelu_pair(total)
                slopes.append((stage_at, slope.astype(bf16)))
                kept = (kept[0] + value, kept[1] + slope, kept[2] + slope * hidden)
            for stage_at, slope in slopes:
                stage_ref[stage_at, inner] = slope
            pool[:, cols], pool_slope[:, cols], pool_bend[:, cols] = kept

        stage.save(slope_hbm, index)
        stage.next_load(features, index)

        @pl.when(index == 2)
        def _():
            sums_high.middle()

        @pl.when(index == pieces // 2 - 1)
        def _():
            norm_coefs(2, sums_high.finish(), row_total, half_width)

        hook_in(10, index, pieces)

    stage.last_saves(slope_hbm)
    cores_arrive(3)
    cores_arrive(4)
    for which in range(2, 5):
        sends_leave(which)

    pooled = (pool[...] * (1.0 / PIX)).astype(bf16)
    mem.pooled[...] = pooled
    proj_hidden = dot(pooled, whole(3))
    sum_four = Sum(4)
    sum_four.start(column_sums(proj_hidden), column_sums(proj_hidden * proj_hidden))
    pl.loop(0, 2)(lambda block: turn_weight(3, block))
    sum_four.middle()
    pl.loop(2, 4)(lambda block: turn_weight(3, block))
    totals = sum_four.finish()
    stage.first_loads(slope_hbm)
    norm_coefs(3, totals, view_total)
    value, slope = gelu_pair(proj_hidden * coef[0:1, :P_HID] + coef[1:2, :P_HID])
    proj_act = value.astype(bf16)
    mem.proj_act[...] = proj_act
    mem.proj_slope[...] = slope
    mem.proj_hidden[...] = proj_hidden

    def weight_five(block):
        return weights[4][block // plan.x, block % plan.x]

    parts = P_HID // P_OUT
    embedding = jnp.zeros((views, P_OUT), f32)
    for block in range(parts):
        embedding = embedding + dot_cols(proj_act[:, block * P_OUT : (block + 1) * P_OUT], weight_five(block))

    images = views // 2
    order = jnp.broadcast_to(ins.order[...], (images, views))
    image_row = lax.broadcasted_iota(jnp.int32, (images, views), 0)
    selectors = [(order == 2 * image_row + which).astype(f32) for which in range(2)]
    embeds = [exact_dot(selector, embedding) for selector in selectors]
    moments = [exact_rows(embed, embed) for embed in embeds]
    packed, diagonal = pack_pair(*moments)
    packed, extra = sum_matrix(0, packed, [diagonal] + [column_sums(embed) for embed in embeds])
    moments = unpack_pair(packed, extra[0])
    eye = (
        lax.broadcasted_iota(jnp.int32, (P_OUT, P_OUT), 0) == lax.broadcasted_iota(jnp.int32, (P_OUT, P_OUT), 1)
    ).astype(f32)
    centred, covariances = [], []
    for which in range(2):
        mean = extra[1 + which] / image_total
        centred.append(embeds[which] - mean)
        covariances.append(moments[which] / image_total - exact_rows(mean, mean) + ridge_term * eye)
    inverses = inverse_factors(covariances)
    whitened = [exact_cols(centred[which], inverses[which]) for which in range(2)]
    scalings = [
        lax.rsqrt(jnp.mean(white * white, axis=1, keepdims=True) + norm_epsilon) for white in whitened
    ]
    units = [white * scaling for white, scaling in zip(whitened, scalings)]
    difference = units[0] - units[1]
    objective_row = column_sums(difference * difference) * (1.0 / P_OUT)
    unit_grads = [difference * (2.0 / P_OUT), difference * (-2.0 / P_OUT)]
    white_grads = []
    for which in range(2):
        inner = jnp.mean(whitened[which] * unit_grads[which], axis=1, keepdims=True)
        white_grads.append(
            scalings[which] * unit_grads[which] - whitened[which] * (scalings[which] ** 3 * inner)
        )
    directs = [exact_dot(white_grads[which], inverses[which]) for which in range(2)]
    products = [exact_rows(white_grads[which], whitened[which]) for which in range(2)]
    packed, diagonal = pack_pair(*products)
    packed, extra = sum_matrix(
        1, packed, [diagonal] + [column_sums(grad) for grad in white_grads] + [objective_row]
    )
    products = unpack_pair(packed, extra[0])
    embed_grad = jnp.zeros((views, P_OUT), f32)
    for which in range(2):
        symmetric = exact_rows(inverses[which], exact_dot(products[which], inverses[which]))
        mean_grad = exact_dot(extra[1 + which], inverses[which])
        grad = directs[which] - (exact_dot(centred[which], symmetric) + mean_grad) / image_total
        embed_grad = embed_grad + exact_rows(selectors[which], grad)
    objective_row = extra[3]
    embed_low = embed_grad.astype(bf16)

    proj_act, proj_hidden = mem.proj_act[...], mem.proj_hidden[...]
    act_grad = jnp.concatenate([dot(embed_low, weight_five(block)) for block in range(parts)], axis=1)
    upstream = act_grad * mem.proj_slope[...]
    plain = column_sums(upstream)
    sum_four_back = Sum(5)
    sum_four_back.start(plain, xhat_sum(3, plain, column_sums(upstream * proj_hidden)))
    for block in range(parts):
        weights[4][block // plan.x, block % plan.x] = dot_rows(
            embed_low, proj_act[:, block * P_OUT : (block + 1) * P_OUT]
        ).astype(bf16)
    pl.loop(0, 4)(lambda block: turn_weight(2, block))
    sum_four_back.middle()
    turn_rows(act_two)
    grad_coefs(3, sum_four_back.finish(), view_total)
    four_low = (
        upstream * coef[0:1, :P_HID] - coef[1:2, :P_HID] - proj_hidden * coef[2:3, :P_HID]
    ).astype(bf16)
    @pl.loop(0, BLOCKS)
    def _(block):
        cols = pl.ds(pl.multiple_of(block * C_MID, LANES), C_MID)
        right = jnp.concatenate(
            [
                weights[3][block, :, :, half * C_MID : (half + 1) * C_MID].reshape(C_MID, C_MID)
                for half in range(P_HID // C_MID)
            ],
            axis=0,
        )
        grad = dot(four_low, right) * (1.0 / PIX)
        row_sums[0:1, cols] = column_sums(grad * pool_slope[:, cols])
        row_sums[1:2, cols] = column_sums(grad * pool_bend[:, cols])
        pool_slope[:, cols] = grad

    plain = row_sums[0:1, :]
    sum_three_back = Sum(6)
    sum_three_back.start(plain, xhat_sum(2, plain, row_sums[1:2, :]))
    grad_four = dot_rows(mem.pooled[...], four_low).astype(bf16)
    weights[3][...] = grad_four.reshape(weights[3].shape)
    sum_three_back.middle()
    hook(23)
    grad_coefs(2, sum_three_back.finish(), row_total)
    pool[...] = pool_slope[...] * coef[0:1, :]

    clear_sums()

    @pl.loop(0, pieces)
    def _(index):
        stage.copy(slope_hbm, index, True).wait()
        stage.next_load(slope_hbm, index)

        @pl.loop(0, C_MID // LANES)
        def _(part):
            inner = pl.ds(pl.multiple_of(part * LANES, LANES), LANES)
            cols = piece_columns(index, part)
            spread, shift_row, bend_row = pool[:, cols], coef[1:2, cols], coef[2:3, cols]
            grads = []
            for pixel in range(SIDE):
                hidden_at = hidden_rows(index, pixel, views)
                hidden = hidden_three[hidden_at, inner].astype(f32)
                slope = stage_ref[stage.rows(index, pixel, views), inner].astype(f32)
                grads.append((hidden_at, (slope * spread - shift_row - hidden * bend_row).astype(bf16)))
            for hidden_at, grad in grads:
                hidden_three[hidden_at, inner] = grad

        hook_in(11, index, pieces)

    @pl.loop(0, 3)
    def _(index):
        at = long_rows(0, index)
        left = jnp.concatenate([hidden_three[long_rows(block, index), :] for block in range(BLOCKS)], axis=1)
        upstream = dot(left, weights[2][...].reshape(C_IN, C_MID)) * slope_two[at, :].astype(f32)
        slope_two[at, :] = upstream.astype(bf16)
        count_in(slice(0, C_MID), upstream, hidden_two[at, :].astype(f32))
        hook_in(12, index, 3)

    sums = row_sums[0:1, :C_MID], row_sums[1:2, :C_MID]
    sum_two_back = Sum(7)
    sum_two_back.start(sums[0], xhat_sum(1, *sums))

    @pl.loop(0, BLOCKS)
    def _(block):
        grad = dot(turned(act_two), hidden_three[pl.ds(pl.multiple_of(block * rows, 16), tall), :])
        weights[2][block] = grad.astype(bf16).reshape(plan.z, plan.x, -1, C_MID)

        @pl.when(block == 1)
        def _():
            sum_two_back.middle()

        hook_in(13, block, BLOCKS)

    clear_sums()
    grad_coefs(1, sum_two_back.finish(), row_total)

    def apply_grad(hidden_ref, grad_ref, put, site):
        @pl.loop(0, PIX)
        def _(pixel):
            place = pl.ds(pl.multiple_of(pixel * views, 16), views)
            for block in range(C_MID // LANES):
                cols = slice(block * LANES, (block + 1) * LANES)
                grad = (
                    grad_ref[place, cols].astype(f32) * coef[0:1, cols]
                    - coef[1:2, cols]
                    - hidden_ref[place, cols].astype(f32) * coef[2:3, cols]
                )
                put(pixel, cols, grad.astype(bf16))
            hook_in(site, pixel, SIDE, SIDE - 1, SIDE)

    def put_two(pixel, cols, value):
        put_padded(padded_two)(pixel, cols, value)
        slope_two[pl.ds(pl.multiple_of(pixel * views, 16), views), cols] = value

    apply_grad(hidden_two, slope_two, put_two, 14)
    turn_rows(slope_two)
    column_places = [
        hidden_three.at[pl.ds(2 * rows, rows)],
        hidden_three.at[pl.ds(3 * rows, rows)],
        hidden_two.at[pl.ds(0, rows)],
        hidden_three.at[pl.ds(2 * rows, rows)],
    ]
    column_loads = [feature_copy(block, column_places[block]) for block in range(BLOCKS)]
    for copy in column_loads[:3]:
        copy.start()
    def tap_grad(tap):
        down, across = tap // 3, tap % 3
        left = padded_one[pl.ds(down, SIDE), pl.ds(pl.multiple_of(across * views, 16), chunk), :]
        right = jnp.concatenate([left.reshape(rows, C_MID), jnp.zeros((tall - rows, C_MID), bf16)], axis=0)
        grad = dot(turned(slope_two), right).astype(bf16).T
        stage_ref[pl.ds(pl.multiple_of(tap * C_MID, 16), C_MID), :] = grad

    @pl.loop(0, 7)
    def _(tap):
        tap_grad(tap)
        hook_in(15, tap, 7)

    def second_back(half, first, count):
        at = image_rows(first, count)
        width = C_MID // 2
        cols = pl.ds(pl.multiple_of(half * width, LANES), width)
        right = weights[1][:, :, :, cols].reshape(9 * C_MID, width)
        upstream = dot(patch(padded_two, first, count, True), right) * slope_one[at, cols].astype(f32)
        slope_one[at, cols] = upstream.astype(bf16)
        count_in(cols, upstream, hidden_one[at, cols].astype(f32))

    found = [moves(16, item) for item in range(4)]

    @pl.loop(0, 2)
    def _(half):
        second_back(half, 0, 4)
        when_at(half, (found[0], found[2]))
        second_back(half, 4, 3)
        when_at(half, (found[1], found[3]))

    sums = row_sums[0:1, :C_MID], row_sums[1:2, :C_MID]
    sum_one_back = Sum(8)
    sum_one_back.start(sums[0], xhat_sum(0, *sums))

    @pl.loop(7, 9)
    def _(tap):
        tap_grad(tap)

        @pl.when(tap == 7)
        def _():
            sum_one_back.middle()

        hook_in(17, tap, 2, 7)

    grad_coefs(0, sum_one_back.finish(), row_total)

    def put_one(pixel, cols, value):
        put_rows(pixel, cols, value)
        slope_one[pl.ds(pl.multiple_of(pixel * views, 16), views), cols] = value

    apply_grad(hidden_one, slope_one, put_one, 18)
    turn_rows(slope_one)

    def block_grad(block):
        if block != 1:
            column_loads[block].wait()
        start = 3 * rows if block == 1 else 2 * rows
        right = hidden_two[...] if block == 2 else hidden_three[start : start + tall, :]
        grad = dot(turned(slope_one), right).astype(bf16).T
        mem.g1[block] = grad.reshape(plan.x, -1, C_MID)

    column_loads[1].wait()
    tail = Ring(hidden_two, 0)
    for block in range(BLOCKS):
        block_grad(block)
        if block == 0:
            column_loads[3].start()
        hook(19, block)
        if block == 2:
            tail.first_loads(slope_hbm)

    sum_last = Sum(9)

    @pl.loop(0, pieces)
    def _(index):
        block = index // CHUNKS
        back = dot(act_two[span(lax.rem(index, CHUNKS)), :], weights[0][block].reshape(C_MID, C_MID))
        tail.copy(slope_hbm, index, True).wait()
        cols = pl.ds(pl.multiple_of(block * C_MID, LANES), C_MID)
        found = []
        for pixel in range(SIDE):
            at = tail.rows(index, pixel, views)
            summed = hidden_two[at, :].astype(f32) * pool_slope[:, cols]
            found.append((at, (summed + back[pixel * views : (pixel + 1) * views]).astype(bf16)))
        for at, grad in found:
            hidden_two[at, :] = grad
        tail.save(outs.features_grad, index)
        tail.next_load(slope_hbm, index)
        hook_in(20, index, pieces)
        if plan.inside:

            @pl.when(index == LAST_SUM)
            def _():
                sum_last.start(mem.squares[...], mem.squares[...])

            @pl.when(index == LAST_SUM + 3)
            def _():
                sum_last.middle()

    tail.last_saves(outs.features_grad)
    squares = mem.squares[...]
    if plan.inside:
        squares = sum_last.finish()[0:1]
    norm_grads = mem.norm_grads[...]
    scalars = outs.scalars
    norm_squares = column_sums(norm_grads * norm_grads)
    for place in range(norm_squares.shape[1] // LANES):
        squares = squares + norm_squares[:, place * LANES : (place + 1) * LANES]
    scalars[...] = jnp.zeros_like(scalars)
    squares = jnp.sum(squares, axis=1, keepdims=True)
    norm = jnp.sqrt(squares)
    found = (jnp.sum(objective_row, axis=1, keepdims=True) / image_total, squares, norm, clip_factor(norm))
    for place, value in enumerate(found):
        scalars[place : place + 1, :] = jnp.broadcast_to(value, (1, LANES))
    if plan.inside:
        owner = (dp_me * plan.fsdp + fsdp_me) * LANES
        outs.norm_grad[...] = mem.norm_grads[:, pl.ds(pl.multiple_of(owner, LANES), LANES)]
    else:
        outs.norm_grad[...] = norm_grads
    if not plan.inside:
        stores = [
            pltpu.make_async_copy(gradients[which], outs.grads[which], mem.bulk_send.at[which])
            for which in range(5)
        ]
        for store in stores:
            store.start()
        for store in stores:
            store.wait()


def weight_shapes():
    return (
        (4, 2, 256, C_MID),
        (4, 2, 576, C_MID),
        (BLOCKS, 4, 2, 64, C_MID),
        (4, 2, 256, P_HID),
        (4, 2, P_OUT, P_OUT),
    )


def run_kernel(plan, features, order, shards, norm):
    rows, views = plan.rows, plan.views
    in_vmem = pl.BlockSpec(memory_space=pltpu.VMEM)
    anywhere = pl.BlockSpec(memory_space=pl.ANY)
    shapes = weight_shapes()
    operands = [features, order, norm, *shards]
    in_specs = [anywhere, in_vmem, in_vmem] + [in_vmem if plan.inside else anywhere] * 5
    results = [
        ((rows, C_IN), bf16, anywhere),
        ((rows, C_IN), bf16, anywhere),
        (norm.shape, f32, in_vmem),
        ((8, LANES), f32, in_vmem),
    ]
    for which, shard in enumerate(shards):
        if plan.inside:
            results.append((shard.shape, f32, in_vmem))
        else:
            results.append(((9 * C_MID, C_MID) if which == 1 else shapes[which], bf16, anywhere))
    dma = pltpu.SemaphoreType.DMA

    def sum_room(width):
        return SumRoom(
            pltpu.VMEM((plan.dp, 2, width), f32),
            pltpu.VMEM((plan.fsdp, 2, width), f32),
            dma((plan.dp,)),
            dma((plan.dp,)),
            dma((plan.fsdp,)),
            dma((plan.fsdp,)),
        )

    def matrix_room():
        size = plan.embed_rows
        return MatrixRoom(
            pltpu.VMEM((plan.dp, size, P_OUT), f32),
            pltpu.VMEM((plan.dp, size, P_OUT), f32),
            pltpu.VMEM((plan.fsdp, size, P_OUT), f32),
            pltpu.VMEM((plan.dp, size, P_OUT), f32),
            dma((plan.dp,)),
            dma((plan.dp,)),
            dma((plan.fsdp,)),
            dma((plan.fsdp,)),
            dma((plan.dp,)),
            dma((plan.dp,)),
        )

    scratch = Mem(
        w=[pltpu.VMEM(shape, bf16) for shape in shapes],
        g1=pltpu.VMEM(shapes[0], bf16),
        row_sums=pltpu.VMEM((2, C_IN), f32),
        r3=pltpu.VMEM(shapes[2], bf16),
        r4=pltpu.VMEM(shapes[3], bf16),
        r5=pltpu.VMEM(shapes[4], bf16),
        stage=pltpu.VMEM((max(SLOTS * plan.chunk, 9 * C_MID), C_MID), bf16),
        stage_sem=dma((2, SLOTS)),
        column_sem=dma((BLOCKS,)),
        h1=pltpu.VMEM((rows, C_MID), bf16),
        d1=pltpu.VMEM((plan.tall, C_MID), bf16),
        h2=pltpu.VMEM((plan.tall, C_MID), bf16),
        d2=pltpu.VMEM((plan.tall, C_MID), bf16),
        a2=pltpu.VMEM((plan.tall, C_MID), bf16),
        h3=pltpu.VMEM((3 * rows + plan.tall, C_MID), bf16),
        pad1=pltpu.VMEM((SIDE + 2, (SIDE + 2) * views, C_MID), bf16),
        pad2=pltpu.VMEM((SIDE + 2, (SIDE + 2) * views, C_MID), bf16),
        pool=pltpu.VMEM((views, C_IN), f32),
        pool_slope=pltpu.VMEM((views, C_IN), f32),
        pool_bend=pltpu.VMEM((views, C_IN), f32),
        pooled=pltpu.VMEM((views, C_IN), bf16),
        proj_act=pltpu.VMEM((views, P_HID), bf16),
        proj_slope=pltpu.VMEM((views, P_HID), f32),
        proj_hidden=pltpu.VMEM((views, P_HID), f32),
        coef=pltpu.VMEM((8, C_IN), f32),
        stats=pltpu.VMEM((2, norm_width()), f32),
        norm=pltpu.VMEM((2, norm_width()), f32),
        norm_grads=pltpu.VMEM((2, norm_width()), f32),
        norm_tiles=pltpu.VMEM((plan.dp, plan.fsdp, 2, LANES), f32),
        norm_s0=dma((plan.dp,)),
        norm_r0=dma((plan.dp,)),
        norm_s1=dma((plan.fsdp,)),
        norm_r1=dma((plan.fsdp,)),
        bulk_send=dma((COPIES,)),
        bulk_recv=dma((COPIES,)),
        mats=[matrix_room(), matrix_room()],
        sums=[
            sum_room(width)
            for width in (C_MID, C_MID, C_IN // 2, C_IN // 2, P_HID, C_IN, LANES)
        ],
        squares=pltpu.VMEM((1, LANES), f32),
    )
    values = pl.pallas_call(
        lambda *refs: kernel(plan, *refs),
        out_shape=[jax.ShapeDtypeStruct(shape, kind) for shape, kind, _ in results],
        in_specs=in_specs,
        out_specs=[spec for _, _, spec in results],
        scratch_shapes=[scratch],
        compiler_params=pltpu.CompilerParams(
            collective_id=1, has_side_effects=True, vmem_limit_bytes=63 * 2**20
        ),
        name="train_step",
    )(*operands)
    return Outs(*values[:4], values[4:])


def norm_width():
    return 2 * C_MID + C_IN + P_HID


def clip_factor(norm):
    return clip_level / jnp.maximum(norm, clip_level)


def adam_update(weight, moment_one, moment_two, gradient, step_rate, weight_decay):
    first_new = beta_first * moment_one + (1.0 - beta_first) * gradient
    second_new = beta_second * moment_two + (1.0 - beta_second) * gradient * gradient
    first_hat = first_new / (1.0 - beta_first**STEP)
    second_hat = second_new / (1.0 - beta_second**STEP)
    weight_new = weight - step_rate * (
        first_hat / (jnp.sqrt(second_hat) + adam_epsilon) + weight_decay * weight
    )
    return (weight_new, first_new, second_new)


def finish_kernel(rates, decays, *refs):
    count = len(rates)
    low, scalars = refs[0], refs[1]
    refs = refs[2:]
    given, wide, loss, norm, updated = refs[: 4 * count], *refs[4 * count : 4 * count + 3], refs[4 * count + 3 : -2]
    rooms, sems = refs[-2], refs[-1]
    wide[...] = low[...].astype(f32)
    step = pl.program_id(0)

    def load(place):
        return pltpu.make_async_copy(given[place], rooms[place], sems.at[place])

    def store(place):
        return pltpu.make_async_copy(rooms[place], updated[place], sems.at[place])

    @pl.when(step == 0)
    def _():
        loss[0, 0] = scalars[0, 0]
        norm[0, 0] = scalars[2, 0]
        for place in range(4 * count):
            load(place).start()

    @pl.when(step == 2)
    def _():
        for place in range(4 * count):
            load(place).wait()
        for place in range(count):
            weight, first, second, grad = (rooms[part * count + place][...] for part in range(4))
            found = adam_update(weight, first, second, grad * scalars[3, 0], rates[place], decays[place])
            for part in range(3):
                rooms[part * count + place][...] = found[part]
        for place in range(3 * count):
            store(place).start()

    @pl.when(step == CHUNKS - 1)
    def _():
        for place in range(3 * count):
            store(place).wait()


def finish(features_grad, scalars, masters, firsts, seconds, grads, rates, decays):
    rows = features_grad.shape[0]
    arrays = [*masters, *firsts, *seconds, *grads]
    moving = pl.BlockSpec((rows // CHUNKS, C_IN), lambda index: (index, 0))
    single = pl.BlockSpec(memory_space=pltpu.SMEM)
    anywhere = pl.BlockSpec(memory_space=pl.ANY)
    count = len(masters)
    values = pl.pallas_call(
        lambda *refs: finish_kernel(rates, decays, *refs),
        grid=(CHUNKS,),
        in_specs=[moving, single] + [anywhere] * (4 * count),
        out_specs=[moving, single, single] + [anywhere] * (3 * count),
        out_shape=[jax.ShapeDtypeStruct((rows, C_IN), f32)]
        + [jax.ShapeDtypeStruct((1, 1), f32)] * 2
        + [jax.ShapeDtypeStruct(array.shape, f32) for array in arrays[: 3 * count]],
        scratch_shapes=[
            [pltpu.VMEM(array.shape, f32) for array in arrays],
            pltpu.SemaphoreType.DMA((4 * count,)),
        ],
        compiler_params=pltpu.CompilerParams(vmem_limit_bytes=62 * 2**20),
        name="finish",
    )(features_grad, scalars, *arrays)
    groups = [values[3 + part * count : 3 + (part + 1) * count] for part in range(3)]
    return values[0], values[1].reshape(()), values[2].reshape(()), *groups


def gather_full(weight):
    outer = lax.all_gather(weight.astype(bf16), FSDP, axis=0, tiled=True)
    return lax.all_gather(outer, DP, axis=1, tiled=True)


def scatter_full(gradient):
    inner = lax.psum_scatter(gradient.astype(f32), DP, scatter_dimension=1, tiled=True)
    return lax.psum_scatter(inner, FSDP, scatter_dimension=0, tiled=True)


def body(features, view_order, *state):
    masters, firsts, seconds = state[:6], state[6:12], state[12:18]
    dp_size, fsdp_size = lax.axis_size(DP), lax.axis_size(FSDP)
    views = features.shape[0]
    inside = dp_size == 4 and fsdp_size == 8
    plan = Plan(dp_size, fsdp_size, views, inside)
    pixels = jnp.swapaxes(features, 0, 1).reshape(-1, C_IN)
    norm_params = masters[5]
    shapes = weight_shapes()
    if inside:
        shards = list(masters[:4]) + [masters[4].T]
        norm = norm_params
    else:
        full = [gather_full(weight) for weight in masters[:5]]
        shards = [
            full[0].reshape(shapes[0]),
            full[1].reshape(shapes[1]),
            full[2].reshape(C_MID, BLOCKS, C_MID).swapaxes(0, 1).reshape(shapes[2]),
            full[3].reshape(shapes[3]),
            full[4].reshape(4, 2, P_OUT, P_OUT).swapaxes(2, 3),
        ]
        norm = lax.all_gather(norm_params.astype(bf16), (DP, FSDP), axis=1, tiled=True).astype(f32)
    got = run_kernel(plan, pixels, view_order, shards, norm)
    grads = list(got.grads)
    scalars = got.scalars
    turned = [list(group) for group in (masters, firsts, seconds)]
    if inside:
        owned = grads
        for group in turned:
            group[4] = group[4].T
    else:
        whole_grads = [
            grads[0].reshape(C_IN, C_MID),
            grads[1],
            grads[2].reshape(BLOCKS, C_MID, C_MID).swapaxes(0, 1).reshape(C_MID, C_IN),
            grads[3].reshape(C_IN, P_HID),
            grads[4].swapaxes(2, 3).reshape(P_HID, P_OUT),
        ]
        owned = [scatter_full(gradient) for gradient in whole_grads]
        squares = scalars[1, 0] + lax.psum(sum(jnp.sum(grad * grad) for grad in owned), (DP, FSDP))
        norm_value = jnp.sqrt(squares)
        scalars = scalars.at[2].set(norm_value).at[3].set(clip_factor(norm_value))
    width = norm_params.shape[1]
    if inside:
        owned.append(got.norm_grad)
    else:
        owner = lax.axis_index((DP, FSDP))
        owned.append(lax.dynamic_slice_in_dim(got.norm_grad, owner * width, width, 1))
    step_rates = (
        C_IN ** (-0.5),
        (9 * C_MID) ** (-0.5),
        C_MID ** (-0.5),
        C_IN ** (-0.5),
        P_HID ** (-0.5),
        norm_rate,
    )
    decays = (decay_rate, decay_rate, decay_rate, decay_rate, decay_rate, 0.0)
    input_grad, loss, grad_norm, *updates = finish(
        got.features_grad, scalars, *turned, owned, step_rates, decays
    )
    if inside:
        updates = [[*group[:4], group[4].T, group[5]] for group in updates]
    return (
        loss,
        jnp.swapaxes(input_grad.reshape(PIX, views, C_IN), 0, 1),
        grad_norm,
        *updates[0],
        *updates[1],
        *updates[2],
    )


def solution(mesh):
    views = P((DP, FSDP), None, None)
    split = P(FSDP, DP)
    norm = P(None, (DP, FSDP))
    params = (split,) * 5 + (norm,)
    return jax.shard_map(
        body,
        mesh=mesh,
        in_specs=(views, P((DP, FSDP), None)) + params * 3,
        out_specs=(P(), views, P()) + params * 3,
        check_vma=False,
    )
```

```python
from typing import Any, NamedTuple

import jax
import jax.numpy as jnp
from jax import lax
from jax.experimental import pallas as pl
from jax.experimental.pallas import tpu as pltpu
from jax.sharding import PartitionSpec as P

C_IN = 2048
C_MID = 512
P_HID = 1024
P_OUT = 128
SIDE = 7
STEP = 10
PIX = 49
LANES = 128
BLOCKS = C_IN // C_MID
CHUNKS = SIDE
SLOTS = 6
LAST_SUM = 23
COPIES = 360


highest = lax.Precision.HIGHEST
bf16 = jnp.bfloat16
f32 = jnp.float32
norm_epsilon = 1e-05
ridge_term = 0.01
clip_level = 0.1
beta_first = 0.9
beta_second = 0.999
adam_epsilon = 1e-08
decay_rate = 0.05
norm_rate = 0.5
bell_scale = 0.3989422804014327
root_half = 0.5**0.5
bell_rate = -0.7213475204444817
DP, FSDP = "dp", "fsdp"


def gelu_pair(values):
    below = 0.5 + 0.5 * lax.erf(values * root_half)
    bell = jnp.exp2(values * values * bell_rate)
    return values * below, below + values * bell * bell_scale


def dot(left, right):
    return jnp.dot(left, right, preferred_element_type=f32)


def dot_cols(left, right):
    return lax.dot_general(left, right, (((1,), (1,)), ((), ())), preferred_element_type=f32)


def dot_rows(left, right):
    return lax.dot_general(left, right, (((0,), (0,)), ((), ())), preferred_element_type=f32)


def exact_cols(left, right):
    return lax.dot_general(
        left, right, (((1,), (1,)), ((), ())), precision=highest, preferred_element_type=f32
    )


def exact_rows(left, right):
    return lax.dot_general(
        left, right, (((0,), (0,)), ((), ())), precision=highest, preferred_element_type=f32
    )


def exact_dot(left, right):
    return jnp.dot(left, right, precision=highest, preferred_element_type=f32)


def inverse_factors(matrices):
    row_top = lax.broadcasted_iota(jnp.int32, (8, P_OUT), 0)
    row_all = lax.broadcasted_iota(jnp.int32, (P_OUT, P_OUT), 0)
    col_all = lax.broadcasted_iota(jnp.int32, (P_OUT, P_OUT), 1)

    def one_step(place, left, right):
        scale = lax.rsqrt(left[place : place + 1, place : place + 1])
        left_row = left[place : place + 1, :] * scale
        right_row = right[place : place + 1, :] * scale
        column = left[:, place : place + 1] * scale
        left = left - column * left_row
        right = right - column * right_row
        here = row_top == place
        left = jnp.concatenate([jnp.where(here, 0.0, left[:8]), left[8:]], axis=0)
        right = jnp.concatenate(
            [jnp.where(here, jnp.broadcast_to(right_row, (8, P_OUT)), right[:8]), right[8:]], axis=0
        )
        return left, right

    def panel(_, pairs):
        pairs = list(pairs)
        for place in range(8):
            for which in range(len(pairs)):
                pairs[which] = one_step(place, *pairs[which])
        return tuple(
            (
                pltpu.roll(jnp.concatenate([left[8:], left[:8]], axis=0), P_OUT - 8, 1),
                jnp.concatenate([right[8:], right[:8]], axis=0),
            )
            for left, right in pairs
        )

    pairs = tuple((matrix, (row_all == col_all).astype(f32)) for matrix in matrices)
    done = [[] for _ in matrices]
    size = P_OUT // 4
    for _ in range(4):
        pairs = lax.fori_loop(0, size // 8, panel, pairs)
        for found, (_, right) in zip(done, pairs):
            found.append(right[-size:])
        pairs = tuple((left[:-size], right[:-size]) for left, right in pairs)
    return [jnp.concatenate(found, axis=0) for found in done]


def pack_pair(first, second):
    row = lax.broadcasted_iota(jnp.int32, (P_OUT, P_OUT), 0)
    col = lax.broadcasted_iota(jnp.int32, (P_OUT, P_OUT), 1)
    packed = jnp.where(row >= col, first, second.T)
    diagonal = jnp.sum(jnp.where(row == col, second, 0.0), axis=0, keepdims=True)
    return packed, diagonal


def unpack_pair(packed, diagonal):
    row = lax.broadcasted_iota(jnp.int32, (P_OUT, P_OUT), 0)
    col = lax.broadcasted_iota(jnp.int32, (P_OUT, P_OUT), 1)
    turned = packed.T
    first = jnp.where(row >= col, packed, turned)
    second = jnp.where(row < col, packed, jnp.where(row == col, diagonal, turned))
    return first, second


GATHER_AT = {
    (0, 1): 1,
    (0, 3): 1,
    (1, 0): 1,
    (2, 0): 1,
    (4, 0): 5,
    (5, 0): 1,
    (5, 1): 1,
    (5, 2): 1,
    (5, 4): 1,
    (5, 5): 1,
    (5, 6): 1,
    (7, 0): 1,
    (8, 6): 1,
    (9, 2): 1,
    (9, 5): 1,
    (9, 8): 1,
    (21, 0): 7,
}
REDUCE_AT = {
    (11, 6): ((4, 0, 1),),
    (11, 20): ((4, 0, 2),),
    (12, 1): ((4, 0, 3),),
    (13, 3): ((2, 0, 0), (2, 1, 0), (2, 2, 0), (2, 3, 0)),
    (14, 3): ((4, 9, 4), (2, 0, 1)),
    (14, 6): ((2, 1, 1),),
    (15, 0): ((2, 2, 1), (2, 0, 2)),
    (15, 1): ((2, 3, 1),),
    (15, 2): ((1, 0, 0), (2, 1, 2)),
    (15, 3): ((2, 2, 2), (2, 0, 3)),
    (15, 4): ((1, 1, 0), (1, 0, 1), (2, 3, 2)),
    (15, 5): ((2, 1, 3), (2, 2, 3)),
    (15, 6): ((1, 2, 0), (1, 1, 1), (2, 3, 3)),
    (16, 0): ((1, 0, 2), (1, 2, 1), (2, 9, 4)),
    (16, 1): ((1, 1, 2), (1, 0, 3)),
    (16, 2): ((1, 2, 2), (1, 1, 3)),
    (17, 1): ((1, 3, 0),),
    (18, 2): ((1, 2, 3),),
    (18, 6): ((1, 3, 1),),
    (19, 0): ((0, 0, 0), (1, 3, 2)),
    (19, 1): ((0, 1, 0), (0, 0, 1), (1, 3, 3)),
    (19, 2): ((0, 2, 0), (0, 1, 1), (0, 0, 2)),
    (19, 3): ((0, 3, 0), (0, 2, 1), (0, 1, 2), (0, 0, 3)),
    (20, 2): ((0, 3, 1), (0, 2, 2), (0, 1, 3)),
    (20, 7): ((0, 3, 2), (0, 2, 3)),
    (20, 12): ((0, 3, 3), (1, 9, 4)),
    (20, 19): ((0, 9, 4),),
    (23, 0): ((4, 0, 0),),
}


class Ins(NamedTuple):
    features: Any
    order: Any
    norm: Any
    shards: Any


class Outs(NamedTuple):
    slope: Any
    features_grad: Any
    norm_grad: Any
    scalars: Any
    grads: Any


class SumRoom(NamedTuple):
    dp: Any
    fsdp: Any
    s0: Any
    r0: Any
    s1: Any
    r1: Any


class MatrixRoom(NamedTuple):
    pack: Any
    dp: Any
    fsdp: Any
    all: Any
    s0: Any
    r0: Any
    s1: Any
    r1: Any
    s2: Any
    r2: Any


class Mem(NamedTuple):
    w: Any
    g1: Any
    row_sums: Any
    r3: Any
    r1: Any
    left_rooms: Any
    right_rooms: Any
    factor_sems: Any
    four_low: Any
    r5: Any
    stage: Any
    stage_sem: Any
    column_sem: Any
    h1: Any
    d1: Any
    h2: Any
    d2: Any
    a2: Any
    h3: Any
    pad1: Any
    pad2: Any
    pool: Any
    pool_slope: Any
    pool_bend: Any
    pooled: Any
    proj_act: Any
    proj_slope: Any
    proj_hidden: Any
    coef: Any
    stats: Any
    norm: Any
    norm_grads: Any
    norm_tiles: Any
    norm_s0: Any
    norm_r0: Any
    norm_s1: Any
    norm_r1: Any
    bulk_send: Any
    bulk_recv: Any
    mats: Any
    sums: Any
    squares: Any


class Plan:
    def __init__(self, dp_size, fsdp_size, views, inside):
        self.dp = dp_size
        self.fsdp = fsdp_size
        self.devices = dp_size * fsdp_size
        self.views = views
        self.rows = views * PIX
        self.tall = -(-self.rows // C_MID) * C_MID
        self.chunk = views * SIDE
        self.inside = inside
        self.z = 4
        self.x = 2
        self.half = (128, 288, 32, 128, 16)
        self.width = (128, 128, 512, 256, 128)
        piece = P_OUT + 8
        self.embed_rows = -(-piece // (8 * dp_size)) * 8


def kernel(plan, *refs):
    ins, outs, mem = Ins(*refs[:3], refs[3:8]), Outs(*refs[8:12], refs[12:17]), refs[17]
    views, chunk, rows, tall = plan.views, plan.chunk, plan.rows, plan.tall
    row_total = float(rows * plan.devices)
    view_total = float(views * plan.devices)
    image_total = float(views * plan.devices // 2)
    dp_me, fsdp_me = lax.axis_index(DP), lax.axis_index(FSDP)
    y_me, c_me = dp_me // 2, dp_me % 2
    z_me, x_me = fsdp_me // 2, fsdp_me % 2
    y_other, c_other, x_other = 1 - y_me, 1 - c_me, 1 - x_me

    barrier = pltpu.get_barrier_semaphore()

    @pl.loop(1, plan.dp)
    def _(step):
        pl.semaphore_signal(
            barrier, 1, device_id={DP: lax.rem(dp_me + step, plan.dp)}, device_id_type=pl.DeviceIdType.MESH
        )

    @pl.loop(1, plan.fsdp)
    def _(step):
        pl.semaphore_signal(
            barrier, 1, device_id={FSDP: lax.rem(fsdp_me + step, plan.fsdp)}, device_id_type=pl.DeviceIdType.MESH
        )

    pl.semaphore_wait(barrier, plan.dp + plan.fsdp - 2)

    def share(axis, size, me, source_of, slots, send, recv):
        def outgoing(step):
            partner = lax.rem(me + step, size)
            return pltpu.make_async_remote_copy(
                src_ref=source_of(partner),
                dst_ref=slots.at[me],
                send_sem=send.at[step],
                recv_sem=recv.at[me],
                device_id={axis: partner},
                device_id_type=pl.DeviceIdType.MESH,
            )

        def incoming(step):
            source = lax.rem(me + step, size)
            return pltpu.make_async_remote_copy(
                src_ref=slots.at[source],
                dst_ref=slots.at[source],
                send_sem=send.at[step],
                recv_sem=recv.at[source],
                device_id={axis: source},
                device_id_type=pl.DeviceIdType.MESH,
            )

        def start():
            pl.loop(1, size)(lambda step: outgoing(step).start())

        def wait():
            pl.loop(1, size)(lambda step: incoming(step).wait_recv())
            pl.loop(1, size)(lambda step: outgoing(step).wait_send())

        return start, wait

    def add_slots(slots, size):
        total = slots[0]
        for place in range(1, size):
            total = total + slots[place]
        return total

    class Sum:
        def __init__(self, which):
            part = mem.sums[(0, 1, 2, 3, 4, 4, 5, 0, 1, 6)[which]]
            self.dp_slots, self.fsdp_slots = part.dp, part.fsdp
            self.dp_copy = share(
                DP, plan.dp, dp_me, lambda _: self.dp_slots.at[dp_me], self.dp_slots, part.s0, part.r0
            )
            self.fsdp_copy = share(
                FSDP, plan.fsdp, fsdp_me, lambda _: self.fsdp_slots.at[fsdp_me], self.fsdp_slots, part.s1, part.r1
            )

        def start(self, *values):
            for place, value in enumerate(values):
                self.dp_slots[dp_me, place : place + 1, :] = value
            self.dp_copy[0]()

        def middle(self):
            self.dp_copy[1]()
            self.fsdp_slots[fsdp_me] = add_slots(self.dp_slots, plan.dp)
            self.fsdp_copy[0]()

        def finish(self):
            self.fsdp_copy[1]()
            return add_slots(self.fsdp_slots, plan.fsdp)

        def all(self, *values):
            self.start(*values)
            self.middle()
            return self.finish()

    def sum_matrix(which, matrix, extra):
        part = mem.mats[which]
        size = plan.embed_rows
        pack = part.pack
        flat = jnp.concatenate(
            [matrix] + extra + [jnp.zeros((size * plan.dp - P_OUT - len(extra), P_OUT), f32)], axis=0
        )
        for place in range(plan.dp):
            pack[place] = flat[place * size : (place + 1) * size]
        start, wait = share(DP, plan.dp, dp_me, lambda to: pack.at[to], part.dp, part.s0, part.r0)
        start()
        part.dp[dp_me] = pack[dp_me]
        wait()
        part.fsdp[fsdp_me] = add_slots(part.dp, plan.dp)
        start, wait = share(
            FSDP, plan.fsdp, fsdp_me, lambda _: part.fsdp.at[fsdp_me], part.fsdp, part.s1, part.r1
        )
        start()
        wait()
        part.all[dp_me] = add_slots(part.fsdp, plan.fsdp)
        start, wait = share(
            DP, plan.dp, dp_me, lambda _: part.all.at[dp_me], part.all, part.s2, part.r2
        )
        start()
        wait()
        total = jnp.concatenate([part.all[place] for place in range(plan.dp)], axis=0)
        return total[:P_OUT], [total[P_OUT + place : P_OUT + place + 1] for place in range(len(extra))]

    weights = mem.w
    everything = slice(None)

    def row_span(which, half):
        if isinstance(half, tuple):
            return half
        size = plan.half[which]
        if half is None:
            return 0, 2 * size
        return half * size, size

    def column_span(which, dp_index):
        width = plan.width[which]
        return pl.ds(pl.multiple_of(dp_index * width, width), width)

    def places(which, z_index, x_index, dp_index, half, flat=True):
        start, size = row_span(which, half)
        if which == 1 and flat:
            z_list = range(plan.z) if z_index is None else [z_index]
            x_list = range(plan.x) if x_index is None else [x_index]
            return [
                (
                    pl.ds(pl.multiple_of((z_one * plan.x + x_one) * 576 + start, 16), size),
                    column_span(which, dp_index),
                )
                for z_one in z_list
                for x_one in x_list
            ]
        z_one = everything if z_index is None else z_index
        x_one = everything if x_index is None else x_index
        if which == 2:
            return [(dp_index, z_one, x_one, pl.ds(start, size), everything)]
        if which == 4:
            return [(z_one, x_one, pl.ds(pl.multiple_of(dp_index * 32 + start, 16), size), everything)]
        return [(z_one, x_one, pl.ds(start, size), column_span(which, dp_index))]

    recv_parts = {
        1: lambda index: mem.h3.at[index],
        0: lambda index: mem.r1.at[index],
        2: lambda index: mem.r3.at[index],
        4: lambda index: mem.r5.at[index],
    }

    counter = [0]

    class Batch:
        def __init__(self, sources, targets, landings, axis, partner):
            base = counter[0]
            counter[0] += len(sources)
            send, recv = mem.bulk_send, mem.bulk_recv
            self.out = [
                pltpu.make_async_remote_copy(
                    src_ref=source,
                    dst_ref=target,
                    send_sem=send.at[base + place],
                    recv_sem=recv.at[base + place],
                    device_id={axis: partner},
                    device_id_type=pl.DeviceIdType.MESH,
                )
                for place, (source, target) in enumerate(zip(sources, targets))
            ]
            self.come = [
                pltpu.make_async_remote_copy(
                    src_ref=landing,
                    dst_ref=landing,
                    send_sem=send.at[base + place],
                    recv_sem=recv.at[base + place],
                    device_id={axis: partner},
                    device_id_type=pl.DeviceIdType.MESH,
                )
                for place, landing in enumerate(landings)
            ]

        def start(self):
            for copy in self.out:
                copy.start()

        def arrive(self):
            for copy in self.come:
                copy.wait_recv()

        def leave(self):
            for copy in self.out:
                copy.wait_send()

    class LineBatch:
        def __init__(self, source_of, target_of, landing_of):
            base = counter[0]
            counter[0] += plan.z
            send, recv = mem.bulk_send, mem.bulk_recv
            self.out, self.come = [], []
            for step in range(1, plan.z):
                z_to = (z_me + step) % plan.z
                self.out.append(
                    pltpu.make_async_remote_copy(
                        src_ref=source_of(z_to),
                        dst_ref=target_of(z_to),
                        send_sem=send.at[base + step],
                        recv_sem=recv.at[base + z_me],
                        device_id={FSDP: z_to * plan.x + x_me},
                        device_id_type=pl.DeviceIdType.MESH,
                    )
                )
                self.come.append(
                    pltpu.make_async_remote_copy(
                        src_ref=landing_of(z_to),
                        dst_ref=landing_of(z_to),
                        send_sem=send.at[base + step],
                        recv_sem=recv.at[base + z_to],
                        device_id={FSDP: z_to * plan.x + x_me},
                        device_id_type=pl.DeviceIdType.MESH,
                    )
                )

        start, arrive, leave = Batch.start, Batch.arrive, Batch.leave

    def pick(ref, indexes):
        return [ref.at[index] for index in indexes]

    def own_dp(y_index, c_index):
        return y_index * 2 + c_index

    x_partner = z_me * plan.x + x_other
    y_partner = own_dp(y_other, c_me)
    c_partner = own_dp(y_me, c_other)
    dp_far = own_dp(y_other, c_other)

    class Gather:
        def __init__(self, which, start, size):
            ref = weights[which]
            self.which, self.rows = which, (start, size)
            both, low, high = (start, size), (start, size // 2), (start + size // 2, size // 2)

            def at(*index):
                return pick(ref, places(which, *index, False))

            own = at(z_me, x_me, dp_me, both)[0]
            self.line = LineBatch(
                lambda _: own, lambda _: own, lambda z_from: at(z_from, x_me, dp_me, both)[0]
            )
            sent, come = at(None, x_me, dp_me, low), at(None, x_other, dp_me, low)
            x_first = Batch(sent, sent, come, FSDP, x_partner)
            sent, come = at(None, x_me, dp_me, high), at(None, x_me, y_partner, high)
            y_first = Batch(sent, sent, come, DP, y_partner)
            sent, come = at(None, None, dp_me, low), at(None, None, y_partner, low)
            y_second = Batch(sent, sent, come, DP, y_partner)
            sent = at(None, x_me, dp_me, high) + at(None, x_me, y_partner, high)
            come = at(None, x_other, dp_me, high) + at(None, x_other, y_partner, high)
            x_second = Batch(sent, sent, come, FSDP, x_partner)
            sent = at(None, None, dp_me, both) + at(None, None, y_partner, both)
            come = at(None, None, c_partner, both) + at(None, None, dp_far, both)
            core = Batch(sent, sent, come, DP, c_partner)
            self.stages = ((self.line,), (x_first, y_first), (y_second, x_second), (core,))

        def put_own(self):
            index = places(self.which, z_me, x_me, dp_me, self.rows, False)[0]
            shard = ins.shards[self.which][self.rows[0] : self.rows[0] + self.rows[1], :]
            weights[self.which][index] = shard.astype(bf16)

        def start(self, stage):
            for batch in self.stages[stage]:
                batch.start()

        def arrive(self, stage):
            for batch in self.stages[stage]:
                batch.arrive()

        def leave(self):
            for stage in self.stages:
                for batch in stage:
                    batch.leave()

    class Piece:
        def __init__(self, which, ref, room, z_index):
            def at(*index):
                return pick(ref, places(which, z_index, *index))

            def land(*index):
                return [room(index_one) for index_one in places(which, z_index, *index)]

            self.z = z_index
            self.core = Batch(
                at(None, c_partner, None) + at(None, dp_far, None),
                land(None, c_partner, None) + land(None, dp_far, None),
                land(None, dp_me, None) + land(None, y_partner, None),
                DP,
                c_partner,
            )
            self.y_first = Batch(
                at(None, y_partner, 0), land(None, dp_far, 0), land(None, c_partner, 0), DP, y_partner
            )
            self.x_first = Batch(
                at(x_other, dp_me, 1) + at(x_other, y_partner, 1),
                land(x_other, c_partner, 1) + land(x_other, dp_far, 1),
                land(x_me, c_partner, 1) + land(x_me, dp_far, 1),
                FSDP,
                x_partner,
            )
            self.x_second = Batch(
                at(x_other, dp_me, 0), land(x_other, dp_far, 0), land(x_me, dp_far, 0), FSDP, x_partner
            )
            self.y_second = Batch(
                at(x_me, y_partner, 1), land(x_other, dp_far, 1), land(x_other, c_partner, 1), DP, y_partner
            )

    def put_gradient(which, total):
        outs.grads[which][...] = total
        squares = jnp.sum(total * total, axis=0, keepdims=True)
        folded = squares[:, :LANES]
        for place in range(1, squares.shape[1] // LANES):
            folded = folded + squares[:, place * LANES : (place + 1) * LANES]
        mem.squares[...] += folded

    class Reduce:
        def __init__(self, which, ref, cut):
            self.which, self.ref, self.room = which, ref, recv_parts[which]
            self.pieces = [
                Piece(which, ref, self.room, z_index) for z_index in (range(plan.z) if cut else [None])
            ]
            self.base = counter[0]
            counter[0] += plan.z

        def line_copy(self, z_to):
            return pltpu.make_async_remote_copy(
                src_ref=self.ref.at[places(self.which, z_to, x_me, dp_me, None)[0]],
                dst_ref=self.room(places(self.which, z_me, x_other, dp_far, None)[0]),
                send_sem=mem.bulk_send.at[self.base + z_to],
                recv_sem=mem.bulk_recv.at[self.base + z_me],
                device_id={FSDP: z_to * plan.x + x_me},
                device_id_type=pl.DeviceIdType.MESH,
            )

        def line_room(self, z_from):
            return self.room(places(self.which, z_from, x_other, dp_far, None)[0])

        def add(self, z_index, pairs):
            def one(z_one):
                for here, there in pairs:
                    for x_step in range(plan.x) if here[0] is None else [None]:
                        x_here = x_step if here[0] is None else here[0]
                        x_there = x_step if there[0] is None else there[0]
                        index = places(self.which, z_one, x_here, *here[1:])[0]
                        other = places(self.which, z_one, x_there, *there[1:])[0]
                        total = self.ref[index].astype(f32) + self.room(other)[...].astype(f32)
                        self.ref[index] = total.astype(bf16)

            if z_index is None:
                pl.loop(0, plan.z)(one)
            else:
                one(z_index)

        def core_start(self, place=0):
            if plan.inside:
                self.pieces[place].core.start()

        def core_add(self, place=0):
            if plan.inside:
                piece = self.pieces[place]
                piece.core.arrive()
                self.add(piece.z, [((None, dp_me, None),) * 2, ((None, y_partner, None),) * 2])
                piece.y_first.start()
                piece.x_first.start()

        def first_add(self, place=0):
            if plan.inside:
                piece = self.pieces[place]
                piece.y_first.arrive()
                self.add(piece.z, [((None, dp_me, 0), (None, c_partner, 0))])
                piece.x_second.start()
                piece.x_first.arrive()
                self.add(
                    piece.z, [((x_me, dp_me, 1), (x_me, c_partner, 1)), ((x_me, y_partner, 1), (x_me, dp_far, 1))]
                )
                piece.y_second.start()

        def second_add(self, place=0):
            if plan.inside:
                piece = self.pieces[place]
                piece.x_second.arrive()
                piece.y_second.arrive()
                self.add(
                    piece.z, [((x_me, dp_me, 0), (x_me, dp_far, 0)), ((x_me, dp_me, 1), (x_other, c_partner, 1))]
                )
                if piece.z is None:
                    for step in range(1, plan.z):
                        self.line_copy((z_me + step) % plan.z).start()
                else:

                    @pl.when(z_me != piece.z)
                    def _():
                        self.line_copy(piece.z).start()

        def finish(self):
            if not plan.inside:
                return
            total = self.ref[places(self.which, z_me, x_me, dp_me, None)[0]].astype(f32)
            for step in range(1, plan.z):
                z_from = (z_me + step) % plan.z
                room = self.line_room(z_from)
                pltpu.make_async_remote_copy(
                    src_ref=room,
                    dst_ref=room,
                    send_sem=mem.bulk_send.at[self.base + z_from],
                    recv_sem=mem.bulk_recv.at[self.base + z_from],
                    device_id={FSDP: z_from * plan.x + x_me},
                    device_id_type=pl.DeviceIdType.MESH,
                ).wait_recv()
                total = total + room[...].astype(f32)
            put_gradient(self.which, total)
            for step in range(1, plan.z):
                self.line_copy((z_me + step) % plan.z).wait_send()
            for piece in self.pieces:
                for batch in (piece.core, piece.y_first, piece.x_first, piece.x_second, piece.y_second):
                    batch.leave()

    gathers, steps = [], []
    if plan.inside:
        for which, cuts in enumerate((2, 3, 1, 2, 1)):
            size = 2 * plan.half[which] // cuts
            gathers += [Gather(which, cut * size, size) for cut in range(cuts)]

    def line_step(place):
        gathers[place].arrive(0)
        gathers[place].start(1)
        if place + 1 < len(gathers):
            gathers[place + 1].start(0)

    def first_step(place):
        gathers[place].arrive(1)
        gathers[place].start(2)

    def second_step(place):
        gathers[place].arrive(2)
        gathers[place].start(3)

    for place in range(len(gathers)):
        steps.append((line_step, place))
        if place > 0:
            steps.append((second_step, place - 1))
        steps.append((first_step, place))
    if plan.inside:
        steps.append((second_step, len(gathers) - 1))

    def take(count):
        taken, steps[:] = steps[:count], steps[count:]
        return [lambda one=one: one[0](one[1]) for one in taken]

    def moves(site, item):
        found = take(GATHER_AT.get((site, item), 0)) if plan.inside else []
        for which, piece, kind in REDUCE_AT.get((site, item), ()):
            one = reduces[which]
            found.append(
                one.finish
                if kind == 4
                else lambda one=one, kind=kind, piece=piece: (
                    one.core_start,
                    one.core_add,
                    one.first_add,
                    one.second_add,
                )[kind](piece)
            )
        return found

    def hook(site, item=0):
        for move in moves(site, item):
            move()

    def hook_in(site, index, count, first=0, stride=1):
        for item in range(count):
            found = moves(site, item)
            if found and plan.inside:

                @pl.when(index == first + item * stride)
                def _(found=found):
                    for move in found:
                        move()

    def cores_arrive(which):
        for one in gathers:
            if one.which == which:
                one.arrive(3)

    gradients = [mem.g1, mem.stage.at[pl.ds(0, 9 * C_MID)], weights[2], weights[3], weights[4]]
    reduces = [None if which == 3 else Reduce(which, gradients[which], which < 3) for which in range(5)]
    assert counter[0] <= COPIES
    mem.squares[...] = jnp.zeros((1, LANES), f32)

    if plan.inside:
        gathers[0].put_own()
        gathers[0].start(0)
        for one in gathers[1:]:
            one.put_own()
        tiles = mem.norm_tiles
        tiles[dp_me, fsdp_me] = ins.norm[...].astype(bf16).astype(f32)
        norm_dp = share(
            DP, plan.dp, dp_me, lambda _: tiles.at[dp_me, fsdp_me], tiles.at[:, fsdp_me], mem.norm_s0, mem.norm_r0
        )
        norm_dp[0]()
    else:
        loads = [
            pltpu.make_async_copy(ins.shards[which], weights[which], mem.bulk_send.at[which])
            for which in range(5)
        ]
        for load in loads:
            load.start()

    pieces = BLOCKS * CHUNKS

    def hidden_rows(index, pixel=0, count=chunk):
        return pl.ds(pl.multiple_of(index * chunk + pixel * views, 16), count)

    class Ring:
        def __init__(self, ref, start):
            self.ref, self.base = ref, start

        def rows(self, index, pixel=0, count=chunk):
            return pl.ds(
                pl.multiple_of(self.base + lax.rem(index, SLOTS) * chunk + pixel * views, 16), count
            )

        def copy(self, array, index, into):
            block, place = index // CHUNKS, lax.rem(index, CHUNKS)
            outer = array.at[
                pl.ds(pl.multiple_of(place * chunk, 16), chunk),
                pl.ds(pl.multiple_of(block * C_MID, LANES), C_MID),
            ]
            inner = self.ref.at[self.rows(index)]
            source, target = (outer, inner) if into else (inner, outer)
            return pltpu.make_async_copy(
                source, target, mem.stage_sem.at[0 if into else 1, lax.rem(index, SLOTS)]
            )

        def first_loads(self, array):
            for index in range(3):
                self.copy(array, index, True).start()

        def next_load(self, array, index):
            @pl.when(index + 3 < pieces)
            def _():
                self.copy(array, index + 3, True).start()

        def save(self, array, index):
            self.copy(array, index, False).start()

            @pl.when(index >= 2)
            def _():
                self.copy(array, index - 2, False).wait()

        def last_saves(self, array):
            for index in (pieces - 2, pieces - 1):
                self.copy(array, index, False).wait()

    stage_ref = mem.stage
    stage = Ring(stage_ref, 0)

    def piece_columns(index, part):
        return pl.ds(pl.multiple_of(index // CHUNKS * C_MID + part * LANES, LANES), LANES)

    features, slope_hbm = ins.features, outs.slope
    hidden_three = mem.h3

    def feature_copy(block, target):
        return pltpu.make_async_copy(
            features.at[:, pl.ds(block * C_MID, C_MID)], target, mem.column_sem.at[block]
        )

    feature_loads = [
        feature_copy(block, hidden_three.at[pl.ds(block * rows, rows)]) for block in range(BLOCKS)
    ]
    for copy in feature_loads:
        copy.start()
    stage.first_loads(features)

    padded_one, padded_two = mem.pad1, mem.pad2
    for padded in (padded_one, padded_two):
        for edge in (0, SIDE + 1):
            padded[edge] = jnp.zeros((padded.shape[1], C_MID), bf16)
        for edge in (0, SIDE + 1):
            padded[:, pl.ds(edge * views, views), :] = jnp.zeros((SIDE + 2, views, C_MID), bf16)
    rest = jnp.zeros((tall - rows, C_MID), bf16)
    for ref, end in ((mem.d1, rows), (mem.h2, rows), (mem.d2, rows), (mem.a2, rows), (hidden_three, BLOCKS * rows)):
        ref[end : end + tall - rows, :] = rest

    if plan.inside:
        norm_dp[1]()
        norm_out = []
        norm_in = []
        for step in range(1, plan.fsdp):
            partner = (fsdp_me + step) % plan.fsdp
            norm_out.append(
                pltpu.make_async_remote_copy(
                    src_ref=tiles.at[:, fsdp_me],
                    dst_ref=tiles.at[:, fsdp_me],
                    send_sem=mem.norm_s1.at[step],
                    recv_sem=mem.norm_r1.at[fsdp_me],
                    device_id={FSDP: partner},
                    device_id_type=pl.DeviceIdType.MESH,
                )
            )
            norm_in.append(
                pltpu.make_async_remote_copy(
                    src_ref=tiles.at[:, partner],
                    dst_ref=tiles.at[:, partner],
                    send_sem=mem.norm_s1.at[step],
                    recv_sem=mem.norm_r1.at[partner],
                    device_id={FSDP: partner},
                    device_id_type=pl.DeviceIdType.MESH,
                )
            )
        for copy in norm_out:
            copy.start()
        hook(21)
        for copy in norm_in:
            copy.wait_recv()
        for copy in norm_out:
            copy.wait_send()
        norm_all = mem.norm
        for dp_one in range(plan.dp):
            for fsdp_one in range(plan.fsdp):
                start = (dp_one * plan.fsdp + fsdp_one) * LANES
                norm_all[:, start : start + LANES] = tiles[dp_one, fsdp_one]
    else:
        for copy in loads:
            copy.wait()
        norm_all = mem.norm
        norm_all[...] = ins.norm[...]

    starts = (0, C_MID, 2 * C_MID, 2 * C_MID + C_IN, 2 * C_MID + C_IN + P_HID)

    def gain(layer):
        return norm_all[0:1, starts[layer] : starts[layer + 1]]

    coef, stats = mem.coef, mem.stats

    def norm_coefs(layer, totals, count, low=0):
        width = totals.shape[1]
        here, there = slice(low, low + width), slice(starts[layer] + low, starts[layer] + low + width)
        mean = totals[0:1] / count
        scaling = lax.rsqrt(totals[1:2] / count - mean * mean + norm_epsilon)
        slope = scaling * norm_all[0:1, there]
        stats[0:1, there] = mean
        stats[1:2, there] = scaling
        coef[0:1, here] = slope
        coef[1:2, here] = norm_all[1:2, there] - mean * slope

    def grad_coefs(layer, totals, count):
        width = starts[layer + 1] - starts[layer]
        mean = stats[0:1, starts[layer] : starts[layer + 1]]
        scaling = stats[1:2, starts[layer] : starts[layer + 1]]
        mem.norm_grads[0:1, starts[layer] : starts[layer + 1]] = totals[1:2]
        mem.norm_grads[1:2, starts[layer] : starts[layer + 1]] = totals[0:1]
        slope = scaling * gain(layer)
        bend = slope * scaling * totals[1:2] / count
        coef[0:1, :width] = slope
        coef[1:2, :width] = slope * totals[0:1] / count - mean * bend
        coef[2:3, :width] = bend

    def xhat_sum(layer, plain, product):
        mean = stats[0:1, starts[layer] : starts[layer + 1]]
        scaling = stats[1:2, starts[layer] : starts[layer + 1]]
        return scaling * (product - mean * plain)

    zero_row = jnp.zeros((1, C_MID), f32)

    def column_sums(value):
        return jnp.sum(value, axis=0, keepdims=True)

    def whole(which):
        value = weights[which][...]
        return value.reshape(-1, value.shape[-1])

    row_sums = mem.row_sums

    def clear_sums():
        row_sums[...] = jnp.zeros_like(row_sums)

    def count_in(cols, value, other):
        row_sums[0:1, cols] += column_sums(value)
        row_sums[1:2, cols] += column_sums(value * other)

    def own_columns(side):
        core = (c_me + side) % 2
        return [
            pl.ds(pl.multiple_of(half * (C_MID // 2) + core * LANES, LANES), LANES) for half in range(2)
        ]

    def turn_rows(ref):
        @pl.loop(0, tall // C_MID)
        def _(block):
            at = pl.ds(pl.multiple_of(block * C_MID, C_MID), C_MID)
            ref[at, :] = ref[at, :].T

    def turned(ref):
        return jnp.concatenate([ref[start : start + C_MID, :] for start in range(0, tall, C_MID)], axis=1)

    def sends_leave(which):
        for one in gathers:
            if one.which == which:
                one.leave()

    def turn_weight(which, block):
        ref = weights[which]
        if which == 1:
            groups = [block * 8 + group for group in range(8)]
            ats = [
                (group // 18, group // 9 % 2, pl.ds(pl.multiple_of(group % 9 * 64, 64), 64), everything)
                for group in groups
            ]
            value = jnp.concatenate([ref[at] for at in ats], axis=0).T
            for place, at in enumerate(ats):
                ref[at] = value[place * 64 : (place + 1) * 64, :]
        elif which == 3:
            for half in range(P_HID // C_MID):
                cols = slice(half * C_MID, (half + 1) * C_MID)
                value = ref[block, :, :, cols]
                ref[block, :, :, cols] = value.reshape(C_MID, C_MID).T.reshape(value.shape)
        else:
            value = ref[block]
            ref[block] = value.reshape(C_MID, C_MID).T.reshape(value.shape)

    hidden_one, slope_one = mem.h1, mem.d1
    hidden_two, slope_two = mem.h2, mem.d2
    act_two = mem.a2
    long = rows // 3

    def span(index):
        return pl.ds(pl.multiple_of(index * chunk, 16), chunk)

    def long_rows(block, index):
        return pl.ds(pl.multiple_of(block * rows + index * long, 16), long)

    def put_sides(ref, at, sides, hidden):
        for place, cols in enumerate(sides):
            part = hidden[:, place * LANES : (place + 1) * LANES]
            ref[at, cols] = part.astype(bf16)
            count_in(cols, part, part)

    for copy in feature_loads:
        copy.wait()
    clear_sums()

    @pl.loop(0, 2)
    def _(side):
        sides = own_columns(side)

        @pl.loop(0, 3)
        def _(index):
            left = jnp.concatenate([hidden_three[long_rows(block, index), :] for block in range(BLOCKS)], axis=1)
            right = jnp.concatenate([weights[0][:, :, :, cols].reshape(C_IN, LANES) for cols in sides], axis=1)
            put_sides(hidden_one, long_rows(0, index), sides, dot(left, right))

            hook_in(0, side * 3 + index, 6)

        @pl.when(side == 0)
        def _():
            cores_arrive(0)

    sum_one = Sum(0)
    sum_one.start(row_sums[0:1, :C_MID], row_sums[1:2, :C_MID])
    hook(1)
    sends_leave(0)
    pl.loop(0, 2)(lambda block: turn_weight(0, block))
    sum_one.middle()
    pl.loop(2, 4)(lambda block: turn_weight(0, block))
    hook(2)
    clear_sums()
    norm_coefs(0, sum_one.finish(), row_total)

    def activate(hidden_ref, slope_ref, put, site):
        @pl.loop(0, PIX)
        def _(pixel):
            place = pl.ds(pl.multiple_of(pixel * views, 16), views)
            for block in range(C_MID // LANES):
                cols = slice(block * LANES, (block + 1) * LANES)
                out = hidden_ref[place, cols].astype(f32) * coef[0:1, cols] + coef[1:2, cols]
                value, slope = gelu_pair(out)
                slope_ref[place, cols] = slope.astype(bf16)
                put(pixel, cols, value.astype(bf16))
            hook_in(site, pixel, SIDE, SIDE - 1, SIDE)

    def put_padded(padded):
        def put(pixel, cols, value):
            padded[pixel // SIDE + 1, pl.ds(pl.multiple_of((pixel % SIDE + 1) * views, 16), views), cols] = value

        return put

    activate(hidden_one, slope_one, put_padded(padded_one), 3)
    hook(4)

    def patch(padded, first, count, flip):
        found = []
        for vertical in range(3):
            for lateral in range(3):
                down, across = (2 - vertical, 2 - lateral) if flip else (vertical, lateral)
                piece = padded[pl.ds(first + down, count), across * views : across * views + chunk, :]
                found.append(piece.reshape(count * chunk, C_MID))
        return jnp.concatenate(found, axis=1)

    def image_rows(first, count):
        return pl.ds(pl.multiple_of(first * chunk, 16), count * chunk)

    def second_part(sides, first, count):
        right = jnp.concatenate([weights[1][:, :, :, cols].reshape(9 * C_MID, LANES) for cols in sides], axis=1)
        hidden = dot(patch(padded_one, first, count, False), right)
        put_sides(hidden_two, image_rows(first, count), sides, hidden)

    @pl.loop(0, 2)
    def _(side):
        sides = own_columns(side)

        @pl.loop(0, 3)
        def _(index):
            second_part(sides, 2 * index, 2)
            hook_in(5, side * 4 + index, 8)

        second_part(sides, 6, 1)

        @pl.when(side == 0)
        def _():
            cores_arrive(1)

    sum_two = Sum(1)
    sum_two.start(row_sums[0:1, :C_MID], row_sums[1:2, :C_MID])
    hook(6)
    sends_leave(1)
    pl.loop(0, 4)(lambda block: turn_weight(1, block))
    sum_two.middle()
    pl.loop(4, 9)(lambda block: turn_weight(1, block))
    hook(7)
    clear_sums()
    norm_coefs(1, sum_two.finish(), row_total)

    def put_rows(pixel, cols, value):
        act_two[pl.ds(pl.multiple_of(pixel * views, 16), views), cols] = value

    activate(hidden_two, slope_two, put_rows, 8)
    cores_arrive(2)

    def weight_three(block):
        return weights[2][block].reshape(C_MID, C_MID)

    sums_low, sums_high = Sum(2), Sum(3)
    half_width = C_IN // 2

    @pl.loop(0, BLOCKS)
    def _(block):
        cols = pl.ds(pl.multiple_of(block * C_MID, LANES), C_MID)

        @pl.loop(0, 3)
        def _(index):
            hidden = dot(act_two[long_rows(0, index), :], weight_three(block))
            hidden_three[long_rows(block, index), :] = hidden.astype(bf16)
            count_in(cols, hidden, hidden)
            hook_in(9, block * 3 + index, 12)

        @pl.when(block == 1)
        def _():
            sums_low.start(row_sums[0:1, :half_width], row_sums[1:2, :half_width])

        @pl.when(block == 2)
        def _():
            sums_low.middle()

    sums_high.start(row_sums[0:1, half_width:], row_sums[1:2, half_width:])
    norm_coefs(2, sums_low.finish(), row_total)

    hook(22)

    pool, pool_slope, pool_bend = mem.pool, mem.pool_slope, mem.pool_bend
    for ref in (pool, pool_slope, pool_bend):
        ref[...] = jnp.zeros_like(ref)

    @pl.loop(0, pieces)
    def _(index):
        stage.copy(features, index, True).wait()

        @pl.loop(0, C_MID // LANES)
        def _(part):
            inner = pl.ds(pl.multiple_of(part * LANES, LANES), LANES)
            cols = piece_columns(index, part)
            slope_row, shift_row = coef[0:1, cols], coef[1:2, cols]
            kept = (pool[:, cols], pool_slope[:, cols], pool_bend[:, cols])
            slopes = []
            for pixel in range(SIDE):
                stage_at, hidden_at = stage.rows(index, pixel, views), hidden_rows(index, pixel, views)
                hidden = hidden_three[hidden_at, inner].astype(f32)
                total = hidden * slope_row + shift_row + stage_ref[stage_at, inner].astype(f32)
                value, slope = gelu_pair(total)
                slopes.append((stage_at, slope.astype(bf16)))
                kept = (kept[0] + value, kept[1] + slope, kept[2] + slope * hidden)
            for stage_at, slope in slopes:
                stage_ref[stage_at, inner] = slope
            pool[:, cols], pool_slope[:, cols], pool_bend[:, cols] = kept

        stage.save(slope_hbm, index)
        stage.next_load(features, index)

        @pl.when(index == 2)
        def _():
            sums_high.middle()

        @pl.when(index == pieces // 2 - 1)
        def _():
            norm_coefs(2, sums_high.finish(), row_total, half_width)

        hook_in(10, index, pieces)

    stage.last_saves(slope_hbm)
    cores_arrive(3)
    cores_arrive(4)
    for which in range(2, 5):
        sends_leave(which)

    pooled = (pool[...] * (1.0 / PIX)).astype(bf16)
    mem.pooled[...] = pooled
    if plan.inside:
        wide_at = C_IN // plan.fsdp
        low_at = P_HID // plan.dp
        left_rooms, right_rooms = mem.left_rooms, mem.right_rooms

        def wide_columns(fsdp_one):
            return pl.ds(pl.multiple_of(fsdp_one * wide_at, LANES), wide_at)

        def low_columns(dp_one):
            return pl.ds(pl.multiple_of(dp_one * low_at, LANES), low_at)

        sems = mem.factor_sems
        left_first = share(
            FSDP, plan.fsdp, fsdp_me, lambda to: mem.pooled.at[:, wide_columns(to)], left_rooms.at[dp_me], sems.at[0], sems.at[1]
        )
        left_second = share(
            DP, plan.dp, dp_me, lambda _: left_rooms.at[dp_me], left_rooms, sems.at[2], sems.at[3]
        )
        right_first = share(
            DP, plan.dp, dp_me, lambda to: mem.four_low.at[:, low_columns(to)], right_rooms.at[fsdp_me], sems.at[4], sems.at[5]
        )
        right_second = share(
            FSDP, plan.fsdp, fsdp_me, lambda _: right_rooms.at[fsdp_me], right_rooms, sems.at[6], sems.at[7]
        )
        left_first[0]()
        left_rooms[dp_me, fsdp_me] = mem.pooled[:, wide_columns(fsdp_me)]

    proj_hidden = dot(pooled, whole(3))
    sum_four = Sum(4)
    sum_four.start(column_sums(proj_hidden), column_sums(proj_hidden * proj_hidden))
    pl.loop(0, 2)(lambda block: turn_weight(3, block))
    sum_four.middle()
    pl.loop(2, 4)(lambda block: turn_weight(3, block))
    if plan.inside:
        left_first[1]()
        left_second[0]()
    totals = sum_four.finish()
    stage.first_loads(slope_hbm)
    norm_coefs(3, totals, view_total)
    value, slope = gelu_pair(proj_hidden * coef[0:1, :P_HID] + coef[1:2, :P_HID])
    proj_act = value.astype(bf16)
    mem.proj_act[...] = proj_act
    mem.proj_slope[...] = slope
    mem.proj_hidden[...] = proj_hidden

    def weight_five(block):
        return weights[4][block // plan.x, block % plan.x]

    parts = P_HID // P_OUT
    embedding = jnp.zeros((views, P_OUT), f32)
    for block in range(parts):
        embedding = embedding + dot_cols(proj_act[:, block * P_OUT : (block + 1) * P_OUT], weight_five(block))

    images = views // 2
    order = jnp.broadcast_to(ins.order[...], (images, views))
    image_row = lax.broadcasted_iota(jnp.int32, (images, views), 0)
    selectors = [(order == 2 * image_row + which).astype(f32) for which in range(2)]
    embeds = [exact_dot(selector, embedding) for selector in selectors]
    moments = [exact_rows(embed, embed) for embed in embeds]
    packed, diagonal = pack_pair(*moments)
    packed, extra = sum_matrix(0, packed, [diagonal] + [column_sums(embed) for embed in embeds])
    moments = unpack_pair(packed, extra[0])
    eye = (
        lax.broadcasted_iota(jnp.int32, (P_OUT, P_OUT), 0) == lax.broadcasted_iota(jnp.int32, (P_OUT, P_OUT), 1)
    ).astype(f32)
    centred, covariances = [], []
    for which in range(2):
        mean = extra[1 + which] / image_total
        centred.append(embeds[which] - mean)
        covariances.append(moments[which] / image_total - exact_rows(mean, mean) + ridge_term * eye)
    inverses = inverse_factors(covariances)
    whitened = [exact_cols(centred[which], inverses[which]) for which in range(2)]
    scalings = [
        lax.rsqrt(jnp.mean(white * white, axis=1, keepdims=True) + norm_epsilon) for white in whitened
    ]
    units = [white * scaling for white, scaling in zip(whitened, scalings)]
    difference = units[0] - units[1]
    objective_row = column_sums(difference * difference) * (1.0 / P_OUT)
    unit_grads = [difference * (2.0 / P_OUT), difference * (-2.0 / P_OUT)]
    white_grads = []
    for which in range(2):
        inner = jnp.mean(whitened[which] * unit_grads[which], axis=1, keepdims=True)
        white_grads.append(
            scalings[which] * unit_grads[which] - whitened[which] * (scalings[which] ** 3 * inner)
        )
    directs = [exact_dot(white_grads[which], inverses[which]) for which in range(2)]
    products = [exact_rows(white_grads[which], whitened[which]) for which in range(2)]
    packed, diagonal = pack_pair(*products)
    packed, extra = sum_matrix(
        1, packed, [diagonal] + [column_sums(grad) for grad in white_grads] + [objective_row]
    )
    products = unpack_pair(packed, extra[0])
    embed_grad = jnp.zeros((views, P_OUT), f32)
    for which in range(2):
        symmetric = exact_rows(inverses[which], exact_dot(products[which], inverses[which]))
        mean_grad = exact_dot(extra[1 + which], inverses[which])
        grad = directs[which] - (exact_dot(centred[which], symmetric) + mean_grad) / image_total
        embed_grad = embed_grad + exact_rows(selectors[which], grad)
    objective_row = extra[3]
    embed_low = embed_grad.astype(bf16)

    proj_act, proj_hidden = mem.proj_act[...], mem.proj_hidden[...]
    act_grad = jnp.concatenate([dot(embed_low, weight_five(block)) for block in range(parts)], axis=1)
    upstream = act_grad * mem.proj_slope[...]
    plain = column_sums(upstream)
    sum_four_back = Sum(5)
    sum_four_back.start(plain, xhat_sum(3, plain, column_sums(upstream * proj_hidden)))
    for block in range(parts):
        weights[4][block // plan.x, block % plan.x] = dot_rows(
            embed_low, proj_act[:, block * P_OUT : (block + 1) * P_OUT]
        ).astype(bf16)
    pl.loop(0, 4)(lambda block: turn_weight(2, block))
    sum_four_back.middle()
    turn_rows(act_two)
    grad_coefs(3, sum_four_back.finish(), view_total)
    four_low = (
        upstream * coef[0:1, :P_HID] - coef[1:2, :P_HID] - proj_hidden * coef[2:3, :P_HID]
    ).astype(bf16)
    mem.four_low[...] = four_low
    if plan.inside:
        right_first[0]()
        right_rooms[fsdp_me, dp_me] = mem.four_low[:, low_columns(dp_me)]

    @pl.loop(0, BLOCKS)
    def _(block):
        cols = pl.ds(pl.multiple_of(block * C_MID, LANES), C_MID)
        right = jnp.concatenate(
            [
                weights[3][block, :, :, half * C_MID : (half + 1) * C_MID].reshape(C_MID, C_MID)
                for half in range(P_HID // C_MID)
            ],
            axis=0,
        )
        grad = dot(four_low, right) * (1.0 / PIX)
        row_sums[0:1, cols] = column_sums(grad * pool_slope[:, cols])
        row_sums[1:2, cols] = column_sums(grad * pool_bend[:, cols])
        pool_slope[:, cols] = grad

    plain = row_sums[0:1, :]
    sum_three_back = Sum(6)
    sum_three_back.start(plain, xhat_sum(2, plain, row_sums[1:2, :]))
    if plan.inside:
        left_second[1]()
    else:
        grad_four = dot_rows(mem.pooled[...], four_low).astype(bf16)
        weights[3][...] = grad_four.reshape(weights[3].shape)
    sum_three_back.middle()
    if plan.inside:
        right_first[1]()
        right_second[0]()
    hook(23)
    grad_coefs(2, sum_three_back.finish(), row_total)
    pool[...] = pool_slope[...] * coef[0:1, :]

    clear_sums()

    @pl.loop(0, pieces)
    def _(index):
        stage.copy(slope_hbm, index, True).wait()
        stage.next_load(slope_hbm, index)

        @pl.loop(0, C_MID // LANES)
        def _(part):
            inner = pl.ds(pl.multiple_of(part * LANES, LANES), LANES)
            cols = piece_columns(index, part)
            spread, shift_row, bend_row = pool[:, cols], coef[1:2, cols], coef[2:3, cols]
            grads = []
            for pixel in range(SIDE):
                hidden_at = hidden_rows(index, pixel, views)
                hidden = hidden_three[hidden_at, inner].astype(f32)
                slope = stage_ref[stage.rows(index, pixel, views), inner].astype(f32)
                grads.append((hidden_at, (slope * spread - shift_row - hidden * bend_row).astype(bf16)))
            for hidden_at, grad in grads:
                hidden_three[hidden_at, inner] = grad

        hook_in(11, index, pieces)

    @pl.loop(0, 3)
    def _(index):
        at = long_rows(0, index)
        left = jnp.concatenate([hidden_three[long_rows(block, index), :] for block in range(BLOCKS)], axis=1)
        upstream = dot(left, weights[2][...].reshape(C_IN, C_MID)) * slope_two[at, :].astype(f32)
        slope_two[at, :] = upstream.astype(bf16)
        count_in(slice(0, C_MID), upstream, hidden_two[at, :].astype(f32))
        hook_in(12, index, 3)

    sums = row_sums[0:1, :C_MID], row_sums[1:2, :C_MID]
    sum_two_back = Sum(7)
    sum_two_back.start(sums[0], xhat_sum(1, *sums))

    @pl.loop(0, BLOCKS)
    def _(block):
        grad = dot(turned(act_two), hidden_three[pl.ds(pl.multiple_of(block * rows, 16), tall), :])
        weights[2][block] = grad.astype(bf16).reshape(plan.z, plan.x, -1, C_MID)

        @pl.when(block == 1)
        def _():
            sum_two_back.middle()

        hook_in(13, block, BLOCKS)

    clear_sums()
    grad_coefs(1, sum_two_back.finish(), row_total)

    def apply_grad(hidden_ref, grad_ref, put, site):
        @pl.loop(0, PIX)
        def _(pixel):
            place = pl.ds(pl.multiple_of(pixel * views, 16), views)
            for block in range(C_MID // LANES):
                cols = slice(block * LANES, (block + 1) * LANES)
                grad = (
                    grad_ref[place, cols].astype(f32) * coef[0:1, cols]
                    - coef[1:2, cols]
                    - hidden_ref[place, cols].astype(f32) * coef[2:3, cols]
                )
                put(pixel, cols, grad.astype(bf16))
            hook_in(site, pixel, SIDE, SIDE - 1, SIDE)

    def put_two(pixel, cols, value):
        put_padded(padded_two)(pixel, cols, value)
        slope_two[pl.ds(pl.multiple_of(pixel * views, 16), views), cols] = value

    apply_grad(hidden_two, slope_two, put_two, 14)
    if plan.inside:
        right_second[1]()
        order_all = [(dp_one, fsdp_one) for dp_one in range(plan.dp) for fsdp_one in range(plan.fsdp)]
        left = jnp.concatenate([left_rooms[dp_one, fsdp_one] for dp_one, fsdp_one in order_all], axis=0)
        right = jnp.concatenate([right_rooms[fsdp_one, dp_one] for dp_one, fsdp_one in order_all], axis=0)
        put_gradient(3, dot_rows(left, right))
    turn_rows(slope_two)
    column_places = [
        hidden_three.at[pl.ds(2 * rows, rows)],
        hidden_three.at[pl.ds(3 * rows, rows)],
        hidden_two.at[pl.ds(0, rows)],
        hidden_three.at[pl.ds(2 * rows, rows)],
    ]
    column_loads = [feature_copy(block, column_places[block]) for block in range(BLOCKS)]
    for copy in column_loads[:3]:
        copy.start()
    def tap_grad(tap):
        down, across = tap // 3, tap % 3
        left = padded_one[pl.ds(down, SIDE), pl.ds(pl.multiple_of(across * views, 16), chunk), :]
        right = jnp.concatenate([left.reshape(rows, C_MID), jnp.zeros((tall - rows, C_MID), bf16)], axis=0)
        grad = dot(turned(slope_two), right).astype(bf16).T
        stage_ref[pl.ds(pl.multiple_of(tap * C_MID, 16), C_MID), :] = grad

    @pl.loop(0, 7)
    def _(tap):
        tap_grad(tap)
        hook_in(15, tap, 7)

    def second_back(first, count):
        at = image_rows(first, count)
        upstream = dot(patch(padded_two, first, count, True), weights[1][...].reshape(9 * C_MID, C_MID))
        upstream = upstream * slope_one[at, :].astype(f32)
        slope_one[at, :] = upstream.astype(bf16)
        count_in(slice(0, C_MID), upstream, hidden_one[at, :].astype(f32))

    @pl.loop(0, 3)
    def _(index):
        second_back(2 * index, 2)
        hook_in(16, index, 3)

    second_back(6, 1)
    hook(16, 3)
    sums = row_sums[0:1, :C_MID], row_sums[1:2, :C_MID]
    sum_one_back = Sum(8)
    sum_one_back.start(sums[0], xhat_sum(0, *sums))

    @pl.loop(7, 9)
    def _(tap):
        tap_grad(tap)

        @pl.when(tap == 7)
        def _():
            sum_one_back.middle()

        hook_in(17, tap, 2, 7)

    grad_coefs(0, sum_one_back.finish(), row_total)

    def put_one(pixel, cols, value):
        put_rows(pixel, cols, value)
        slope_one[pl.ds(pl.multiple_of(pixel * views, 16), views), cols] = value

    apply_grad(hidden_one, slope_one, put_one, 18)
    turn_rows(slope_one)

    def block_grad(block):
        if block != 1:
            column_loads[block].wait()
        start = 3 * rows if block == 1 else 2 * rows
        right = hidden_two[...] if block == 2 else hidden_three[start : start + tall, :]
        grad = dot(turned(slope_one), right).astype(bf16).T
        mem.g1[block] = grad.reshape(plan.x, -1, C_MID)

    column_loads[1].wait()
    tail = Ring(hidden_two, 0)
    for block in range(BLOCKS):
        block_grad(block)
        if block == 0:
            column_loads[3].start()
        hook(19, block)
        if block == 2:
            tail.first_loads(slope_hbm)

    sum_last = Sum(9)

    @pl.loop(0, pieces)
    def _(index):
        block = index // CHUNKS
        back = dot(act_two[span(lax.rem(index, CHUNKS)), :], weights[0][block].reshape(C_MID, C_MID))
        tail.copy(slope_hbm, index, True).wait()
        cols = pl.ds(pl.multiple_of(block * C_MID, LANES), C_MID)
        for pixel in range(SIDE):
            at = tail.rows(index, pixel, views)
            summed = hidden_two[at, :].astype(f32) * pool_slope[:, cols]
            hidden_two[at, :] = (summed + back[pixel * views : (pixel + 1) * views]).astype(bf16)
        tail.save(outs.features_grad, index)
        tail.next_load(slope_hbm, index)
        hook_in(20, index, pieces)
        if plan.inside:

            @pl.when(index == LAST_SUM)
            def _():
                sum_last.start(mem.squares[...], mem.squares[...])

            @pl.when(index == LAST_SUM + 3)
            def _():
                sum_last.middle()

    tail.last_saves(outs.features_grad)
    squares = mem.squares[...]
    if plan.inside:
        squares = sum_last.finish()[0:1]
    norm_grads = mem.norm_grads[...]
    scalars = outs.scalars
    norm_squares = column_sums(norm_grads * norm_grads)
    for place in range(norm_squares.shape[1] // LANES):
        squares = squares + norm_squares[:, place * LANES : (place + 1) * LANES]
    scalars[...] = jnp.zeros_like(scalars)
    squares = jnp.sum(squares, axis=1, keepdims=True)
    norm = jnp.sqrt(squares)
    found = (jnp.sum(objective_row, axis=1, keepdims=True) / image_total, squares, norm, clip_factor(norm))
    for place, value in enumerate(found):
        scalars[place : place + 1, :] = jnp.broadcast_to(value, (1, LANES))
    if plan.inside:
        owner = (dp_me * plan.fsdp + fsdp_me) * LANES
        outs.norm_grad[...] = mem.norm_grads[:, pl.ds(pl.multiple_of(owner, LANES), LANES)]
    else:
        outs.norm_grad[...] = norm_grads
    if not plan.inside:
        stores = [
            pltpu.make_async_copy(gradients[which], outs.grads[which], mem.bulk_send.at[which])
            for which in range(5)
        ]
        for store in stores:
            store.start()
        for store in stores:
            store.wait()


def weight_shapes():
    return (
        (4, 2, 256, C_MID),
        (4, 2, 576, C_MID),
        (BLOCKS, 4, 2, 64, C_MID),
        (4, 2, 256, P_HID),
        (4, 2, P_OUT, P_OUT),
    )


def run_kernel(plan, features, order, shards, norm):
    rows, views = plan.rows, plan.views
    in_vmem = pl.BlockSpec(memory_space=pltpu.VMEM)
    anywhere = pl.BlockSpec(memory_space=pl.ANY)
    shapes = weight_shapes()
    operands = [features, order, norm, *shards]
    in_specs = [anywhere, in_vmem, in_vmem] + [in_vmem if plan.inside else anywhere] * 5
    results = [
        ((rows, C_IN), bf16, anywhere),
        ((rows, C_IN), bf16, anywhere),
        (norm.shape, f32, in_vmem),
        ((8, LANES), f32, in_vmem),
    ]
    for which, shard in enumerate(shards):
        if plan.inside:
            results.append((shard.shape, f32, in_vmem))
        else:
            results.append(((9 * C_MID, C_MID) if which == 1 else shapes[which], bf16, anywhere))
    dma = pltpu.SemaphoreType.DMA

    def sum_room(width):
        return SumRoom(
            pltpu.VMEM((plan.dp, 2, width), f32),
            pltpu.VMEM((plan.fsdp, 2, width), f32),
            dma((plan.dp,)),
            dma((plan.dp,)),
            dma((plan.fsdp,)),
            dma((plan.fsdp,)),
        )

    def matrix_room():
        size = plan.embed_rows
        return MatrixRoom(
            pltpu.VMEM((plan.dp, size, P_OUT), f32),
            pltpu.VMEM((plan.dp, size, P_OUT), f32),
            pltpu.VMEM((plan.fsdp, size, P_OUT), f32),
            pltpu.VMEM((plan.dp, size, P_OUT), f32),
            dma((plan.dp,)),
            dma((plan.dp,)),
            dma((plan.fsdp,)),
            dma((plan.fsdp,)),
            dma((plan.dp,)),
            dma((plan.dp,)),
        )

    scratch = Mem(
        w=[pltpu.VMEM(shape, bf16) for shape in shapes],
        g1=pltpu.VMEM(shapes[0], bf16),
        row_sums=pltpu.VMEM((2, C_IN), f32),
        r3=pltpu.VMEM(shapes[2], bf16),
        r1=pltpu.VMEM(shapes[0], bf16),
        left_rooms=pltpu.VMEM((plan.dp, plan.fsdp, views, C_IN // plan.fsdp) if plan.inside else (8, LANES), bf16),
        right_rooms=pltpu.VMEM((plan.fsdp, plan.dp, views, P_HID // plan.dp) if plan.inside else (8, LANES), bf16),
        factor_sems=dma((8, max(plan.dp, plan.fsdp))),
        four_low=pltpu.VMEM((views, P_HID), bf16),
        r5=pltpu.VMEM(shapes[4], bf16),
        stage=pltpu.VMEM((max(SLOTS * plan.chunk, 9 * C_MID), C_MID), bf16),
        stage_sem=dma((2, SLOTS)),
        column_sem=dma((BLOCKS,)),
        h1=pltpu.VMEM((rows, C_MID), bf16),
        d1=pltpu.VMEM((plan.tall, C_MID), bf16),
        h2=pltpu.VMEM((plan.tall, C_MID), bf16),
        d2=pltpu.VMEM((plan.tall, C_MID), bf16),
        a2=pltpu.VMEM((plan.tall, C_MID), bf16),
        h3=pltpu.VMEM((3 * rows + plan.tall, C_MID), bf16),
        pad1=pltpu.VMEM((SIDE + 2, (SIDE + 2) * views, C_MID), bf16),
        pad2=pltpu.VMEM((SIDE + 2, (SIDE + 2) * views, C_MID), bf16),
        pool=pltpu.VMEM((views, C_IN), f32),
        pool_slope=pltpu.VMEM((views, C_IN), f32),
        pool_bend=pltpu.VMEM((views, C_IN), f32),
        pooled=pltpu.VMEM((views, C_IN), bf16),
        proj_act=pltpu.VMEM((views, P_HID), bf16),
        proj_slope=pltpu.VMEM((views, P_HID), f32),
        proj_hidden=pltpu.VMEM((views, P_HID), f32),
        coef=pltpu.VMEM((8, C_IN), f32),
        stats=pltpu.VMEM((2, norm_width()), f32),
        norm=pltpu.VMEM((2, norm_width()), f32),
        norm_grads=pltpu.VMEM((2, norm_width()), f32),
        norm_tiles=pltpu.VMEM((plan.dp, plan.fsdp, 2, LANES), f32),
        norm_s0=dma((plan.dp,)),
        norm_r0=dma((plan.dp,)),
        norm_s1=dma((plan.fsdp,)),
        norm_r1=dma((plan.fsdp,)),
        bulk_send=dma((COPIES,)),
        bulk_recv=dma((COPIES,)),
        mats=[matrix_room(), matrix_room()],
        sums=[
            sum_room(width)
            for width in (C_MID, C_MID, C_IN // 2, C_IN // 2, P_HID, C_IN, LANES)
        ],
        squares=pltpu.VMEM((1, LANES), f32),
    )
    values = pl.pallas_call(
        lambda *refs: kernel(plan, *refs),
        out_shape=[jax.ShapeDtypeStruct(shape, kind) for shape, kind, _ in results],
        in_specs=in_specs,
        out_specs=[spec for _, _, spec in results],
        scratch_shapes=[scratch],
        compiler_params=pltpu.CompilerParams(
            collective_id=1, has_side_effects=True, vmem_limit_bytes=63 * 2**20
        ),
        name="train_step",
    )(*operands)
    return Outs(*values[:4], values[4:])


def norm_width():
    return 2 * C_MID + C_IN + P_HID


def clip_factor(norm):
    return clip_level / jnp.maximum(norm, clip_level)


def adam_update(weight, moment_one, moment_two, gradient, step_rate, weight_decay):
    first_new = beta_first * moment_one + (1.0 - beta_first) * gradient
    second_new = beta_second * moment_two + (1.0 - beta_second) * gradient * gradient
    first_hat = first_new / (1.0 - beta_first**STEP)
    second_hat = second_new / (1.0 - beta_second**STEP)
    weight_new = weight - step_rate * (
        first_hat / (jnp.sqrt(second_hat) + adam_epsilon) + weight_decay * weight
    )
    return (weight_new, first_new, second_new)


def finish_kernel(rates, decays, *refs):
    count = len(rates)
    low, scalars = refs[0], refs[1]
    refs = refs[2:]
    given, wide, loss, norm, updated = refs[: 4 * count], *refs[4 * count : 4 * count + 3], refs[4 * count + 3 : -2]
    rooms, sems = refs[-2], refs[-1]
    wide[...] = low[...].astype(f32)
    step = pl.program_id(0)

    def load(place):
        return pltpu.make_async_copy(given[place], rooms[place], sems.at[place])

    def store(place):
        return pltpu.make_async_copy(rooms[place], updated[place], sems.at[place])

    @pl.when(step == 0)
    def _():
        loss[0, 0] = scalars[0, 0]
        norm[0, 0] = scalars[2, 0]
        for place in range(4 * count):
            load(place).start()

    @pl.when(step == 2)
    def _():
        for place in range(4 * count):
            load(place).wait()
        for place in range(count):
            weight, first, second, grad = (rooms[part * count + place][...] for part in range(4))
            found = adam_update(weight, first, second, grad * scalars[3, 0], rates[place], decays[place])
            for part in range(3):
                rooms[part * count + place][...] = found[part]
        for place in range(3 * count):
            store(place).start()

    @pl.when(step == CHUNKS - 1)
    def _():
        for place in range(3 * count):
            store(place).wait()


def finish(features_grad, scalars, masters, firsts, seconds, grads, rates, decays):
    rows = features_grad.shape[0]
    arrays = [*masters, *firsts, *seconds, *grads]
    moving = pl.BlockSpec((rows // CHUNKS, C_IN), lambda index: (index, 0))
    single = pl.BlockSpec(memory_space=pltpu.SMEM)
    anywhere = pl.BlockSpec(memory_space=pl.ANY)
    count = len(masters)
    values = pl.pallas_call(
        lambda *refs: finish_kernel(rates, decays, *refs),
        grid=(CHUNKS,),
        in_specs=[moving, single] + [anywhere] * (4 * count),
        out_specs=[moving, single, single] + [anywhere] * (3 * count),
        out_shape=[jax.ShapeDtypeStruct((rows, C_IN), f32)]
        + [jax.ShapeDtypeStruct((1, 1), f32)] * 2
        + [jax.ShapeDtypeStruct(array.shape, f32) for array in arrays[: 3 * count]],
        scratch_shapes=[
            [pltpu.VMEM(array.shape, f32) for array in arrays],
            pltpu.SemaphoreType.DMA((4 * count,)),
        ],
        compiler_params=pltpu.CompilerParams(vmem_limit_bytes=62 * 2**20),
        name="finish",
    )(features_grad, scalars, *arrays)
    groups = [values[3 + part * count : 3 + (part + 1) * count] for part in range(3)]
    return values[0], values[1].reshape(()), values[2].reshape(()), *groups


def gather_full(weight):
    outer = lax.all_gather(weight.astype(bf16), FSDP, axis=0, tiled=True)
    return lax.all_gather(outer, DP, axis=1, tiled=True)


def scatter_full(gradient):
    inner = lax.psum_scatter(gradient.astype(f32), DP, scatter_dimension=1, tiled=True)
    return lax.psum_scatter(inner, FSDP, scatter_dimension=0, tiled=True)


def body(features, view_order, *state):
    masters, firsts, seconds = state[:6], state[6:12], state[12:18]
    dp_size, fsdp_size = lax.axis_size(DP), lax.axis_size(FSDP)
    views = features.shape[0]
    inside = dp_size == 4 and fsdp_size == 8
    plan = Plan(dp_size, fsdp_size, views, inside)
    pixels = jnp.swapaxes(features, 0, 1).reshape(-1, C_IN)
    norm_params = masters[5]
    shapes = weight_shapes()
    if inside:
        shards = list(masters[:4]) + [masters[4].T]
        norm = norm_params
    else:
        full = [gather_full(weight) for weight in masters[:5]]
        shards = [
            full[0].reshape(shapes[0]),
            full[1].reshape(shapes[1]),
            full[2].reshape(C_MID, BLOCKS, C_MID).swapaxes(0, 1).reshape(shapes[2]),
            full[3].reshape(shapes[3]),
            full[4].reshape(4, 2, P_OUT, P_OUT).swapaxes(2, 3),
        ]
        norm = lax.all_gather(norm_params.astype(bf16), (DP, FSDP), axis=1, tiled=True).astype(f32)
    got = run_kernel(plan, pixels, view_order, shards, norm)
    grads = list(got.grads)
    scalars = got.scalars
    turned = [list(group) for group in (masters, firsts, seconds)]
    if inside:
        owned = grads
        for group in turned:
            group[4] = group[4].T
    else:
        whole_grads = [
            grads[0].reshape(C_IN, C_MID),
            grads[1],
            grads[2].reshape(BLOCKS, C_MID, C_MID).swapaxes(0, 1).reshape(C_MID, C_IN),
            grads[3].reshape(C_IN, P_HID),
            grads[4].swapaxes(2, 3).reshape(P_HID, P_OUT),
        ]
        owned = [scatter_full(gradient) for gradient in whole_grads]
        squares = scalars[1, 0] + lax.psum(sum(jnp.sum(grad * grad) for grad in owned), (DP, FSDP))
        norm_value = jnp.sqrt(squares)
        scalars = scalars.at[2].set(norm_value).at[3].set(clip_factor(norm_value))
    width = norm_params.shape[1]
    if inside:
        owned.append(got.norm_grad)
    else:
        owner = lax.axis_index((DP, FSDP))
        owned.append(lax.dynamic_slice_in_dim(got.norm_grad, owner * width, width, 1))
    step_rates = (
        C_IN ** (-0.5),
        (9 * C_MID) ** (-0.5),
        C_MID ** (-0.5),
        C_IN ** (-0.5),
        P_HID ** (-0.5),
        norm_rate,
    )
    decays = (decay_rate, decay_rate, decay_rate, decay_rate, decay_rate, 0.0)
    input_grad, loss, grad_norm, *updates = finish(
        got.features_grad, scalars, *turned, owned, step_rates, decays
    )
    if inside:
        updates = [[*group[:4], group[4].T, group[5]] for group in updates]
    return (
        loss,
        jnp.swapaxes(input_grad.reshape(PIX, views, C_IN), 0, 1),
        grad_norm,
        *updates[0],
        *updates[1],
        *updates[2],
    )


def solution(mesh):
    views = P((DP, FSDP), None, None)
    split = P(FSDP, DP)
    norm = P(None, (DP, FSDP))
    params = (split,) * 5 + (norm,)
    return jax.shard_map(
        body,
        mesh=mesh,
        in_specs=(views, P((DP, FSDP), None)) + params * 3,
        out_specs=(P(), views, P()) + params * 3,
        check_vma=False,
    )
```

```python
from typing import Any, NamedTuple

import jax
import jax.numpy as jnp
from jax import lax
from jax.experimental import pallas as pl
from jax.experimental.pallas import tpu as pltpu
from jax.sharding import PartitionSpec as P

C_IN = 2048
C_MID = 512
P_HID = 1024
P_OUT = 128
SIDE = 7
STEP = 10
PIX = 49
LANES = 128
BLOCKS = C_IN // C_MID
CHUNKS = SIDE
SLOTS = 6
LAST_SUM = 23
COPIES = 360


highest = lax.Precision.HIGHEST
bf16 = jnp.bfloat16
f32 = jnp.float32
norm_epsilon = 1e-05
ridge_term = 0.01
clip_level = 0.1
beta_first = 0.9
beta_second = 0.999
adam_epsilon = 1e-08
decay_rate = 0.05
norm_rate = 0.5
bell_scale = 0.3989422804014327
root_half = 0.5**0.5
bell_rate = -0.7213475204444817
DP, FSDP = "dp", "fsdp"


def gelu_pair(values):
    below = 0.5 + 0.5 * lax.erf(values * root_half)
    bell = jnp.exp2(values * values * bell_rate)
    return values * below, below + values * bell * bell_scale


def dot(left, right):
    return jnp.dot(left, right, preferred_element_type=f32)


def dot_cols(left, right):
    return lax.dot_general(left, right, (((1,), (1,)), ((), ())), preferred_element_type=f32)


def dot_rows(left, right):
    return lax.dot_general(left, right, (((0,), (0,)), ((), ())), preferred_element_type=f32)


def exact_cols(left, right):
    return lax.dot_general(
        left, right, (((1,), (1,)), ((), ())), precision=highest, preferred_element_type=f32
    )


def exact_rows(left, right):
    return lax.dot_general(
        left, right, (((0,), (0,)), ((), ())), precision=highest, preferred_element_type=f32
    )


def exact_dot(left, right):
    return jnp.dot(left, right, precision=highest, preferred_element_type=f32)


def inverse_factors(matrices):
    row_top = lax.broadcasted_iota(jnp.int32, (8, P_OUT), 0)
    row_all = lax.broadcasted_iota(jnp.int32, (P_OUT, P_OUT), 0)
    col_all = lax.broadcasted_iota(jnp.int32, (P_OUT, P_OUT), 1)

    def one_step(place, left, right):
        scale = lax.rsqrt(left[place : place + 1, place : place + 1])
        left_row = left[place : place + 1, :] * scale
        right_row = right[place : place + 1, :] * scale
        column = left[:, place : place + 1] * scale
        left = left - column * left_row
        right = right - column * right_row
        here = row_top == place
        left = jnp.concatenate([jnp.where(here, 0.0, left[:8]), left[8:]], axis=0)
        right = jnp.concatenate(
            [jnp.where(here, jnp.broadcast_to(right_row, (8, P_OUT)), right[:8]), right[8:]], axis=0
        )
        return left, right

    def panel(_, pairs):
        pairs = list(pairs)
        for place in range(8):
            for which in range(len(pairs)):
                pairs[which] = one_step(place, *pairs[which])
        return tuple(
            (
                pltpu.roll(jnp.concatenate([left[8:], left[:8]], axis=0), P_OUT - 8, 1),
                jnp.concatenate([right[8:], right[:8]], axis=0),
            )
            for left, right in pairs
        )

    pairs = tuple((matrix, (row_all == col_all).astype(f32)) for matrix in matrices)
    done = [[] for _ in matrices]
    size = P_OUT // 4
    for _ in range(4):
        pairs = lax.fori_loop(0, size // 8, panel, pairs)
        for found, (_, right) in zip(done, pairs):
            found.append(right[-size:])
        pairs = tuple((left[:-size], right[:-size]) for left, right in pairs)
    return [jnp.concatenate(found, axis=0) for found in done]


def pack_pair(first, second):
    row = lax.broadcasted_iota(jnp.int32, (P_OUT, P_OUT), 0)
    col = lax.broadcasted_iota(jnp.int32, (P_OUT, P_OUT), 1)
    packed = jnp.where(row >= col, first, second.T)
    diagonal = jnp.sum(jnp.where(row == col, second, 0.0), axis=0, keepdims=True)
    return packed, diagonal


def unpack_pair(packed, diagonal):
    row = lax.broadcasted_iota(jnp.int32, (P_OUT, P_OUT), 0)
    col = lax.broadcasted_iota(jnp.int32, (P_OUT, P_OUT), 1)
    turned = packed.T
    first = jnp.where(row >= col, packed, turned)
    second = jnp.where(row < col, packed, jnp.where(row == col, diagonal, turned))
    return first, second


GATHER_AT = {
    (0, 1): 1,
    (0, 3): 1,
    (1, 0): 1,
    (2, 0): 1,
    (4, 0): 5,
    (5, 0): 1,
    (5, 1): 1,
    (5, 2): 1,
    (5, 4): 1,
    (5, 5): 1,
    (5, 6): 1,
    (7, 0): 1,
    (8, 6): 1,
    (9, 2): 1,
    (9, 5): 1,
    (9, 8): 1,
    (21, 0): 7,
}
REDUCE_AT = {
    (11, 6): ((4, 0, 1),),
    (11, 20): ((4, 0, 2),),
    (12, 1): ((4, 0, 3),),
    (13, 3): ((2, 0, 0), (2, 1, 0), (2, 2, 0), (2, 3, 0)),
    (14, 3): ((4, 9, 4), (2, 0, 1)),
    (14, 6): ((2, 1, 1),),
    (15, 0): ((2, 2, 1), (2, 0, 2)),
    (15, 1): ((2, 3, 1),),
    (15, 2): ((1, 0, 0), (2, 1, 2)),
    (15, 3): ((2, 2, 2), (2, 0, 3)),
    (15, 4): ((1, 1, 0), (1, 0, 1), (2, 3, 2)),
    (15, 5): ((2, 1, 3), (2, 2, 3)),
    (15, 6): ((1, 2, 0), (1, 1, 1), (2, 3, 3)),
    (16, 0): ((1, 0, 2), (1, 2, 1), (2, 9, 4)),
    (16, 1): ((1, 1, 2), (1, 0, 3)),
    (16, 2): ((1, 2, 2), (1, 1, 3)),
    (17, 1): ((1, 3, 0),),
    (18, 2): ((1, 2, 3),),
    (18, 6): ((1, 3, 1),),
    (19, 0): ((0, 0, 0), (1, 3, 2)),
    (19, 1): ((0, 1, 0), (0, 0, 1), (1, 3, 3)),
    (19, 2): ((0, 2, 0), (0, 1, 1), (0, 0, 2)),
    (19, 3): ((0, 3, 0), (0, 2, 1), (0, 1, 2), (0, 0, 3)),
    (20, 2): ((0, 3, 1), (0, 2, 2), (0, 1, 3)),
    (20, 7): ((0, 3, 2), (0, 2, 3)),
    (20, 12): ((0, 3, 3), (1, 9, 4)),
    (20, 19): ((0, 9, 4),),
    (23, 0): ((4, 0, 0),),
}


class Ins(NamedTuple):
    features: Any
    order: Any
    norm: Any
    shards: Any


class Outs(NamedTuple):
    slope: Any
    features_grad: Any
    norm_grad: Any
    scalars: Any
    grads: Any


class SumRoom(NamedTuple):
    dp: Any
    fsdp: Any
    s0: Any
    r0: Any
    s1: Any
    r1: Any


class MatrixRoom(NamedTuple):
    pack: Any
    dp: Any
    fsdp: Any
    all: Any
    s0: Any
    r0: Any
    s1: Any
    r1: Any
    s2: Any
    r2: Any


class Mem(NamedTuple):
    w: Any
    g1: Any
    row_sums: Any
    r3: Any
    r1: Any
    left_rooms: Any
    right_rooms: Any
    factor_sems: Any
    four_low: Any
    r5: Any
    stage: Any
    stage_sem: Any
    column_sem: Any
    h1: Any
    d1: Any
    h2: Any
    d2: Any
    a2: Any
    h3: Any
    pad1: Any
    pad2: Any
    pool: Any
    pool_slope: Any
    pool_bend: Any
    pooled: Any
    proj_act: Any
    proj_slope: Any
    proj_hidden: Any
    coef: Any
    stats: Any
    norm: Any
    norm_grads: Any
    norm_tiles: Any
    norm_s0: Any
    norm_r0: Any
    norm_s1: Any
    norm_r1: Any
    bulk_send: Any
    bulk_recv: Any
    mats: Any
    sums: Any
    squares: Any


class Plan:
    def __init__(self, dp_size, fsdp_size, views, inside):
        self.dp = dp_size
        self.fsdp = fsdp_size
        self.devices = dp_size * fsdp_size
        self.views = views
        self.rows = views * PIX
        self.tall = -(-self.rows // C_MID) * C_MID
        self.chunk = views * SIDE
        self.inside = inside
        self.z = 4
        self.x = 2
        self.half = (128, 288, 32, 128, 16)
        self.width = (128, 128, 512, 256, 128)
        piece = P_OUT + 8
        self.embed_rows = -(-piece // (8 * dp_size)) * 8


def kernel(plan, *refs):
    ins, outs, mem = Ins(*refs[:3], refs[3:8]), Outs(*refs[8:12], refs[12:17]), refs[17]
    views, chunk, rows, tall = plan.views, plan.chunk, plan.rows, plan.tall
    row_total = float(rows * plan.devices)
    view_total = float(views * plan.devices)
    image_total = float(views * plan.devices // 2)
    dp_me, fsdp_me = lax.axis_index(DP), lax.axis_index(FSDP)
    y_me, c_me = dp_me // 2, dp_me % 2
    z_me, x_me = fsdp_me // 2, fsdp_me % 2
    y_other, c_other, x_other = 1 - y_me, 1 - c_me, 1 - x_me

    barrier = pltpu.get_barrier_semaphore()

    @pl.loop(1, plan.dp)
    def _(step):
        pl.semaphore_signal(
            barrier, 1, device_id={DP: lax.rem(dp_me + step, plan.dp)}, device_id_type=pl.DeviceIdType.MESH
        )

    @pl.loop(1, plan.fsdp)
    def _(step):
        pl.semaphore_signal(
            barrier, 1, device_id={FSDP: lax.rem(fsdp_me + step, plan.fsdp)}, device_id_type=pl.DeviceIdType.MESH
        )

    pl.semaphore_wait(barrier, plan.dp + plan.fsdp - 2)

    def share(axis, size, me, source_of, slots, send, recv):
        def outgoing(step):
            partner = lax.rem(me + step, size)
            return pltpu.make_async_remote_copy(
                src_ref=source_of(partner),
                dst_ref=slots.at[me],
                send_sem=send.at[step],
                recv_sem=recv.at[me],
                device_id={axis: partner},
                device_id_type=pl.DeviceIdType.MESH,
            )

        def incoming(step):
            source = lax.rem(me + step, size)
            return pltpu.make_async_remote_copy(
                src_ref=slots.at[source],
                dst_ref=slots.at[source],
                send_sem=send.at[step],
                recv_sem=recv.at[source],
                device_id={axis: source},
                device_id_type=pl.DeviceIdType.MESH,
            )

        def start():
            pl.loop(1, size)(lambda step: outgoing(step).start())

        def wait():
            pl.loop(1, size)(lambda step: incoming(step).wait_recv())
            pl.loop(1, size)(lambda step: outgoing(step).wait_send())

        return start, wait

    def add_slots(slots, size):
        total = slots[0]
        for place in range(1, size):
            total = total + slots[place]
        return total

    class Sum:
        def __init__(self, which):
            part = mem.sums[(0, 1, 2, 3, 4, 4, 5, 0, 1, 6)[which]]
            self.dp_slots, self.fsdp_slots = part.dp, part.fsdp
            self.dp_copy = share(
                DP, plan.dp, dp_me, lambda _: self.dp_slots.at[dp_me], self.dp_slots, part.s0, part.r0
            )
            self.fsdp_copy = share(
                FSDP, plan.fsdp, fsdp_me, lambda _: self.fsdp_slots.at[fsdp_me], self.fsdp_slots, part.s1, part.r1
            )

        def start(self, *values):
            for place, value in enumerate(values):
                self.dp_slots[dp_me, place : place + 1, :] = value
            self.dp_copy[0]()

        def middle(self):
            self.dp_copy[1]()
            self.fsdp_slots[fsdp_me] = add_slots(self.dp_slots, plan.dp)
            self.fsdp_copy[0]()

        def finish(self):
            self.fsdp_copy[1]()
            return add_slots(self.fsdp_slots, plan.fsdp)

        def all(self, *values):
            self.start(*values)
            self.middle()
            return self.finish()

    def sum_matrix(which, matrix, extra):
        part = mem.mats[which]
        size = plan.embed_rows
        pack = part.pack
        flat = jnp.concatenate(
            [matrix] + extra + [jnp.zeros((size * plan.dp - P_OUT - len(extra), P_OUT), f32)], axis=0
        )
        for place in range(plan.dp):
            pack[place] = flat[place * size : (place + 1) * size]
        start, wait = share(DP, plan.dp, dp_me, lambda to: pack.at[to], part.dp, part.s0, part.r0)
        start()
        part.dp[dp_me] = pack[dp_me]
        wait()
        part.fsdp[fsdp_me] = add_slots(part.dp, plan.dp)
        start, wait = share(
            FSDP, plan.fsdp, fsdp_me, lambda _: part.fsdp.at[fsdp_me], part.fsdp, part.s1, part.r1
        )
        start()
        wait()
        part.all[dp_me] = add_slots(part.fsdp, plan.fsdp)
        start, wait = share(
            DP, plan.dp, dp_me, lambda _: part.all.at[dp_me], part.all, part.s2, part.r2
        )
        start()
        wait()
        total = jnp.concatenate([part.all[place] for place in range(plan.dp)], axis=0)
        return total[:P_OUT], [total[P_OUT + place : P_OUT + place + 1] for place in range(len(extra))]

    weights = mem.w
    everything = slice(None)

    def row_span(which, half):
        if isinstance(half, tuple):
            return half
        size = plan.half[which]
        if half is None:
            return 0, 2 * size
        return half * size, size

    def column_span(which, dp_index):
        width = plan.width[which]
        return pl.ds(pl.multiple_of(dp_index * width, width), width)

    def places(which, z_index, x_index, dp_index, half, flat=True):
        start, size = row_span(which, half)
        if which == 1 and flat:
            z_list = range(plan.z) if z_index is None else [z_index]
            x_list = range(plan.x) if x_index is None else [x_index]
            return [
                (
                    pl.ds(pl.multiple_of((z_one * plan.x + x_one) * 576 + start, 16), size),
                    column_span(which, dp_index),
                )
                for z_one in z_list
                for x_one in x_list
            ]
        z_one = everything if z_index is None else z_index
        x_one = everything if x_index is None else x_index
        if which == 2:
            return [(dp_index, z_one, x_one, pl.ds(start, size), everything)]
        if which == 4:
            return [(z_one, x_one, pl.ds(pl.multiple_of(dp_index * 32 + start, 16), size), everything)]
        return [(z_one, x_one, pl.ds(start, size), column_span(which, dp_index))]

    recv_parts = {
        1: lambda index: mem.h3.at[index],
        0: lambda index: mem.r1.at[index],
        2: lambda index: mem.r3.at[index],
        4: lambda index: mem.r5.at[index],
    }

    counter = [0]

    class Batch:
        def __init__(self, sources, targets, landings, axis, partner):
            base = counter[0]
            counter[0] += len(sources)
            send, recv = mem.bulk_send, mem.bulk_recv
            self.out = [
                pltpu.make_async_remote_copy(
                    src_ref=source,
                    dst_ref=target,
                    send_sem=send.at[base + place],
                    recv_sem=recv.at[base + place],
                    device_id={axis: partner},
                    device_id_type=pl.DeviceIdType.MESH,
                )
                for place, (source, target) in enumerate(zip(sources, targets))
            ]
            self.come = [
                pltpu.make_async_remote_copy(
                    src_ref=landing,
                    dst_ref=landing,
                    send_sem=send.at[base + place],
                    recv_sem=recv.at[base + place],
                    device_id={axis: partner},
                    device_id_type=pl.DeviceIdType.MESH,
                )
                for place, landing in enumerate(landings)
            ]

        def start(self):
            for copy in self.out:
                copy.start()

        def arrive(self):
            for copy in self.come:
                copy.wait_recv()

        def leave(self):
            for copy in self.out:
                copy.wait_send()

    class LineBatch:
        def __init__(self, source_of, target_of, landing_of):
            base = counter[0]
            counter[0] += plan.z
            send, recv = mem.bulk_send, mem.bulk_recv
            self.out, self.come = [], []
            for step in range(1, plan.z):
                z_to = (z_me + step) % plan.z
                self.out.append(
                    pltpu.make_async_remote_copy(
                        src_ref=source_of(z_to),
                        dst_ref=target_of(z_to),
                        send_sem=send.at[base + step],
                        recv_sem=recv.at[base + z_me],
                        device_id={FSDP: z_to * plan.x + x_me},
                        device_id_type=pl.DeviceIdType.MESH,
                    )
                )
                self.come.append(
                    pltpu.make_async_remote_copy(
                        src_ref=landing_of(z_to),
                        dst_ref=landing_of(z_to),
                        send_sem=send.at[base + step],
                        recv_sem=recv.at[base + z_to],
                        device_id={FSDP: z_to * plan.x + x_me},
                        device_id_type=pl.DeviceIdType.MESH,
                    )
                )

        start, arrive, leave = Batch.start, Batch.arrive, Batch.leave

    def pick(ref, indexes):
        return [ref.at[index] for index in indexes]

    def own_dp(y_index, c_index):
        return y_index * 2 + c_index

    x_partner = z_me * plan.x + x_other
    y_partner = own_dp(y_other, c_me)
    c_partner = own_dp(y_me, c_other)
    dp_far = own_dp(y_other, c_other)

    class Gather:
        def __init__(self, which, start, size):
            ref = weights[which]
            self.which, self.rows = which, (start, size)
            both, low, high = (start, size), (start, size // 2), (start + size // 2, size // 2)

            def at(*index):
                return pick(ref, places(which, *index, False))

            own = at(z_me, x_me, dp_me, both)[0]
            self.line = LineBatch(
                lambda _: own, lambda _: own, lambda z_from: at(z_from, x_me, dp_me, both)[0]
            )
            sent, come = at(None, x_me, dp_me, low), at(None, x_other, dp_me, low)
            x_first = Batch(sent, sent, come, FSDP, x_partner)
            sent, come = at(None, x_me, dp_me, high), at(None, x_me, y_partner, high)
            y_first = Batch(sent, sent, come, DP, y_partner)
            sent, come = at(None, None, dp_me, low), at(None, None, y_partner, low)
            y_second = Batch(sent, sent, come, DP, y_partner)
            sent = at(None, x_me, dp_me, high) + at(None, x_me, y_partner, high)
            come = at(None, x_other, dp_me, high) + at(None, x_other, y_partner, high)
            x_second = Batch(sent, sent, come, FSDP, x_partner)
            sent = at(None, None, dp_me, both) + at(None, None, y_partner, both)
            come = at(None, None, c_partner, both) + at(None, None, dp_far, both)
            core = Batch(sent, sent, come, DP, c_partner)
            self.stages = ((self.line,), (x_first, y_first), (y_second, x_second), (core,))

        def put_own(self):
            index = places(self.which, z_me, x_me, dp_me, self.rows, False)[0]
            shard = ins.shards[self.which][self.rows[0] : self.rows[0] + self.rows[1], :]
            weights[self.which][index] = shard.astype(bf16)

        def start(self, stage):
            for batch in self.stages[stage]:
                batch.start()

        def arrive(self, stage):
            for batch in self.stages[stage]:
                batch.arrive()

        def leave(self):
            for stage in self.stages:
                for batch in stage:
                    batch.leave()

    class Piece:
        def __init__(self, which, ref, room, z_index):
            def at(*index):
                return pick(ref, places(which, z_index, *index))

            def land(*index):
                return [room(index_one) for index_one in places(which, z_index, *index)]

            self.z = z_index
            self.core = Batch(
                at(None, c_partner, None) + at(None, dp_far, None),
                land(None, c_partner, None) + land(None, dp_far, None),
                land(None, dp_me, None) + land(None, y_partner, None),
                DP,
                c_partner,
            )
            self.y_first = Batch(
                at(None, y_partner, 0), land(None, dp_far, 0), land(None, c_partner, 0), DP, y_partner
            )
            self.x_first = Batch(
                at(x_other, dp_me, 1) + at(x_other, y_partner, 1),
                land(x_other, c_partner, 1) + land(x_other, dp_far, 1),
                land(x_me, c_partner, 1) + land(x_me, dp_far, 1),
                FSDP,
                x_partner,
            )
            self.x_second = Batch(
                at(x_other, dp_me, 0), land(x_other, dp_far, 0), land(x_me, dp_far, 0), FSDP, x_partner
            )
            self.y_second = Batch(
                at(x_me, y_partner, 1), land(x_other, dp_far, 1), land(x_other, c_partner, 1), DP, y_partner
            )

    def put_gradient(which, total):
        outs.grads[which][...] = total
        squares = jnp.sum(total * total, axis=0, keepdims=True)
        folded = squares[:, :LANES]
        for place in range(1, squares.shape[1] // LANES):
            folded = folded + squares[:, place * LANES : (place + 1) * LANES]
        mem.squares[...] += folded

    class Reduce:
        def __init__(self, which, ref, cut):
            self.which, self.ref, self.room = which, ref, recv_parts[which]
            self.pieces = [
                Piece(which, ref, self.room, z_index) for z_index in (range(plan.z) if cut else [None])
            ]
            self.base = counter[0]
            counter[0] += plan.z

        def line_copy(self, z_to):
            return pltpu.make_async_remote_copy(
                src_ref=self.ref.at[places(self.which, z_to, x_me, dp_me, None)[0]],
                dst_ref=self.room(places(self.which, z_me, x_other, dp_far, None)[0]),
                send_sem=mem.bulk_send.at[self.base + z_to],
                recv_sem=mem.bulk_recv.at[self.base + z_me],
                device_id={FSDP: z_to * plan.x + x_me},
                device_id_type=pl.DeviceIdType.MESH,
            )

        def line_room(self, z_from):
            return self.room(places(self.which, z_from, x_other, dp_far, None)[0])

        def add(self, z_index, pairs):
            def one(z_one):
                for here, there in pairs:
                    for x_step in range(plan.x) if here[0] is None else [None]:
                        x_here = x_step if here[0] is None else here[0]
                        x_there = x_step if there[0] is None else there[0]
                        index = places(self.which, z_one, x_here, *here[1:])[0]
                        other = places(self.which, z_one, x_there, *there[1:])[0]
                        total = self.ref[index].astype(f32) + self.room(other)[...].astype(f32)
                        self.ref[index] = total.astype(bf16)

            if z_index is None:
                pl.loop(0, plan.z)(one)
            else:
                one(z_index)

        def core_start(self, place=0):
            if plan.inside:
                self.pieces[place].core.start()

        def core_add(self, place=0):
            if plan.inside:
                piece = self.pieces[place]
                piece.core.arrive()
                self.add(piece.z, [((None, dp_me, None),) * 2, ((None, y_partner, None),) * 2])
                piece.y_first.start()
                piece.x_first.start()

        def first_add(self, place=0):
            if plan.inside:
                piece = self.pieces[place]
                piece.y_first.arrive()
                self.add(piece.z, [((None, dp_me, 0), (None, c_partner, 0))])
                piece.x_second.start()
                piece.x_first.arrive()
                self.add(
                    piece.z, [((x_me, dp_me, 1), (x_me, c_partner, 1)), ((x_me, y_partner, 1), (x_me, dp_far, 1))]
                )
                piece.y_second.start()

        def second_add(self, place=0):
            if plan.inside:
                piece = self.pieces[place]
                piece.x_second.arrive()
                piece.y_second.arrive()
                self.add(
                    piece.z, [((x_me, dp_me, 0), (x_me, dp_far, 0)), ((x_me, dp_me, 1), (x_other, c_partner, 1))]
                )
                if piece.z is None:
                    for step in range(1, plan.z):
                        self.line_copy((z_me + step) % plan.z).start()
                else:

                    @pl.when(z_me != piece.z)
                    def _():
                        self.line_copy(piece.z).start()

        def finish(self):
            if not plan.inside:
                return
            total = self.ref[places(self.which, z_me, x_me, dp_me, None)[0]].astype(f32)
            for step in range(1, plan.z):
                z_from = (z_me + step) % plan.z
                room = self.line_room(z_from)
                pltpu.make_async_remote_copy(
                    src_ref=room,
                    dst_ref=room,
                    send_sem=mem.bulk_send.at[self.base + z_from],
                    recv_sem=mem.bulk_recv.at[self.base + z_from],
                    device_id={FSDP: z_from * plan.x + x_me},
                    device_id_type=pl.DeviceIdType.MESH,
                ).wait_recv()
                total = total + room[...].astype(f32)
            put_gradient(self.which, total)
            for step in range(1, plan.z):
                self.line_copy((z_me + step) % plan.z).wait_send()
            for piece in self.pieces:
                for batch in (piece.core, piece.y_first, piece.x_first, piece.x_second, piece.y_second):
                    batch.leave()

    gathers, steps = [], []
    if plan.inside:
        for which, cuts in enumerate((2, 3, 1, 2, 1)):
            size = 2 * plan.half[which] // cuts
            gathers += [Gather(which, cut * size, size) for cut in range(cuts)]

    def line_step(place):
        gathers[place].arrive(0)
        gathers[place].start(1)
        if place + 1 < len(gathers):
            gathers[place + 1].start(0)

    def first_step(place):
        gathers[place].arrive(1)
        gathers[place].start(2)

    def second_step(place):
        gathers[place].arrive(2)
        gathers[place].start(3)

    for place in range(len(gathers)):
        steps.append((line_step, place))
        if place > 0:
            steps.append((second_step, place - 1))
        steps.append((first_step, place))
    if plan.inside:
        steps.append((second_step, len(gathers) - 1))

    def take(count):
        taken, steps[:] = steps[:count], steps[count:]
        return [lambda one=one: one[0](one[1]) for one in taken]

    def moves(site, item):
        found = take(GATHER_AT.get((site, item), 0)) if plan.inside else []
        for which, piece, kind in REDUCE_AT.get((site, item), ()):
            one = reduces[which]
            found.append(
                one.finish
                if kind == 4
                else lambda one=one, kind=kind, piece=piece: (
                    one.core_start,
                    one.core_add,
                    one.first_add,
                    one.second_add,
                )[kind](piece)
            )
        return found

    def hook(site, item=0):
        for move in moves(site, item):
            move()

    def hook_in(site, index, count, first=0, stride=1):
        for item in range(count):
            found = moves(site, item)
            if found and plan.inside:

                @pl.when(index == first + item * stride)
                def _(found=found):
                    for move in found:
                        move()

    def cores_arrive(which):
        for one in gathers:
            if one.which == which:
                one.arrive(3)

    gradients = [mem.g1, mem.stage.at[pl.ds(0, 9 * C_MID)], weights[2], weights[3], weights[4]]
    reduces = [None if which == 3 else Reduce(which, gradients[which], which < 3) for which in range(5)]
    assert counter[0] <= COPIES
    mem.squares[...] = jnp.zeros((1, LANES), f32)

    if plan.inside:
        gathers[0].put_own()
        gathers[0].start(0)
        for one in gathers[1:]:
            one.put_own()
        tiles = mem.norm_tiles
        tiles[dp_me, fsdp_me] = ins.norm[...].astype(bf16).astype(f32)
        norm_dp = share(
            DP, plan.dp, dp_me, lambda _: tiles.at[dp_me, fsdp_me], tiles.at[:, fsdp_me], mem.norm_s0, mem.norm_r0
        )
        norm_dp[0]()
    else:
        loads = [
            pltpu.make_async_copy(ins.shards[which], weights[which], mem.bulk_send.at[which])
            for which in range(5)
        ]
        for load in loads:
            load.start()

    pieces = BLOCKS * CHUNKS

    def hidden_rows(index, pixel=0, count=chunk):
        return pl.ds(pl.multiple_of(index * chunk + pixel * views, 16), count)

    class Ring:
        def __init__(self, ref, start):
            self.ref, self.base = ref, start

        def rows(self, index, pixel=0, count=chunk):
            return pl.ds(
                pl.multiple_of(self.base + lax.rem(index, SLOTS) * chunk + pixel * views, 16), count
            )

        def copy(self, array, index, into):
            block, place = index // CHUNKS, lax.rem(index, CHUNKS)
            outer = array.at[
                pl.ds(pl.multiple_of(place * chunk, 16), chunk),
                pl.ds(pl.multiple_of(block * C_MID, LANES), C_MID),
            ]
            inner = self.ref.at[self.rows(index)]
            source, target = (outer, inner) if into else (inner, outer)
            return pltpu.make_async_copy(
                source, target, mem.stage_sem.at[0 if into else 1, lax.rem(index, SLOTS)]
            )

        def first_loads(self, array):
            for index in range(3):
                self.copy(array, index, True).start()

        def next_load(self, array, index):
            @pl.when(index + 3 < pieces)
            def _():
                self.copy(array, index + 3, True).start()

        def save(self, array, index):
            self.copy(array, index, False).start()

            @pl.when(index >= 2)
            def _():
                self.copy(array, index - 2, False).wait()

        def last_saves(self, array):
            for index in (pieces - 2, pieces - 1):
                self.copy(array, index, False).wait()

    stage_ref = mem.stage
    stage = Ring(stage_ref, 0)

    def piece_columns(index, part):
        return pl.ds(pl.multiple_of(index // CHUNKS * C_MID + part * LANES, LANES), LANES)

    features, slope_hbm = ins.features, outs.slope
    hidden_three = mem.h3

    def feature_copy(block, target):
        return pltpu.make_async_copy(
            features.at[:, pl.ds(block * C_MID, C_MID)], target, mem.column_sem.at[block]
        )

    feature_loads = [
        feature_copy(block, hidden_three.at[pl.ds(block * rows, rows)]) for block in range(BLOCKS)
    ]
    for copy in feature_loads:
        copy.start()
    stage.first_loads(features)

    padded_one, padded_two = mem.pad1, mem.pad2
    for padded in (padded_one, padded_two):
        for edge in (0, SIDE + 1):
            padded[edge] = jnp.zeros((padded.shape[1], C_MID), bf16)
        for edge in (0, SIDE + 1):
            padded[:, pl.ds(edge * views, views), :] = jnp.zeros((SIDE + 2, views, C_MID), bf16)
    rest = jnp.zeros((tall - rows, C_MID), bf16)
    for ref, end in ((mem.d1, rows), (mem.h2, rows), (mem.d2, rows), (mem.a2, rows), (hidden_three, BLOCKS * rows)):
        ref[end : end + tall - rows, :] = rest

    if plan.inside:
        norm_dp[1]()
        norm_out = []
        norm_in = []
        for step in range(1, plan.fsdp):
            partner = (fsdp_me + step) % plan.fsdp
            norm_out.append(
                pltpu.make_async_remote_copy(
                    src_ref=tiles.at[:, fsdp_me],
                    dst_ref=tiles.at[:, fsdp_me],
                    send_sem=mem.norm_s1.at[step],
                    recv_sem=mem.norm_r1.at[fsdp_me],
                    device_id={FSDP: partner},
                    device_id_type=pl.DeviceIdType.MESH,
                )
            )
            norm_in.append(
                pltpu.make_async_remote_copy(
                    src_ref=tiles.at[:, partner],
                    dst_ref=tiles.at[:, partner],
                    send_sem=mem.norm_s1.at[step],
                    recv_sem=mem.norm_r1.at[partner],
                    device_id={FSDP: partner},
                    device_id_type=pl.DeviceIdType.MESH,
                )
            )
        for copy in norm_out:
            copy.start()
        hook(21)
        for copy in norm_in:
            copy.wait_recv()
        for copy in norm_out:
            copy.wait_send()
        norm_all = mem.norm
        for dp_one in range(plan.dp):
            for fsdp_one in range(plan.fsdp):
                start = (dp_one * plan.fsdp + fsdp_one) * LANES
                norm_all[:, start : start + LANES] = tiles[dp_one, fsdp_one]
    else:
        for copy in loads:
            copy.wait()
        norm_all = mem.norm
        norm_all[...] = ins.norm[...]

    starts = (0, C_MID, 2 * C_MID, 2 * C_MID + C_IN, 2 * C_MID + C_IN + P_HID)

    def gain(layer):
        return norm_all[0:1, starts[layer] : starts[layer + 1]]

    coef, stats = mem.coef, mem.stats

    def norm_coefs(layer, totals, count, low=0):
        width = totals.shape[1]
        here, there = slice(low, low + width), slice(starts[layer] + low, starts[layer] + low + width)
        mean = totals[0:1] / count
        scaling = lax.rsqrt(totals[1:2] / count - mean * mean + norm_epsilon)
        slope = scaling * norm_all[0:1, there]
        stats[0:1, there] = mean
        stats[1:2, there] = scaling
        coef[0:1, here] = slope
        coef[1:2, here] = norm_all[1:2, there] - mean * slope

    def grad_coefs(layer, totals, count):
        width = starts[layer + 1] - starts[layer]
        mean = stats[0:1, starts[layer] : starts[layer + 1]]
        scaling = stats[1:2, starts[layer] : starts[layer + 1]]
        mem.norm_grads[0:1, starts[layer] : starts[layer + 1]] = totals[1:2]
        mem.norm_grads[1:2, starts[layer] : starts[layer + 1]] = totals[0:1]
        slope = scaling * gain(layer)
        bend = slope * scaling * totals[1:2] / count
        coef[0:1, :width] = slope
        coef[1:2, :width] = slope * totals[0:1] / count - mean * bend
        coef[2:3, :width] = bend

    def xhat_sum(layer, plain, product):
        mean = stats[0:1, starts[layer] : starts[layer + 1]]
        scaling = stats[1:2, starts[layer] : starts[layer + 1]]
        return scaling * (product - mean * plain)

    zero_row = jnp.zeros((1, C_MID), f32)

    def column_sums(value):
        return jnp.sum(value, axis=0, keepdims=True)

    def whole(which):
        value = weights[which][...]
        return value.reshape(-1, value.shape[-1])

    row_sums = mem.row_sums

    def clear_sums():
        row_sums[...] = jnp.zeros_like(row_sums)

    def count_in(cols, value, other):
        row_sums[0:1, cols] += column_sums(value)
        row_sums[1:2, cols] += column_sums(value * other)

    def own_columns(side):
        core = (c_me + side) % 2
        return [
            pl.ds(pl.multiple_of(half * (C_MID // 2) + core * LANES, LANES), LANES) for half in range(2)
        ]

    def turn_rows(ref):
        @pl.loop(0, tall // C_MID)
        def _(block):
            at = pl.ds(pl.multiple_of(block * C_MID, C_MID), C_MID)
            ref[at, :] = ref[at, :].T

    def turned(ref):
        return jnp.concatenate([ref[start : start + C_MID, :] for start in range(0, tall, C_MID)], axis=1)

    def sends_leave(which):
        for one in gathers:
            if one.which == which:
                one.leave()

    def turn_weight(which, block):
        ref = weights[which]
        if which == 1:
            groups = [block * 8 + group for group in range(8)]
            ats = [
                (group // 18, group // 9 % 2, pl.ds(pl.multiple_of(group % 9 * 64, 64), 64), everything)
                for group in groups
            ]
            value = jnp.concatenate([ref[at] for at in ats], axis=0).T
            for place, at in enumerate(ats):
                ref[at] = value[place * 64 : (place + 1) * 64, :]
        elif which == 3:
            for half in range(P_HID // C_MID):
                cols = slice(half * C_MID, (half + 1) * C_MID)
                value = ref[block, :, :, cols]
                ref[block, :, :, cols] = value.reshape(C_MID, C_MID).T.reshape(value.shape)
        else:
            value = ref[block]
            ref[block] = value.reshape(C_MID, C_MID).T.reshape(value.shape)

    hidden_one, slope_one = mem.h1, mem.d1
    hidden_two, slope_two = mem.h2, mem.d2
    act_two = mem.a2
    long = rows // 3

    def span(index):
        return pl.ds(pl.multiple_of(index * chunk, 16), chunk)

    def long_rows(block, index):
        return pl.ds(pl.multiple_of(block * rows + index * long, 16), long)

    def put_sides(ref, at, sides, hidden):
        for place, cols in enumerate(sides):
            part = hidden[:, place * LANES : (place + 1) * LANES]
            ref[at, cols] = part.astype(bf16)
            count_in(cols, part, part)

    for copy in feature_loads:
        copy.wait()
    clear_sums()

    @pl.loop(0, 2)
    def _(side):
        sides = own_columns(side)

        @pl.loop(0, 3)
        def _(index):
            left = jnp.concatenate([hidden_three[long_rows(block, index), :] for block in range(BLOCKS)], axis=1)
            right = jnp.concatenate([weights[0][:, :, :, cols].reshape(C_IN, LANES) for cols in sides], axis=1)
            put_sides(hidden_one, long_rows(0, index), sides, dot(left, right))

            hook_in(0, side * 3 + index, 6)

        @pl.when(side == 0)
        def _():
            cores_arrive(0)

    sum_one = Sum(0)
    sum_one.start(row_sums[0:1, :C_MID], row_sums[1:2, :C_MID])
    hook(1)
    sends_leave(0)
    pl.loop(0, 2)(lambda block: turn_weight(0, block))
    sum_one.middle()
    pl.loop(2, 4)(lambda block: turn_weight(0, block))
    hook(2)
    clear_sums()
    norm_coefs(0, sum_one.finish(), row_total)

    def activate(hidden_ref, slope_ref, put, site):
        @pl.loop(0, PIX)
        def _(pixel):
            place = pl.ds(pl.multiple_of(pixel * views, 16), views)
            for block in range(C_MID // LANES):
                cols = slice(block * LANES, (block + 1) * LANES)
                out = hidden_ref[place, cols].astype(f32) * coef[0:1, cols] + coef[1:2, cols]
                value, slope = gelu_pair(out)
                slope_ref[place, cols] = slope.astype(bf16)
                put(pixel, cols, value.astype(bf16))
            hook_in(site, pixel, SIDE, SIDE - 1, SIDE)

    def put_padded(padded):
        def put(pixel, cols, value):
            padded[pixel // SIDE + 1, pl.ds(pl.multiple_of((pixel % SIDE + 1) * views, 16), views), cols] = value

        return put

    activate(hidden_one, slope_one, put_padded(padded_one), 3)
    hook(4)

    def patch(padded, first, count, flip):
        found = []
        for vertical in range(3):
            for lateral in range(3):
                down, across = (2 - vertical, 2 - lateral) if flip else (vertical, lateral)
                piece = padded[pl.ds(first + down, count), across * views : across * views + chunk, :]
                found.append(piece.reshape(count * chunk, C_MID))
        return jnp.concatenate(found, axis=1)

    def image_rows(first, count):
        return pl.ds(pl.multiple_of(first * chunk, 16), count * chunk)

    def second_part(sides, first, count):
        right = jnp.concatenate([weights[1][:, :, :, cols].reshape(9 * C_MID, LANES) for cols in sides], axis=1)
        hidden = dot(patch(padded_one, first, count, False), right)
        put_sides(hidden_two, image_rows(first, count), sides, hidden)

    @pl.loop(0, 2)
    def _(side):
        sides = own_columns(side)

        @pl.loop(0, 3)
        def _(index):
            second_part(sides, 2 * index, 2)
            hook_in(5, side * 4 + index, 8)

        second_part(sides, 6, 1)

        @pl.when(side == 0)
        def _():
            cores_arrive(1)

    sum_two = Sum(1)
    sum_two.start(row_sums[0:1, :C_MID], row_sums[1:2, :C_MID])
    hook(6)
    sends_leave(1)
    pl.loop(0, 4)(lambda block: turn_weight(1, block))
    sum_two.middle()
    pl.loop(4, 9)(lambda block: turn_weight(1, block))
    hook(7)
    clear_sums()
    norm_coefs(1, sum_two.finish(), row_total)

    def put_rows(pixel, cols, value):
        act_two[pl.ds(pl.multiple_of(pixel * views, 16), views), cols] = value

    activate(hidden_two, slope_two, put_rows, 8)
    cores_arrive(2)

    def weight_three(block):
        return weights[2][block].reshape(C_MID, C_MID)

    sums_low, sums_high = Sum(2), Sum(3)
    half_width = C_IN // 2

    @pl.loop(0, BLOCKS)
    def _(block):
        cols = pl.ds(pl.multiple_of(block * C_MID, LANES), C_MID)

        @pl.loop(0, 3)
        def _(index):
            hidden = dot(act_two[long_rows(0, index), :], weight_three(block))
            hidden_three[long_rows(block, index), :] = hidden.astype(bf16)
            count_in(cols, hidden, hidden)
            hook_in(9, block * 3 + index, 12)

        @pl.when(block == 1)
        def _():
            sums_low.start(row_sums[0:1, :half_width], row_sums[1:2, :half_width])

        @pl.when(block == 2)
        def _():
            sums_low.middle()

    sums_high.start(row_sums[0:1, half_width:], row_sums[1:2, half_width:])
    norm_coefs(2, sums_low.finish(), row_total)

    hook(22)

    pool, pool_slope, pool_bend = mem.pool, mem.pool_slope, mem.pool_bend
    for ref in (pool, pool_slope, pool_bend):
        ref[...] = jnp.zeros_like(ref)

    @pl.loop(0, pieces)
    def _(index):
        stage.copy(features, index, True).wait()

        @pl.loop(0, C_MID // LANES)
        def _(part):
            inner = pl.ds(pl.multiple_of(part * LANES, LANES), LANES)
            cols = piece_columns(index, part)
            slope_row, shift_row = coef[0:1, cols], coef[1:2, cols]
            kept = (pool[:, cols], pool_slope[:, cols], pool_bend[:, cols])
            for pixel in range(SIDE):
                stage_at, hidden_at = stage.rows(index, pixel, views), hidden_rows(index, pixel, views)
                hidden = hidden_three[hidden_at, inner].astype(f32)
                total = hidden * slope_row + shift_row + stage_ref[stage_at, inner].astype(f32)
                value, slope = gelu_pair(total)
                stage_ref[stage_at, inner] = slope.astype(bf16)
                kept = (kept[0] + value, kept[1] + slope, kept[2] + slope * hidden)
            pool[:, cols], pool_slope[:, cols], pool_bend[:, cols] = kept

        stage.save(slope_hbm, index)
        stage.next_load(features, index)

        @pl.when(index == 2)
        def _():
            sums_high.middle()

        @pl.when(index == pieces // 2 - 1)
        def _():
            norm_coefs(2, sums_high.finish(), row_total, half_width)

        hook_in(10, index, pieces)

    stage.last_saves(slope_hbm)
    cores_arrive(3)
    cores_arrive(4)
    for which in range(2, 5):
        sends_leave(which)

    pooled = (pool[...] * (1.0 / PIX)).astype(bf16)
    mem.pooled[...] = pooled
    if plan.inside:
        wide_at = C_IN // plan.fsdp
        low_at = P_HID // plan.dp
        left_rooms, right_rooms = mem.left_rooms, mem.right_rooms

        def wide_columns(fsdp_one):
            return pl.ds(pl.multiple_of(fsdp_one * wide_at, LANES), wide_at)

        def low_columns(dp_one):
            return pl.ds(pl.multiple_of(dp_one * low_at, LANES), low_at)

        sems = mem.factor_sems
        left_first = share(
            FSDP, plan.fsdp, fsdp_me, lambda to: mem.pooled.at[:, wide_columns(to)], left_rooms.at[dp_me], sems.at[0], sems.at[1]
        )
        left_second = share(
            DP, plan.dp, dp_me, lambda _: left_rooms.at[dp_me], left_rooms, sems.at[2], sems.at[3]
        )
        right_first = share(
            DP, plan.dp, dp_me, lambda to: mem.four_low.at[:, low_columns(to)], right_rooms.at[fsdp_me], sems.at[4], sems.at[5]
        )
        right_second = share(
            FSDP, plan.fsdp, fsdp_me, lambda _: right_rooms.at[fsdp_me], right_rooms, sems.at[6], sems.at[7]
        )
        left_rooms[dp_me, fsdp_me] = mem.pooled[:, wide_columns(fsdp_me)]

    proj_hidden = dot(pooled, whole(3))
    sum_four = Sum(4)
    sum_four.start(column_sums(proj_hidden), column_sums(proj_hidden * proj_hidden))
    pl.loop(0, 2)(lambda block: turn_weight(3, block))
    sum_four.middle()
    pl.loop(2, 4)(lambda block: turn_weight(3, block))
    totals = sum_four.finish()
    stage.first_loads(slope_hbm)
    norm_coefs(3, totals, view_total)
    value, slope = gelu_pair(proj_hidden * coef[0:1, :P_HID] + coef[1:2, :P_HID])
    proj_act = value.astype(bf16)
    mem.proj_act[...] = proj_act
    mem.proj_slope[...] = slope
    mem.proj_hidden[...] = proj_hidden

    def weight_five(block):
        return weights[4][block // plan.x, block % plan.x]

    parts = P_HID // P_OUT
    embedding = jnp.zeros((views, P_OUT), f32)
    for block in range(parts):
        embedding = embedding + dot_cols(proj_act[:, block * P_OUT : (block + 1) * P_OUT], weight_five(block))

    images = views // 2
    order = jnp.broadcast_to(ins.order[...], (images, views))
    image_row = lax.broadcasted_iota(jnp.int32, (images, views), 0)
    selectors = [(order == 2 * image_row + which).astype(f32) for which in range(2)]
    embeds = [exact_dot(selector, embedding) for selector in selectors]
    moments = [exact_rows(embed, embed) for embed in embeds]
    packed, diagonal = pack_pair(*moments)
    packed, extra = sum_matrix(0, packed, [diagonal] + [column_sums(embed) for embed in embeds])
    moments = unpack_pair(packed, extra[0])
    eye = (
        lax.broadcasted_iota(jnp.int32, (P_OUT, P_OUT), 0) == lax.broadcasted_iota(jnp.int32, (P_OUT, P_OUT), 1)
    ).astype(f32)
    centred, covariances = [], []
    for which in range(2):
        mean = extra[1 + which] / image_total
        centred.append(embeds[which] - mean)
        covariances.append(moments[which] / image_total - exact_rows(mean, mean) + ridge_term * eye)
    inverses = inverse_factors(covariances)
    whitened = [exact_cols(centred[which], inverses[which]) for which in range(2)]
    scalings = [
        lax.rsqrt(jnp.mean(white * white, axis=1, keepdims=True) + norm_epsilon) for white in whitened
    ]
    units = [white * scaling for white, scaling in zip(whitened, scalings)]
    difference = units[0] - units[1]
    objective_row = column_sums(difference * difference) * (1.0 / P_OUT)
    unit_grads = [difference * (2.0 / P_OUT), difference * (-2.0 / P_OUT)]
    white_grads = []
    for which in range(2):
        inner = jnp.mean(whitened[which] * unit_grads[which], axis=1, keepdims=True)
        white_grads.append(
            scalings[which] * unit_grads[which] - whitened[which] * (scalings[which] ** 3 * inner)
        )
    directs = [exact_dot(white_grads[which], inverses[which]) for which in range(2)]
    products = [exact_rows(white_grads[which], whitened[which]) for which in range(2)]
    packed, diagonal = pack_pair(*products)
    packed, extra = sum_matrix(
        1, packed, [diagonal] + [column_sums(grad) for grad in white_grads] + [objective_row]
    )
    products = unpack_pair(packed, extra[0])
    embed_grad = jnp.zeros((views, P_OUT), f32)
    for which in range(2):
        symmetric = exact_rows(inverses[which], exact_dot(products[which], inverses[which]))
        mean_grad = exact_dot(extra[1 + which], inverses[which])
        grad = directs[which] - (exact_dot(centred[which], symmetric) + mean_grad) / image_total
        embed_grad = embed_grad + exact_rows(selectors[which], grad)
    objective_row = extra[3]
    embed_low = embed_grad.astype(bf16)

    proj_act, proj_hidden = mem.proj_act[...], mem.proj_hidden[...]
    act_grad = jnp.concatenate([dot(embed_low, weight_five(block)) for block in range(parts)], axis=1)
    upstream = act_grad * mem.proj_slope[...]
    plain = column_sums(upstream)
    sum_four_back = Sum(5)
    sum_four_back.start(plain, xhat_sum(3, plain, column_sums(upstream * proj_hidden)))
    for block in range(parts):
        weights[4][block // plan.x, block % plan.x] = dot_rows(
            embed_low, proj_act[:, block * P_OUT : (block + 1) * P_OUT]
        ).astype(bf16)
    pl.loop(0, 4)(lambda block: turn_weight(2, block))
    sum_four_back.middle()
    turn_rows(act_two)
    grad_coefs(3, sum_four_back.finish(), view_total)
    four_low = (
        upstream * coef[0:1, :P_HID] - coef[1:2, :P_HID] - proj_hidden * coef[2:3, :P_HID]
    ).astype(bf16)
    mem.four_low[...] = four_low
    if plan.inside:
        right_rooms[fsdp_me, dp_me] = mem.four_low[:, low_columns(dp_me)]

    @pl.loop(0, BLOCKS)
    def _(block):
        cols = pl.ds(pl.multiple_of(block * C_MID, LANES), C_MID)
        right = jnp.concatenate(
            [
                weights[3][block, :, :, half * C_MID : (half + 1) * C_MID].reshape(C_MID, C_MID)
                for half in range(P_HID // C_MID)
            ],
            axis=0,
        )
        grad = dot(four_low, right) * (1.0 / PIX)
        row_sums[0:1, cols] = column_sums(grad * pool_slope[:, cols])
        row_sums[1:2, cols] = column_sums(grad * pool_bend[:, cols])
        pool_slope[:, cols] = grad

    plain = row_sums[0:1, :]
    sum_three_back = Sum(6)
    sum_three_back.start(plain, xhat_sum(2, plain, row_sums[1:2, :]))
    if not plan.inside:
        grad_four = dot_rows(mem.pooled[...], four_low).astype(bf16)
        weights[3][...] = grad_four.reshape(weights[3].shape)
    sum_three_back.middle()
    hook(23)
    grad_coefs(2, sum_three_back.finish(), row_total)
    pool[...] = pool_slope[...] * coef[0:1, :]

    if plan.inside:
        left_first[0]()
        right_first[0]()
    clear_sums()

    @pl.loop(0, pieces)
    def _(index):
        stage.copy(slope_hbm, index, True).wait()
        stage.next_load(slope_hbm, index)

        @pl.loop(0, C_MID // LANES)
        def _(part):
            inner = pl.ds(pl.multiple_of(part * LANES, LANES), LANES)
            cols = piece_columns(index, part)
            spread, shift_row, bend_row = pool[:, cols], coef[1:2, cols], coef[2:3, cols]
            for pixel in range(SIDE):
                hidden_at = hidden_rows(index, pixel, views)
                hidden = hidden_three[hidden_at, inner].astype(f32)
                slope = stage_ref[stage.rows(index, pixel, views), inner].astype(f32)
                hidden_three[hidden_at, inner] = (slope * spread - shift_row - hidden * bend_row).astype(bf16)

        hook_in(11, index, pieces)
        if plan.inside:

            @pl.when(index == pieces // 2)
            def _():
                left_first[1]()
                left_second[0]()
                right_first[1]()
                right_second[0]()

    @pl.loop(0, 3)
    def _(index):
        at = long_rows(0, index)
        left = jnp.concatenate([hidden_three[long_rows(block, index), :] for block in range(BLOCKS)], axis=1)
        upstream = dot(left, weights[2][...].reshape(C_IN, C_MID)) * slope_two[at, :].astype(f32)
        slope_two[at, :] = upstream.astype(bf16)
        count_in(slice(0, C_MID), upstream, hidden_two[at, :].astype(f32))
        hook_in(12, index, 3)

    sums = row_sums[0:1, :C_MID], row_sums[1:2, :C_MID]
    sum_two_back = Sum(7)
    sum_two_back.start(sums[0], xhat_sum(1, *sums))

    @pl.loop(0, BLOCKS)
    def _(block):
        grad = dot(turned(act_two), hidden_three[pl.ds(pl.multiple_of(block * rows, 16), tall), :])
        weights[2][block] = grad.astype(bf16).reshape(plan.z, plan.x, -1, C_MID)

        @pl.when(block == 1)
        def _():
            sum_two_back.middle()

        hook_in(13, block, BLOCKS)

    clear_sums()
    grad_coefs(1, sum_two_back.finish(), row_total)

    def apply_grad(hidden_ref, grad_ref, put, site):
        @pl.loop(0, PIX)
        def _(pixel):
            place = pl.ds(pl.multiple_of(pixel * views, 16), views)
            for block in range(C_MID // LANES):
                cols = slice(block * LANES, (block + 1) * LANES)
                grad = (
                    grad_ref[place, cols].astype(f32) * coef[0:1, cols]
                    - coef[1:2, cols]
                    - hidden_ref[place, cols].astype(f32) * coef[2:3, cols]
                )
                put(pixel, cols, grad.astype(bf16))
            hook_in(site, pixel, SIDE, SIDE - 1, SIDE)

    def put_two(pixel, cols, value):
        put_padded(padded_two)(pixel, cols, value)
        slope_two[pl.ds(pl.multiple_of(pixel * views, 16), views), cols] = value

    apply_grad(hidden_two, slope_two, put_two, 14)
    if plan.inside:
        left_second[1]()
        right_second[1]()
        order_all = [(dp_one, fsdp_one) for dp_one in range(plan.dp) for fsdp_one in range(plan.fsdp)]
        left = jnp.concatenate([left_rooms[dp_one, fsdp_one] for dp_one, fsdp_one in order_all], axis=0)
        right = jnp.concatenate([right_rooms[fsdp_one, dp_one] for dp_one, fsdp_one in order_all], axis=0)
        put_gradient(3, dot_rows(left, right))
    turn_rows(slope_two)
    column_places = [
        hidden_three.at[pl.ds(2 * rows, rows)],
        hidden_three.at[pl.ds(3 * rows, rows)],
        hidden_two.at[pl.ds(0, rows)],
        hidden_three.at[pl.ds(2 * rows, rows)],
    ]
    column_loads = [feature_copy(block, column_places[block]) for block in range(BLOCKS)]
    for copy in column_loads[:3]:
        copy.start()
    def tap_grad(tap):
        down, across = tap // 3, tap % 3
        left = padded_one[pl.ds(down, SIDE), pl.ds(pl.multiple_of(across * views, 16), chunk), :]
        right = jnp.concatenate([left.reshape(rows, C_MID), jnp.zeros((tall - rows, C_MID), bf16)], axis=0)
        grad = dot(turned(slope_two), right).astype(bf16).T
        stage_ref[pl.ds(pl.multiple_of(tap * C_MID, 16), C_MID), :] = grad

    @pl.loop(0, 7)
    def _(tap):
        tap_grad(tap)
        hook_in(15, tap, 7)

    def second_back(first, count):
        at = image_rows(first, count)
        upstream = dot(patch(padded_two, first, count, True), weights[1][...].reshape(9 * C_MID, C_MID))
        upstream = upstream * slope_one[at, :].astype(f32)
        slope_one[at, :] = upstream.astype(bf16)
        count_in(slice(0, C_MID), upstream, hidden_one[at, :].astype(f32))

    @pl.loop(0, 3)
    def _(index):
        second_back(2 * index, 2)
        hook_in(16, index, 3)

    second_back(6, 1)
    hook(16, 3)
    sums = row_sums[0:1, :C_MID], row_sums[1:2, :C_MID]
    sum_one_back = Sum(8)
    sum_one_back.start(sums[0], xhat_sum(0, *sums))

    @pl.loop(7, 9)
    def _(tap):
        tap_grad(tap)

        @pl.when(tap == 7)
        def _():
            sum_one_back.middle()

        hook_in(17, tap, 2, 7)

    grad_coefs(0, sum_one_back.finish(), row_total)

    def put_one(pixel, cols, value):
        put_rows(pixel, cols, value)
        slope_one[pl.ds(pl.multiple_of(pixel * views, 16), views), cols] = value

    apply_grad(hidden_one, slope_one, put_one, 18)
    turn_rows(slope_one)

    def block_grad(block):
        if block != 1:
            column_loads[block].wait()
        start = 3 * rows if block == 1 else 2 * rows
        right = hidden_two[...] if block == 2 else hidden_three[start : start + tall, :]
        grad = dot(turned(slope_one), right).astype(bf16).T
        mem.g1[block] = grad.reshape(plan.x, -1, C_MID)

    column_loads[1].wait()
    tail = Ring(hidden_two, 0)
    for block in range(BLOCKS):
        block_grad(block)
        if block == 0:
            column_loads[3].start()
        hook(19, block)
        if block == 2:
            tail.first_loads(slope_hbm)

    sum_last = Sum(9)

    @pl.loop(0, pieces)
    def _(index):
        block = index // CHUNKS
        back = dot(act_two[span(lax.rem(index, CHUNKS)), :], weights[0][block].reshape(C_MID, C_MID))
        tail.copy(slope_hbm, index, True).wait()
        cols = pl.ds(pl.multiple_of(block * C_MID, LANES), C_MID)
        for pixel in range(SIDE):
            at = tail.rows(index, pixel, views)
            summed = hidden_two[at, :].astype(f32) * pool_slope[:, cols]
            hidden_two[at, :] = (summed + back[pixel * views : (pixel + 1) * views]).astype(bf16)
        tail.save(outs.features_grad, index)
        tail.next_load(slope_hbm, index)
        hook_in(20, index, pieces)
        if plan.inside:

            @pl.when(index == LAST_SUM)
            def _():
                sum_last.start(mem.squares[...], mem.squares[...])

            @pl.when(index == LAST_SUM + 3)
            def _():
                sum_last.middle()

    tail.last_saves(outs.features_grad)
    squares = mem.squares[...]
    if plan.inside:
        squares = sum_last.finish()[0:1]
    norm_grads = mem.norm_grads[...]
    scalars = outs.scalars
    norm_squares = column_sums(norm_grads * norm_grads)
    for place in range(norm_squares.shape[1] // LANES):
        squares = squares + norm_squares[:, place * LANES : (place + 1) * LANES]
    scalars[...] = jnp.zeros_like(scalars)
    squares = jnp.sum(squares, axis=1, keepdims=True)
    norm = jnp.sqrt(squares)
    found = (jnp.sum(objective_row, axis=1, keepdims=True) / image_total, squares, norm, clip_factor(norm))
    for place, value in enumerate(found):
        scalars[place : place + 1, :] = jnp.broadcast_to(value, (1, LANES))
    if plan.inside:
        owner = (dp_me * plan.fsdp + fsdp_me) * LANES
        outs.norm_grad[...] = mem.norm_grads[:, pl.ds(pl.multiple_of(owner, LANES), LANES)]
    else:
        outs.norm_grad[...] = norm_grads
    if not plan.inside:
        stores = [
            pltpu.make_async_copy(gradients[which], outs.grads[which], mem.bulk_send.at[which])
            for which in range(5)
        ]
        for store in stores:
            store.start()
        for store in stores:
            store.wait()


def weight_shapes():
    return (
        (4, 2, 256, C_MID),
        (4, 2, 576, C_MID),
        (BLOCKS, 4, 2, 64, C_MID),
        (4, 2, 256, P_HID),
        (4, 2, P_OUT, P_OUT),
    )


def run_kernel(plan, features, order, shards, norm):
    rows, views = plan.rows, plan.views
    in_vmem = pl.BlockSpec(memory_space=pltpu.VMEM)
    anywhere = pl.BlockSpec(memory_space=pl.ANY)
    shapes = weight_shapes()
    operands = [features, order, norm, *shards]
    in_specs = [anywhere, in_vmem, in_vmem] + [in_vmem if plan.inside else anywhere] * 5
    results = [
        ((rows, C_IN), bf16, anywhere),
        ((rows, C_IN), bf16, anywhere),
        (norm.shape, f32, in_vmem),
        ((8, LANES), f32, in_vmem),
    ]
    for which, shard in enumerate(shards):
        if plan.inside:
            results.append((shard.shape, f32, in_vmem))
        else:
            results.append(((9 * C_MID, C_MID) if which == 1 else shapes[which], bf16, anywhere))
    dma = pltpu.SemaphoreType.DMA

    def sum_room(width):
        return SumRoom(
            pltpu.VMEM((plan.dp, 2, width), f32),
            pltpu.VMEM((plan.fsdp, 2, width), f32),
            dma((plan.dp,)),
            dma((plan.dp,)),
            dma((plan.fsdp,)),
            dma((plan.fsdp,)),
        )

    def matrix_room():
        size = plan.embed_rows
        return MatrixRoom(
            pltpu.VMEM((plan.dp, size, P_OUT), f32),
            pltpu.VMEM((plan.dp, size, P_OUT), f32),
            pltpu.VMEM((plan.fsdp, size, P_OUT), f32),
            pltpu.VMEM((plan.dp, size, P_OUT), f32),
            dma((plan.dp,)),
            dma((plan.dp,)),
            dma((plan.fsdp,)),
            dma((plan.fsdp,)),
            dma((plan.dp,)),
            dma((plan.dp,)),
        )

    scratch = Mem(
        w=[pltpu.VMEM(shape, bf16) for shape in shapes],
        g1=pltpu.VMEM(shapes[0], bf16),
        row_sums=pltpu.VMEM((2, C_IN), f32),
        r3=pltpu.VMEM(shapes[2], bf16),
        r1=pltpu.VMEM(shapes[0], bf16),
        left_rooms=pltpu.VMEM((plan.dp, plan.fsdp, views, C_IN // plan.fsdp) if plan.inside else (8, LANES), bf16),
        right_rooms=pltpu.VMEM((plan.fsdp, plan.dp, views, P_HID // plan.dp) if plan.inside else (8, LANES), bf16),
        factor_sems=dma((8, max(plan.dp, plan.fsdp))),
        four_low=pltpu.VMEM((views, P_HID), bf16),
        r5=pltpu.VMEM(shapes[4], bf16),
        stage=pltpu.VMEM((max(SLOTS * plan.chunk, 9 * C_MID), C_MID), bf16),
        stage_sem=dma((2, SLOTS)),
        column_sem=dma((BLOCKS,)),
        h1=pltpu.VMEM((rows, C_MID), bf16),
        d1=pltpu.VMEM((plan.tall, C_MID), bf16),
        h2=pltpu.VMEM((plan.tall, C_MID), bf16),
        d2=pltpu.VMEM((plan.tall, C_MID), bf16),
        a2=pltpu.VMEM((plan.tall, C_MID), bf16),
        h3=pltpu.VMEM((3 * rows + plan.tall, C_MID), bf16),
        pad1=pltpu.VMEM((SIDE + 2, (SIDE + 2) * views, C_MID), bf16),
        pad2=pltpu.VMEM((SIDE + 2, (SIDE + 2) * views, C_MID), bf16),
        pool=pltpu.VMEM((views, C_IN), f32),
        pool_slope=pltpu.VMEM((views, C_IN), f32),
        pool_bend=pltpu.VMEM((views, C_IN), f32),
        pooled=pltpu.VMEM((views, C_IN), bf16),
        proj_act=pltpu.VMEM((views, P_HID), bf16),
        proj_slope=pltpu.VMEM((views, P_HID), f32),
        proj_hidden=pltpu.VMEM((views, P_HID), f32),
        coef=pltpu.VMEM((8, C_IN), f32),
        stats=pltpu.VMEM((2, norm_width()), f32),
        norm=pltpu.VMEM((2, norm_width()), f32),
        norm_grads=pltpu.VMEM((2, norm_width()), f32),
        norm_tiles=pltpu.VMEM((plan.dp, plan.fsdp, 2, LANES), f32),
        norm_s0=dma((plan.dp,)),
        norm_r0=dma((plan.dp,)),
        norm_s1=dma((plan.fsdp,)),
        norm_r1=dma((plan.fsdp,)),
        bulk_send=dma((COPIES,)),
        bulk_recv=dma((COPIES,)),
        mats=[matrix_room(), matrix_room()],
        sums=[
            sum_room(width)
            for width in (C_MID, C_MID, C_IN // 2, C_IN // 2, P_HID, C_IN, LANES)
        ],
        squares=pltpu.VMEM((1, LANES), f32),
    )
    values = pl.pallas_call(
        lambda *refs: kernel(plan, *refs),
        out_shape=[jax.ShapeDtypeStruct(shape, kind) for shape, kind, _ in results],
        in_specs=in_specs,
        out_specs=[spec for _, _, spec in results],
        scratch_shapes=[scratch],
        compiler_params=pltpu.CompilerParams(
            collective_id=1, has_side_effects=True, vmem_limit_bytes=63 * 2**20
        ),
        name="train_step",
    )(*operands)
    return Outs(*values[:4], values[4:])


def norm_width():
    return 2 * C_MID + C_IN + P_HID


def clip_factor(norm):
    return clip_level / jnp.maximum(norm, clip_level)


def adam_update(weight, moment_one, moment_two, gradient, step_rate, weight_decay):
    first_new = beta_first * moment_one + (1.0 - beta_first) * gradient
    second_new = beta_second * moment_two + (1.0 - beta_second) * gradient * gradient
    first_hat = first_new / (1.0 - beta_first**STEP)
    second_hat = second_new / (1.0 - beta_second**STEP)
    weight_new = weight - step_rate * (
        first_hat / (jnp.sqrt(second_hat) + adam_epsilon) + weight_decay * weight
    )
    return (weight_new, first_new, second_new)


def finish_kernel(rates, decays, *refs):
    count = len(rates)
    low, scalars = refs[0], refs[1]
    refs = refs[2:]
    given, wide, loss, norm, updated = refs[: 4 * count], *refs[4 * count : 4 * count + 3], refs[4 * count + 3 : -2]
    rooms, sems = refs[-2], refs[-1]
    wide[...] = low[...].astype(f32)
    step = pl.program_id(0)

    def load(place):
        return pltpu.make_async_copy(given[place], rooms[place], sems.at[place])

    def store(place):
        return pltpu.make_async_copy(rooms[place], updated[place], sems.at[place])

    @pl.when(step == 0)
    def _():
        loss[0, 0] = scalars[0, 0]
        norm[0, 0] = scalars[2, 0]
        for place in range(4 * count):
            load(place).start()

    @pl.when(step == 2)
    def _():
        for place in range(4 * count):
            load(place).wait()
        for place in range(count):
            weight, first, second, grad = (rooms[part * count + place][...] for part in range(4))
            found = adam_update(weight, first, second, grad * scalars[3, 0], rates[place], decays[place])
            for part in range(3):
                rooms[part * count + place][...] = found[part]
        for place in range(3 * count):
            store(place).start()

    @pl.when(step == CHUNKS - 1)
    def _():
        for place in range(3 * count):
            store(place).wait()


def finish(features_grad, scalars, masters, firsts, seconds, grads, rates, decays):
    rows = features_grad.shape[0]
    arrays = [*masters, *firsts, *seconds, *grads]
    moving = pl.BlockSpec((rows // CHUNKS, C_IN), lambda index: (index, 0))
    single = pl.BlockSpec(memory_space=pltpu.SMEM)
    anywhere = pl.BlockSpec(memory_space=pl.ANY)
    count = len(masters)
    values = pl.pallas_call(
        lambda *refs: finish_kernel(rates, decays, *refs),
        grid=(CHUNKS,),
        in_specs=[moving, single] + [anywhere] * (4 * count),
        out_specs=[moving, single, single] + [anywhere] * (3 * count),
        out_shape=[jax.ShapeDtypeStruct((rows, C_IN), f32)]
        + [jax.ShapeDtypeStruct((1, 1), f32)] * 2
        + [jax.ShapeDtypeStruct(array.shape, f32) for array in arrays[: 3 * count]],
        scratch_shapes=[
            [pltpu.VMEM(array.shape, f32) for array in arrays],
            pltpu.SemaphoreType.DMA((4 * count,)),
        ],
        compiler_params=pltpu.CompilerParams(vmem_limit_bytes=62 * 2**20),
        name="finish",
    )(features_grad, scalars, *arrays)
    groups = [values[3 + part * count : 3 + (part + 1) * count] for part in range(3)]
    return values[0], values[1].reshape(()), values[2].reshape(()), *groups


def gather_full(weight):
    outer = lax.all_gather(weight.astype(bf16), FSDP, axis=0, tiled=True)
    return lax.all_gather(outer, DP, axis=1, tiled=True)


def scatter_full(gradient):
    inner = lax.psum_scatter(gradient.astype(f32), DP, scatter_dimension=1, tiled=True)
    return lax.psum_scatter(inner, FSDP, scatter_dimension=0, tiled=True)


def body(features, view_order, *state):
    masters, firsts, seconds = state[:6], state[6:12], state[12:18]
    dp_size, fsdp_size = lax.axis_size(DP), lax.axis_size(FSDP)
    views = features.shape[0]
    inside = dp_size == 4 and fsdp_size == 8
    plan = Plan(dp_size, fsdp_size, views, inside)
    pixels = jnp.swapaxes(features, 0, 1).reshape(-1, C_IN)
    norm_params = masters[5]
    shapes = weight_shapes()
    if inside:
        shards = list(masters[:4]) + [masters[4].T]
        norm = norm_params
    else:
        full = [gather_full(weight) for weight in masters[:5]]
        shards = [
            full[0].reshape(shapes[0]),
            full[1].reshape(shapes[1]),
            full[2].reshape(C_MID, BLOCKS, C_MID).swapaxes(0, 1).reshape(shapes[2]),
            full[3].reshape(shapes[3]),
            full[4].reshape(4, 2, P_OUT, P_OUT).swapaxes(2, 3),
        ]
        norm = lax.all_gather(norm_params.astype(bf16), (DP, FSDP), axis=1, tiled=True).astype(f32)
    got = run_kernel(plan, pixels, view_order, shards, norm)
    grads = list(got.grads)
    scalars = got.scalars
    turned = [list(group) for group in (masters, firsts, seconds)]
    if inside:
        owned = grads
        for group in turned:
            group[4] = group[4].T
    else:
        whole_grads = [
            grads[0].reshape(C_IN, C_MID),
            grads[1],
            grads[2].reshape(BLOCKS, C_MID, C_MID).swapaxes(0, 1).reshape(C_MID, C_IN),
            grads[3].reshape(C_IN, P_HID),
            grads[4].swapaxes(2, 3).reshape(P_HID, P_OUT),
        ]
        owned = [scatter_full(gradient) for gradient in whole_grads]
        squares = scalars[1, 0] + lax.psum(sum(jnp.sum(grad * grad) for grad in owned), (DP, FSDP))
        norm_value = jnp.sqrt(squares)
        scalars = scalars.at[2].set(norm_value).at[3].set(clip_factor(norm_value))
    width = norm_params.shape[1]
    if inside:
        owned.append(got.norm_grad)
    else:
        owner = lax.axis_index((DP, FSDP))
        owned.append(lax.dynamic_slice_in_dim(got.norm_grad, owner * width, width, 1))
    step_rates = (
        C_IN ** (-0.5),
        (9 * C_MID) ** (-0.5),
        C_MID ** (-0.5),
        C_IN ** (-0.5),
        P_HID ** (-0.5),
        norm_rate,
    )
    decays = (decay_rate, decay_rate, decay_rate, decay_rate, decay_rate, 0.0)
    input_grad, loss, grad_norm, *updates = finish(
        got.features_grad, scalars, *turned, owned, step_rates, decays
    )
    if inside:
        updates = [[*group[:4], group[4].T, group[5]] for group in updates]
    return (
        loss,
        jnp.swapaxes(input_grad.reshape(PIX, views, C_IN), 0, 1),
        grad_norm,
        *updates[0],
        *updates[1],
        *updates[2],
    )


def solution(mesh):
    views = P((DP, FSDP), None, None)
    split = P(FSDP, DP)
    norm = P(None, (DP, FSDP))
    params = (split,) * 5 + (norm,)
    return jax.shard_map(
        body,
        mesh=mesh,
        in_specs=(views, P((DP, FSDP), None)) + params * 3,
        out_specs=(P(), views, P()) + params * 3,
        check_vma=False,
    )
```

```python
from typing import Any, NamedTuple

import jax
import jax.numpy as jnp
from jax import lax
from jax.experimental import pallas as pl
from jax.experimental.pallas import tpu as pltpu
from jax.sharding import PartitionSpec as P

C_IN = 2048
C_MID = 512
P_HID = 1024
P_OUT = 128
SIDE = 7
STEP = 10
PIX = 49
LANES = 128
BLOCKS = C_IN // C_MID
CHUNKS = SIDE
SLOTS = 6
LAST_SUM = 23
COPIES = 360


highest = lax.Precision.HIGHEST
bf16 = jnp.bfloat16
f32 = jnp.float32
norm_epsilon = 1e-05
ridge_term = 0.01
clip_level = 0.1
beta_first = 0.9
beta_second = 0.999
adam_epsilon = 1e-08
decay_rate = 0.05
norm_rate = 0.5
bell_scale = 0.3989422804014327
root_half = 0.5**0.5
bell_rate = -0.7213475204444817
DP, FSDP = "dp", "fsdp"


def gelu_pair(values):
    below = 0.5 + 0.5 * lax.erf(values * root_half)
    bell = jnp.exp2(values * values * bell_rate)
    return values * below, below + values * bell * bell_scale


def dot(left, right):
    return jnp.dot(left, right, preferred_element_type=f32)


def dot_cols(left, right):
    return lax.dot_general(left, right, (((1,), (1,)), ((), ())), preferred_element_type=f32)


def dot_rows(left, right):
    return lax.dot_general(left, right, (((0,), (0,)), ((), ())), preferred_element_type=f32)


def exact_cols(left, right):
    return lax.dot_general(
        left, right, (((1,), (1,)), ((), ())), precision=highest, preferred_element_type=f32
    )


def exact_rows(left, right):
    return lax.dot_general(
        left, right, (((0,), (0,)), ((), ())), precision=highest, preferred_element_type=f32
    )


def exact_dot(left, right):
    return jnp.dot(left, right, precision=highest, preferred_element_type=f32)


def inverse_factors(matrices):
    row_top = lax.broadcasted_iota(jnp.int32, (8, P_OUT), 0)
    row_all = lax.broadcasted_iota(jnp.int32, (P_OUT, P_OUT), 0)
    col_all = lax.broadcasted_iota(jnp.int32, (P_OUT, P_OUT), 1)

    def one_step(place, left, right):
        scale = lax.rsqrt(left[place : place + 1, place : place + 1])
        left_row = left[place : place + 1, :] * scale
        right_row = right[place : place + 1, :] * scale
        column = left[:, place : place + 1] * scale
        left = left - column * left_row
        right = right - column * right_row
        here = row_top == place
        left = jnp.concatenate([jnp.where(here, 0.0, left[:8]), left[8:]], axis=0)
        right = jnp.concatenate(
            [jnp.where(here, jnp.broadcast_to(right_row, (8, P_OUT)), right[:8]), right[8:]], axis=0
        )
        return left, right

    def panel(_, pairs):
        pairs = list(pairs)
        for place in range(8):
            for which in range(len(pairs)):
                pairs[which] = one_step(place, *pairs[which])
        return tuple(
            (
                pltpu.roll(jnp.concatenate([left[8:], left[:8]], axis=0), P_OUT - 8, 1),
                jnp.concatenate([right[8:], right[:8]], axis=0),
            )
            for left, right in pairs
        )

    pairs = tuple((matrix, (row_all == col_all).astype(f32)) for matrix in matrices)
    return [right for _, right in lax.fori_loop(0, P_OUT // 8, panel, pairs)]


def pack_pair(first, second):
    row = lax.broadcasted_iota(jnp.int32, (P_OUT, P_OUT), 0)
    col = lax.broadcasted_iota(jnp.int32, (P_OUT, P_OUT), 1)
    packed = jnp.where(row >= col, first, second.T)
    diagonal = jnp.sum(jnp.where(row == col, second, 0.0), axis=0, keepdims=True)
    return packed, diagonal


def unpack_pair(packed, diagonal):
    row = lax.broadcasted_iota(jnp.int32, (P_OUT, P_OUT), 0)
    col = lax.broadcasted_iota(jnp.int32, (P_OUT, P_OUT), 1)
    turned = packed.T
    first = jnp.where(row >= col, packed, turned)
    second = jnp.where(row < col, packed, jnp.where(row == col, diagonal, turned))
    return first, second


GATHER_AT = {
    (0, 1): 1,
    (0, 3): 1,
    (1, 0): 1,
    (2, 0): 1,
    (4, 0): 5,
    (5, 0): 1,
    (5, 1): 1,
    (5, 2): 1,
    (5, 4): 1,
    (5, 5): 1,
    (5, 6): 1,
    (7, 0): 1,
    (8, 6): 1,
    (9, 2): 1,
    (9, 5): 1,
    (9, 8): 1,
    (21, 0): 7,
}
REDUCE_AT = {
    (11, 6): ((4, 0, 1),),
    (11, 20): ((4, 0, 2),),
    (12, 1): ((4, 0, 3),),
    (13, 3): ((2, 0, 0), (2, 1, 0), (2, 2, 0), (2, 3, 0)),
    (14, 3): ((4, 9, 4), (2, 0, 1)),
    (14, 6): ((2, 1, 1),),
    (15, 0): ((2, 2, 1), (2, 0, 2)),
    (15, 1): ((2, 3, 1),),
    (15, 2): ((1, 0, 0), (2, 1, 2)),
    (15, 3): ((2, 2, 2), (2, 0, 3)),
    (15, 4): ((1, 1, 0), (1, 0, 1), (2, 3, 2)),
    (15, 5): ((2, 1, 3), (2, 2, 3)),
    (15, 6): ((1, 2, 0), (1, 1, 1), (2, 3, 3)),
    (16, 0): ((1, 0, 2), (1, 2, 1), (2, 9, 4)),
    (16, 1): ((1, 1, 2), (1, 0, 3)),
    (16, 2): ((1, 2, 2), (1, 1, 3)),
    (17, 1): ((1, 3, 0),),
    (18, 2): ((1, 2, 3),),
    (18, 6): ((1, 3, 1),),
    (19, 0): ((0, 0, 0), (1, 3, 2)),
    (19, 1): ((0, 1, 0), (0, 0, 1), (1, 3, 3)),
    (19, 2): ((0, 2, 0), (0, 1, 1), (0, 0, 2)),
    (19, 3): ((0, 3, 0), (0, 2, 1), (0, 1, 2), (0, 0, 3)),
    (20, 2): ((0, 3, 1), (0, 2, 2), (0, 1, 3)),
    (20, 7): ((0, 3, 2), (0, 2, 3)),
    (20, 12): ((0, 3, 3), (1, 9, 4)),
    (20, 19): ((0, 9, 4),),
    (23, 0): ((4, 0, 0),),
}


class Ins(NamedTuple):
    features: Any
    order: Any
    norm: Any
    shards: Any


class Outs(NamedTuple):
    slope: Any
    features_grad: Any
    norm_grad: Any
    scalars: Any
    grads: Any


class SumRoom(NamedTuple):
    dp: Any
    fsdp: Any
    s0: Any
    r0: Any
    s1: Any
    r1: Any


class MatrixRoom(NamedTuple):
    pack: Any
    dp: Any
    fsdp: Any
    all: Any
    s0: Any
    r0: Any
    s1: Any
    r1: Any
    s2: Any
    r2: Any


class Mem(NamedTuple):
    w: Any
    g1: Any
    row_sums: Any
    r3: Any
    r1: Any
    left_rooms: Any
    right_rooms: Any
    factor_sems: Any
    four_low: Any
    r5: Any
    stage: Any
    stage_sem: Any
    column_sem: Any
    h1: Any
    d1: Any
    h2: Any
    d2: Any
    a2: Any
    h3: Any
    pad1: Any
    pad2: Any
    pool: Any
    pool_slope: Any
    pool_bend: Any
    pooled: Any
    proj_act: Any
    proj_slope: Any
    proj_hidden: Any
    coef: Any
    stats: Any
    norm: Any
    norm_grads: Any
    norm_tiles: Any
    norm_s0: Any
    norm_r0: Any
    norm_s1: Any
    norm_r1: Any
    bulk_send: Any
    bulk_recv: Any
    mats: Any
    sums: Any
    squares: Any


class Plan:
    def __init__(self, dp_size, fsdp_size, views, inside):
        self.dp = dp_size
        self.fsdp = fsdp_size
        self.devices = dp_size * fsdp_size
        self.views = views
        self.rows = views * PIX
        self.tall = -(-self.rows // C_MID) * C_MID
        self.chunk = views * SIDE
        self.inside = inside
        self.z = 4
        self.x = 2
        self.half = (128, 288, 32, 128, 16)
        self.width = (128, 128, 512, 256, 128)
        piece = P_OUT + 8
        self.embed_rows = -(-piece // (8 * dp_size)) * 8


def kernel(plan, *refs):
    ins, outs, mem = Ins(*refs[:3], refs[3:8]), Outs(*refs[8:12], refs[12:17]), refs[17]
    views, chunk, rows, tall = plan.views, plan.chunk, plan.rows, plan.tall
    row_total = float(rows * plan.devices)
    view_total = float(views * plan.devices)
    image_total = float(views * plan.devices // 2)
    dp_me, fsdp_me = lax.axis_index(DP), lax.axis_index(FSDP)
    y_me, c_me = dp_me // 2, dp_me % 2
    z_me, x_me = fsdp_me // 2, fsdp_me % 2
    y_other, c_other, x_other = 1 - y_me, 1 - c_me, 1 - x_me

    barrier = pltpu.get_barrier_semaphore()

    @pl.loop(1, plan.dp)
    def _(step):
        pl.semaphore_signal(
            barrier, 1, device_id={DP: lax.rem(dp_me + step, plan.dp)}, device_id_type=pl.DeviceIdType.MESH
        )

    @pl.loop(1, plan.fsdp)
    def _(step):
        pl.semaphore_signal(
            barrier, 1, device_id={FSDP: lax.rem(fsdp_me + step, plan.fsdp)}, device_id_type=pl.DeviceIdType.MESH
        )

    pl.semaphore_wait(barrier, plan.dp + plan.fsdp - 2)

    def share(axis, size, me, source_of, slots, send, recv):
        def outgoing(step):
            partner = lax.rem(me + step, size)
            return pltpu.make_async_remote_copy(
                src_ref=source_of(partner),
                dst_ref=slots.at[me],
                send_sem=send.at[step],
                recv_sem=recv.at[me],
                device_id={axis: partner},
                device_id_type=pl.DeviceIdType.MESH,
            )

        def incoming(step):
            source = lax.rem(me + step, size)
            return pltpu.make_async_remote_copy(
                src_ref=slots.at[source],
                dst_ref=slots.at[source],
                send_sem=send.at[step],
                recv_sem=recv.at[source],
                device_id={axis: source},
                device_id_type=pl.DeviceIdType.MESH,
            )

        def start():
            pl.loop(1, size)(lambda step: outgoing(step).start())

        def wait():
            pl.loop(1, size)(lambda step: incoming(step).wait_recv())
            pl.loop(1, size)(lambda step: outgoing(step).wait_send())

        return start, wait

    def add_slots(slots, size):
        total = slots[0]
        for place in range(1, size):
            total = total + slots[place]
        return total

    class Sum:
        def __init__(self, which):
            part = mem.sums[(0, 1, 2, 3, 4, 4, 5, 0, 1, 6)[which]]
            self.dp_slots, self.fsdp_slots = part.dp, part.fsdp
            self.dp_copy = share(
                DP, plan.dp, dp_me, lambda _: self.dp_slots.at[dp_me], self.dp_slots, part.s0, part.r0
            )
            self.fsdp_copy = share(
                FSDP, plan.fsdp, fsdp_me, lambda _: self.fsdp_slots.at[fsdp_me], self.fsdp_slots, part.s1, part.r1
            )

        def start(self, *values):
            for place, value in enumerate(values):
                self.dp_slots[dp_me, place : place + 1, :] = value
            self.dp_copy[0]()

        def middle(self):
            self.dp_copy[1]()
            self.fsdp_slots[fsdp_me] = add_slots(self.dp_slots, plan.dp)
            self.fsdp_copy[0]()

        def finish(self):
            self.fsdp_copy[1]()
            return add_slots(self.fsdp_slots, plan.fsdp)

        def all(self, *values):
            self.start(*values)
            self.middle()
            return self.finish()

    def sum_matrix(which, matrix, extra):
        part = mem.mats[which]
        size = plan.embed_rows
        pack = part.pack
        flat = jnp.concatenate(
            [matrix] + extra + [jnp.zeros((size * plan.dp - P_OUT - len(extra), P_OUT), f32)], axis=0
        )
        for place in range(plan.dp):
            pack[place] = flat[place * size : (place + 1) * size]
        start, wait = share(DP, plan.dp, dp_me, lambda to: pack.at[to], part.dp, part.s0, part.r0)
        start()
        part.dp[dp_me] = pack[dp_me]
        wait()
        part.fsdp[fsdp_me] = add_slots(part.dp, plan.dp)
        start, wait = share(
            FSDP, plan.fsdp, fsdp_me, lambda _: part.fsdp.at[fsdp_me], part.fsdp, part.s1, part.r1
        )
        start()
        wait()
        part.all[dp_me] = add_slots(part.fsdp, plan.fsdp)
        start, wait = share(
            DP, plan.dp, dp_me, lambda _: part.all.at[dp_me], part.all, part.s2, part.r2
        )
        start()
        wait()
        total = jnp.concatenate([part.all[place] for place in range(plan.dp)], axis=0)
        return total[:P_OUT], [total[P_OUT + place : P_OUT + place + 1] for place in range(len(extra))]

    weights = mem.w
    everything = slice(None)

    def row_span(which, half):
        if isinstance(half, tuple):
            return half
        size = plan.half[which]
        if half is None:
            return 0, 2 * size
        return half * size, size

    def column_span(which, dp_index):
        width = plan.width[which]
        return pl.ds(pl.multiple_of(dp_index * width, width), width)

    def places(which, z_index, x_index, dp_index, half, flat=True):
        start, size = row_span(which, half)
        if which == 1 and flat:
            z_list = range(plan.z) if z_index is None else [z_index]
            x_list = range(plan.x) if x_index is None else [x_index]
            return [
                (
                    pl.ds(pl.multiple_of((z_one * plan.x + x_one) * 576 + start, 16), size),
                    column_span(which, dp_index),
                )
                for z_one in z_list
                for x_one in x_list
            ]
        z_one = everything if z_index is None else z_index
        x_one = everything if x_index is None else x_index
        if which == 2:
            return [(dp_index, z_one, x_one, pl.ds(start, size), everything)]
        if which == 4:
            return [(z_one, x_one, pl.ds(pl.multiple_of(dp_index * 32 + start, 16), size), everything)]
        return [(z_one, x_one, pl.ds(start, size), column_span(which, dp_index))]

    recv_parts = {
        1: lambda index: mem.h3.at[index],
        0: lambda index: mem.r1.at[index],
        2: lambda index: mem.r3.at[index],
        4: lambda index: mem.r5.at[index],
    }

    counter = [0]

    class Batch:
        def __init__(self, sources, targets, landings, axis, partner):
            base = counter[0]
            counter[0] += len(sources)
            send, recv = mem.bulk_send, mem.bulk_recv
            self.out = [
                pltpu.make_async_remote_copy(
                    src_ref=source,
                    dst_ref=target,
                    send_sem=send.at[base + place],
                    recv_sem=recv.at[base + place],
                    device_id={axis: partner},
                    device_id_type=pl.DeviceIdType.MESH,
                )
                for place, (source, target) in enumerate(zip(sources, targets))
            ]
            self.come = [
                pltpu.make_async_remote_copy(
                    src_ref=landing,
                    dst_ref=landing,
                    send_sem=send.at[base + place],
                    recv_sem=recv.at[base + place],
                    device_id={axis: partner},
                    device_id_type=pl.DeviceIdType.MESH,
                )
                for place, landing in enumerate(landings)
            ]

        def start(self):
            for copy in self.out:
                copy.start()

        def arrive(self):
            for copy in self.come:
                copy.wait_recv()

        def leave(self):
            for copy in self.out:
                copy.wait_send()

    class LineBatch:
        def __init__(self, source_of, target_of, landing_of):
            base = counter[0]
            counter[0] += plan.z
            send, recv = mem.bulk_send, mem.bulk_recv
            self.out, self.come = [], []
            for step in range(1, plan.z):
                z_to = (z_me + step) % plan.z
                self.out.append(
                    pltpu.make_async_remote_copy(
                        src_ref=source_of(z_to),
                        dst_ref=target_of(z_to),
                        send_sem=send.at[base + step],
                        recv_sem=recv.at[base + z_me],
                        device_id={FSDP: z_to * plan.x + x_me},
                        device_id_type=pl.DeviceIdType.MESH,
                    )
                )
                self.come.append(
                    pltpu.make_async_remote_copy(
                        src_ref=landing_of(z_to),
                        dst_ref=landing_of(z_to),
                        send_sem=send.at[base + step],
                        recv_sem=recv.at[base + z_to],
                        device_id={FSDP: z_to * plan.x + x_me},
                        device_id_type=pl.DeviceIdType.MESH,
                    )
                )

        start, arrive, leave = Batch.start, Batch.arrive, Batch.leave

    def pick(ref, indexes):
        return [ref.at[index] for index in indexes]

    def own_dp(y_index, c_index):
        return y_index * 2 + c_index

    x_partner = z_me * plan.x + x_other
    y_partner = own_dp(y_other, c_me)
    c_partner = own_dp(y_me, c_other)
    dp_far = own_dp(y_other, c_other)

    class Gather:
        def __init__(self, which, start, size):
            ref = weights[which]
            self.which, self.rows = which, (start, size)
            both, low, high = (start, size), (start, size // 2), (start + size // 2, size // 2)

            def at(*index):
                return pick(ref, places(which, *index, False))

            own = at(z_me, x_me, dp_me, both)[0]
            self.line = LineBatch(
                lambda _: own, lambda _: own, lambda z_from: at(z_from, x_me, dp_me, both)[0]
            )
            sent, come = at(None, x_me, dp_me, low), at(None, x_other, dp_me, low)
            x_first = Batch(sent, sent, come, FSDP, x_partner)
            sent, come = at(None, x_me, dp_me, high), at(None, x_me, y_partner, high)
            y_first = Batch(sent, sent, come, DP, y_partner)
            sent, come = at(None, None, dp_me, low), at(None, None, y_partner, low)
            y_second = Batch(sent, sent, come, DP, y_partner)
            sent = at(None, x_me, dp_me, high) + at(None, x_me, y_partner, high)
            come = at(None, x_other, dp_me, high) + at(None, x_other, y_partner, high)
            x_second = Batch(sent, sent, come, FSDP, x_partner)
            sent = at(None, None, dp_me, both) + at(None, None, y_partner, both)
            come = at(None, None, c_partner, both) + at(None, None, dp_far, both)
            core = Batch(sent, sent, come, DP, c_partner)
            self.stages = ((self.line,), (x_first, y_first), (y_second, x_second), (core,))

        def put_own(self):
            index = places(self.which, z_me, x_me, dp_me, self.rows, False)[0]
            shard = ins.shards[self.which][self.rows[0] : self.rows[0] + self.rows[1], :]
            weights[self.which][index] = shard.astype(bf16)

        def start(self, stage):
            for batch in self.stages[stage]:
                batch.start()

        def arrive(self, stage):
            for batch in self.stages[stage]:
                batch.arrive()

        def leave(self):
            for stage in self.stages:
                for batch in stage:
                    batch.leave()

    class Piece:
        def __init__(self, which, ref, room, z_index):
            def at(*index):
                return pick(ref, places(which, z_index, *index))

            def land(*index):
                return [room(index_one) for index_one in places(which, z_index, *index)]

            self.z = z_index
            self.core = Batch(
                at(None, c_partner, None) + at(None, dp_far, None),
                land(None, c_partner, None) + land(None, dp_far, None),
                land(None, dp_me, None) + land(None, y_partner, None),
                DP,
                c_partner,
            )
            self.y_first = Batch(
                at(None, y_partner, 0), land(None, dp_far, 0), land(None, c_partner, 0), DP, y_partner
            )
            self.x_first = Batch(
                at(x_other, dp_me, 1) + at(x_other, y_partner, 1),
                land(x_other, c_partner, 1) + land(x_other, dp_far, 1),
                land(x_me, c_partner, 1) + land(x_me, dp_far, 1),
                FSDP,
                x_partner,
            )
            self.x_second = Batch(
                at(x_other, dp_me, 0), land(x_other, dp_far, 0), land(x_me, dp_far, 0), FSDP, x_partner
            )
            self.y_second = Batch(
                at(x_me, y_partner, 1), land(x_other, dp_far, 1), land(x_other, c_partner, 1), DP, y_partner
            )

    def put_gradient(which, total):
        outs.grads[which][...] = total
        squares = jnp.sum(total * total, axis=0, keepdims=True)
        folded = squares[:, :LANES]
        for place in range(1, squares.shape[1] // LANES):
            folded = folded + squares[:, place * LANES : (place + 1) * LANES]
        mem.squares[...] += folded

    class Reduce:
        def __init__(self, which, ref, cut):
            self.which, self.ref, self.room = which, ref, recv_parts[which]
            self.pieces = [
                Piece(which, ref, self.room, z_index) for z_index in (range(plan.z) if cut else [None])
            ]
            self.base = counter[0]
            counter[0] += plan.z

        def line_copy(self, z_to):
            return pltpu.make_async_remote_copy(
                src_ref=self.ref.at[places(self.which, z_to, x_me, dp_me, None)[0]],
                dst_ref=self.room(places(self.which, z_me, x_other, dp_far, None)[0]),
                send_sem=mem.bulk_send.at[self.base + z_to],
                recv_sem=mem.bulk_recv.at[self.base + z_me],
                device_id={FSDP: z_to * plan.x + x_me},
                device_id_type=pl.DeviceIdType.MESH,
            )

        def line_room(self, z_from):
            return self.room(places(self.which, z_from, x_other, dp_far, None)[0])

        def add(self, z_index, pairs):
            def one(z_one):
                for here, there in pairs:
                    for x_step in range(plan.x) if here[0] is None else [None]:
                        x_here = x_step if here[0] is None else here[0]
                        x_there = x_step if there[0] is None else there[0]
                        index = places(self.which, z_one, x_here, *here[1:])[0]
                        other = places(self.which, z_one, x_there, *there[1:])[0]
                        total = self.ref[index].astype(f32) + self.room(other)[...].astype(f32)
                        self.ref[index] = total.astype(bf16)

            if z_index is None:
                pl.loop(0, plan.z)(one)
            else:
                one(z_index)

        def core_start(self, place=0):
            if plan.inside:
                self.pieces[place].core.start()

        def core_add(self, place=0):
            if plan.inside:
                piece = self.pieces[place]
                piece.core.arrive()
                self.add(piece.z, [((None, dp_me, None),) * 2, ((None, y_partner, None),) * 2])
                piece.y_first.start()
                piece.x_first.start()

        def first_add(self, place=0):
            if plan.inside:
                piece = self.pieces[place]
                piece.y_first.arrive()
                self.add(piece.z, [((None, dp_me, 0), (None, c_partner, 0))])
                piece.x_second.start()
                piece.x_first.arrive()
                self.add(
                    piece.z, [((x_me, dp_me, 1), (x_me, c_partner, 1)), ((x_me, y_partner, 1), (x_me, dp_far, 1))]
                )
                piece.y_second.start()

        def second_add(self, place=0):
            if plan.inside:
                piece = self.pieces[place]
                piece.x_second.arrive()
                piece.y_second.arrive()
                self.add(
                    piece.z, [((x_me, dp_me, 0), (x_me, dp_far, 0)), ((x_me, dp_me, 1), (x_other, c_partner, 1))]
                )
                if piece.z is None:
                    for step in range(1, plan.z):
                        self.line_copy((z_me + step) % plan.z).start()
                else:

                    @pl.when(z_me != piece.z)
                    def _():
                        self.line_copy(piece.z).start()

        def finish(self):
            if not plan.inside:
                return
            total = self.ref[places(self.which, z_me, x_me, dp_me, None)[0]].astype(f32)
            for step in range(1, plan.z):
                z_from = (z_me + step) % plan.z
                room = self.line_room(z_from)
                pltpu.make_async_remote_copy(
                    src_ref=room,
                    dst_ref=room,
                    send_sem=mem.bulk_send.at[self.base + z_from],
                    recv_sem=mem.bulk_recv.at[self.base + z_from],
                    device_id={FSDP: z_from * plan.x + x_me},
                    device_id_type=pl.DeviceIdType.MESH,
                ).wait_recv()
                total = total + room[...].astype(f32)
            put_gradient(self.which, total)
            for step in range(1, plan.z):
                self.line_copy((z_me + step) % plan.z).wait_send()
            for piece in self.pieces:
                for batch in (piece.core, piece.y_first, piece.x_first, piece.x_second, piece.y_second):
                    batch.leave()

    gathers, steps = [], []
    if plan.inside:
        for which, cuts in enumerate((2, 3, 1, 2, 1)):
            size = 2 * plan.half[which] // cuts
            gathers += [Gather(which, cut * size, size) for cut in range(cuts)]

    def line_step(place):
        gathers[place].arrive(0)
        gathers[place].start(1)
        if place + 1 < len(gathers):
            gathers[place + 1].start(0)

    def first_step(place):
        gathers[place].arrive(1)
        gathers[place].start(2)

    def second_step(place):
        gathers[place].arrive(2)
        gathers[place].start(3)

    for place in range(len(gathers)):
        steps.append((line_step, place))
        if place > 0:
            steps.append((second_step, place - 1))
        steps.append((first_step, place))
    if plan.inside:
        steps.append((second_step, len(gathers) - 1))

    def take(count):
        taken, steps[:] = steps[:count], steps[count:]
        return [lambda one=one: one[0](one[1]) for one in taken]

    def moves(site, item):
        found = take(GATHER_AT.get((site, item), 0)) if plan.inside else []
        for which, piece, kind in REDUCE_AT.get((site, item), ()):
            one = reduces[which]
            found.append(
                one.finish
                if kind == 4
                else lambda one=one, kind=kind, piece=piece: (
                    one.core_start,
                    one.core_add,
                    one.first_add,
                    one.second_add,
                )[kind](piece)
            )
        return found

    def hook(site, item=0):
        for move in moves(site, item):
            move()

    def hook_in(site, index, count, first=0, stride=1):
        for item in range(count):
            found = moves(site, item)
            if found and plan.inside:

                @pl.when(index == first + item * stride)
                def _(found=found):
                    for move in found:
                        move()

    def cores_arrive(which):
        for one in gathers:
            if one.which == which:
                one.arrive(3)

    gradients = [mem.g1, mem.stage.at[pl.ds(0, 9 * C_MID)], weights[2], weights[3], weights[4]]
    reduces = [None if which == 3 else Reduce(which, gradients[which], which < 3) for which in range(5)]
    assert counter[0] <= COPIES
    mem.squares[...] = jnp.zeros((1, LANES), f32)

    if plan.inside:
        gathers[0].put_own()
        gathers[0].start(0)
        for one in gathers[1:]:
            one.put_own()
        tiles = mem.norm_tiles
        tiles[dp_me, fsdp_me] = ins.norm[...].astype(bf16).astype(f32)
        norm_dp = share(
            DP, plan.dp, dp_me, lambda _: tiles.at[dp_me, fsdp_me], tiles.at[:, fsdp_me], mem.norm_s0, mem.norm_r0
        )
        norm_dp[0]()
    else:
        loads = [
            pltpu.make_async_copy(ins.shards[which], weights[which], mem.bulk_send.at[which])
            for which in range(5)
        ]
        for load in loads:
            load.start()

    pieces = BLOCKS * CHUNKS

    def hidden_rows(index, pixel=0, count=chunk):
        return pl.ds(pl.multiple_of(index * chunk + pixel * views, 16), count)

    class Ring:
        def __init__(self, ref, start):
            self.ref, self.base = ref, start

        def rows(self, index, pixel=0, count=chunk):
            return pl.ds(
                pl.multiple_of(self.base + lax.rem(index, SLOTS) * chunk + pixel * views, 16), count
            )

        def copy(self, array, index, into):
            block, place = index // CHUNKS, lax.rem(index, CHUNKS)
            outer = array.at[
                pl.ds(pl.multiple_of(place * chunk, 16), chunk),
                pl.ds(pl.multiple_of(block * C_MID, LANES), C_MID),
            ]
            inner = self.ref.at[self.rows(index)]
            source, target = (outer, inner) if into else (inner, outer)
            return pltpu.make_async_copy(
                source, target, mem.stage_sem.at[0 if into else 1, lax.rem(index, SLOTS)]
            )

        def first_loads(self, array):
            for index in range(3):
                self.copy(array, index, True).start()

        def next_load(self, array, index):
            @pl.when(index + 3 < pieces)
            def _():
                self.copy(array, index + 3, True).start()

        def save(self, array, index):
            self.copy(array, index, False).start()

            @pl.when(index >= 2)
            def _():
                self.copy(array, index - 2, False).wait()

        def last_saves(self, array):
            for index in (pieces - 2, pieces - 1):
                self.copy(array, index, False).wait()

    stage_ref = mem.stage
    stage = Ring(stage_ref, 0)

    def piece_columns(index, part):
        return pl.ds(pl.multiple_of(index // CHUNKS * C_MID + part * LANES, LANES), LANES)

    features, slope_hbm = ins.features, outs.slope
    hidden_three = mem.h3

    def feature_copy(block, target):
        return pltpu.make_async_copy(
            features.at[:, pl.ds(block * C_MID, C_MID)], target, mem.column_sem.at[block]
        )

    feature_loads = [
        feature_copy(block, hidden_three.at[pl.ds(block * rows, rows)]) for block in range(BLOCKS)
    ]
    for copy in feature_loads:
        copy.start()
    stage.first_loads(features)

    padded_one, padded_two = mem.pad1, mem.pad2
    for padded in (padded_one, padded_two):
        for edge in (0, SIDE + 1):
            padded[edge] = jnp.zeros((padded.shape[1], C_MID), bf16)
        for edge in (0, SIDE + 1):
            padded[:, pl.ds(edge * views, views), :] = jnp.zeros((SIDE + 2, views, C_MID), bf16)
    rest = jnp.zeros((tall - rows, C_MID), bf16)
    for ref, end in ((mem.d1, rows), (mem.h2, rows), (mem.d2, rows), (mem.a2, rows), (hidden_three, BLOCKS * rows)):
        ref[end : end + tall - rows, :] = rest

    if plan.inside:
        norm_dp[1]()
        norm_out = []
        norm_in = []
        for step in range(1, plan.fsdp):
            partner = (fsdp_me + step) % plan.fsdp
            norm_out.append(
                pltpu.make_async_remote_copy(
                    src_ref=tiles.at[:, fsdp_me],
                    dst_ref=tiles.at[:, fsdp_me],
                    send_sem=mem.norm_s1.at[step],
                    recv_sem=mem.norm_r1.at[fsdp_me],
                    device_id={FSDP: partner},
                    device_id_type=pl.DeviceIdType.MESH,
                )
            )
            norm_in.append(
                pltpu.make_async_remote_copy(
                    src_ref=tiles.at[:, partner],
                    dst_ref=tiles.at[:, partner],
                    send_sem=mem.norm_s1.at[step],
                    recv_sem=mem.norm_r1.at[partner],
                    device_id={FSDP: partner},
                    device_id_type=pl.DeviceIdType.MESH,
                )
            )
        for copy in norm_out:
            copy.start()
        hook(21)
        for copy in norm_in:
            copy.wait_recv()
        for copy in norm_out:
            copy.wait_send()
        norm_all = mem.norm
        for dp_one in range(plan.dp):
            for fsdp_one in range(plan.fsdp):
                start = (dp_one * plan.fsdp + fsdp_one) * LANES
                norm_all[:, start : start + LANES] = tiles[dp_one, fsdp_one]
    else:
        for copy in loads:
            copy.wait()
        norm_all = mem.norm
        norm_all[...] = ins.norm[...]

    starts = (0, C_MID, 2 * C_MID, 2 * C_MID + C_IN, 2 * C_MID + C_IN + P_HID)

    def gain(layer):
        return norm_all[0:1, starts[layer] : starts[layer + 1]]

    coef, stats = mem.coef, mem.stats

    def norm_coefs(layer, totals, count, low=0):
        width = totals.shape[1]
        here, there = slice(low, low + width), slice(starts[layer] + low, starts[layer] + low + width)
        mean = totals[0:1] / count
        scaling = lax.rsqrt(totals[1:2] / count - mean * mean + norm_epsilon)
        slope = scaling * norm_all[0:1, there]
        stats[0:1, there] = mean
        stats[1:2, there] = scaling
        coef[0:1, here] = slope
        coef[1:2, here] = norm_all[1:2, there] - mean * slope

    def grad_coefs(layer, totals, count):
        width = starts[layer + 1] - starts[layer]
        mean = stats[0:1, starts[layer] : starts[layer + 1]]
        scaling = stats[1:2, starts[layer] : starts[layer + 1]]
        mem.norm_grads[0:1, starts[layer] : starts[layer + 1]] = totals[1:2]
        mem.norm_grads[1:2, starts[layer] : starts[layer + 1]] = totals[0:1]
        slope = scaling * gain(layer)
        bend = slope * scaling * totals[1:2] / count
        coef[0:1, :width] = slope
        coef[1:2, :width] = slope * totals[0:1] / count - mean * bend
        coef[2:3, :width] = bend

    def xhat_sum(layer, plain, product):
        mean = stats[0:1, starts[layer] : starts[layer + 1]]
        scaling = stats[1:2, starts[layer] : starts[layer + 1]]
        return scaling * (product - mean * plain)

    zero_row = jnp.zeros((1, C_MID), f32)

    def column_sums(value):
        return jnp.sum(value, axis=0, keepdims=True)

    def whole(which):
        value = weights[which][...]
        return value.reshape(-1, value.shape[-1])

    row_sums = mem.row_sums

    def clear_sums():
        row_sums[...] = jnp.zeros_like(row_sums)

    def count_in(cols, value, other):
        row_sums[0:1, cols] += column_sums(value)
        row_sums[1:2, cols] += column_sums(value * other)

    def own_columns(side):
        core = (c_me + side) % 2
        return [
            pl.ds(pl.multiple_of(half * (C_MID // 2) + core * LANES, LANES), LANES) for half in range(2)
        ]

    def turn_rows(ref):
        @pl.loop(0, tall // C_MID)
        def _(block):
            at = pl.ds(pl.multiple_of(block * C_MID, C_MID), C_MID)
            ref[at, :] = ref[at, :].T

    def turned(ref):
        return jnp.concatenate([ref[start : start + C_MID, :] for start in range(0, tall, C_MID)], axis=1)

    def sends_leave(which):
        for one in gathers:
            if one.which == which:
                one.leave()

    def turn_weight(which, block):
        ref = weights[which]
        if which == 1:
            groups = [block * 8 + group for group in range(8)]
            ats = [
                (group // 18, group // 9 % 2, pl.ds(pl.multiple_of(group % 9 * 64, 64), 64), everything)
                for group in groups
            ]
            value = jnp.concatenate([ref[at] for at in ats], axis=0).T
            for place, at in enumerate(ats):
                ref[at] = value[place * 64 : (place + 1) * 64, :]
        elif which == 3:
            for half in range(P_HID // C_MID):
                cols = slice(half * C_MID, (half + 1) * C_MID)
                value = ref[block, :, :, cols]
                ref[block, :, :, cols] = value.reshape(C_MID, C_MID).T.reshape(value.shape)
        else:
            value = ref[block]
            ref[block] = value.reshape(C_MID, C_MID).T.reshape(value.shape)

    hidden_one, slope_one = mem.h1, mem.d1
    hidden_two, slope_two = mem.h2, mem.d2
    act_two = mem.a2
    long = rows // 3

    def span(index):
        return pl.ds(pl.multiple_of(index * chunk, 16), chunk)

    def long_rows(block, index):
        return pl.ds(pl.multiple_of(block * rows + index * long, 16), long)

    def put_sides(ref, at, sides, hidden):
        for place, cols in enumerate(sides):
            part = hidden[:, place * LANES : (place + 1) * LANES]
            ref[at, cols] = part.astype(bf16)
            count_in(cols, part, part)

    for copy in feature_loads:
        copy.wait()
    clear_sums()

    @pl.loop(0, 2)
    def _(side):
        sides = own_columns(side)

        @pl.loop(0, 3)
        def _(index):
            left = jnp.concatenate([hidden_three[long_rows(block, index), :] for block in range(BLOCKS)], axis=1)
            right = jnp.concatenate([weights[0][:, :, :, cols].reshape(C_IN, LANES) for cols in sides], axis=1)
            put_sides(hidden_one, long_rows(0, index), sides, dot(left, right))

            hook_in(0, side * 3 + index, 6)

        @pl.when(side == 0)
        def _():
            cores_arrive(0)

    sum_one = Sum(0)
    sum_one.start(row_sums[0:1, :C_MID], row_sums[1:2, :C_MID])
    hook(1)
    sends_leave(0)
    pl.loop(0, 2)(lambda block: turn_weight(0, block))
    sum_one.middle()
    pl.loop(2, 4)(lambda block: turn_weight(0, block))
    hook(2)
    clear_sums()
    norm_coefs(0, sum_one.finish(), row_total)

    def activate(hidden_ref, slope_ref, put, site):
        @pl.loop(0, PIX)
        def _(pixel):
            place = pl.ds(pl.multiple_of(pixel * views, 16), views)
            for block in range(C_MID // LANES):
                cols = slice(block * LANES, (block + 1) * LANES)
                out = hidden_ref[place, cols].astype(f32) * coef[0:1, cols] + coef[1:2, cols]
                value, slope = gelu_pair(out)
                slope_ref[place, cols] = slope.astype(bf16)
                put(pixel, cols, value.astype(bf16))
            hook_in(site, pixel, SIDE, SIDE - 1, SIDE)

    def put_padded(padded):
        def put(pixel, cols, value):
            padded[pixel // SIDE + 1, pl.ds(pl.multiple_of((pixel % SIDE + 1) * views, 16), views), cols] = value

        return put

    activate(hidden_one, slope_one, put_padded(padded_one), 3)
    hook(4)

    def patch(padded, first, count, flip):
        found = []
        for vertical in range(3):
            for lateral in range(3):
                down, across = (2 - vertical, 2 - lateral) if flip else (vertical, lateral)
                piece = padded[pl.ds(first + down, count), across * views : across * views + chunk, :]
                found.append(piece.reshape(count * chunk, C_MID))
        return jnp.concatenate(found, axis=1)

    def image_rows(first, count):
        return pl.ds(pl.multiple_of(first * chunk, 16), count * chunk)

    def second_part(sides, first, count):
        right = jnp.concatenate([weights[1][:, :, :, cols].reshape(9 * C_MID, LANES) for cols in sides], axis=1)
        hidden = dot(patch(padded_one, first, count, False), right)
        put_sides(hidden_two, image_rows(first, count), sides, hidden)

    @pl.loop(0, 2)
    def _(side):
        sides = own_columns(side)

        @pl.loop(0, 3)
        def _(index):
            second_part(sides, 2 * index, 2)
            hook_in(5, side * 4 + index, 8)

        second_part(sides, 6, 1)

        @pl.when(side == 0)
        def _():
            cores_arrive(1)

    sum_two = Sum(1)
    sum_two.start(row_sums[0:1, :C_MID], row_sums[1:2, :C_MID])
    hook(6)
    sends_leave(1)
    pl.loop(0, 4)(lambda block: turn_weight(1, block))
    sum_two.middle()
    pl.loop(4, 9)(lambda block: turn_weight(1, block))
    hook(7)
    clear_sums()
    norm_coefs(1, sum_two.finish(), row_total)

    def put_rows(pixel, cols, value):
        act_two[pl.ds(pl.multiple_of(pixel * views, 16), views), cols] = value

    activate(hidden_two, slope_two, put_rows, 8)
    cores_arrive(2)

    def weight_three(block):
        return weights[2][block].reshape(C_MID, C_MID)

    sums_low, sums_high = Sum(2), Sum(3)
    half_width = C_IN // 2

    @pl.loop(0, BLOCKS)
    def _(block):
        cols = pl.ds(pl.multiple_of(block * C_MID, LANES), C_MID)

        @pl.loop(0, 3)
        def _(index):
            hidden = dot(act_two[long_rows(0, index), :], weight_three(block))
            hidden_three[long_rows(block, index), :] = hidden.astype(bf16)
            count_in(cols, hidden, hidden)
            hook_in(9, block * 3 + index, 12)

        @pl.when(block == 1)
        def _():
            sums_low.start(row_sums[0:1, :half_width], row_sums[1:2, :half_width])

        @pl.when(block == 2)
        def _():
            sums_low.middle()

    sums_high.start(row_sums[0:1, half_width:], row_sums[1:2, half_width:])
    norm_coefs(2, sums_low.finish(), row_total)

    hook(22)

    pool, pool_slope, pool_bend = mem.pool, mem.pool_slope, mem.pool_bend
    for ref in (pool, pool_slope, pool_bend):
        ref[...] = jnp.zeros_like(ref)

    @pl.loop(0, pieces)
    def _(index):
        stage.copy(features, index, True).wait()

        @pl.loop(0, C_MID // LANES)
        def _(part):
            inner = pl.ds(pl.multiple_of(part * LANES, LANES), LANES)
            cols = piece_columns(index, part)
            slope_row, shift_row = coef[0:1, cols], coef[1:2, cols]
            kept = (pool[:, cols], pool_slope[:, cols], pool_bend[:, cols])
            for pixel in range(SIDE):
                stage_at, hidden_at = stage.rows(index, pixel, views), hidden_rows(index, pixel, views)
                hidden = hidden_three[hidden_at, inner].astype(f32)
                total = hidden * slope_row + shift_row + stage_ref[stage_at, inner].astype(f32)
                value, slope = gelu_pair(total)
                stage_ref[stage_at, inner] = slope.astype(bf16)
                kept = (kept[0] + value, kept[1] + slope, kept[2] + slope * hidden)
            pool[:, cols], pool_slope[:, cols], pool_bend[:, cols] = kept

        stage.save(slope_hbm, index)
        stage.next_load(features, index)

        @pl.when(index == 2)
        def _():
            sums_high.middle()

        @pl.when(index == pieces // 2 - 1)
        def _():
            norm_coefs(2, sums_high.finish(), row_total, half_width)

        hook_in(10, index, pieces)

    stage.last_saves(slope_hbm)
    cores_arrive(3)
    cores_arrive(4)
    for which in range(2, 5):
        sends_leave(which)

    pooled = (pool[...] * (1.0 / PIX)).astype(bf16)
    mem.pooled[...] = pooled
    if plan.inside:
        wide_at = C_IN // plan.fsdp
        low_at = P_HID // plan.dp
        left_rooms, right_rooms = mem.left_rooms, mem.right_rooms

        def wide_columns(fsdp_one):
            return pl.ds(pl.multiple_of(fsdp_one * wide_at, LANES), wide_at)

        def low_columns(dp_one):
            return pl.ds(pl.multiple_of(dp_one * low_at, LANES), low_at)

        sems = mem.factor_sems
        left_first = share(
            FSDP, plan.fsdp, fsdp_me, lambda to: mem.pooled.at[:, wide_columns(to)], left_rooms.at[dp_me], sems.at[0], sems.at[1]
        )
        left_second = share(
            DP, plan.dp, dp_me, lambda _: left_rooms.at[dp_me], left_rooms, sems.at[2], sems.at[3]
        )
        right_first = share(
            DP, plan.dp, dp_me, lambda to: mem.four_low.at[:, low_columns(to)], right_rooms.at[fsdp_me], sems.at[4], sems.at[5]
        )
        right_second = share(
            FSDP, plan.fsdp, fsdp_me, lambda _: right_rooms.at[fsdp_me], right_rooms, sems.at[6], sems.at[7]
        )
        left_rooms[dp_me, fsdp_me] = mem.pooled[:, wide_columns(fsdp_me)]

    proj_hidden = dot(pooled, whole(3))
    sum_four = Sum(4)
    sum_four.start(column_sums(proj_hidden), column_sums(proj_hidden * proj_hidden))
    pl.loop(0, 2)(lambda block: turn_weight(3, block))
    sum_four.middle()
    pl.loop(2, 4)(lambda block: turn_weight(3, block))
    totals = sum_four.finish()
    stage.first_loads(slope_hbm)
    norm_coefs(3, totals, view_total)
    value, slope = gelu_pair(proj_hidden * coef[0:1, :P_HID] + coef[1:2, :P_HID])
    proj_act = value.astype(bf16)
    mem.proj_act[...] = proj_act
    mem.proj_slope[...] = slope
    mem.proj_hidden[...] = proj_hidden

    def weight_five(block):
        return weights[4][block // plan.x, block % plan.x]

    parts = P_HID // P_OUT
    embedding = jnp.zeros((views, P_OUT), f32)
    for block in range(parts):
        embedding = embedding + dot_cols(proj_act[:, block * P_OUT : (block + 1) * P_OUT], weight_five(block))

    images = views // 2
    order = jnp.broadcast_to(ins.order[...], (images, views))
    image_row = lax.broadcasted_iota(jnp.int32, (images, views), 0)
    selectors = [(order == 2 * image_row + which).astype(f32) for which in range(2)]
    embeds = [exact_dot(selector, embedding) for selector in selectors]
    moments = [exact_rows(embed, embed) for embed in embeds]
    packed, diagonal = pack_pair(*moments)
    packed, extra = sum_matrix(0, packed, [diagonal] + [column_sums(embed) for embed in embeds])
    moments = unpack_pair(packed, extra[0])
    eye = (
        lax.broadcasted_iota(jnp.int32, (P_OUT, P_OUT), 0) == lax.broadcasted_iota(jnp.int32, (P_OUT, P_OUT), 1)
    ).astype(f32)
    centred, covariances = [], []
    for which in range(2):
        mean = extra[1 + which] / image_total
        centred.append(embeds[which] - mean)
        covariances.append(moments[which] / image_total - exact_rows(mean, mean) + ridge_term * eye)
    inverses = inverse_factors(covariances)
    whitened = [exact_cols(centred[which], inverses[which]) for which in range(2)]
    scalings = [
        lax.rsqrt(jnp.mean(white * white, axis=1, keepdims=True) + norm_epsilon) for white in whitened
    ]
    units = [white * scaling for white, scaling in zip(whitened, scalings)]
    difference = units[0] - units[1]
    objective_row = column_sums(difference * difference) * (1.0 / P_OUT)
    unit_grads = [difference * (2.0 / P_OUT), difference * (-2.0 / P_OUT)]
    white_grads = []
    for which in range(2):
        inner = jnp.mean(whitened[which] * unit_grads[which], axis=1, keepdims=True)
        white_grads.append(
            scalings[which] * unit_grads[which] - whitened[which] * (scalings[which] ** 3 * inner)
        )
    directs = [exact_dot(white_grads[which], inverses[which]) for which in range(2)]
    products = [exact_rows(white_grads[which], whitened[which]) for which in range(2)]
    packed, diagonal = pack_pair(*products)
    packed, extra = sum_matrix(
        1, packed, [diagonal] + [column_sums(grad) for grad in white_grads] + [objective_row]
    )
    products = unpack_pair(packed, extra[0])
    embed_grad = jnp.zeros((views, P_OUT), f32)
    for which in range(2):
        symmetric = exact_rows(inverses[which], exact_dot(products[which], inverses[which]))
        mean_grad = exact_dot(extra[1 + which], inverses[which])
        grad = directs[which] - (exact_dot(centred[which], symmetric) + mean_grad) / image_total
        embed_grad = embed_grad + exact_rows(selectors[which], grad)
    objective_row = extra[3]
    embed_low = embed_grad.astype(bf16)

    proj_act, proj_hidden = mem.proj_act[...], mem.proj_hidden[...]
    act_grad = jnp.concatenate([dot(embed_low, weight_five(block)) for block in range(parts)], axis=1)
    upstream = act_grad * mem.proj_slope[...]
    plain = column_sums(upstream)
    sum_four_back = Sum(5)
    sum_four_back.start(plain, xhat_sum(3, plain, column_sums(upstream * proj_hidden)))
    for block in range(parts):
        weights[4][block // plan.x, block % plan.x] = dot_rows(
            embed_low, proj_act[:, block * P_OUT : (block + 1) * P_OUT]
        ).astype(bf16)
    pl.loop(0, 4)(lambda block: turn_weight(2, block))
    sum_four_back.middle()
    turn_rows(act_two)
    grad_coefs(3, sum_four_back.finish(), view_total)
    four_low = (
        upstream * coef[0:1, :P_HID] - coef[1:2, :P_HID] - proj_hidden * coef[2:3, :P_HID]
    ).astype(bf16)
    mem.four_low[...] = four_low
    if plan.inside:
        right_rooms[fsdp_me, dp_me] = mem.four_low[:, low_columns(dp_me)]

    @pl.loop(0, BLOCKS)
    def _(block):
        cols = pl.ds(pl.multiple_of(block * C_MID, LANES), C_MID)
        right = jnp.concatenate(
            [
                weights[3][block, :, :, half * C_MID : (half + 1) * C_MID].reshape(C_MID, C_MID)
                for half in range(P_HID // C_MID)
            ],
            axis=0,
        )
        grad = dot(four_low, right) * (1.0 / PIX)
        row_sums[0:1, cols] = column_sums(grad * pool_slope[:, cols])
        row_sums[1:2, cols] = column_sums(grad * pool_bend[:, cols])
        pool_slope[:, cols] = grad

    plain = row_sums[0:1, :]
    sum_three_back = Sum(6)
    sum_three_back.start(plain, xhat_sum(2, plain, row_sums[1:2, :]))
    if not plan.inside:
        grad_four = dot_rows(mem.pooled[...], four_low).astype(bf16)
        weights[3][...] = grad_four.reshape(weights[3].shape)
    sum_three_back.middle()
    hook(23)
    grad_coefs(2, sum_three_back.finish(), row_total)
    pool[...] = pool_slope[...] * coef[0:1, :]

    if plan.inside:
        left_first[0]()
        right_first[0]()
    clear_sums()

    @pl.loop(0, pieces)
    def _(index):
        stage.copy(slope_hbm, index, True).wait()
        stage.next_load(slope_hbm, index)

        @pl.loop(0, C_MID // LANES)
        def _(part):
            inner = pl.ds(pl.multiple_of(part * LANES, LANES), LANES)
            cols = piece_columns(index, part)
            spread, shift_row, bend_row = pool[:, cols], coef[1:2, cols], coef[2:3, cols]
            for pixel in range(SIDE):
                hidden_at = hidden_rows(index, pixel, views)
                hidden = hidden_three[hidden_at, inner].astype(f32)
                slope = stage_ref[stage.rows(index, pixel, views), inner].astype(f32)
                hidden_three[hidden_at, inner] = (slope * spread - shift_row - hidden * bend_row).astype(bf16)

        hook_in(11, index, pieces)
        if plan.inside:

            @pl.when(index == pieces // 2)
            def _():
                left_first[1]()
                left_second[0]()
                right_first[1]()
                right_second[0]()

    @pl.loop(0, 3)
    def _(index):
        at = long_rows(0, index)
        left = jnp.concatenate([hidden_three[long_rows(block, index), :] for block in range(BLOCKS)], axis=1)
        upstream = dot(left, weights[2][...].reshape(C_IN, C_MID)) * slope_two[at, :].astype(f32)
        slope_two[at, :] = upstream.astype(bf16)
        count_in(slice(0, C_MID), upstream, hidden_two[at, :].astype(f32))
        hook_in(12, index, 3)

    sums = row_sums[0:1, :C_MID], row_sums[1:2, :C_MID]
    sum_two_back = Sum(7)
    sum_two_back.start(sums[0], xhat_sum(1, *sums))

    @pl.loop(0, BLOCKS)
    def _(block):
        grad = dot(turned(act_two), hidden_three[pl.ds(pl.multiple_of(block * rows, 16), tall), :])
        weights[2][block] = grad.astype(bf16).reshape(plan.z, plan.x, -1, C_MID)

        @pl.when(block == 1)
        def _():
            sum_two_back.middle()

        hook_in(13, block, BLOCKS)

    clear_sums()
    grad_coefs(1, sum_two_back.finish(), row_total)

    def apply_grad(hidden_ref, grad_ref, put, site):
        @pl.loop(0, PIX)
        def _(pixel):
            place = pl.ds(pl.multiple_of(pixel * views, 16), views)
            for block in range(C_MID // LANES):
                cols = slice(block * LANES, (block + 1) * LANES)
                grad = (
                    grad_ref[place, cols].astype(f32) * coef[0:1, cols]
                    - coef[1:2, cols]
                    - hidden_ref[place, cols].astype(f32) * coef[2:3, cols]
                )
                put(pixel, cols, grad.astype(bf16))
            hook_in(site, pixel, SIDE, SIDE - 1, SIDE)

    def put_two(pixel, cols, value):
        put_padded(padded_two)(pixel, cols, value)
        slope_two[pl.ds(pl.multiple_of(pixel * views, 16), views), cols] = value

    apply_grad(hidden_two, slope_two, put_two, 14)
    if plan.inside:
        left_second[1]()
        right_second[1]()
        order_all = [(dp_one, fsdp_one) for dp_one in range(plan.dp) for fsdp_one in range(plan.fsdp)]
        left = jnp.concatenate([left_rooms[dp_one, fsdp_one] for dp_one, fsdp_one in order_all], axis=0)
        right = jnp.concatenate([right_rooms[fsdp_one, dp_one] for dp_one, fsdp_one in order_all], axis=0)
        put_gradient(3, dot_rows(left, right))
    turn_rows(slope_two)
    column_places = [
        hidden_three.at[pl.ds(2 * rows, rows)],
        hidden_three.at[pl.ds(3 * rows, rows)],
        hidden_two.at[pl.ds(0, rows)],
        hidden_three.at[pl.ds(2 * rows, rows)],
    ]
    column_loads = [feature_copy(block, column_places[block]) for block in range(BLOCKS)]
    for copy in column_loads[:3]:
        copy.start()
    def tap_grad(tap):
        down, across = tap // 3, tap % 3
        left = padded_one[pl.ds(down, SIDE), pl.ds(pl.multiple_of(across * views, 16), chunk), :]
        right = jnp.concatenate([left.reshape(rows, C_MID), jnp.zeros((tall - rows, C_MID), bf16)], axis=0)
        grad = dot(turned(slope_two), right).astype(bf16).T
        stage_ref[pl.ds(pl.multiple_of(tap * C_MID, 16), C_MID), :] = grad

    @pl.loop(0, 7)
    def _(tap):
        tap_grad(tap)
        hook_in(15, tap, 7)

    def second_back(first, count):
        at = image_rows(first, count)
        upstream = dot(patch(padded_two, first, count, True), weights[1][...].reshape(9 * C_MID, C_MID))
        upstream = upstream * slope_one[at, :].astype(f32)
        slope_one[at, :] = upstream.astype(bf16)
        count_in(slice(0, C_MID), upstream, hidden_one[at, :].astype(f32))

    @pl.loop(0, 3)
    def _(index):
        second_back(2 * index, 2)
        hook_in(16, index, 3)

    second_back(6, 1)
    hook(16, 3)
    sums = row_sums[0:1, :C_MID], row_sums[1:2, :C_MID]
    sum_one_back = Sum(8)
    sum_one_back.start(sums[0], xhat_sum(0, *sums))

    @pl.loop(7, 9)
    def _(tap):
        tap_grad(tap)

        @pl.when(tap == 7)
        def _():
            sum_one_back.middle()

        hook_in(17, tap, 2, 7)

    grad_coefs(0, sum_one_back.finish(), row_total)

    def put_one(pixel, cols, value):
        put_rows(pixel, cols, value)
        slope_one[pl.ds(pl.multiple_of(pixel * views, 16), views), cols] = value

    apply_grad(hidden_one, slope_one, put_one, 18)
    turn_rows(slope_one)

    def block_grad(block):
        if block != 1:
            column_loads[block].wait()
        start = 3 * rows if block == 1 else 2 * rows
        right = hidden_two[...] if block == 2 else hidden_three[start : start + tall, :]
        grad = dot(turned(slope_one), right).astype(bf16).T
        mem.g1[block] = grad.reshape(plan.x, -1, C_MID)

    column_loads[1].wait()
    tail = Ring(hidden_two, 0)
    for block in range(BLOCKS):
        block_grad(block)
        if block == 0:
            column_loads[3].start()
        hook(19, block)
        if block == 2:
            tail.first_loads(slope_hbm)

    sum_last = Sum(9)

    @pl.loop(0, pieces)
    def _(index):
        block = index // CHUNKS
        back = dot(act_two[span(lax.rem(index, CHUNKS)), :], weights[0][block].reshape(C_MID, C_MID))
        tail.copy(slope_hbm, index, True).wait()
        cols = pl.ds(pl.multiple_of(block * C_MID, LANES), C_MID)
        for pixel in range(SIDE):
            at = tail.rows(index, pixel, views)
            summed = hidden_two[at, :].astype(f32) * pool_slope[:, cols]
            hidden_two[at, :] = (summed + back[pixel * views : (pixel + 1) * views]).astype(bf16)
        tail.save(outs.features_grad, index)
        tail.next_load(slope_hbm, index)
        hook_in(20, index, pieces)
        if plan.inside:

            @pl.when(index == LAST_SUM)
            def _():
                sum_last.start(mem.squares[...], mem.squares[...])

            @pl.when(index == LAST_SUM + 3)
            def _():
                sum_last.middle()

    tail.last_saves(outs.features_grad)
    squares = mem.squares[...]
    if plan.inside:
        squares = sum_last.finish()[0:1]
    norm_grads = mem.norm_grads[...]
    scalars = outs.scalars
    norm_squares = column_sums(norm_grads * norm_grads)
    for place in range(norm_squares.shape[1] // LANES):
        squares = squares + norm_squares[:, place * LANES : (place + 1) * LANES]
    scalars[...] = jnp.zeros_like(scalars)
    squares = jnp.sum(squares, axis=1, keepdims=True)
    norm = jnp.sqrt(squares)
    found = (jnp.sum(objective_row, axis=1, keepdims=True) / image_total, squares, norm, clip_factor(norm))
    for place, value in enumerate(found):
        scalars[place : place + 1, :] = jnp.broadcast_to(value, (1, LANES))
    if plan.inside:
        owner = (dp_me * plan.fsdp + fsdp_me) * LANES
        outs.norm_grad[...] = mem.norm_grads[:, pl.ds(pl.multiple_of(owner, LANES), LANES)]
    else:
        outs.norm_grad[...] = norm_grads
    if not plan.inside:
        stores = [
            pltpu.make_async_copy(gradients[which], outs.grads[which], mem.bulk_send.at[which])
            for which in range(5)
        ]
        for store in stores:
            store.start()
        for store in stores:
            store.wait()


def weight_shapes():
    return (
        (4, 2, 256, C_MID),
        (4, 2, 576, C_MID),
        (BLOCKS, 4, 2, 64, C_MID),
        (4, 2, 256, P_HID),
        (4, 2, P_OUT, P_OUT),
    )


def run_kernel(plan, features, order, shards, norm):
    rows, views = plan.rows, plan.views
    in_vmem = pl.BlockSpec(memory_space=pltpu.VMEM)
    anywhere = pl.BlockSpec(memory_space=pl.ANY)
    shapes = weight_shapes()
    operands = [features, order, norm, *shards]
    in_specs = [anywhere, in_vmem, in_vmem] + [in_vmem if plan.inside else anywhere] * 5
    results = [
        ((rows, C_IN), bf16, anywhere),
        ((rows, C_IN), bf16, anywhere),
        (norm.shape, f32, in_vmem),
        ((8, LANES), f32, in_vmem),
    ]
    for which, shard in enumerate(shards):
        if plan.inside:
            results.append((shard.shape, f32, in_vmem))
        else:
            results.append(((9 * C_MID, C_MID) if which == 1 else shapes[which], bf16, anywhere))
    dma = pltpu.SemaphoreType.DMA

    def sum_room(width):
        return SumRoom(
            pltpu.VMEM((plan.dp, 2, width), f32),
            pltpu.VMEM((plan.fsdp, 2, width), f32),
            dma((plan.dp,)),
            dma((plan.dp,)),
            dma((plan.fsdp,)),
            dma((plan.fsdp,)),
        )

    def matrix_room():
        size = plan.embed_rows
        return MatrixRoom(
            pltpu.VMEM((plan.dp, size, P_OUT), f32),
            pltpu.VMEM((plan.dp, size, P_OUT), f32),
            pltpu.VMEM((plan.fsdp, size, P_OUT), f32),
            pltpu.VMEM((plan.dp, size, P_OUT), f32),
            dma((plan.dp,)),
            dma((plan.dp,)),
            dma((plan.fsdp,)),
            dma((plan.fsdp,)),
            dma((plan.dp,)),
            dma((plan.dp,)),
        )

    scratch = Mem(
        w=[pltpu.VMEM(shape, bf16) for shape in shapes],
        g1=pltpu.VMEM(shapes[0], bf16),
        row_sums=pltpu.VMEM((2, C_IN), f32),
        r3=pltpu.VMEM(shapes[2], bf16),
        r1=pltpu.VMEM(shapes[0], bf16),
        left_rooms=pltpu.VMEM((plan.dp, plan.fsdp, views, C_IN // plan.fsdp) if plan.inside else (8, LANES), bf16),
        right_rooms=pltpu.VMEM((plan.fsdp, plan.dp, views, P_HID // plan.dp) if plan.inside else (8, LANES), bf16),
        factor_sems=dma((8, max(plan.dp, plan.fsdp))),
        four_low=pltpu.VMEM((views, P_HID), bf16),
        r5=pltpu.VMEM(shapes[4], bf16),
        stage=pltpu.VMEM((max(SLOTS * plan.chunk, 9 * C_MID), C_MID), bf16),
        stage_sem=dma((2, SLOTS)),
        column_sem=dma((BLOCKS,)),
        h1=pltpu.VMEM((rows, C_MID), bf16),
        d1=pltpu.VMEM((plan.tall, C_MID), bf16),
        h2=pltpu.VMEM((plan.tall, C_MID), bf16),
        d2=pltpu.VMEM((plan.tall, C_MID), bf16),
        a2=pltpu.VMEM((plan.tall, C_MID), bf16),
        h3=pltpu.VMEM((3 * rows + plan.tall, C_MID), bf16),
        pad1=pltpu.VMEM((SIDE + 2, (SIDE + 2) * views, C_MID), bf16),
        pad2=pltpu.VMEM((SIDE + 2, (SIDE + 2) * views, C_MID), bf16),
        pool=pltpu.VMEM((views, C_IN), f32),
        pool_slope=pltpu.VMEM((views, C_IN), f32),
        pool_bend=pltpu.VMEM((views, C_IN), f32),
        pooled=pltpu.VMEM((views, C_IN), bf16),
        proj_act=pltpu.VMEM((views, P_HID), bf16),
        proj_slope=pltpu.VMEM((views, P_HID), f32),
        proj_hidden=pltpu.VMEM((views, P_HID), f32),
        coef=pltpu.VMEM((8, C_IN), f32),
        stats=pltpu.VMEM((2, norm_width()), f32),
        norm=pltpu.VMEM((2, norm_width()), f32),
        norm_grads=pltpu.VMEM((2, norm_width()), f32),
        norm_tiles=pltpu.VMEM((plan.dp, plan.fsdp, 2, LANES), f32),
        norm_s0=dma((plan.dp,)),
        norm_r0=dma((plan.dp,)),
        norm_s1=dma((plan.fsdp,)),
        norm_r1=dma((plan.fsdp,)),
        bulk_send=dma((COPIES,)),
        bulk_recv=dma((COPIES,)),
        mats=[matrix_room(), matrix_room()],
        sums=[
            sum_room(width)
            for width in (C_MID, C_MID, C_IN // 2, C_IN // 2, P_HID, C_IN, LANES)
        ],
        squares=pltpu.VMEM((1, LANES), f32),
    )
    values = pl.pallas_call(
        lambda *refs: kernel(plan, *refs),
        out_shape=[jax.ShapeDtypeStruct(shape, kind) for shape, kind, _ in results],
        in_specs=in_specs,
        out_specs=[spec for _, _, spec in results],
        scratch_shapes=[scratch],
        compiler_params=pltpu.CompilerParams(
            collective_id=1, has_side_effects=True, vmem_limit_bytes=63 * 2**20
        ),
        name="train_step",
    )(*operands)
    return Outs(*values[:4], values[4:])


def norm_width():
    return 2 * C_MID + C_IN + P_HID


def clip_factor(norm):
    return clip_level / jnp.maximum(norm, clip_level)


def adam_update(weight, moment_one, moment_two, gradient, step_rate, weight_decay):
    first_new = beta_first * moment_one + (1.0 - beta_first) * gradient
    second_new = beta_second * moment_two + (1.0 - beta_second) * gradient * gradient
    first_hat = first_new / (1.0 - beta_first**STEP)
    second_hat = second_new / (1.0 - beta_second**STEP)
    weight_new = weight - step_rate * (
        first_hat / (jnp.sqrt(second_hat) + adam_epsilon) + weight_decay * weight
    )
    return (weight_new, first_new, second_new)


def finish_kernel(rates, decays, *refs):
    count = len(rates)
    low, scalars = refs[0], refs[1]
    refs = refs[2:]
    given, wide, loss, norm, updated = refs[: 4 * count], *refs[4 * count : 4 * count + 3], refs[4 * count + 3 : -2]
    rooms, sems = refs[-2], refs[-1]
    wide[...] = low[...].astype(f32)
    step = pl.program_id(0)

    def load(place):
        return pltpu.make_async_copy(given[place], rooms[place], sems.at[place])

    def store(place):
        return pltpu.make_async_copy(rooms[place], updated[place], sems.at[place])

    @pl.when(step == 0)
    def _():
        loss[0, 0] = scalars[0, 0]
        norm[0, 0] = scalars[2, 0]
        for place in range(4 * count):
            load(place).start()

    @pl.when(step == 2)
    def _():
        for place in range(4 * count):
            load(place).wait()
        for place in range(count):
            weight, first, second, grad = (rooms[part * count + place][...] for part in range(4))
            found = adam_update(weight, first, second, grad * scalars[3, 0], rates[place], decays[place])
            for part in range(3):
                rooms[part * count + place][...] = found[part]
        for place in range(3 * count):
            store(place).start()

    @pl.when(step == CHUNKS - 1)
    def _():
        for place in range(3 * count):
            store(place).wait()


def finish(features_grad, scalars, masters, firsts, seconds, grads, rates, decays):
    rows = features_grad.shape[0]
    arrays = [*masters, *firsts, *seconds, *grads]
    moving = pl.BlockSpec((rows // CHUNKS, C_IN), lambda index: (index, 0))
    single = pl.BlockSpec(memory_space=pltpu.SMEM)
    anywhere = pl.BlockSpec(memory_space=pl.ANY)
    count = len(masters)
    values = pl.pallas_call(
        lambda *refs: finish_kernel(rates, decays, *refs),
        grid=(CHUNKS,),
        in_specs=[moving, single] + [anywhere] * (4 * count),
        out_specs=[moving, single, single] + [anywhere] * (3 * count),
        out_shape=[jax.ShapeDtypeStruct((rows, C_IN), f32)]
        + [jax.ShapeDtypeStruct((1, 1), f32)] * 2
        + [jax.ShapeDtypeStruct(array.shape, f32) for array in arrays[: 3 * count]],
        scratch_shapes=[
            [pltpu.VMEM(array.shape, f32) for array in arrays],
            pltpu.SemaphoreType.DMA((4 * count,)),
        ],
        compiler_params=pltpu.CompilerParams(vmem_limit_bytes=62 * 2**20),
        name="finish",
    )(features_grad, scalars, *arrays)
    groups = [values[3 + part * count : 3 + (part + 1) * count] for part in range(3)]
    return values[0], values[1].reshape(()), values[2].reshape(()), *groups


def gather_full(weight):
    outer = lax.all_gather(weight.astype(bf16), FSDP, axis=0, tiled=True)
    return lax.all_gather(outer, DP, axis=1, tiled=True)


def scatter_full(gradient):
    inner = lax.psum_scatter(gradient.astype(f32), DP, scatter_dimension=1, tiled=True)
    return lax.psum_scatter(inner, FSDP, scatter_dimension=0, tiled=True)


def body(features, view_order, *state):
    masters, firsts, seconds = state[:6], state[6:12], state[12:18]
    dp_size, fsdp_size = lax.axis_size(DP), lax.axis_size(FSDP)
    views = features.shape[0]
    inside = dp_size == 4 and fsdp_size == 8
    plan = Plan(dp_size, fsdp_size, views, inside)
    pixels = jnp.swapaxes(features, 0, 1).reshape(-1, C_IN)
    norm_params = masters[5]
    shapes = weight_shapes()
    if inside:
        shards = list(masters[:4]) + [masters[4].T]
        norm = norm_params
    else:
        full = [gather_full(weight) for weight in masters[:5]]
        shards = [
            full[0].reshape(shapes[0]),
            full[1].reshape(shapes[1]),
            full[2].reshape(C_MID, BLOCKS, C_MID).swapaxes(0, 1).reshape(shapes[2]),
            full[3].reshape(shapes[3]),
            full[4].reshape(4, 2, P_OUT, P_OUT).swapaxes(2, 3),
        ]
        norm = lax.all_gather(norm_params.astype(bf16), (DP, FSDP), axis=1, tiled=True).astype(f32)
    got = run_kernel(plan, pixels, view_order, shards, norm)
    grads = list(got.grads)
    scalars = got.scalars
    turned = [list(group) for group in (masters, firsts, seconds)]
    if inside:
        owned = grads
        for group in turned:
            group[4] = group[4].T
    else:
        whole_grads = [
            grads[0].reshape(C_IN, C_MID),
            grads[1],
            grads[2].reshape(BLOCKS, C_MID, C_MID).swapaxes(0, 1).reshape(C_MID, C_IN),
            grads[3].reshape(C_IN, P_HID),
            grads[4].swapaxes(2, 3).reshape(P_HID, P_OUT),
        ]
        owned = [scatter_full(gradient) for gradient in whole_grads]
        squares = scalars[1, 0] + lax.psum(sum(jnp.sum(grad * grad) for grad in owned), (DP, FSDP))
        norm_value = jnp.sqrt(squares)
        scalars = scalars.at[2].set(norm_value).at[3].set(clip_factor(norm_value))
    width = norm_params.shape[1]
    if inside:
        owned.append(got.norm_grad)
    else:
        owner = lax.axis_index((DP, FSDP))
        owned.append(lax.dynamic_slice_in_dim(got.norm_grad, owner * width, width, 1))
    step_rates = (
        C_IN ** (-0.5),
        (9 * C_MID) ** (-0.5),
        C_MID ** (-0.5),
        C_IN ** (-0.5),
        P_HID ** (-0.5),
        norm_rate,
    )
    decays = (decay_rate, decay_rate, decay_rate, decay_rate, decay_rate, 0.0)
    input_grad, loss, grad_norm, *updates = finish(
        got.features_grad, scalars, *turned, owned, step_rates, decays
    )
    if inside:
        updates = [[*group[:4], group[4].T, group[5]] for group in updates]
    return (
        loss,
        jnp.swapaxes(input_grad.reshape(PIX, views, C_IN), 0, 1),
        grad_norm,
        *updates[0],
        *updates[1],
        *updates[2],
    )


def solution(mesh):
    views = P((DP, FSDP), None, None)
    split = P(FSDP, DP)
    norm = P(None, (DP, FSDP))
    params = (split,) * 5 + (norm,)
    return jax.shard_map(
        body,
        mesh=mesh,
        in_specs=(views, P((DP, FSDP), None)) + params * 3,
        out_specs=(P(), views, P()) + params * 3,
        check_vma=False,
    )
```
